32 devices in a mesh: seq: 16 (over z, y, x), batch: 2 (over core).
Axes of the slice: x: 2, y: 2, z: 4, core: 2. Of those that a mesh axis runs over, the one named last changes fastest.
Arguments:
- tokens: bfloat16 [4, 1024, 2304], P('batch', 'seq'), may hold values from -6 to 6
- segments: int32 [4, 1024], P('batch', 'seq'), may hold values from 0 to 8, as said below
- positions: int32 [4, 1024], P('batch', 'seq'), may hold values from 0 to 1023, as said below
- cotangent: bfloat16 [4, 1024, 2304], P('batch', 'seq'), may hold values from -6 to 6
- query_codes: int32 [2304, 2048], P('seq'), may hold values from -128 to 127
- key_codes: int32 [2304, 1024], P('seq'), may hold values from -128 to 127
- value_codes: int32 [2304, 1024], P('seq'), may hold values from -128 to 127
- output_codes: int32 [2048, 2304], P('seq'), may hold values from -128 to 127
- gate_codes: int32 [2304, 9216], P('seq'), may hold values from -128 to 127
- up_codes: int32 [2304, 9216], P('seq'), may hold values from -128 to 127
- down_codes: int32 [9216, 2304], P('seq'), may hold values from -128 to 127
- query_scale: float32 [2048], replicated, may hold values from 0.00014 to 0.0014
- key_scale: float32 [1024], replicated, may hold values from 0.00014 to 0.0014
- value_scale: float32 [1024], replicated, may hold values from 0.00014 to 0.00056
- output_scale: float32 [2304], replicated, may hold values from 0.00015 to 0.0006
- gate_scale: float32 [9216], replicated, may hold values from 0.00014 to 0.00056
- up_scale: float32 [9216], replicated, may hold values from 0.00014 to 0.00056
- down_scale: float32 [2304], replicated, may hold values from 7e-05 to 0.00028
- attention_gain: float32 [2304], replicated, may hold values from 0.1 to 1.9
- attention_post_gain: float32 [2304], replicated, may hold values from 0.1 to 1.9
- feed_gain: float32 [2304], replicated, may hold values from 0.1 to 1.9
- feed_post_gain: float32 [2304], replicated, may hold values from 0.1 to 1.9
Outputs:
- out_tokens: bfloat16 [4, 1024, 2304], P('batch', 'seq')
- grad_tokens: bfloat16 [4, 1024, 2304], P('batch', 'seq')
- grad_query: float32 [2304, 2048], P('seq')
- grad_key: float32 [2304, 1024], P('seq')
- grad_value: float32 [2304, 1024], P('seq')
- grad_output: float32 [2048, 2304], P('seq')
- grad_gate: float32 [2304, 9216], P('seq')
- grad_up: float32 [2304, 9216], P('seq')
- grad_down: float32 [9216, 2304], P('seq')
- grad_attention_gain: float32 [2304], replicated
- grad_attention_post: float32 [2304], replicated
- grad_feed_gain: float32 [2304], replicated
- grad_feed_post: float32 [2304], replicated
The draws below stay inside these ranges and needn't reach their ends.
Inputs may be any that keep to these rules, and one draw needn't show every extreme that they name: `segments`: along each sequence the numbers start at 0, never fall and rise by one where a document begins; in each group of 2 sequences on one index of batch, one sequence is a single document, and the other sequence holds exactly 9 documents. `positions`: A token's index in its sequence minus the index of the first token of its document (the first token with the same segment number).
All inputs are finite; a program needn't handle non-finite values.
Results may differ from the reference program's by a relative error of at most 0.024.
Values may be sent and summed in bfloat16 or wider, within the bound.
A program may use at most 1.1875 GiB of HBM per device.

```python
import math
import jax
import jax.numpy as jnp
from jax import lax

D = 2304
HEADS = 8
KV_HEADS = 4
HEAD = 256
FF = 9216
SEQ_GROUP = 2
LENGTH = 1024
SEQS = 4
QB = 512


def cut_row(key):
    order = jax.random.permutation(key, LENGTH - 1)
    marks = (order < LENGTH // 128).astype(jnp.int32)
    return jnp.concatenate([jnp.zeros((1,), jnp.int32), marks])


def segment_layout(key):
    key = jax.random.fold_in(key, 7)
    pick_key, cut_key = jax.random.split(key)
    chosen = jax.random.randint(pick_key, (SEQS // SEQ_GROUP, 1), 0, SEQ_GROUP)
    member = jnp.arange(SEQS, dtype=jnp.int32).reshape(SEQS // SEQ_GROUP, SEQ_GROUP)
    whole = (member % SEQ_GROUP == chosen).reshape(SEQS, 1)
    cuts = jax.vmap(cut_row)(jax.random.split(cut_key, SEQS))
    numbers = jnp.cumsum(cuts, axis=1)
    return jnp.where(whole, 0, numbers).astype(jnp.int32)


def draw_segments(key, part):
    return segment_layout(key)


def draw_positions(key, part):
    numbers = segment_layout(key)
    index = jnp.arange(LENGTH, dtype=jnp.int32)
    rising = jnp.concatenate([jnp.ones((SEQS, 1), jnp.bool_), numbers[:, 1:] > numbers[:, :-1]], axis=1)
    starts = lax.cummax(jnp.where(rising, index[None, :], 0), axis=1)
    return (index[None, :] - starts).astype(jnp.int32)


def chosen_head(key):
    return jax.random.randint(key, (), 0, HEADS)


def spread_scales(key, count, lower, upper):
    fraction = jax.random.uniform(key, (count,), jnp.float32)
    return jnp.exp(jnp.log(lower) + fraction * (jnp.log(upper) - jnp.log(lower)))


def draw_query_scale(key, part):
    head = chosen_head(key)
    key = jax.random.fold_in(key, 11)
    base = spread_scales(key, HEADS * HEAD, 0.00014, 0.00056)
    owner = jnp.arange(HEADS * HEAD, dtype=jnp.int32) // HEAD
    return jnp.where(owner == head, 2.5 * base, base).astype(jnp.float32)


def draw_key_scale(key, part):
    head = chosen_head(key) // (HEADS // KV_HEADS)
    key = jax.random.fold_in(key, 13)
    base = spread_scales(key, KV_HEADS * HEAD, 0.00014, 0.00056)
    owner = jnp.arange(KV_HEADS * HEAD, dtype=jnp.int32) // HEAD
    return jnp.where(owner == head, 2.5 * base, base).astype(jnp.float32)


def plant(array, stream_key, least, largest):
    longest = array.shape.index(max(array.shape))
    spots = []
    for shift in (0, 1):
        where = [jax.random.randint(jax.random.fold_in(stream_key, axis), (), 0, length) for axis, length in enumerate(array.shape)]
        where[longest] = (where[longest] + shift) % array.shape[longest]
        spots.append(tuple(where))
    return array.at[spots[0]].set(least).at[spots[1]].set(largest)


def steps_of(key, dims, pieces, low, largest):
    def one(axis_at, shards_of):
        heights = jax.random.uniform(jax.random.fold_in(jax.random.fold_in(key, 6), axis_at), (shards_of,), jnp.float32, low / len(pieces), largest / len(pieces))
        return jnp.repeat(jnp.exp(heights), dims[axis_at] // shards_of).reshape((-1,) + (1,) * (len(dims) - axis_at - 1))

    loudness = one(*pieces[0])
    for cut in pieces[1:]:
        loudness = loudness * one(*cut)
    return loudness


def normal_values(stream_key, dims, scale, reach, cuts=(), held_as=jnp.bfloat16):
    values = jax.random.normal(stream_key, dims, jnp.float32) * scale
    if len(cuts) > 0:
        values = steps_of(stream_key, dims, cuts, -0.22, 0.18) * values
    return jnp.clip(values, min=-reach, max=reach).astype(held_as)


def setup_inputs(seed: int = 0) -> dict:
    key_list = jax.random.split(jax.random.key(seed), 23)
    tokens = normal_values(key_list[0], (SEQS, LENGTH, D), 1.0, 6.0, ((0, 2), (1, 16)))
    segments = draw_segments(jax.random.fold_in(key_list[22], 71), 0)
    positions = draw_positions(jax.random.fold_in(key_list[22], 71), 0)
    cotangent = normal_values(key_list[3], (SEQS, LENGTH, D), 1.0, 6.0, ((0, 2), (1, 16)))
    query_codes = plant(jax.random.randint(key_list[4], (D, HEADS * HEAD), -128, 128), jax.random.fold_in(key_list[4], 1), -128, 127).astype(jnp.int32)
    key_codes = plant(jax.random.randint(key_list[5], (D, KV_HEADS * HEAD), -128, 128), jax.random.fold_in(key_list[5], 1), -128, 127).astype(jnp.int32)
    value_codes = plant(jax.random.randint(key_list[6], (D, KV_HEADS * HEAD), -128, 128), jax.random.fold_in(key_list[6], 1), -128, 127).astype(jnp.int32)
    output_codes = plant(jax.random.randint(key_list[7], (HEADS * HEAD, D), -128, 128), jax.random.fold_in(key_list[7], 1), -128, 127).astype(jnp.int32)
    gate_codes = plant(jax.random.randint(key_list[8], (D, FF), -128, 128), jax.random.fold_in(key_list[8], 1), -128, 127).astype(jnp.int32)
    up_codes = plant(jax.random.randint(key_list[9], (D, FF), -128, 128), jax.random.fold_in(key_list[9], 1), -128, 127).astype(jnp.int32)
    down_codes = plant(jax.random.randint(key_list[10], (FF, D), -128, 128), jax.random.fold_in(key_list[10], 1), -128, 127).astype(jnp.int32)
    query_scale = draw_query_scale(jax.random.fold_in(key_list[22], 71), 0)
    key_scale = draw_key_scale(jax.random.fold_in(key_list[22], 71), 0)
    value_scale = jnp.clip(jnp.exp(jax.random.uniform(key_list[13], (KV_HEADS * HEAD,), jnp.float32, math.log(0.00014), math.log(0.00056))), 0.00014, 0.00056)
    output_scale = jnp.clip(jnp.exp(jax.random.uniform(key_list[14], (D,), jnp.float32, math.log(0.00015), math.log(0.0006))), 0.00015, 0.0006)
    gate_scale = jnp.clip(jnp.exp(jax.random.uniform(key_list[15], (FF,), jnp.float32, math.log(0.00014), math.log(0.00056))), 0.00014, 0.00056)
    up_scale = jnp.clip(jnp.exp(jax.random.uniform(key_list[16], (FF,), jnp.float32, math.log(0.00014), math.log(0.00056))), 0.00014, 0.00056)
    down_scale = jnp.clip(jnp.exp(jax.random.uniform(key_list[17], (D,), jnp.float32, math.log(7.000000186963007e-05), math.log(0.00028))), 7.000000186963007e-05, 0.00028)
    attention_gain = jnp.clip(1.0 + 0.18 * jax.random.normal(key_list[18], (D,), jnp.float32), 0.1, 1.9)
    attention_post_gain = jnp.clip(1.0 + 0.18 * jax.random.normal(key_list[19], (D,), jnp.float32), 0.1, 1.9)
    feed_gain = jnp.clip(1.0 + 0.18 * jax.random.normal(key_list[20], (D,), jnp.float32), 0.1, 1.9)
    feed_post_gain = jnp.clip(1.0 + 0.18 * jax.random.normal(key_list[21], (D,), jnp.float32), 0.1, 1.9)
    return dict(tokens=tokens, segments=segments, positions=positions, cotangent=cotangent, query_codes=query_codes, key_codes=key_codes, value_codes=value_codes, output_codes=output_codes, gate_codes=gate_codes, up_codes=up_codes, down_codes=down_codes, query_scale=query_scale, key_scale=key_scale, value_scale=value_scale, output_scale=output_scale, gate_scale=gate_scale, up_scale=up_scale, down_scale=down_scale, attention_gain=attention_gain, attention_post_gain=attention_post_gain, feed_gain=feed_gain, feed_post_gain=feed_post_gain)


@jax.custom_vjp
def low(v):
    return lax.optimization_barrier(v.astype(jnp.bfloat16)).astype(jnp.float32)

@jax.custom_vjp
def low_back(v):
    return v

def low_keep(v):
    return (low(v), None)

def low_pass(kept, grad):
    return (grad,)

def back_keep(v):
    return (v, None)

def back_low(kept, grad):
    return (low(grad),)
low.defvjp(low_keep, low_pass)
low_back.defvjp(back_keep, back_low)
cap_limit = 50.0

def normed(value, gain):
    return value * lax.rsqrt(lax.optimization_barrier(jnp.mean(value * value, axis=-1, keepdims=True)) + 1e-06) * gain

def angles(places, head):
    freqs = 10000.0 ** (-(jnp.arange(head // 2, dtype=jnp.float32) * 2.0 / head))
    return places.astype(jnp.float32)[..., None] * freqs

def rotate(values, turn, sign):
    cosine = jnp.cos(turn)[..., None, :]
    sine = sign * jnp.sin(turn)[..., None, :]
    half = values.shape[-1] // 2
    first = values[..., :half]
    second = values[..., half:]
    return jnp.concatenate([first * cosine - second * sine, second * cosine + first * sine], axis=-1)

def levels(codes, step):
    offset = jnp.where(step > 1.0, 0.5 * step, 0.0)
    return jnp.floor(codes / step) * step + offset

def width_step(number):
    remainder = number % 3
    return jnp.where(remainder == 0, 1.0, jnp.where(remainder == 1, 16.0, 64.0)).astype(jnp.float32)

def product(left, right):
    return jnp.dot(left, right, precision=lax.Precision.HIGHEST, preferred_element_type=jnp.float32)

def reference(tokens, segments, positions, cotangent, query_codes, key_codes, value_codes, output_codes, gate_codes, up_codes, down_codes, query_scale, key_scale, value_scale, output_scale, gate_scale, up_scale, down_scale, attention_gain, attention_post_gain, feed_gain, feed_post_gain):
    codes = [c.astype(jnp.float32) for c in (query_codes, key_codes, value_codes, output_codes, gate_codes, up_codes, down_codes)]
    scales = [query_scale, key_scale, value_scale, output_scale, gate_scale, up_scale, down_scale]
    fixed = [code * column[None, :] for code, column in zip(codes, scales)]
    gains = [attention_gain, attention_post_gain, feed_gain, feed_post_gain]
    pairs = HEADS // KV_HEADS
    scale = HEAD ** (-0.5)
    blocks = LENGTH // QB
    token_index = jnp.arange(LENGTH, dtype=jnp.int32)

    def layer(source, segment_row, place_row, number, weights, gain_list):
        step = width_step(number)
        matrices = [low(weight - master + levels(code, step) * column[None, :]) for weight, master, code, column in zip(weights, fixed, codes, scales)]
        query_matrix, key_matrix, value_matrix, output_matrix, gate_matrix, up_matrix, down_matrix = matrices
        turn = angles(place_row, HEAD)
        first_normed = low(normed(source, gain_list[0]))
        query_lin = low_back(product(first_normed, query_matrix))
        key_lin = low_back(product(first_normed, key_matrix))
        value_lin = low_back(product(first_normed, value_matrix))
        queries = low(rotate(query_lin.reshape(LENGTH, HEADS, HEAD), turn, 1.0)).reshape(LENGTH, KV_HEADS, pairs, HEAD)
        keys = low(rotate(key_lin.reshape(LENGTH, KV_HEADS, HEAD), turn, 1.0))
        values = low(value_lin.reshape(LENGTH, KV_HEADS, HEAD))

        def one_block(items):
            block_queries, block_index, block_segments = items
            raw = jnp.einsum('qgjd,kgd->qgjk', block_queries, keys, precision=lax.Precision.HIGHEST, preferred_element_type=jnp.float32) * scale
            raw = low_back(raw)
            allowed = (block_segments[:, None] == segment_row[None, :]) & (token_index[None, :] <= block_index[:, None])
            kernel = jnp.where(allowed[:, None, None, :], jnp.exp(cap_limit * jnp.tanh(raw / cap_limit)), 0.0)
            total = lax.optimization_barrier(jnp.sum(kernel, axis=-1))
            summed = low_back(jnp.einsum('qgjk,kgd->qgjd', low(kernel), values, precision=lax.Precision.HIGHEST, preferred_element_type=jnp.float32))
            return summed / total[..., None]
        attended = lax.map(jax.checkpoint(one_block), (queries.reshape(blocks, QB, KV_HEADS, pairs, HEAD), token_index.reshape(blocks, QB), segment_row.reshape(blocks, QB)))
        attended = low(attended.reshape(LENGTH, HEADS * HEAD))
        attention_raw = low_back(product(attended, output_matrix))
        mixed = source + normed(attention_raw, gain_list[1])
        second_normed = low(normed(mixed, gain_list[2]))
        gate = low_back(product(second_normed, gate_matrix))
        upward = low_back(product(second_normed, up_matrix))
        hidden = low(jax.nn.gelu(gate, approximate=True) * upward)
        down_raw = low_back(product(hidden, down_matrix))
        return mixed + normed(down_raw, gain_list[3])

    def forward(values_in, weights, gain_list):

        def one_sequence(carry, items):
            return (carry, layer(items[0], items[1], items[2], items[3], weights, gain_list))
        _, outs = lax.scan(jax.checkpoint(one_sequence), jnp.zeros((), jnp.float32), (values_in, segments, positions, jnp.arange(SEQS, dtype=jnp.int32)))
        return outs
    result, pull = jax.vjp(forward, tokens.astype(jnp.float32), fixed, gains)
    grad_in, grad_weights, grad_gains = pull(cotangent.astype(jnp.float32))
    return (result.astype(jnp.bfloat16), grad_in.astype(jnp.bfloat16), grad_weights[0], grad_weights[1], grad_weights[2], grad_weights[3], grad_weights[4], grad_weights[5], grad_weights[6], grad_gains[0], grad_gains[1], grad_gains[2], grad_gains[3])
```

```python
import functools

import jax
import jax.numpy as jnp
from jax import lax
from jax.experimental import pallas as pl
from jax.experimental.pallas import tpu as pltpu
from jax.sharding import PartitionSpec as P

D = 2304
HEADS = 8
KV_HEADS = 4
HEAD = 256
FF = 9216
MESH = pl.DeviceIdType.MESH
F32 = jnp.float32
BF16 = jnp.bfloat16


cap_limit = 50.0


class Grid:
    def __init__(self, n):
        self.n = n
        self.planes = 4 if n % 8 == 0 else 2
        self.plane = n // self.planes
        wide = 1
        while wide * wide < self.plane:
            wide *= 2
        self.wide = wide

    def snake(self, p):
        y, x = p // self.wide, p % self.wide
        return y * self.wide + x + (y % 2) * (self.wide - 1 - 2 * x)


def remote(src, dst, send, recv, chip, core):
    return pltpu.make_async_remote_copy(
        src_ref=src, dst_ref=dst, send_sem=send, recv_sem=recv, device_id=(chip, core), device_id_type=MESH
    )


def greet(barrier, chip, core):
    pl.semaphore_signal(barrier, inc=1, device_id=(chip, core), device_id_type=MESH)


def places(grid, levels):
    c, b = lax.axis_index("seq"), lax.axis_index("batch")
    pn = grid.plane
    z, p = c // pn, c % pn
    q = grid.snake(p)
    zi = z % levels
    right = z * pn + grid.snake((q + 1) % pn)
    left = z * pn + grid.snake((q + pn - 1) % pn)
    return c, b, z, q, zi, right, left


def enter(grid, levels, halves):
    c, b, z, q, zi, right, left = places(grid, levels)
    barrier = pltpu.get_barrier_semaphore()
    greet(barrier, right, b)
    greet(barrier, left, b)
    pl.when(zi > 0)(lambda: greet(barrier, c - grid.plane, b))
    pl.when(zi < levels - 1)(lambda: greet(barrier, c + grid.plane, b))
    if halves:
        greet(barrier, (c + grid.n // 2) % grid.n, b)
    count = 2 + jnp.where(zi > 0, 1, 0) + jnp.where(zi < levels - 1, 1, 0) + (1 if halves else 0)
    pl.semaphore_wait(barrier, count)


def line_order(levels):
    return [(0, 0)] + [(sign, d) for d in range(1, levels) for sign in (-1, 1)]


def present(zi, sign, d, levels):
    if d == 0:
        return None
    return (zi - d >= 0) if sign < 0 else (zi + d < levels)


def guarded(condition, action):
    if condition is None:
        action()
    else:
        pl.when(condition)(action)


def gather_kernel(grid, levels, halves, x_ref, pos_ref, out_ref, posout_ref, zs, zr, rs, rr, ls, xs, xr, ps, pr):
    n, pn = grid.n, grid.plane
    steps = pn // 2
    c, b, z, q, zi, right, left = places(grid, levels)
    rows = x_ref.shape[1]
    half = rows // 2
    enter(grid, levels, halves)

    def slot(zj, qj):
        return zj * pn + grid.snake((qj + pn) % pn)

    def block(us, zj, qj, part=None):
        u0, nu = us
        at = out_ref.at[pl.ds(u0, nu), slot(zj, qj)]
        if part is None:
            return at
        return out_ref.at[pl.ds(u0, nu), slot(zj, qj), pl.ds(part * half, half)]

    own = slot(zi, q)
    member = c // (n // 2)
    partner = (c + n // 2) % n
    if halves:
        local = pltpu.make_async_copy(x_ref.at[member], out_ref.at[member, own], ls.at[0])
        swap = remote(x_ref.at[1 - member], out_ref.at[member, own], xs.at[0], xr.at[0], partner, b)
        swap.start()
        passes = [(member, 1), (1 - member, 1)]
    else:
        local = pltpu.make_async_copy(x_ref, out_ref.at[:, own], ls.at[0])
        passes = [(0, 2)]
    local.start()

    def z_copy(k, us, zj, sign):
        way = 0 if sign > 0 else 1
        return remote(
            block(us, zj, q), block(us, zj, q), zs.at[k, way, zj], zr.at[k, way, zj], c + sign * pn, b
        )

    def r_copy(k, us, zj, way, step):
        part = way if step == steps else None
        place = q - (step - 1) if way == 0 else q + (step - 1)
        ref = block(us, zj, place, part)
        return remote(ref, ref, rs.at[k, way, step - 1, zj], rr.at[k, way, step - 1, zj], right if way == 0 else left, b)

    def r_landing(k, us, zj, way, step):
        part = way if step == steps else None
        place = q - step if way == 0 else q + step
        ref = block(us, zj, place, part)
        return remote(ref, ref, rs.at[k, way, step - 1, zj], rr.at[k, way, step - 1, zj], right, b)

    def arrive(k, us, sign, d):
        zj = zi + sign * d

        def go():
            if d > 0:
                z_copy(k, us, zj, -sign).wait_recv()
            if sign <= 0:
                pl.when(zi < levels - 1)(lambda: z_copy(k, us, zj, 1).start())
            if sign >= 0:
                pl.when(zi > 0)(lambda: z_copy(k, us, zj, -1).start())
            for way in (0, 1):
                r_copy(k, us, zj, way, 1).start()

        guarded(present(zi, sign, d, levels), go)

    def onward(k, us, sign, d):
        zj = zi + sign * d

        def go():
            for step in range(1, steps + 1):
                for way in (0, 1):
                    r_landing(k, us, zj, way, step).wait_recv()
                    if step < steps:
                        r_copy(k, us, zj, way, step + 1).start()

        guarded(present(zi, sign, d, levels), go)

    def finish(k, us, sign, d):
        zj = zi + sign * d

        def go():
            if sign <= 0:
                pl.when(zi < levels - 1)(lambda: z_copy(k, us, zj, 1).wait_send())
            if sign >= 0:
                pl.when(zi > 0)(lambda: z_copy(k, us, zj, -1).wait_send())
            for way in (0, 1):
                for step in range(1, steps + 1):
                    r_copy(k, us, zj, way, step).wait_send()

        guarded(present(zi, sign, d, levels), go)

    if pos_ref is not None:
        size = levels * pn
        base = c - c % size
        for off in range(1, size):
            to = base + (c % size + off) % size
            remote(pos_ref, posout_ref.at[c % size], ps.at[off], pr.at[c % size], to, b).start()
    local.wait()
    groups = [(k, us, sign, d) for k, us in enumerate(passes) for sign, d in line_order(levels)]
    if halves:
        swap_in = remote(x_ref.at[1 - member], out_ref.at[1 - member, own], xs.at[0], xr.at[0], partner, b)
    for i, group in enumerate(groups):
        if halves and group[0] == 1 and group[3] == 0:
            swap_in.wait_recv()
        arrive(*group)
        if i > 0:
            onward(*groups[i - 1])
    onward(*groups[-1])
    for group in groups:
        finish(*group)
    if halves:
        swap.wait_send()


def gather(grid, x, levels, halves, cid):
    n, pn = grid.n, grid.plane
    count = levels * pn
    steps = pn // 2
    passes = 2 if halves else 1

    def kernel(x_ref, out_ref, *sems):
        gather_kernel(grid, levels, halves, x_ref, None, out_ref, None, *sems, None, None)

    return pl.pallas_call(
        kernel,
        out_shape=jax.ShapeDtypeStruct((2, count) + x.shape[1:], x.dtype),
        in_specs=[pl.BlockSpec(memory_space=pl.ANY)],
        out_specs=pl.BlockSpec(memory_space=pl.ANY),
        scratch_shapes=[
            pltpu.SemaphoreType.DMA((passes, 2, levels)),
            pltpu.SemaphoreType.DMA((passes, 2, levels)),
            pltpu.SemaphoreType.DMA((passes, 2, steps, levels)),
            pltpu.SemaphoreType.DMA((passes, 2, steps, levels)),
            pltpu.SemaphoreType.DMA((1,)),
            pltpu.SemaphoreType.DMA((1,)),
            pltpu.SemaphoreType.DMA((1,)),
        ],
        compiler_params=pltpu.CompilerParams(collective_id=cid, has_side_effects=True),
        name="gather_%d" % count,
    )(x)


def scatter_kernel(
    grid, levels, halves, p_ref, out_ref, acc, ring_half, ring_full, line, swapped, ls, zs, zr, rs, rr, xs, xr
):
    n, pn = grid.n, grid.plane
    steps = pn // 2
    c, b, z, q, zi, right, left = places(grid, levels)
    rows = p_ref.shape[2]
    half = rows // 2
    member = c // (n // 2)
    partner = (c + n // 2) % n

    def slot(zj, qj):
        return zj * pn + grid.snake((qj + 2 * pn) % pn)

    load = pltpu.make_async_copy(p_ref, acc, ls.at[0])
    load.start()
    enter(grid, levels, halves)
    load.wait()
    passes = [(1 - member, 1), (member, 1)] if halves else [(0, 2)]
    far_first = [(sign, d) for d in range(levels - 1, 0, -1) for sign in (-1, 1)] + [(0, 0)]

    def block(us, zj, qj, part=None):
        u0, nu = us
        if part is None:
            return acc.at[pl.ds(u0, nu), slot(zj, qj)]
        return acc.at[pl.ds(u0, nu), slot(zj, qj), pl.ds(part * half, half)]

    def add(us, into, others, lo, count):
        u0, nu = us

        def one(i, carry):
            u, r = u0 + i // (count // 16), lo + (i % (count // 16)) * 16
            total = into(u, r)[...].astype(F32)
            for other in others:
                total = total + other(u, r)[...].astype(F32)
            into(u, r)[...] = total.astype(BF16)
            return carry

        lax.fori_loop(0, nu * (count // 16), one, 0)

    def acc_at(s):
        return lambda u, r: acc.at[u, s, pl.ds(r, 16)]

    def full_at(way, step, zj):
        return lambda u, r: ring_full.at[way, step - 2, zj, u, pl.ds(r, 16)]

    def half_at(way, zj):
        return lambda u, r: ring_half.at[way, zj, u, pl.ds(r - way * half, 16)]

    def line_at(way, zj):
        return lambda u, r: line.at[way, zj, u, pl.ds(r, 16)]

    def r_copy(k, us, zj, way, step):
        u0, nu = us
        sign = 1 if way == 0 else -1
        target = q + sign * (steps + 1 - step)
        if step == 1:
            src, dst = block(us, zj, target, way), ring_half.at[way, zj, pl.ds(u0, nu)]
        else:
            src, dst = block(us, zj, target), ring_full.at[way, step - 2, zj, pl.ds(u0, nu)]
        return remote(src, dst, rs.at[k, way, step - 1, zj], rr.at[k, way, step - 1, zj], right if way == 0 else left, b)

    def z_copy(k, us, zj, way):
        u0, nu = us
        return remote(
            block(us, zj, q),
            line.at[way, zj, pl.ds(u0, nu)],
            zs.at[k, way, zj],
            zr.at[k, way, zj],
            c + (pn if way == 0 else -pn),
            b,
        )

    def begin(k, us, sign, d):
        def go():
            for way in (0, 1):
                r_copy(k, us, zi + sign * d, way, 1).start()

        guarded(present(zi, sign, d, levels), go)

    def onward(k, us, sign, d):
        zj = zi + sign * d

        def go():
            for step in range(1, steps + 1):
                for way in (0, 1):
                    r_copy(k, us, zj, way, step).wait_recv()
                    if step < steps:
                        s = slot(zj, q + (1 if way == 0 else -1) * (steps - step))
                        if step == 1:
                            add(us, acc_at(s), [half_at(way, zj)], way * half, half)
                        else:
                            add(us, acc_at(s), [full_at(way, step, zj)], 0, rows)
                        r_copy(k, us, zj, way, step + 1).start()
            s = slot(zj, q)
            if steps > 1:
                add(us, acc_at(s), [full_at(0, steps, zj), full_at(1, steps, zj)], 0, rows)
            else:
                add(us, acc_at(s), [half_at(0, zj)], 0, half)
                add(us, acc_at(s), [half_at(1, zj)], half, half)
            if sign > 0:

                def below():
                    z_copy(k, us, zj, 0).wait_recv()
                    add(us, acc_at(s), [line_at(0, zj)], 0, rows)

                pl.when(zi > 0)(below)
                z_copy(k, us, zj, 0).start()
            elif sign < 0:

                def above():
                    z_copy(k, us, zj, 1).wait_recv()
                    add(us, acc_at(s), [line_at(1, zj)], 0, rows)

                pl.when(zi < levels - 1)(above)
                z_copy(k, us, zj, 1).start()
            else:

                def below():
                    z_copy(k, us, zj, 0).wait_recv()
                    add(us, acc_at(s), [line_at(0, zj)], 0, rows)

                def above():
                    z_copy(k, us, zj, 1).wait_recv()
                    add(us, acc_at(s), [line_at(1, zj)], 0, rows)

                pl.when(zi > 0)(below)
                pl.when(zi < levels - 1)(above)

        guarded(present(zi, sign, d, levels), go)

    def finish(k, us, sign, d):
        zj = zi + sign * d

        def go():
            for way in (0, 1):
                for step in range(1, steps + 1):
                    r_copy(k, us, zj, way, step).wait_send()
            if sign != 0:
                z_copy(k, us, zj, 0 if sign > 0 else 1).wait_send()

        guarded(present(zi, sign, d, levels), go)

    groups = [(k, us, sign, d) for k, us in enumerate(passes) for sign, d in far_first]
    own = slot(zi, q)
    if halves:
        swap = remote(acc.at[1 - member, own], swapped, xs.at[0], xr.at[0], partner, b)
    begin(*groups[0])
    for i, group in enumerate(groups):
        if i + 1 < len(groups):
            begin(*groups[i + 1])
        onward(*group)
        if halves and group[0] == 0 and group[3] == 0:
            swap.start()

    def give(src, u):
        def one(i, carry):
            out_ref[u, pl.ds(i * 16, 16)] = src.at[pl.ds(i * 16, 16)][...]
            return carry

        lax.fori_loop(0, rows // 16, one, 0)

    if halves:
        give(acc.at[member, own], member)
        swap.wait_recv()
        give(swapped, 1 - member)
    else:
        give(acc.at[0, own], 0)
        give(acc.at[1, own], 1)
    for group in groups:
        finish(*group)
    if halves:
        swap.wait_send()


def scatter_part(grid, p, levels, halves, cid):
    pn = grid.plane
    steps = pn // 2
    passes = 2 if halves else 1
    _, count, rows, width = p.shape
    return pl.pallas_call(
        functools.partial(scatter_kernel, grid, levels, halves),
        out_shape=jax.ShapeDtypeStruct((2, rows, width), BF16),
        in_specs=[pl.BlockSpec(memory_space=pl.ANY)],
        out_specs=pl.BlockSpec(memory_space=pltpu.VMEM),
        scratch_shapes=[
            pltpu.VMEM((2, count, rows, width), BF16),
            pltpu.VMEM((2, levels, 2, rows // 2, width), BF16),
            pltpu.VMEM((2, max(steps - 1, 1), levels, 2, rows, width), BF16),
            pltpu.VMEM((2, levels, 2, rows, width), BF16),
            pltpu.VMEM((rows, width), BF16),
            pltpu.SemaphoreType.DMA((1,)),
            pltpu.SemaphoreType.DMA((passes, 2, levels)),
            pltpu.SemaphoreType.DMA((passes, 2, levels)),
            pltpu.SemaphoreType.DMA((passes, 2, steps, levels)),
            pltpu.SemaphoreType.DMA((passes, 2, steps, levels)),
            pltpu.SemaphoreType.DMA((1,)),
            pltpu.SemaphoreType.DMA((1,)),
        ],
        compiler_params=pltpu.CompilerParams(
            collective_id=cid, has_side_effects=True, vmem_limit_bytes=60 * 2**20
        ),
        name="scatter_%d" % count,
    )(p)


def scatter(grid, p, levels, halves, cid):
    _, count, rows, width = p.shape
    blocks = 2 * (2 * levels * (grid.plane // 2 + 2) + count)
    parts = 1
    while blocks * rows * (width // parts) * 2 > 48 * 2**20:
        parts += 1
        while width % (128 * parts):
            parts += 1
    piece = width // parts
    outs = [scatter_part(grid, p[..., i * piece : (i + 1) * piece], levels, halves, cid) for i in range(parts)]
    return outs[0] if parts == 1 else jnp.concatenate(outs, axis=-1)


def exchange_kernel(grid, pick, x_ref, small_ref, out_ref, all_ref, ls, ss, sr, fs, fr, ts, tr):
    n = grid.n
    c, b = lax.axis_index("seq"), lax.axis_index("batch")
    barrier = pltpu.get_barrier_semaphore()
    greet(barrier, c, 1 - b)
    for off in range(1, n):
        greet(barrier, (c + off) % n, b)
    pl.semaphore_wait(barrier, n)

    def out_copy(i):
        to = (c + 2 * i + b) % n
        return remote(x_ref.at[pick(to)], out_ref.at[c], ss.at[i], sr.at[i], to, b)

    def landed(i):
        frm = (c + n - 2 * i - b) % n
        return remote(x_ref.at[0], out_ref.at[frm], ss.at[i], sr.at[i], c, 1 - b)

    def pass_on(i):
        frm = (c + n - 2 * i - b) % n
        return remote(out_ref.at[frm], out_ref.at[frm], fs.at[i], fr.at[i], c, 1 - b)

    def passed(i):
        frm = (c + n - 2 * i - (1 - b)) % n
        return remote(out_ref.at[frm], out_ref.at[frm], fs.at[i], fr.at[i], c, 1 - b)

    def tell(off):
        return remote(small_ref, all_ref.at[c], ts.at[off], tr.at[off], (c + off) % n, b)

    def told(off):
        return remote(small_ref, all_ref.at[(c + n - off) % n], ts.at[off], tr.at[off], (c + off) % n, b)

    for off in range(1, n):
        tell(off).start()
    keep = pltpu.make_async_copy(small_ref, all_ref.at[c], ts.at[0])
    keep.start()
    local = pltpu.make_async_copy(x_ref.at[pick(c)], out_ref.at[c], ls.at[0])
    for i in range(1, n // 2):
        out_copy(i).start()
    pl.when(b == 1)(lambda: out_copy(0).start())

    def own():
        local.start()
        local.wait()

    pl.when(b == 0)(own)
    pl.when(b == 1)(lambda: landed(0).wait_recv())
    pass_on(0).start()
    for i in range(1, n // 2):
        landed(i).wait_recv()
        pass_on(i).start()
    keep.wait()
    for off in range(1, n):
        told(off).wait_recv()
    for i in range(n // 2):
        passed(i).wait_recv()
    for i in range(n // 2):
        pass_on(i).wait_send()
    for i in range(1, n // 2):
        out_copy(i).wait_send()
    pl.when(b == 1)(lambda: out_copy(0).wait_send())
    for off in range(1, n):
        tell(off).wait_send()


def exchange(grid, x, small, pick, cid):
    n = grid.n
    sems = [pltpu.SemaphoreType.DMA((n // 2,)) for _ in range(4)]
    return pl.pallas_call(
        functools.partial(exchange_kernel, grid, pick),
        out_shape=(
            jax.ShapeDtypeStruct((n,) + x.shape[1:], x.dtype),
            jax.ShapeDtypeStruct((n,) + small.shape, small.dtype),
        ),
        in_specs=[pl.BlockSpec(memory_space=pl.ANY)] * 2,
        out_specs=(pl.BlockSpec(memory_space=pl.ANY),) * 2,
        scratch_shapes=[pltpu.SemaphoreType.DMA((1,))]
        + sems
        + [pltpu.SemaphoreType.DMA((n,)), pltpu.SemaphoreType.DMA((n,))],
        compiler_params=pltpu.CompilerParams(collective_id=cid, has_side_effects=True),
        name="exchange",
    )(x, small)


def return_kernel(grid, x_ref, out_ref, mine, theirs, ls, ps, pr, ss, sr, fs, fr):
    n = grid.n
    c, b = lax.axis_index("seq"), lax.axis_index("batch")
    half = n // 2
    barrier = pltpu.get_barrier_semaphore()
    greet(barrier, c, 1 - b)
    for off in range(1, n):
        greet(barrier, (c + off) % n, b)

    def target(i, core):
        return (c + 2 * i + core) % n

    def load(i):
        return pltpu.make_async_copy(x_ref.at[target(i, b)], mine.at[i], ls.at[i])

    def give(i):
        return remote(x_ref.at[target(i, 1 - b)], theirs.at[i], ps.at[i], pr.at[i], c, 1 - b)

    def out_copy(i):
        return remote(mine.at[i], out_ref.at[c], ss.at[i], sr.at[i], target(i, b), b)

    def frm(i, core):
        return (c + n - 2 * i - core) % n

    def landed(i):
        return remote(mine.at[i], out_ref.at[frm(i, b)], ss.at[i], sr.at[i], c, 1 - b)

    def pass_on(i):
        at = out_ref.at[frm(i, b)]
        return remote(at, at, fs.at[i], fr.at[i], c, 1 - b)

    def passed(i):
        at = out_ref.at[frm(i, 1 - b)]
        return remote(at, at, fs.at[i], fr.at[i], c, 1 - b)

    local = pltpu.make_async_copy(mine.at[0], out_ref.at[c], ss.at[0])
    for i in range(half):
        load(i).start()
    pl.semaphore_wait(barrier, n)
    order = list(range(1, half)) + [0]
    for i in order:
        give(i).start()
    rows = x_ref.shape[1]
    step = 16 if rows % 16 == 0 else rows
    for i in order:
        load(i).wait()
        give(i).wait_recv()

        def one(r, carry):
            at = pl.ds(pl.multiple_of(r * step, step), step)
            mine[i, at] = (mine[i, at].astype(F32) + theirs[i, at].astype(F32)).astype(BF16)
            return carry

        lax.fori_loop(0, rows // step, one, 0)
        if i > 0:
            out_copy(i).start()
        else:
            pl.when(b == 1)(lambda: out_copy(0).start())
            pl.when(b == 0)(lambda: local.start())
    for i in order:
        if i > 0:
            landed(i).wait_recv()
        else:
            pl.when(b == 1)(lambda: landed(0).wait_recv())
            pl.when(b == 0)(lambda: local.wait())
        pass_on(i).start()
    for i in range(half):
        passed(i).wait_recv()
    for i in range(half):
        give(i).wait_send()
        pass_on(i).wait_send()
    for i in range(1, half):
        out_copy(i).wait_send()
    pl.when(b == 1)(lambda: out_copy(0).wait_send())


def give_back(grid, x, cid):
    n = grid.n
    shape = (n // 2,) + x.shape[1:]
    return pl.pallas_call(
        functools.partial(return_kernel, grid),
        out_shape=jax.ShapeDtypeStruct(x.shape, x.dtype),
        in_specs=[pl.BlockSpec(memory_space=pl.ANY)],
        out_specs=pl.BlockSpec(memory_space=pl.ANY),
        scratch_shapes=[pltpu.VMEM(shape, BF16), pltpu.VMEM(shape, BF16)]
        + [pltpu.SemaphoreType.DMA((n // 2,)) for _ in range(7)],
        compiler_params=pltpu.CompilerParams(collective_id=cid, has_side_effects=True, vmem_limit_bytes=40 * 2**20),
        name="give_back",
    )(x)


def pair_kernel(x_ref, out_ref, other, ss, sr):
    c, b = lax.axis_index("seq"), lax.axis_index("batch")
    barrier = pltpu.get_barrier_semaphore()
    greet(barrier, c, 1 - b)
    pl.semaphore_wait(barrier, 1)
    copy = remote(x_ref, other, ss.at[0], sr.at[0], c, 1 - b)
    copy.start()
    copy.wait()

    def one(r, carry):
        at = pl.ds(pl.multiple_of(r * 16, 16), 16)
        out_ref[at] = x_ref[at].astype(F32) + other[at].astype(F32)
        return carry

    lax.fori_loop(0, x_ref.shape[0] // 16, one, 0)


def pair_sum(x, cid):
    return pl.pallas_call(
        pair_kernel,
        out_shape=jax.ShapeDtypeStruct(x.shape, F32),
        in_specs=[pl.BlockSpec(memory_space=pltpu.VMEM)],
        out_specs=pl.BlockSpec(memory_space=pltpu.VMEM),
        scratch_shapes=[pltpu.VMEM(x.shape, BF16), pltpu.SemaphoreType.DMA((1,)), pltpu.SemaphoreType.DMA((1,))],
        compiler_params=pltpu.CompilerParams(collective_id=cid, has_side_effects=True, vmem_limit_bytes=40 * 2**20),
        name="pair_sum",
    )(x)


def normed(value, gain):
    return value * lax.rsqrt(jnp.mean(value * value, axis=-1, keepdims=True) + 1e-06) * gain


def angles(places, head):
    freqs = 10000.0 ** (-(jnp.arange(head // 2, dtype=F32) * 2.0 / head))
    return places.astype(F32)[..., None] * freqs


def rotate(values, cosine, sine):
    half = values.shape[-1] // 2
    first = values[..., :half]
    second = values[..., half:]
    return jnp.concatenate([first * cosine - second * sine, second * cosine + first * sine], axis=-1)


def width_step(number):
    remainder = number % 3
    return jnp.where(remainder == 0, 1.0, jnp.where(remainder == 1, 16.0, 64.0)).astype(F32)


def dequantized(codes, column_scale, step):
    offset = jnp.where(step > 1.0, 0.5 * step, 0.0)
    level = jnp.floor(codes.astype(F32) / step) * step + offset
    return (level * column_scale[None, :]).astype(BF16)


def dot(left, right):
    return jnp.dot(left, right, preferred_element_type=F32)


def dot_t(left, right):
    return lax.dot_general(left, right, (((1,), (1,)), ((), ())), preferred_element_type=F32)


def t_dot(left, right):
    return lax.dot_general(left, right, (((0,), (0,)), ((), ())), preferred_element_type=F32)


def on_device(
    grid,
    tokens,
    segments,
    positions,
    cotangent,
    query_codes,
    key_codes,
    value_codes,
    output_codes,
    gate_codes,
    up_codes,
    down_codes,
    query_scale,
    key_scale,
    value_scale,
    output_scale,
    gate_scale,
    up_scale,
    down_scale,
    attention_gain,
    attention_post_gain,
    feed_gain,
    feed_post_gain,
):
    n = grid.n
    group, block, _ = tokens.shape
    length = n * block
    pairs = HEADS // KV_HEADS
    scale = HEAD ** (-0.5)
    chip, core = lax.axis_index("seq"), lax.axis_index("batch")
    half = n // 2
    member = chip // half
    head = chip % HEADS
    kv_head = head // pairs
    parts = half // HEADS
    copies = n // HEADS
    asked = length // parts
    first_asked = ((chip % half) // HEADS) * asked
    steps = [width_step(core * group + m) for m in range(group)]
    step = width_step(core * group + member)
    rows_d = D // n
    units = FF // n

    q_parts = jnp.transpose(query_codes.reshape(rows_d, HEADS, HEAD), (1, 0, 2))
    k_parts = jnp.repeat(jnp.transpose(key_codes.reshape(rows_d, KV_HEADS, HEAD), (1, 0, 2)), pairs, axis=0)
    v_parts = jnp.repeat(jnp.transpose(value_codes.reshape(rows_d, KV_HEADS, HEAD), (1, 0, 2)), pairs, axis=0)
    qkv_parts = jnp.concatenate([q_parts, k_parts, v_parts], axis=-1).astype(BF16)
    small = jnp.zeros((8, 128), jnp.int32).at[:group, :block].set(positions)
    qkv_codes, all_places = exchange(grid, qkv_parts, small, lambda to: to % HEADS, 1)
    pair_parts = jnp.concatenate(
        [gate_codes.reshape(rows_d, n, units), up_codes.reshape(rows_d, n, units)], axis=-1
    )
    pair_parts = jnp.transpose(pair_parts, (1, 0, 2)).astype(BF16)
    pair_codes, _ = exchange(grid, pair_parts, small, lambda to: to, 2)
    pair_codes = pair_codes.reshape(D, 2 * units)
    out_low = output_codes.astype(BF16)
    got = [
        lax.ppermute(
            out_low, "seq", [(h * copies + j, h + HEADS * ((j + copies - t) % copies)) for h in range(HEADS) for j in range(copies)]
        )
        for t in range(copies)
    ]
    out_codes = jnp.roll(jnp.stack(got), chip // HEADS, axis=0).reshape(HEAD, D)

    qkv_scale = jnp.concatenate(
        [
            lax.dynamic_slice_in_dim(query_scale, head * HEAD, HEAD),
            lax.dynamic_slice_in_dim(key_scale, kv_head * HEAD, HEAD),
            lax.dynamic_slice_in_dim(value_scale, kv_head * HEAD, HEAD),
        ]
    )
    qkv_matrix = dequantized(qkv_codes.reshape(D, 3 * HEAD), qkv_scale, step)
    out_matrix = dequantized(out_codes, output_scale, step)
    pair_scale = jnp.concatenate(
        [
            lax.dynamic_slice_in_dim(gate_scale, chip * units, units),
            lax.dynamic_slice_in_dim(up_scale, chip * units, units),
        ]
    )
    pair_matrices = [dequantized(pair_codes, pair_scale, s) for s in steps]
    down_matrices = [dequantized(down_codes, down_scale, s) for s in steps]

    source = tokens.astype(F32)
    first_normed = normed(source, attention_gain).astype(BF16)
    seen = gather(grid, first_normed, grid.planes // 2, True, 3).reshape(length, D)
    places_all = lax.dynamic_index_in_dim(all_places[:, :group, :block], member, 1, False).reshape(length)
    turn = angles(places_all, HEAD)
    cosine, sine = jnp.cos(turn), jnp.sin(turn)
    if parts == 1:
        seen_asked, places_asked, cosine_q, sine_q = seen, places_all, cosine, sine
        projected = dot(seen, qkv_matrix)
        q_lin, kv_lin = projected[:, :HEAD], projected[:, HEAD:]
    else:
        seen_asked, places_asked, cosine_q, sine_q = [
            lax.dynamic_slice_in_dim(a, first_asked, asked) for a in (seen, places_all, cosine, sine)
        ]
        q_lin, kv_lin = dot(seen_asked, qkv_matrix[:, :HEAD]), dot(seen, qkv_matrix[:, HEAD:])
    queries = rotate(q_lin, cosine_q, sine_q).astype(BF16)
    keys = rotate(kv_lin[:, :HEAD], cosine, sine).astype(BF16)
    values = kv_lin[:, HEAD:].astype(BF16)
    q_index = first_asked + jnp.arange(asked, dtype=jnp.int32)
    key_index = jnp.arange(length, dtype=jnp.int32)
    allowed = (key_index[None, :] <= q_index[:, None]) & (key_index[None, :] >= (q_index - places_asked)[:, None])
    bent = jnp.tanh(dot_t(queries, keys) * scale / cap_limit)
    kernel = jnp.where(allowed, jnp.exp(cap_limit * bent), 0.0)
    totals = jnp.sum(kernel, axis=-1, keepdims=True)
    kernel_low = kernel.astype(BF16)
    attended = dot(kernel_low, values) / totals
    attended_low = attended.astype(BF16)

    def spread(part):
        if parts > 1:
            part = lax.dynamic_update_slice_in_dim(jnp.zeros((length, D), BF16), part, first_asked, 0)
        return part.reshape(2, half, block, D)

    attention_raw = scatter(
        grid, spread(dot(attended_low, out_matrix).astype(BF16)), grid.planes // 2, True, 4
    ).astype(F32)

    mixed = source + normed(attention_raw, attention_post_gain)
    second_normed = normed(mixed, feed_gain).astype(BF16)
    fed = gather(grid, second_normed, grid.planes, False, 5).reshape(group, length, D)
    gate_up = [dot(fed[m], pair_matrices[m]) for m in range(group)]
    hidden = [(jax.nn.gelu(g[:, :units], approximate=True) * g[:, units:]).astype(BF16) for g in gate_up]
    down_part = jnp.stack([dot(hidden[m], down_matrices[m]).astype(BF16) for m in range(group)])
    down_raw = scatter(grid, down_part.reshape(group, n, block, D), grid.planes, False, 6).astype(F32)
    branch, pull_out = jax.vjp(normed, down_raw, feed_post_gain)
    output = (mixed + branch).astype(BF16)
    upstream = cotangent.astype(F32)
    grad_down_raw, grad_post_feed = pull_out(upstream)
    down_low = gather(grid, grad_down_raw.astype(BF16), grid.planes, False, 5).reshape(group, length, D)
    pair_low, second_part = [], []
    for m in range(group):
        grad_hidden = dot_t(down_low[m], down_matrices[m])
        _, pull_glu = jax.vjp(
            lambda left, right: jax.nn.gelu(left, approximate=True) * right,
            gate_up[m][:, :units],
            gate_up[m][:, units:],
        )
        pair_low.append(jnp.concatenate(pull_glu(grad_hidden), axis=-1).astype(BF16))
        second_part.append(dot_t(pair_low[m], pair_matrices[m]).astype(BF16))
    grad_second = scatter(
        grid, jnp.stack(second_part).reshape(group, n, block, D), grid.planes, False, 6
    ).astype(F32)
    pair_grad = sum(t_dot(fed[m], pair_low[m]) for m in range(group)).astype(BF16)
    down_grad = sum(t_dot(hidden[m], down_low[m]) for m in range(group)).astype(BF16)
    pair_got = give_back(grid, pair_grad.reshape(n, rows_d, 2 * units), 7)
    gate_grad = jnp.transpose(pair_got[..., :units], (1, 0, 2)).reshape(rows_d, FF).astype(F32)
    up_grad = jnp.transpose(pair_got[..., units:], (1, 0, 2)).reshape(rows_d, FF).astype(F32)
    down_grad = pair_sum(down_grad, 8)

    _, pull_feed = jax.vjp(normed, mixed, feed_gain)
    grad_mixed_part, grad_pre_feed = pull_feed(grad_second)
    grad_mixed = upstream + grad_mixed_part
    _, pull_post = jax.vjp(normed, attention_raw, attention_post_gain)
    grad_attention, grad_post_attention = pull_post(grad_mixed)
    attention_low = gather(grid, grad_attention.astype(BF16), grid.planes // 2, True, 3).reshape(length, D)
    if parts > 1:
        attention_low = lax.dynamic_slice_in_dim(attention_low, first_asked, asked)
    grad_attended = dot_t(attention_low, out_matrix)
    grad_sums = (grad_attended / totals).astype(BF16)
    offsets = jnp.sum(grad_attended * attended, axis=-1, keepdims=True) / totals
    grad_kernel = dot_t(grad_sums, values) - offsets
    grad_raw = (kernel * grad_kernel * (1.0 - bent * bent)).astype(BF16)
    grad_q = dot(grad_raw, keys) * scale
    grad_k = t_dot(grad_raw, queries) * scale
    grad_v = t_dot(kernel_low, grad_sums)
    q_low = rotate(grad_q, cosine_q, -sine_q).astype(BF16)
    kv_low = jnp.concatenate([rotate(grad_k, cosine, -sine), grad_v], axis=-1).astype(BF16)
    if parts == 1:
        qkv_low = jnp.concatenate([q_low, kv_low], axis=-1)
        first_part = dot_t(qkv_low, qkv_matrix)
        qkv_grad = t_dot(seen, qkv_low)
    else:
        first_part = dot_t(kv_low, qkv_matrix[:, HEAD:])
        q_back = dot_t(q_low, qkv_matrix[:, :HEAD])
        first_part = lax.dynamic_update_slice_in_dim(
            first_part, lax.dynamic_slice_in_dim(first_part, first_asked, asked) + q_back, first_asked, 0
        )
        qkv_grad = jnp.concatenate([t_dot(seen_asked, q_low), t_dot(seen, kv_low)], axis=-1)
    grad_first = scatter(
        grid, first_part.astype(BF16).reshape(2, half, block, D), grid.planes // 2, True, 4
    ).astype(F32)
    _, pull_in = jax.vjp(normed, source, attention_gain)
    grad_source_part, grad_pre_attention = pull_in(grad_first)
    grad_in = (grad_mixed + grad_source_part).astype(BF16)
    qkv_got = give_back(grid, qkv_grad.astype(BF16).reshape(n, rows_d, 3 * HEAD), 9).astype(F32)
    qkv_got = jnp.sum(qkv_got.reshape(copies, HEADS, rows_d, 3 * HEAD), axis=0)
    query_grad = jnp.transpose(qkv_got[..., :HEAD], (1, 0, 2)).reshape(rows_d, HEADS * HEAD)
    kv_grad = jnp.sum(qkv_got[..., HEAD:].reshape(KV_HEADS, pairs, rows_d, 2 * HEAD), axis=1)
    key_grad = jnp.transpose(kv_grad[..., :HEAD], (1, 0, 2)).reshape(rows_d, KV_HEADS * HEAD)
    value_grad = jnp.transpose(kv_grad[..., HEAD:], (1, 0, 2)).reshape(rows_d, KV_HEADS * HEAD)
    out_part = pair_sum(t_dot(attended_low, attention_low).astype(BF16), 10).astype(BF16)
    out_part = jnp.roll(out_part.reshape(copies, HEAD // copies, D), -(chip // HEADS), axis=0)
    out_grad = sum(
        lax.ppermute(
            out_part[t],
            "seq",
            [(h + HEADS * i, h * copies + (i + t) % copies) for h in range(HEADS) for i in range(copies)],
        ).astype(F32)
        for t in range(copies)
    )
    gains = lax.psum(
        (grad_pre_attention, grad_post_attention, grad_pre_feed, grad_post_feed), ("seq", "batch")
    )
    return (
        output,
        grad_in,
        query_grad,
        key_grad,
        value_grad,
        out_grad,
        gate_grad,
        up_grad,
        down_grad,
    ) + tuple(gains)


def solution(mesh):
    rows = P("seq", None)
    return jax.shard_map(
        functools.partial(on_device, Grid(mesh.shape["seq"])),
        mesh=mesh,
        in_specs=(P("batch", "seq", None), P("batch", "seq"), P("batch", "seq"), P("batch", "seq", None))
        + (rows,) * 7
        + (P(),) * 11,
        out_specs=(P("batch", "seq", None),) * 2 + (rows,) * 7 + (P(),) * 4,
        check_vma=False,
    )
```

```python
import functools

import jax
import jax.numpy as jnp
from jax import lax
from jax.experimental import pallas as pl
from jax.experimental.pallas import tpu as pltpu
from jax.sharding import PartitionSpec as P

D = 2304
HEADS = 8
KV_HEADS = 4
HEAD = 256
FF = 9216
MESH = pl.DeviceIdType.MESH
F32 = jnp.float32
BF16 = jnp.bfloat16


cap_limit = 50.0


class Grid:
    def __init__(self, n):
        self.n = n
        self.planes = 4 if n % 8 == 0 else 2
        self.plane = n // self.planes
        wide = 1
        while wide * wide < self.plane:
            wide *= 2
        self.wide = wide

    def snake(self, p):
        y, x = p // self.wide, p % self.wide
        return y * self.wide + x + (y % 2) * (self.wide - 1 - 2 * x)


def remote(src, dst, send, recv, chip, core):
    return pltpu.make_async_remote_copy(
        src_ref=src, dst_ref=dst, send_sem=send, recv_sem=recv, device_id=(chip, core), device_id_type=MESH
    )


def greet(barrier, chip, core):
    pl.semaphore_signal(barrier, inc=1, device_id=(chip, core), device_id_type=MESH)


class Place:
    def __init__(self, grid, levels):
        self.grid, self.levels = grid, levels
        self.n, self.pn = grid.n, grid.plane
        self.steps = self.pn // 2
        self.c, self.b = lax.axis_index("seq"), lax.axis_index("batch")
        self.z, p = self.c // self.pn, self.c % self.pn
        self.q = grid.snake(p)
        self.zi = self.z % levels
        self.right = self.z * self.pn + grid.snake((self.q + 1) % self.pn)
        self.left = self.z * self.pn + grid.snake((self.q + self.pn - 1) % self.pn)
        self.member = self.c // (self.n // 2)
        self.partner = (self.c + self.n // 2) % self.n

    def slot(self, zj, qj):
        return zj * self.pn + self.grid.snake((qj + 2 * self.pn) % self.pn)

    def sibling(self, src, dst, send, recv):
        return remote(src, dst, send, recv, self.c, 1 - self.b)

    def greet_near(self, halves):
        barrier = pltpu.get_barrier_semaphore()
        zi, levels = self.zi, self.levels
        greet(barrier, self.right, self.b)
        greet(barrier, self.left, self.b)
        pl.when(zi > 0)(lambda: greet(barrier, self.c - self.pn, self.b))
        pl.when(zi < levels - 1)(lambda: greet(barrier, self.c + self.pn, self.b))
        if halves:
            greet(barrier, self.partner, self.b)
        count = 2 + jnp.where(zi > 0, 1, 0) + jnp.where(zi < levels - 1, 1, 0) + (1 if halves else 0)
        pl.semaphore_wait(barrier, count)

    def greet_all(self):
        barrier = pltpu.get_barrier_semaphore()
        greet(barrier, self.c, 1 - self.b)

        def one(off, carry):
            greet(barrier, (self.c + off) % self.n, self.b)
            return carry

        lax.fori_loop(1, self.n, one, 0)
        pl.semaphore_wait(barrier, self.n)


def present(zi, sign, d, levels):
    if d == 0:
        return None
    return (zi - d >= 0) if sign < 0 else (zi + d < levels)


def guarded(condition, action):
    if condition is None:
        action()
    else:
        pl.when(condition)(action)


def dma(*shape):
    return pltpu.SemaphoreType.DMA(shape)


ANY = pl.BlockSpec(memory_space=pl.ANY)
INVMEM = pl.BlockSpec(memory_space=pltpu.VMEM)


def params(cid, mib=None):
    if mib is None:
        return pltpu.CompilerParams(collective_id=cid, has_side_effects=True)
    return pltpu.CompilerParams(collective_id=cid, has_side_effects=True, vmem_limit_bytes=mib * 2**20)


def gather_sems(grid, levels, halves):
    passes, steps = (2 if halves else 1), grid.plane // 2
    return [
        dma(passes, 2, levels),
        dma(passes, 2, levels),
        dma(passes, 2, steps, levels),
        dma(passes, 2, steps, levels),
        dma(3),
    ]


def gather_steps(at, halves, x_ref, out_ref, zs, zr, rs, rr, ls):
    levels, steps, zi, q, pn, b = at.levels, at.steps, at.zi, at.q, at.pn, at.b
    half = x_ref.shape[1] // 2
    own = at.slot(zi, q)
    member = at.member

    def block(us, zj, qj, part=None):
        u0, nu = us
        if part is None:
            return out_ref.at[pl.ds(u0, nu), at.slot(zj, qj)]
        return out_ref.at[pl.ds(u0, nu), at.slot(zj, qj), pl.ds(part * half, half)]

    if halves:
        local = pltpu.make_async_copy(x_ref.at[member], out_ref.at[member, own], ls.at[0])
        swap = remote(x_ref.at[1 - member], out_ref.at[member, own], ls.at[1], ls.at[2], at.partner, b)
        swap_in = remote(x_ref.at[1 - member], out_ref.at[1 - member, own], ls.at[1], ls.at[2], at.partner, b)
        swap.start()
        passes = [(member, 1), (1 - member, 1)]
    else:
        local = pltpu.make_async_copy(x_ref, out_ref.at[:, own], ls.at[0])
        passes = [(0, 2)]
    local.start()

    def z_copy(k, us, zj, sign):
        way = 0 if sign > 0 else 1
        ref = block(us, zj, q)
        return remote(ref, ref, zs.at[k, way, zj], zr.at[k, way, zj], at.c + sign * pn, b)

    def r_copy(k, us, zj, way, step, landing=False):
        away = step if landing else step - 1
        ref = block(us, zj, q - away if way == 0 else q + away, way if step == steps else None)
        to = at.right if way == 0 else at.left
        return remote(ref, ref, rs.at[k, way, step - 1, zj], rr.at[k, way, step - 1, zj], to, b)

    def arrive(k, us, sign, d):
        zj = zi + sign * d

        def go():
            if d > 0:
                z_copy(k, us, zj, -sign).wait_recv()
            if sign <= 0:
                pl.when(zi < levels - 1)(lambda: z_copy(k, us, zj, 1).start())
            if sign >= 0:
                pl.when(zi > 0)(lambda: z_copy(k, us, zj, -1).start())
            for way in (0, 1):
                r_copy(k, us, zj, way, 1).start()

        guarded(present(zi, sign, d, levels), go)

    def onward(k, us, sign, d):
        zj = zi + sign * d

        def go():
            for step in range(1, steps + 1):
                for way in (0, 1):
                    r_copy(k, us, zj, way, step, True).wait_recv()
                    if step < steps:
                        r_copy(k, us, zj, way, step + 1).start()

        guarded(present(zi, sign, d, levels), go)

    def finish(k, us, sign, d):
        zj = zi + sign * d

        def go():
            if sign <= 0:
                pl.when(zi < levels - 1)(lambda: z_copy(k, us, zj, 1).wait_send())
            if sign >= 0:
                pl.when(zi > 0)(lambda: z_copy(k, us, zj, -1).wait_send())
            for way in (0, 1):
                for step in range(1, steps + 1):
                    r_copy(k, us, zj, way, step).wait_send()

        guarded(present(zi, sign, d, levels), go)

    local.wait()
    waves = [
        [(k, us, sign, d) for sign in ((0,) if d == 0 else (-1, 1))] for k, us in enumerate(passes) for d in range(levels)
    ]
    for i, wave in enumerate(waves):
        if halves and wave[0][0] == 1 and wave[0][3] == 0:
            swap_in.wait_recv()
        for group in wave:
            arrive(*group)
        if i == 0:
            yield
        else:
            for group in waves[i - 1]:
                onward(*group)
    for group in waves[-1]:
        onward(*group)
    yield
    for wave in waves:
        for group in wave:
            finish(*group)
    if halves:
        swap.wait_send()


def run(steps):
    for _ in steps:
        pass


def gather(grid, x, levels, halves, cid):
    count = levels * grid.plane

    def kernel(x_ref, out_ref, *sems):
        at = Place(grid, levels)
        at.greet_near(halves)
        run(gather_steps(at, halves, x_ref, out_ref, *sems))

    return pl.pallas_call(
        kernel,
        out_shape=jax.ShapeDtypeStruct((2, count) + x.shape[1:], x.dtype),
        in_specs=[INVMEM],
        out_specs=ANY,
        scratch_shapes=gather_sems(grid, levels, halves),
        compiler_params=params(cid, 50),
        name="gather_%d" % count,
    )(x)


def scatter_scratch(grid, levels, halves, rows, width):
    passes, steps = (2 if halves else 1), grid.plane // 2
    return [
        pltpu.VMEM((2, levels * grid.plane, rows, width), BF16),
        pltpu.VMEM((2, levels, 2, rows // 2, width), BF16),
        pltpu.VMEM((2, max(steps - 1, 1), levels, 2, rows, width), BF16),
        pltpu.VMEM((2, levels, 2, rows, width), BF16),
        pltpu.VMEM((rows, width), BF16),
        dma(3),
        dma(passes, 2, levels),
        dma(passes, 2, levels),
        dma(passes, 2, steps, levels),
        dma(passes, 2, steps, levels),
    ]


def scatter_steps(at, halves, out_ref, acc, ring_half, ring_full, line, swapped, ls, zs, zr, rs, rr):
    levels, steps, zi, q, pn, b = at.levels, at.steps, at.zi, at.q, at.pn, at.b
    rows = acc.shape[2]
    half = rows // 2
    member = at.member
    passes = [(1 - member, 1), (member, 1)] if halves else [(0, 2)]

    def block(us, zj, qj, part=None):
        u0, nu = us
        if part is None:
            return acc.at[pl.ds(u0, nu), at.slot(zj, qj)]
        return acc.at[pl.ds(u0, nu), at.slot(zj, qj), pl.ds(part * half, half)]

    def add(us, s, others, lo, count):
        u0, nu = us

        def one(i, carry):
            u, r = u0 + i // (count // 16), lo + (i % (count // 16)) * 16
            total = acc[u, s, pl.ds(r, 16)].astype(F32)
            for other in others:
                total = total + other(u, r)[...].astype(F32)
            acc[u, s, pl.ds(r, 16)] = total.astype(BF16)
            return carry

        lax.fori_loop(0, nu * (count // 16), one, 0)

    def full_at(way, step, zj):
        return lambda u, r: ring_full.at[way, step - 2, zj, u, pl.ds(r, 16)]

    def half_at(way, zj):
        return lambda u, r: ring_half.at[way, zj, u, pl.ds(r - way * half, 16)]

    def line_at(way, zj):
        return lambda u, r: line.at[way, zj, u, pl.ds(r, 16)]

    def r_copy(k, us, zj, way, step):
        u0, nu = us
        sign = 1 if way == 0 else -1
        target = q + sign * (steps + 1 - step)
        if step == 1:
            src, dst = block(us, zj, target, way), ring_half.at[way, zj, pl.ds(u0, nu)]
        else:
            src, dst = block(us, zj, target), ring_full.at[way, step - 2, zj, pl.ds(u0, nu)]
        to = at.right if way == 0 else at.left
        return remote(src, dst, rs.at[k, way, step - 1, zj], rr.at[k, way, step - 1, zj], to, b)

    def z_copy(k, us, zj, way):
        u0, nu = us
        to = at.c + (pn if way == 0 else -pn)
        return remote(block(us, zj, q), line.at[way, zj, pl.ds(u0, nu)], zs.at[k, way, zj], zr.at[k, way, zj], to, b)

    def begin(k, us, sign, d):
        def go():
            for way in (0, 1):
                r_copy(k, us, zi + sign * d, way, 1).start()

        guarded(present(zi, sign, d, levels), go)

    def onward(k, us, sign, d):
        zj = zi + sign * d

        def go():
            for step in range(1, steps + 1):
                for way in (0, 1):
                    r_copy(k, us, zj, way, step).wait_recv()
                    if step < steps:
                        s = at.slot(zj, q + (1 if way == 0 else -1) * (steps - step))
                        if step == 1:
                            add(us, s, [half_at(way, zj)], way * half, half)
                        else:
                            add(us, s, [full_at(way, step, zj)], 0, rows)
                        r_copy(k, us, zj, way, step + 1).start()
            s = at.slot(zj, q)
            if steps > 1:
                add(us, s, [full_at(0, steps, zj), full_at(1, steps, zj)], 0, rows)
            else:
                add(us, s, [half_at(0, zj)], 0, half)
                add(us, s, [half_at(1, zj)], half, half)

            def passed(way):
                z_copy(k, us, zj, way).wait_recv()
                add(us, s, [line_at(way, zj)], 0, rows)

            if sign >= 0:
                pl.when(zi > 0)(lambda: passed(0))
            if sign <= 0:
                pl.when(zi < levels - 1)(lambda: passed(1))
            if sign > 0:
                z_copy(k, us, zj, 0).start()
            if sign < 0:
                z_copy(k, us, zj, 1).start()

        guarded(present(zi, sign, d, levels), go)

    def finish(k, us, sign, d):
        zj = zi + sign * d

        def go():
            for way in (0, 1):
                for step in range(1, steps + 1):
                    r_copy(k, us, zj, way, step).wait_send()
            if sign != 0:
                z_copy(k, us, zj, 0 if sign > 0 else 1).wait_send()

        guarded(present(zi, sign, d, levels), go)

    waves = [
        [(k, us, sign, d) for sign in ((0,) if d == 0 else (-1, 1))]
        for k, us in enumerate(passes)
        for d in range(levels - 1, -1, -1)
    ]
    own = at.slot(zi, q)
    if halves:
        swap = remote(acc.at[1 - member, own], swapped, ls.at[1], ls.at[2], at.partner, b)
    for group in waves[0]:
        begin(*group)
    yield
    for i, wave in enumerate(waves):
        if i + 1 < len(waves):
            for group in waves[i + 1]:
                begin(*group)
        for group in wave:
            onward(*group)
        if halves and wave[0][0] == 0 and wave[0][3] == 0:
            swap.start()
    yield

    def give(src, u):
        def one(i, carry):
            out_ref[u, pl.ds(i * 16, 16)] = src.at[pl.ds(i * 16, 16)][...]
            return carry

        lax.fori_loop(0, rows // 16, one, 0)

    if halves:
        give(acc.at[member, own], member)
        swap.wait_recv()
        give(swapped, 1 - member)
    else:
        give(acc.at[0, own], 0)
        give(acc.at[1, own], 1)
    for wave in waves:
        for group in wave:
            finish(*group)
    if halves:
        swap.wait_send()


def scatter_parts(grid, levels, rows, width):
    blocks = 2 * (2 * levels * (grid.plane // 2 + 2) + levels * grid.plane)
    parts = 1
    while blocks * rows * (width // parts) * 2 > 40 * 2**20:
        parts += 1
        while width % (128 * parts):
            parts += 1
    return parts


def in_parts(grid, levels, call, p, extra):
    parts = scatter_parts(grid, levels, p.shape[2], p.shape[3])
    if parts == 1:
        return call(p, extra)
    piece = p.shape[3] // parts
    sums, others = [], ()
    for i in range(parts):
        got = call(p[..., i * piece : (i + 1) * piece], extra if i == 0 else None)
        sums.append(got[0])
        others = got[1:] if i == 0 else others
    return (jnp.concatenate(sums, axis=-1),) + tuple(others)


def pairwise(n, c, b):
    def to(i):
        return (c + 2 * i + b) % n

    def frm(i, core):
        return (c + n - 2 * i - core) % n

    return to, frm


def share_steps(at, sources, views, ss, sr, fs, fr):
    n, c, b = at.n, at.c, at.b
    half = n // 2
    to, frm = pairwise(n, c, b)
    kinds = len(sources)

    def out_copy(k, i):
        return remote(sources[k](to(i)), views[k](c), ss.at[k, i], sr.at[k, i], to(i), b)

    def landed(k, i):
        return remote(sources[k](c), views[k](frm(i, b)), ss.at[k, i], sr.at[k, i], to(i), b)

    def pass_on(k, i, core):
        ref = views[k](frm(i, core))
        return at.sibling(ref, ref, fs.at[k, i], fr.at[k, i])

    def local(k):
        return pltpu.make_async_copy(sources[k](c), views[k](c), sr.at[k, 0])

    for k in range(kinds):
        for i in range(1, half):
            out_copy(k, i).start()

        @pl.when(b == 1)
        def _():
            out_copy(k, 0).start()

        @pl.when(b == 0)
        def _():
            local(k).start()

    yield
    for i in range(half):
        for k in range(kinds):
            if i > 0:
                landed(k, i).wait_recv()
            else:
                pl.when(b == 1)(lambda: landed(k, 0).wait_recv())
                pl.when(b == 0)(lambda: local(k).wait())
            pass_on(k, i, b).start()
    for k in range(kinds):
        for i in range(half):
            pass_on(k, i, 1 - b).wait_recv()
        for i in range(half):
            pass_on(k, i, b).wait_send()
        for i in range(1, half):
            out_copy(k, i).wait_send()
        pl.when(b == 1)(lambda: out_copy(k, 0).wait_send())


def share_sems(grid, kinds):
    return [dma(kinds, grid.n // 2) for _ in range(4)]


def tell_steps(at, small_ref, all_ref, ts, tr):
    n, c, b = at.n, at.c, at.b

    def tell(off, slot):
        return remote(small_ref, all_ref.at[slot], ts.at[off], tr.at[off], (c + off) % n, b)

    keep = pltpu.make_async_copy(small_ref, all_ref.at[c], ts.at[0])
    keep.start()
    for off in range(1, n):
        tell(off, c).start()
    yield
    keep.wait()
    for off in range(1, n):
        tell(off, (c + n - off) % n).wait_recv()
    for off in range(1, n):
        tell(off, c).wait_send()


def head_rows_steps(at, x_ref, out_ref, hs, hr, fs, fr):
    c, b = at.c, at.b
    copies = at.n // HEADS
    head, rank = c % HEADS, c // HEADS
    mine = rank % 2 == b

    def out_copy(k):
        to = c // copies + HEADS * (2 * k + b)
        return to, remote(x_ref, out_ref.at[c % copies], hs.at[k], hr.at[c % copies], to, b)

    def landed(j):
        return remote(x_ref, out_ref.at[j], hs.at[0], hr.at[j], head * copies + j, b)

    def here(j):
        return pltpu.make_async_copy(x_ref, out_ref.at[j], hr.at[j])

    def pass_on(j):
        return at.sibling(out_ref.at[j], out_ref.at[j], fs.at[j], fr.at[j])

    for k in range(copies // 2):
        to, copy = out_copy(k)
        pl.when(to != c)(lambda: copy.start())
        pl.when(to == c)(lambda: here(c % copies).start())
    yield

    @pl.when(mine)
    def _():
        for j in range(copies):
            pl.when(head * copies + j != c)(lambda: landed(j).wait_recv())
            pl.when(head * copies + j == c)(lambda: here(j).wait())
            pass_on(j).start()
        for j in range(copies):
            pass_on(j).wait_send()

    @pl.when(jnp.logical_not(mine))
    def _():
        for j in range(copies):
            pass_on(j).wait_recv()

    for k in range(copies // 2):
        to, copy = out_copy(k)
        pl.when(to != c)(lambda: copy.wait_send())


def head_rows_sems(grid):
    copies = grid.n // HEADS
    return [dma(copies), dma(copies), dma(copies), dma(copies)]


def add_rows(into, other, rows):
    step = 16 if rows % 16 == 0 else rows

    def one(r, carry):
        at = pl.ds(pl.multiple_of(r * step, step), step)
        into[at] = (into[at].astype(F32) + other[at].astype(F32)).astype(BF16)
        return carry

    lax.fori_loop(0, rows // step, one, 0)


def return_steps(at, x_ref, out_ref, mine, theirs, ls, ps, pr, ss, sr, fs, fr):
    n, c, b = at.n, at.c, at.b
    half = n // 2
    to, frm = pairwise(n, c, b)
    other_to, _ = pairwise(n, c, 1 - b)

    def load(i):
        return pltpu.make_async_copy(x_ref.at[to(i)], mine.at[i], ls.at[i])

    def give(i):
        return at.sibling(x_ref.at[other_to(i)], theirs.at[i], ps.at[i], pr.at[i])

    def out_copy(i):
        return remote(mine.at[i], out_ref.at[c], ss.at[i], sr.at[i], to(i), b)

    def landed(i):
        return remote(mine.at[i], out_ref.at[frm(i, b)], ss.at[i], sr.at[i], to(i), b)

    def pass_on(i, core):
        ref = out_ref.at[frm(i, core)]
        return at.sibling(ref, ref, fs.at[i], fr.at[i])

    local = pltpu.make_async_copy(mine.at[0], out_ref.at[c], ss.at[0])
    order = list(range(1, half)) + [0]
    for i in order:
        load(i).start()
        give(i).start()
    for i in order:
        load(i).wait()
        give(i).wait_recv()
        add_rows(mine.at[i], theirs.at[i], x_ref.shape[1])
        if i > 0:
            out_copy(i).start()
        else:
            pl.when(b == 1)(lambda: out_copy(0).start())
            pl.when(b == 0)(lambda: local.start())
    yield
    for i in order:
        if i > 0:
            landed(i).wait_recv()
        else:
            pl.when(b == 1)(lambda: landed(0).wait_recv())
            pl.when(b == 0)(lambda: local.wait())
        pass_on(i, b).start()
    for i in range(half):
        pass_on(i, 1 - b).wait_recv()
    for i in range(half):
        give(i).wait_send()
        pass_on(i, b).wait_send()
    for i in range(1, half):
        out_copy(i).wait_send()
    pl.when(b == 1)(lambda: out_copy(0).wait_send())


def return_scratch(grid, shape):
    blocks = (grid.n // 2,) + shape
    return [pltpu.VMEM(blocks, BF16), pltpu.VMEM(blocks, BF16)] + [dma(grid.n // 2) for _ in range(7)]


def head_return_steps(at, x_ref, out_ref, mine, theirs, ls, ps, pr, hs, hr, fs, fr):
    c, b = at.c, at.b
    copies = at.n // HEADS
    head, rank = c % HEADS, c // HEADS
    taken = (c % copies) % 2 == b

    def load(k):
        return pltpu.make_async_copy(x_ref.at[2 * k + b], mine.at[k], ls.at[k])

    def give(k):
        return at.sibling(x_ref.at[2 * k + 1 - b], theirs.at[k], ps.at[k], pr.at[k])

    def out_copy(k):
        to = head * copies + 2 * k + b
        return to, remote(mine.at[k], out_ref.at[rank], hs.at[k], hr.at[rank], to, b)

    def landed(i):
        return remote(mine.at[0], out_ref.at[i], hs.at[0], hr.at[i], c // copies + HEADS * i, b)

    def here(k, i):
        return pltpu.make_async_copy(mine.at[k], out_ref.at[i], hr.at[i])

    def pass_on(i):
        return at.sibling(out_ref.at[i], out_ref.at[i], fs.at[i], fr.at[i])

    for k in range(copies // 2):
        load(k).start()
        give(k).start()
    for k in range(copies // 2):
        load(k).wait()
        give(k).wait_recv()
        add_rows(mine.at[k], theirs.at[k], x_ref.shape[1])
        to, copy = out_copy(k)
        pl.when(to != c)(lambda: copy.start())
        pl.when(to == c)(lambda: here(k, rank).start())
    yield

    @pl.when(taken)
    def _():
        for i in range(copies):
            frm = c // copies + HEADS * i
            pl.when(frm != c)(lambda: landed(i).wait_recv())
            pl.when(frm == c)(lambda: here(0, i).wait())
            pass_on(i).start()
        for i in range(copies):
            pass_on(i).wait_send()

    @pl.when(jnp.logical_not(taken))
    def _():
        for i in range(copies):
            pass_on(i).wait_recv()

    for k in range(copies // 2):
        give(k).wait_send()
        to, copy = out_copy(k)
        pl.when(to != c)(lambda: copy.wait_send())


def head_return_scratch(grid, shape):
    copies = grid.n // HEADS
    blocks = (copies // 2,) + shape
    return [pltpu.VMEM(blocks, BF16), pltpu.VMEM(blocks, BF16)] + [dma(copies) for _ in range(7)]


def pair_steps(at, x_ref, out_ref, other, sems):
    copy = at.sibling(x_ref, other, sems.at[0], sems.at[1])
    copy.start()
    yield
    copy.wait_recv()

    def one(r, carry):
        rows = pl.ds(pl.multiple_of(r * 16, 16), 16)
        out_ref[rows] = x_ref[rows].astype(F32) + other[rows].astype(F32)
        return carry

    lax.fori_loop(0, x_ref.shape[0] // 16, one, 0)
    copy.wait_send()


class Split:
    def __init__(self, refs):
        self.refs = list(refs)

    def take(self, count):
        got, self.refs = self.refs[:count], self.refs[count:]
        return got


def together(*tasks):
    for task in tasks:
        next(task, None)
    for task in tasks:
        run(task)


def open_kernel(grid, x, qkv_parts, out_codes, small, cid):
    n, levels = grid.n, grid.planes // 2
    rows_d, width = qkv_parts.shape[1:]
    flat = rows_d % 16 == 0
    copies = n // HEADS
    gs, ss, ts, hs = gather_sems(grid, levels, True), share_sems(grid, 1), [dma(n), dma(n)], head_rows_sems(grid)

    def kernel(x_ref, w_ref, o_ref, small_ref, seen_ref, codes_ref, rows_ref, all_ref, *scratch):
        at = Place(grid, levels)
        refs = Split(scratch)
        at.greet_all()

        def view(j):
            return codes_ref.at[pl.ds(j * rows_d, rows_d)] if flat else codes_ref.at[j]

        together(
            gather_steps(at, True, x_ref, seen_ref, *refs.take(len(gs))),
            share_steps(at, [lambda to: w_ref.at[to % HEADS]], [view], *refs.take(len(ss))),
            tell_steps(at, small_ref, all_ref, *refs.take(2)),
            head_rows_steps(at, o_ref, rows_ref, *refs.take(4)),
        )

    codes_shape = (n * rows_d, width) if flat else (n, rows_d, width)
    return pl.pallas_call(
        kernel,
        out_shape=(
            jax.ShapeDtypeStruct((2, levels * grid.plane) + x.shape[1:], BF16),
            jax.ShapeDtypeStruct(codes_shape, BF16),
            jax.ShapeDtypeStruct((copies,) + out_codes.shape, BF16),
            jax.ShapeDtypeStruct((n,) + small.shape, small.dtype),
        ),
        in_specs=[INVMEM] * 4,
        out_specs=(ANY,) * 4,
        scratch_shapes=gs + ss + ts + hs,
        compiler_params=params(cid, 50),
        name="open",
    )(x, qkv_parts, out_codes, small)


def scatter_kernel(grid, levels, halves, cid, name, tasks=None):
    made, in_specs, out_shapes, out_specs, extra_scratch = tasks if tasks else (None, [], (), (), [])

    def call(p, extra):
        rows, width = p.shape[2:]
        more = () if extra is None else tuple(extra)
        own = scatter_scratch(grid, levels, halves, rows, width)

        def kernel(*refs):
            refs = Split(refs)
            (p_ref,) = refs.take(1)
            more_refs = refs.take(len(more))
            (out_ref,) = refs.take(1)
            out_refs = refs.take(len(out_shapes) if more else 0)
            mine = refs.take(len(own))
            at = Place(grid, levels)
            load = pltpu.make_async_copy(p_ref, mine[0], mine[5].at[0])
            load.start()
            if more:
                at.greet_all()
            else:
                at.greet_near(halves)
            load.wait()
            others = made(at, more_refs, out_refs, refs) if more else []
            together(scatter_steps(at, halves, out_ref, *mine), *others)

        return pl.pallas_call(
            kernel,
            out_shape=(jax.ShapeDtypeStruct((2, rows, width), BF16),) + (out_shapes if more else ()),
            in_specs=[ANY] + (in_specs if more else []),
            out_specs=(INVMEM,) + (out_specs if more else ()),
            scratch_shapes=own + (extra_scratch if more else []),
            compiler_params=params(cid + (0 if more else 20), 60),
            name=name,
        )(p, *more)

    return call


def feed_windows(grid):
    units = FF // grid.n
    window = 128 * max(-(-((c * units) % 128 + units) // 128) for c in range(grid.n))
    return units, window, lambda c: ((c * units) // 128) * 128


def attention_sums(grid, p, gate_codes, up_codes, cid):
    n, levels = grid.n, grid.planes // 2
    rows_d = gate_codes.shape[0]
    flat = rows_d % 16 == 0
    units, window, start = feed_windows(grid)
    ss = share_sems(grid, 2)

    def tasks(at, ins, outs, refs):
        def source(ref):
            return lambda to: ref.at[:, pl.ds(pl.multiple_of(start(to), 128), window)]

        def view(ref):
            return lambda j: ref.at[pl.ds(j * rows_d, rows_d)] if flat else ref.at[j]

        return [share_steps(at, [source(r) for r in ins], [view(r) for r in outs], *refs.take(len(ss)))]

    shape = (n * rows_d, window) if flat else (n, rows_d, window)
    call = scatter_kernel(
        grid,
        levels,
        True,
        cid,
        "attention_sums",
        (tasks, [INVMEM, INVMEM], (jax.ShapeDtypeStruct(shape, BF16),) * 2, (ANY, ANY), ss),
    )
    return in_parts(grid, levels, call, p, (gate_codes, up_codes))


def feed_sums(grid, p, cid):
    return in_parts(grid, grid.planes, scatter_kernel(grid, grid.planes, False, cid, "feed_sums"), p, None)[0]


def feed_back_sums(grid, p, pair_grad, cid):
    rs = return_scratch(grid, pair_grad.shape[1:])

    def tasks(at, ins, outs, refs):
        return [return_steps(at, ins[0], outs[0], *refs.take(len(rs)))]

    call = scatter_kernel(
        grid,
        grid.planes,
        False,
        cid,
        "feed_back_sums",
        (tasks, [ANY], (jax.ShapeDtypeStruct(pair_grad.shape, BF16),), (ANY,), rs),
    )
    return in_parts(grid, grid.planes, call, p, (pair_grad,))


def attention_back_sums(grid, p, qkv_grad, out_grad, down_grad, cid):
    n, levels = grid.n, grid.planes // 2
    rs, hs = return_scratch(grid, qkv_grad.shape[1:]), head_return_scratch(grid, out_grad.shape[1:])
    ps = [pltpu.VMEM(down_grad.shape, BF16), dma(2)]

    def tasks(at, ins, outs, refs):
        return [
            return_steps(at, ins[0], outs[0], *refs.take(len(rs))),
            head_return_steps(at, ins[1], outs[1], *refs.take(len(hs))),
            pair_steps(at, ins[2], outs[2], *refs.take(2)),
        ]

    call = scatter_kernel(
        grid,
        levels,
        True,
        cid,
        "attention_back_sums",
        (
            tasks,
            [ANY, ANY, INVMEM],
            (
                jax.ShapeDtypeStruct(qkv_grad.shape, BF16),
                jax.ShapeDtypeStruct(out_grad.shape, BF16),
                jax.ShapeDtypeStruct(down_grad.shape, F32),
            ),
            (ANY, ANY, INVMEM),
            rs + hs + ps,
        ),
    )
    return in_parts(grid, levels, call, p, (qkv_grad, out_grad, down_grad))


def gains_kernel(grid, gains, cid):
    n = grid.n
    ss = share_sems(grid, 1)

    def kernel(x_ref, out_ref, total, other, sems, *scratch):
        at = Place(grid, grid.planes)
        at.greet_all()
        copy = at.sibling(x_ref, other, sems.at[0], sems.at[1])
        copy.start()
        copy.wait()
        total[...] = x_ref[...] + other[...]
        together(share_steps(at, [lambda to: total], [lambda j: out_ref.at[j]], *scratch))

    return pl.pallas_call(
        kernel,
        out_shape=jax.ShapeDtypeStruct((n,) + gains.shape, F32),
        in_specs=[INVMEM],
        out_specs=INVMEM,
        scratch_shapes=[pltpu.VMEM(gains.shape, F32), pltpu.VMEM(gains.shape, F32), dma(2)] + ss,
        compiler_params=params(cid),
        name="gains",
    )(gains)


def normed(value, gain):
    return value * lax.rsqrt(jnp.mean(value * value, axis=-1, keepdims=True) + 1e-06) * gain


def angles(places, head):
    freqs = 10000.0 ** (-(jnp.arange(head // 2, dtype=F32) * 2.0 / head))
    return places.astype(F32)[..., None] * freqs


def rotate(values, cosine, sine):
    half = values.shape[-1] // 2
    first = values[..., :half]
    second = values[..., half:]
    return jnp.concatenate([first * cosine - second * sine, second * cosine + first * sine], axis=-1)


def width_step(number):
    remainder = number % 3
    return jnp.where(remainder == 0, 1.0, jnp.where(remainder == 1, 16.0, 64.0)).astype(F32)


def dequantized(codes, column_scale, step):
    offset = jnp.where(step > 1.0, 0.5 * step, 0.0)
    level = jnp.floor(codes.astype(F32) / step) * step + offset
    return (level * column_scale[None, :]).astype(BF16)


def dot(left, right):
    return jnp.dot(left, right, preferred_element_type=F32)


def dot_t(left, right):
    return lax.dot_general(left, right, (((1,), (1,)), ((), ())), preferred_element_type=F32)


def t_dot(left, right):
    return lax.dot_general(left, right, (((0,), (0,)), ((), ())), preferred_element_type=F32)


def unwindowed(grid, got):
    n, rows, window = got.shape
    units = FF // n
    inner = n // HEADS
    whole = inner * units
    got = got.astype(F32).reshape(n // inner, inner, rows, window)
    total = 0.0
    for i in range(inner):
        start = i * units // 128 * 128
        total = total + jnp.pad(got[:, i], ((0, 0), (0, 0), (start, whole - start - window)))
    return jnp.transpose(total, (1, 0, 2)).reshape(rows, FF)


def on_device(
    grid,
    tokens,
    segments,
    positions,
    cotangent,
    query_codes,
    key_codes,
    value_codes,
    output_codes,
    gate_codes,
    up_codes,
    down_codes,
    query_scale,
    key_scale,
    value_scale,
    output_scale,
    gate_scale,
    up_scale,
    down_scale,
    attention_gain,
    attention_post_gain,
    feed_gain,
    feed_post_gain,
):
    n = grid.n
    group, block, _ = tokens.shape
    length = n * block
    pairs = HEADS // KV_HEADS
    scale = HEAD ** (-0.5)
    chip, core = lax.axis_index("seq"), lax.axis_index("batch")
    half = n // 2
    member = chip // half
    head = chip % HEADS
    kv_head = head // pairs
    parts = half // HEADS
    copies = n // HEADS
    asked = length // parts
    first_asked = ((chip % half) // HEADS) * asked
    steps = [width_step(core * group + m) for m in range(group)]
    step = width_step(core * group + member)
    rows_d = D // n
    units, window, _ = feed_windows(grid)

    source = tokens.astype(F32)
    first_normed = normed(source, attention_gain).astype(BF16)
    q_parts = jnp.transpose(query_codes.reshape(rows_d, HEADS, HEAD), (1, 0, 2))
    k_parts = jnp.repeat(jnp.transpose(key_codes.reshape(rows_d, KV_HEADS, HEAD), (1, 0, 2)), pairs, axis=0)
    v_parts = jnp.repeat(jnp.transpose(value_codes.reshape(rows_d, KV_HEADS, HEAD), (1, 0, 2)), pairs, axis=0)
    qkv_parts = jnp.concatenate([q_parts, k_parts, v_parts], axis=-1).astype(BF16)
    small = jnp.zeros((8, 128), jnp.int32).at[:group, :block].set(positions)
    seen, qkv_codes, out_codes, all_places = open_kernel(
        grid, first_normed, qkv_parts, output_codes.astype(BF16), small, 1
    )
    seen = seen.reshape(length, D)

    qkv_scale = jnp.concatenate(
        [
            lax.dynamic_slice_in_dim(query_scale, head * HEAD, HEAD),
            lax.dynamic_slice_in_dim(key_scale, kv_head * HEAD, HEAD),
            lax.dynamic_slice_in_dim(value_scale, kv_head * HEAD, HEAD),
        ]
    )
    qkv_matrix = dequantized(qkv_codes.reshape(D, 3 * HEAD), qkv_scale, step)
    out_matrix = dequantized(out_codes.reshape(HEAD, D), output_scale, step)

    places_all = lax.dynamic_index_in_dim(all_places[:, :group, :block], member, 1, False).reshape(length)
    turn = angles(places_all, HEAD)
    cosine, sine = jnp.cos(turn), jnp.sin(turn)
    if parts == 1:
        seen_asked, places_asked, cosine_q, sine_q = seen, places_all, cosine, sine
        projected = dot(seen, qkv_matrix)
        q_lin, kv_lin = projected[:, :HEAD], projected[:, HEAD:]
    else:
        seen_asked, places_asked, cosine_q, sine_q = [
            lax.dynamic_slice_in_dim(a, first_asked, asked) for a in (seen, places_all, cosine, sine)
        ]
        q_lin, kv_lin = dot(seen_asked, qkv_matrix[:, :HEAD]), dot(seen, qkv_matrix[:, HEAD:])
    queries = rotate(q_lin, cosine_q, sine_q).astype(BF16)
    keys = rotate(kv_lin[:, :HEAD], cosine, sine).astype(BF16)
    values = kv_lin[:, HEAD:].astype(BF16)
    q_index = first_asked + jnp.arange(asked, dtype=jnp.int32)
    key_index = jnp.arange(length, dtype=jnp.int32)
    allowed = (key_index[None, :] <= q_index[:, None]) & (key_index[None, :] >= (q_index - places_asked)[:, None])
    bent = jnp.tanh(dot_t(queries, keys) * scale / cap_limit)
    kernel = jnp.where(allowed, jnp.exp(cap_limit * bent), 0.0)
    totals = jnp.sum(kernel, axis=-1, keepdims=True)
    kernel_low = kernel.astype(BF16)
    attended = dot(kernel_low, values) / totals
    attended_low = attended.astype(BF16)

    def spread(part):
        if parts > 1:
            part = lax.dynamic_update_slice_in_dim(jnp.zeros((length, D), BF16), part, first_asked, 0)
        return part.reshape(2, half, block, D)

    attention_raw, gate_got, up_got = attention_sums(
        grid,
        spread(dot(attended_low, out_matrix).astype(BF16)),
        gate_codes.astype(BF16),
        up_codes.astype(BF16),
        2,
    )
    attention_raw = attention_raw.astype(F32)
    first_column = chip * units // 128 * 128
    inset = chip * units - first_column
    pair_codes = jnp.concatenate([gate_got.reshape(D, window), up_got.reshape(D, window)], axis=-1)
    pair_scale = jnp.concatenate(
        [lax.dynamic_slice_in_dim(s, first_column, window) for s in (gate_scale, up_scale)]
    )
    pair_matrices = [dequantized(pair_codes, pair_scale, s) for s in steps]
    down_matrices = [
        lax.dynamic_update_slice(
            jnp.zeros((window, D), BF16), dequantized(down_codes, down_scale, s), (inset, 0)
        )
        for s in steps
    ]

    mixed = source + normed(attention_raw, attention_post_gain)
    second_normed = normed(mixed, feed_gain).astype(BF16)
    fed = gather(grid, second_normed, grid.planes, False, 3).reshape(group, length, D)
    gate_up = [dot(fed[m], pair_matrices[m]) for m in range(group)]
    hidden = [(jax.nn.gelu(g[:, :window], approximate=True) * g[:, window:]).astype(BF16) for g in gate_up]
    down_part = jnp.stack([dot(hidden[m], down_matrices[m]).astype(BF16) for m in range(group)])
    down_raw = feed_sums(grid, down_part.reshape(group, n, block, D), 4).astype(F32)
    branch, pull_out = jax.vjp(normed, down_raw, feed_post_gain)
    output = (mixed + branch).astype(BF16)
    upstream = cotangent.astype(F32)
    grad_down_raw, grad_post_feed = pull_out(upstream)
    down_low = gather(grid, grad_down_raw.astype(BF16), grid.planes, False, 3).reshape(group, length, D)
    pair_low, second_part = [], []
    for m in range(group):
        grad_hidden = dot_t(down_low[m], down_matrices[m])
        _, pull_glu = jax.vjp(
            lambda left, right: jax.nn.gelu(left, approximate=True) * right,
            gate_up[m][:, :window],
            gate_up[m][:, window:],
        )
        pair_low.append(jnp.concatenate(pull_glu(grad_hidden), axis=-1).astype(BF16))
        second_part.append(dot_t(pair_low[m], pair_matrices[m]).astype(BF16))
    pair_grad = sum(t_dot(fed[m], pair_low[m]) for m in range(group)).astype(BF16)
    down_grad = sum(t_dot(hidden[m], down_low[m]) for m in range(group)).astype(BF16)
    down_grad = lax.dynamic_slice(down_grad, (inset, 0), (units, D))
    grad_second, pair_got = feed_back_sums(
        grid, jnp.stack(second_part).reshape(group, n, block, D), pair_grad.reshape(n, rows_d, 2 * window), 5
    )
    grad_second = grad_second.astype(F32)
    gate_grad, up_grad = (unwindowed(grid, pair_got[..., i * window : (i + 1) * window]) for i in range(2))

    _, pull_feed = jax.vjp(normed, mixed, feed_gain)
    grad_mixed_part, grad_pre_feed = pull_feed(grad_second)
    grad_mixed = upstream + grad_mixed_part
    _, pull_post = jax.vjp(normed, attention_raw, attention_post_gain)
    grad_attention, grad_post_attention = pull_post(grad_mixed)
    attention_low = gather(grid, grad_attention.astype(BF16), grid.planes // 2, True, 6).reshape(length, D)
    if parts > 1:
        attention_low = lax.dynamic_slice_in_dim(attention_low, first_asked, asked)
    grad_attended = dot_t(attention_low, out_matrix)
    grad_sums = (grad_attended / totals).astype(BF16)
    offsets = jnp.sum(grad_attended * attended, axis=-1, keepdims=True) / totals
    grad_kernel = dot_t(grad_sums, values) - offsets
    grad_raw = (kernel * grad_kernel * (1.0 - bent * bent)).astype(BF16)
    grad_q = dot(grad_raw, keys) * scale
    grad_k = t_dot(grad_raw, queries) * scale
    grad_v = t_dot(kernel_low, grad_sums)
    q_low = rotate(grad_q, cosine_q, -sine_q).astype(BF16)
    kv_low = jnp.concatenate([rotate(grad_k, cosine, -sine), grad_v], axis=-1).astype(BF16)
    if parts == 1:
        qkv_low = jnp.concatenate([q_low, kv_low], axis=-1)
        first_part = dot_t(qkv_low, qkv_matrix)
        qkv_grad = t_dot(seen, qkv_low)
    else:
        first_part = dot_t(kv_low, qkv_matrix[:, HEAD:])
        q_back = dot_t(q_low, qkv_matrix[:, :HEAD])
        first_part = lax.dynamic_update_slice_in_dim(
            first_part, lax.dynamic_slice_in_dim(first_part, first_asked, asked) + q_back, first_asked, 0
        )
        qkv_grad = jnp.concatenate([t_dot(seen_asked, q_low), t_dot(seen, kv_low)], axis=-1)
    out_part = t_dot(attended_low, attention_low).astype(BF16).reshape(copies, HEAD // copies, D)
    grad_first, qkv_got, out_got, down_grad = attention_back_sums(
        grid,
        first_part.astype(BF16).reshape(2, half, block, D),
        qkv_grad.astype(BF16).reshape(n, rows_d, 3 * HEAD),
        out_part,
        down_grad,
        7,
    )
    grad_first = grad_first.astype(F32)
    _, pull_in = jax.vjp(normed, source, attention_gain)
    grad_source_part, grad_pre_attention = pull_in(grad_first)
    grad_in = (grad_mixed + grad_source_part).astype(BF16)
    qkv_got = jnp.sum(qkv_got.astype(F32).reshape(copies, HEADS, rows_d, 3 * HEAD), axis=0)
    query_grad = jnp.transpose(qkv_got[..., :HEAD], (1, 0, 2)).reshape(rows_d, HEADS * HEAD)
    kv_grad = jnp.sum(qkv_got[..., HEAD:].reshape(KV_HEADS, pairs, rows_d, 2 * HEAD), axis=1)
    key_grad = jnp.transpose(kv_grad[..., :HEAD], (1, 0, 2)).reshape(rows_d, KV_HEADS * HEAD)
    value_grad = jnp.transpose(kv_grad[..., HEAD:], (1, 0, 2)).reshape(rows_d, KV_HEADS * HEAD)
    out_grad = jnp.sum(out_got.astype(F32), axis=0)
    gains = jnp.stack([grad_pre_attention, grad_post_attention, grad_pre_feed, grad_post_feed])
    gains = jnp.sum(gains_kernel(grid, gains.reshape(8, D // 2), 8), axis=0).reshape(4, D)
    return (
        output,
        grad_in,
        query_grad,
        key_grad,
        value_grad,
        out_grad,
        gate_grad,
        up_grad,
        down_grad,
    ) + tuple(gains[i] for i in range(4))


def solution(mesh):
    rows = P("seq", None)
    return jax.shard_map(
        functools.partial(on_device, Grid(mesh.shape["seq"])),
        mesh=mesh,
        in_specs=(P("batch", "seq", None), P("batch", "seq"), P("batch", "seq"), P("batch", "seq", None))
        + (rows,) * 7
        + (P(),) * 11,
        out_specs=(P("batch", "seq", None),) * 2 + (rows,) * 7 + (P(),) * 4,
        check_vma=False,
    )
```

```python
import functools

import jax
import jax.numpy as jnp
from jax import lax
from jax.experimental import pallas as pl
from jax.experimental.pallas import tpu as pltpu
from jax.sharding import PartitionSpec as P

D = 2304
HEADS = 8
KV_HEADS = 4
HEAD = 256
FF = 9216
MESH = pl.DeviceIdType.MESH
F32 = jnp.float32
BF16 = jnp.bfloat16


cap_limit = 50.0


class Grid:
    def __init__(self, n):
        self.n = n
        self.planes = 4 if n % 8 == 0 else 2
        self.plane = n // self.planes
        wide = 1
        while wide * wide < self.plane:
            wide *= 2
        self.wide = wide

    def snake(self, p):
        y, x = p // self.wide, p % self.wide
        return y * self.wide + x + (y % 2) * (self.wide - 1 - 2 * x)


def remote(src, dst, send, recv, chip, core):
    return pltpu.make_async_remote_copy(
        src_ref=src, dst_ref=dst, send_sem=send, recv_sem=recv, device_id=(chip, core), device_id_type=MESH
    )


def greet(barrier, chip, core):
    pl.semaphore_signal(barrier, inc=1, device_id=(chip, core), device_id_type=MESH)


class Place:
    def __init__(self, grid, levels):
        self.grid, self.levels = grid, levels
        self.n, self.pn = grid.n, grid.plane
        self.steps = self.pn // 2
        self.c, self.b = lax.axis_index("seq"), lax.axis_index("batch")
        self.z, p = self.c // self.pn, self.c % self.pn
        self.q = grid.snake(p)
        self.zi = self.z % levels
        self.right = self.z * self.pn + grid.snake((self.q + 1) % self.pn)
        self.left = self.z * self.pn + grid.snake((self.q + self.pn - 1) % self.pn)
        self.member = self.c // (self.n // 2)
        self.partner = (self.c + self.n // 2) % self.n

    def slot(self, zj, qj):
        return zj * self.pn + self.grid.snake((qj + 2 * self.pn) % self.pn)

    def sibling(self, src, dst, send, recv):
        return remote(src, dst, send, recv, self.c, 1 - self.b)

    def greet_near(self, halves):
        barrier = pltpu.get_barrier_semaphore()
        zi, levels = self.zi, self.levels
        greet(barrier, self.right, self.b)
        greet(barrier, self.left, self.b)
        pl.when(zi > 0)(lambda: greet(barrier, self.c - self.pn, self.b))
        pl.when(zi < levels - 1)(lambda: greet(barrier, self.c + self.pn, self.b))
        if halves:
            greet(barrier, self.partner, self.b)
        count = 2 + jnp.where(zi > 0, 1, 0) + jnp.where(zi < levels - 1, 1, 0) + (1 if halves else 0)
        pl.semaphore_wait(barrier, count)

    def greet_all(self):
        barrier = pltpu.get_barrier_semaphore()
        greet(barrier, self.c, 1 - self.b)

        def one(off, carry):
            greet(barrier, (self.c + off) % self.n, self.b)
            return carry

        lax.fori_loop(1, self.n, one, 0)
        pl.semaphore_wait(barrier, self.n)


def present(zi, sign, d, levels):
    if d == 0:
        return None
    return (zi - d >= 0) if sign < 0 else (zi + d < levels)


def guarded(condition, action):
    if condition is None:
        action()
    else:
        pl.when(condition)(action)


def dma(*shape):
    return pltpu.SemaphoreType.DMA(shape)


ANY = pl.BlockSpec(memory_space=pl.ANY)
INVMEM = pl.BlockSpec(memory_space=pltpu.VMEM)


def params(cid, mib=None):
    if mib is None:
        return pltpu.CompilerParams(collective_id=cid, has_side_effects=True)
    return pltpu.CompilerParams(collective_id=cid, has_side_effects=True, vmem_limit_bytes=mib * 2**20)


def gather_sems(grid, levels, halves):
    passes, steps = (2 if halves else 1), grid.plane // 2
    return [
        dma(passes, 2, levels),
        dma(passes, 2, levels),
        dma(passes, 2, steps, levels),
        dma(passes, 2, steps, levels),
        dma(3),
    ]


def gather_steps(at, halves, x_ref, out_ref, zs, zr, rs, rr, ls):
    levels, steps, zi, q, pn, b = at.levels, at.steps, at.zi, at.q, at.pn, at.b
    half = x_ref.shape[1] // 2
    own = at.slot(zi, q)
    member = at.member

    def block(us, zj, qj, part=None):
        u0, nu = us
        if part is None:
            return out_ref.at[pl.ds(u0, nu), at.slot(zj, qj)]
        return out_ref.at[pl.ds(u0, nu), at.slot(zj, qj), pl.ds(part * half, half)]

    if halves:
        local = pltpu.make_async_copy(x_ref.at[member], out_ref.at[member, own], ls.at[0])
        swap = remote(x_ref.at[1 - member], out_ref.at[member, own], ls.at[1], ls.at[2], at.partner, b)
        swap_in = remote(x_ref.at[1 - member], out_ref.at[1 - member, own], ls.at[1], ls.at[2], at.partner, b)
        swap.start()
        passes = [(member, 1), (1 - member, 1)]
    else:
        local = pltpu.make_async_copy(x_ref, out_ref.at[:, own], ls.at[0])
        passes = [(0, 2)]
    local.start()

    def z_copy(k, us, zj, sign):
        way = 0 if sign > 0 else 1
        ref = block(us, zj, q)
        return remote(ref, ref, zs.at[k, way, zj], zr.at[k, way, zj], at.c + sign * pn, b)

    def r_copy(k, us, zj, way, step, landing=False):
        away = step if landing else step - 1
        ref = block(us, zj, q - away if way == 0 else q + away, way if step == steps else None)
        to = at.right if way == 0 else at.left
        return remote(ref, ref, rs.at[k, way, step - 1, zj], rr.at[k, way, step - 1, zj], to, b)

    def arrive(k, us, sign, d):
        zj = zi + sign * d

        def go():
            if d > 0:
                z_copy(k, us, zj, -sign).wait_recv()
            if sign <= 0:
                pl.when(zi < levels - 1)(lambda: z_copy(k, us, zj, 1).start())
            if sign >= 0:
                pl.when(zi > 0)(lambda: z_copy(k, us, zj, -1).start())
            for way in (0, 1):
                r_copy(k, us, zj, way, 1).start()

        guarded(present(zi, sign, d, levels), go)

    def onward(k, us, sign, d):
        zj = zi + sign * d

        def go():
            for step in range(1, steps + 1):
                for way in (0, 1):
                    r_copy(k, us, zj, way, step, True).wait_recv()
                    if step < steps:
                        r_copy(k, us, zj, way, step + 1).start()

        guarded(present(zi, sign, d, levels), go)

    def finish(k, us, sign, d):
        zj = zi + sign * d

        def go():
            if sign <= 0:
                pl.when(zi < levels - 1)(lambda: z_copy(k, us, zj, 1).wait_send())
            if sign >= 0:
                pl.when(zi > 0)(lambda: z_copy(k, us, zj, -1).wait_send())
            for way in (0, 1):
                for step in range(1, steps + 1):
                    r_copy(k, us, zj, way, step).wait_send()

        guarded(present(zi, sign, d, levels), go)

    local.wait()
    waves = [
        [(k, us, sign, d) for sign in ((0,) if d == 0 else (-1, 1))] for k, us in enumerate(passes) for d in range(levels)
    ]
    for i, wave in enumerate(waves):
        if halves and wave[0][0] == 1 and wave[0][3] == 0:
            swap_in.wait_recv()
        for group in wave:
            arrive(*group)
            yield
        if i > 0:
            for group in waves[i - 1]:
                onward(*group)
                yield
    for group in waves[-1]:
        onward(*group)
        yield
    for wave in waves:
        for group in wave:
            finish(*group)
    if halves:
        swap.wait_send()


def run(steps):
    for _ in steps:
        pass


def gather(grid, x, levels, halves, cid):
    count = levels * grid.plane

    def kernel(x_ref, out_ref, *sems):
        at = Place(grid, levels)
        at.greet_near(halves)
        run(gather_steps(at, halves, x_ref, out_ref, *sems))

    return pl.pallas_call(
        kernel,
        out_shape=jax.ShapeDtypeStruct((2, count) + x.shape[1:], x.dtype),
        in_specs=[INVMEM],
        out_specs=ANY,
        scratch_shapes=gather_sems(grid, levels, halves),
        compiler_params=params(cid, 50),
        name="gather_%d" % count,
    )(x)


class LevelGather:
    def __init__(self, at, x_ref, out_ref, zs, zr, rs, rr, ls):
        self.at, self.x, self.out = at, x_ref, out_ref
        self.zs, self.zr, self.rs, self.rr, self.ls = zs, zr, rs, rr, ls
        self.half = x_ref.shape[1] // 2

    def block(self, zj, qj, part=None):
        if part is None:
            return self.out.at[:, self.at.slot(zj, qj)]
        return self.out.at[:, self.at.slot(zj, qj), pl.ds(part * self.half, self.half)]

    def z_copy(self, zj, way):
        at, ref = self.at, self.block(zj, self.at.q)
        to = at.c + (at.pn if way == 0 else -at.pn)
        return remote(ref, ref, self.zs.at[0, way, zj], self.zr.at[0, way, zj], to, at.b)

    def r_copy(self, zj, way, step, landing=False):
        at = self.at
        away = step if landing else step - 1
        ref = self.block(zj, at.q - away if way == 0 else at.q + away, way if step == at.steps else None)
        to = at.right if way == 0 else at.left
        return remote(ref, ref, self.rs.at[0, way, step - 1, zj], self.rr.at[0, way, step - 1, zj], to, at.b)

    def begin(self):
        local = pltpu.make_async_copy(self.x, self.block(self.at.zi, self.at.q), self.ls.at[0])
        local.start()
        local.wait()
        self.send(0)

    def send(self, offset):
        at = self.at
        zj = at.zi + offset
        pl.when((offset <= 0) & (at.zi < at.levels - 1))(lambda: self.z_copy(zj, 0).start())
        pl.when((offset >= 0) & (at.zi > 0))(lambda: self.z_copy(zj, 1).start())
        for way in (0, 1):
            self.r_copy(zj, way, 1).start()

    def arrive(self, sign, d):
        zj = self.at.zi + sign * d
        self.z_copy(zj, 0 if sign < 0 else 1).wait_recv()
        self.send(sign * d)

    def onward(self, sign, d):
        zj = self.at.zi + sign * d
        for step in range(1, self.at.steps + 1):
            for way in (0, 1):
                self.r_copy(zj, way, step, True).wait_recv()
                if step < self.at.steps:
                    self.r_copy(zj, way, step + 1).start()

    def finish(self):
        at = self.at

        def one(zj, carry):
            pl.when((zj <= at.zi) & (at.zi < at.levels - 1))(lambda: self.z_copy(zj, 0).wait_send())
            pl.when((zj >= at.zi) & (at.zi > 0))(lambda: self.z_copy(zj, 1).wait_send())
            for way in (0, 1):
                for step in range(1, at.steps + 1):
                    self.r_copy(zj, way, step).wait_send()
            return carry

        lax.fori_loop(0, at.levels, one, 0)

    def run(self, compute):
        at = self.at
        zi, levels = at.zi, at.levels

        def one(t, carry):
            pl.when((t < levels) & (zi - t >= 0))(lambda: self.arrive(-1, t))
            pl.when((t < levels) & (zi + t < levels))(lambda: self.arrive(1, t))
            e = t - 2

            def side(i, carry):
                zj = zi + (2 * i - 1) * e
                here = (e >= 0) & (zj >= 0) & (zj < levels) & ((e > 0) | (i == 0))
                pl.when(here)(lambda: compute(zj, e == 0))
                return carry

            lax.fori_loop(0, 2, side, 0)
            d = t - 1
            pl.when((d < levels) & (zi - d >= 0))(lambda: self.onward(-1, d))
            pl.when((d > 0) & (d < levels) & (zi + d < levels))(lambda: self.onward(1, d))
            return carry

        lax.fori_loop(1, levels + 2, one, 0)
        self.finish()


def member_step(core, group, member):
    remainder = (core * group + member) % 3
    return jnp.where(remainder == 0, 1.0, jnp.where(remainder == 1, 16.0, 64.0)).astype(F32)


def dequantize(core, group, codes, row_scale, into, rows, first):
    def one(i, carry):
        value = codes(pl.multiple_of(i * 16, 16)).astype(F32)
        for m in range(group):
            step = member_step(core, group, m)
            offset = jnp.where(step > 1.0, 0.5 * step, 0.0)
            level = jnp.floor(value * (1.0 / step)) * step + offset
            into[m, pl.ds(pl.multiple_of(first + i * 16, 16), 16)] = (level * row_scale[...]).astype(BF16)
        return carry

    lax.fori_loop(0, rows // 16, one, 0)


GELU_A = 0.7978845608028654
GELU_B = 0.044715


class FeedWeights:
    def __init__(self, at, group, units, gate_ref, up_ref, down_ref, kept, refs):
        self.at, self.group, self.units = at, group, units
        self.sources, self.kept = (gate_ref, up_ref, down_ref), kept
        self.pair, self.down, self.codes, self.down_codes, self.sems = refs

    @staticmethod
    def scratch(group, units, window):
        return [
            pltpu.VMEM((group, D, 2 * window), BF16),
            pltpu.VMEM((group, window, D), BF16),
            pltpu.VMEM((D, 2 * window), BF16),
            pltpu.VMEM((units, D), jnp.int32),
            dma(5),
        ]

    def copies(self):
        window = self.codes.shape[1] // 2
        gate, up, down = self.sources
        return [
            pltpu.make_async_copy(gate, self.codes.at[:, pl.ds(0, window)], self.sems.at[0]),
            pltpu.make_async_copy(up, self.codes.at[:, pl.ds(window, window)], self.sems.at[1]),
            pltpu.make_async_copy(down, self.down_codes, self.sems.at[2]),
        ]

    def keeps(self):
        return [
            pltpu.make_async_copy(self.pair, self.kept[0], self.sems.at[3]),
            pltpu.make_async_copy(self.down, self.kept[1], self.sems.at[4]),
        ]

    def load(self):
        for copy in self.copies():
            copy.start()

    def make(self, pair_scale, down_scale):
        at, group, units = self.at, self.group, self.units
        window = self.down.shape[1]
        inset = (at.c * units) % 128
        for copy in self.copies():
            copy.wait()
        dequantize(at.b, group, lambda r: self.codes[pl.ds(r, 16)], pair_scale, self.pair, D, 0)

        def clear(i, carry):
            for m in range(group):
                self.down[m, pl.ds(pl.multiple_of(i * 16, 16), 16)] = jnp.zeros((16, D), BF16)
            return carry

        if window > units:
            lax.fori_loop(0, inset // 16, clear, 0)
            lax.fori_loop((inset + units) // 16, window // 16, clear, 0)
        dequantize(at.b, group, lambda r: self.down_codes[pl.ds(r, 16)], down_scale, self.down, units, inset)
        for copy in self.keeps():
            copy.start()

    def finish(self):
        for copy in self.keeps():
            copy.wait()


def feed_blocks(grid):
    return 4 if grid.plane % 4 == 0 else grid.plane


def each_chunk(grid, group, zj, fresh, loads, stores, compute, after=None):
    size = feed_blocks(grid)
    count = grid.plane // size

    def first(i):
        return zj * grid.plane + i * size

    for m in range(group):
        for copy in loads(m, first(0)):
            copy.start()

    def one(i, carry):
        for m in range(group):
            reads, writes = loads(m, first(i)), stores(m, first(i))

            @pl.when(jnp.logical_not(fresh & (i == 0)))
            def _():
                for copy in writes:
                    copy.wait()

            compute(m, reads)
            for copy in writes:
                copy.start()
        if after is not None:
            after([loads(m, first(i)) for m in range(group)])

        @pl.when(i + 1 < count)
        def _():
            for m in range(group):
                for copy in loads(m, first(i + 1)):
                    copy.start()

        return carry

    lax.fori_loop(0, count, one, 0)


def feed_forward(grid, x, gate_codes, up_codes, down_codes, pair_scale, down_scale, cid):
    group, rows, _ = x.shape
    n, levels = grid.n, grid.planes
    units, window, _ = feed_windows(grid)
    gs, ws = gather_sems(grid, levels, False), FeedWeights.scratch(group, units, window)
    size = feed_blocks(grid)
    count = size * rows

    def kernel(
        x_ref, gate_ref, up_ref, down_ref, ps_ref, ds_ref, all_ref, pair_ref, part_ref, wp_ref, wd_ref, *scratch
    ):
        refs = Split(scratch)
        at = Place(grid, levels)
        weights = FeedWeights(at, group, units, gate_ref, up_ref, down_ref, (wp_ref, wd_ref), refs.take(len(ws)))
        weights.load()
        moving = LevelGather(at, x_ref, all_ref, *refs.take(len(gs)))
        xs, gu, part, sems = refs.take(4)
        at.greet_near(False)
        moving.begin()
        weights.make(ps_ref, ds_ref)

        def loads(m, first):
            return [pltpu.make_async_copy(all_ref.at[m, pl.ds(first, size)], xs.at[m], sems.at[0, m])]

        def stores(m, first):
            return [
                pltpu.make_async_copy(gu.at[m], pair_ref.at[m, pl.ds(first, size)], sems.at[1, m]),
                pltpu.make_async_copy(part.at[m], part_ref.at[m, pl.ds(first, size)], sems.at[2, m]),
            ]

        def compute(m, reads):
            reads[0].wait()
            both = dot(xs[m].reshape(count, D), weights.pair[m])
            gu[m] = both.astype(BF16).reshape(size, rows, 2 * window)
            gate, up = both[:, :window], both[:, window:]
            bend = jnp.tanh(GELU_A * (gate + GELU_B * gate * gate * gate))
            hidden = (0.5 * gate * (1.0 + bend) * up).astype(BF16)
            part[m] = dot(hidden, weights.down[m]).astype(BF16).reshape(size, rows, D)

        moving.run(lambda zj, fresh: each_chunk(grid, group, zj, fresh, loads, stores, compute))
        for m in range(group):
            for copy in stores(m, 0):
                copy.wait()
        weights.finish()

    def blocks(width):
        return jax.ShapeDtypeStruct((group, n, rows, width), BF16)

    return pl.pallas_call(
        kernel,
        out_shape=(
            blocks(D),
            blocks(2 * window),
            blocks(D),
            jax.ShapeDtypeStruct((group, D, 2 * window), BF16),
            jax.ShapeDtypeStruct((group, window, D), BF16),
        ),
        in_specs=[INVMEM, ANY, ANY, ANY, INVMEM, INVMEM],
        out_specs=(ANY,) * 5,
        scratch_shapes=ws
        + gs
        + [
            pltpu.VMEM((group, size, rows, D), BF16),
            pltpu.VMEM((group, size, rows, 2 * window), BF16),
            pltpu.VMEM((group, size, rows, D), BF16),
            dma(3, group),
        ],
        compiler_params=params(cid, 60),
        name="feed_forward",
    )(x, gate_codes, up_codes, down_codes, pair_scale, down_scale)


def feed_backward(grid, x, fed, pair, pair_matrices, down_matrices, cid):
    group, rows, _ = x.shape
    n, levels = grid.n, grid.planes
    units, window, _ = feed_windows(grid)
    gs = gather_sems(grid, levels, False)
    size = feed_blocks(grid)
    count = size * rows
    tile = 256

    def kernel(x_ref, fed_ref, pair_ref, wp_ref, wd_ref, all_ref, part_ref, pg_ref, dg_ref, *scratch):
        refs = Split(scratch)
        at = Place(grid, levels)
        moving = LevelGather(at, x_ref, all_ref, *refs.take(len(gs)))
        wp, wd, xs, ys, gu, part, pair_sum, down_sum, dgu, hid, sems = refs.take(11)
        fetch = [
            pltpu.make_async_copy(wp_ref, wp, sems.at[4, 0]),
            pltpu.make_async_copy(wd_ref, wd, sems.at[4, 1]),
        ]
        for copy in fetch:
            copy.start()
        at.greet_near(False)
        moving.begin()

        def clear(i, carry):
            pair_sum[pl.ds(pl.multiple_of(i * 8, 8), 8)] = jnp.zeros((8, 2 * window), F32)
            return carry

        lax.fori_loop(0, D // 8, clear, 0)

        def clear_down(i, carry):
            down_sum[pl.ds(pl.multiple_of(i * 8, 8), 8)] = jnp.zeros((8, D), F32)
            return carry

        lax.fori_loop(0, window // 8, clear_down, 0)
        for copy in fetch:
            copy.wait()

        def loads(m, first):
            blocks = pl.ds(first, size)
            return [
                pltpu.make_async_copy(all_ref.at[m, blocks], ys.at[m], sems.at[0, m]),
                pltpu.make_async_copy(pair_ref.at[m, blocks], gu.at[m], sems.at[1, m]),
                pltpu.make_async_copy(fed_ref.at[m, blocks], xs.at[m], sems.at[2, m]),
            ]

        def stores(m, first):
            return [pltpu.make_async_copy(part.at[m], part_ref.at[m, pl.ds(first, size)], sems.at[3, m])]

        def compute(m, reads):
            reads[0].wait()
            grad_hidden = dot_t(ys[m].reshape(count, D), wd[m])
            reads[1].wait()
            both = gu[m].reshape(count, 2 * window).astype(F32)
            gate, up = both[:, :window], both[:, window:]
            bend = jnp.tanh(GELU_A * (gate + GELU_B * gate * gate * gate))
            bell = 0.5 * gate * (1.0 + bend)
            slope = 0.5 * (1.0 + bend) + 0.5 * gate * (1.0 - bend * bend) * GELU_A * (1.0 + 3.0 * GELU_B * gate * gate)
            mine = pl.ds(m * count, count)
            dgu[mine, :window] = (grad_hidden * up * slope).astype(BF16)
            dgu[mine, window:] = (grad_hidden * bell).astype(BF16)
            hid[mine] = (bell * up).astype(BF16)
            part[m] = dot_t(dgu[mine], wp[m]).astype(BF16).reshape(size, rows, D)

        def weight_sums(reads):
            for read in reads:
                read[2].wait()

            def one(j, carry):
                cols = pl.ds(pl.multiple_of(j * tile, tile), tile)
                pair_sum[cols] = pair_sum[cols] + t_dot(xs[:, :, :, cols].reshape(group * count, tile), dgu[...])
                down_sum[:, cols] = down_sum[:, cols] + t_dot(hid[...], ys[:, :, :, cols].reshape(group * count, tile))
                return carry

            lax.fori_loop(0, D // tile, one, 0)

        moving.run(lambda zj, fresh: each_chunk(grid, group, zj, fresh, loads, stores, compute, weight_sums))

        def low(i, carry):
            r = pl.ds(pl.multiple_of(i * 16, 16), 16)
            wp[0, r] = pair_sum[r].astype(BF16)
            return carry

        lax.fori_loop(0, D // 16, low, 0)
        give_pair = pltpu.make_async_copy(wp.at[0], pg_ref, sems.at[4, 0])
        give_pair.start()

        def low_down(i, carry):
            r = pl.ds(pl.multiple_of(i * 16, 16), 16)
            wd[0, r] = down_sum[r].astype(BF16)
            return carry

        lax.fori_loop(0, window // 16, low_down, 0)
        give_down = pltpu.make_async_copy(wd.at[0], dg_ref, sems.at[4, 1])
        give_down.start()
        for m in range(group):
            for copy in stores(m, 0):
                copy.wait()
        give_pair.wait()
        give_down.wait()

    def blocks(width):
        return jax.ShapeDtypeStruct((group, n, rows, width), BF16)

    return pl.pallas_call(
        kernel,
        out_shape=(
            blocks(D),
            blocks(D),
            jax.ShapeDtypeStruct((D, 2 * window), BF16),
            jax.ShapeDtypeStruct((window, D), BF16),
        ),
        in_specs=[INVMEM] + [ANY] * 4,
        out_specs=(ANY,) * 4,
        scratch_shapes=gs
        + [
            pltpu.VMEM((group, D, 2 * window), BF16),
            pltpu.VMEM((group, window, D), BF16),
            pltpu.VMEM((group, size, rows, D), BF16),
            pltpu.VMEM((group, size, rows, D), BF16),
            pltpu.VMEM((group, size, rows, 2 * window), BF16),
            pltpu.VMEM((group, size, rows, D), BF16),
            pltpu.VMEM((D, 2 * window), F32),
            pltpu.VMEM((window, D), F32),
            pltpu.VMEM((group * count, 2 * window), BF16),
            pltpu.VMEM((group * count, window), BF16),
            dma(5, group),
        ],
        compiler_params=params(cid, 62),
        name="feed_backward",
    )(x, fed, pair, pair_matrices, down_matrices)


def scatter_scratch(grid, levels, halves, rows, width):
    passes, steps = (2 if halves else 1), grid.plane // 2
    return [
        pltpu.VMEM((2, levels * grid.plane, rows, width), BF16),
        pltpu.VMEM((2, levels, 2, rows // 2, width), BF16),
        pltpu.VMEM((2, max(steps - 1, 1), levels, 2, rows, width), BF16),
        pltpu.VMEM((2, levels, 2, rows, width), BF16),
        pltpu.VMEM((rows, width), BF16),
        dma(3),
        dma(passes, 2, levels),
        dma(passes, 2, levels),
        dma(passes, 2, steps, levels),
        dma(passes, 2, steps, levels),
    ]


def scatter_steps(at, halves, out_ref, acc, ring_half, ring_full, line, swapped, ls, zs, zr, rs, rr):
    levels, steps, zi, q, pn, b = at.levels, at.steps, at.zi, at.q, at.pn, at.b
    rows = acc.shape[2]
    half = rows // 2
    member = at.member
    passes = [(1 - member, 1), (member, 1)] if halves else [(0, 2)]

    def block(us, zj, qj, part=None):
        u0, nu = us
        if part is None:
            return acc.at[pl.ds(u0, nu), at.slot(zj, qj)]
        return acc.at[pl.ds(u0, nu), at.slot(zj, qj), pl.ds(part * half, half)]

    def add(us, s, others, lo, count):
        u0, nu = us

        def one(i, carry):
            u, r = u0 + i // (count // 16), lo + (i % (count // 16)) * 16
            total = acc[u, s, pl.ds(r, 16)].astype(F32)
            for other in others:
                total = total + other(u, r)[...].astype(F32)
            acc[u, s, pl.ds(r, 16)] = total.astype(BF16)
            return carry

        lax.fori_loop(0, nu * (count // 16), one, 0)

    def full_at(way, step, zj):
        return lambda u, r: ring_full.at[way, step - 2, zj, u, pl.ds(r, 16)]

    def half_at(way, zj):
        return lambda u, r: ring_half.at[way, zj, u, pl.ds(r - way * half, 16)]

    def line_at(way, zj):
        return lambda u, r: line.at[way, zj, u, pl.ds(r, 16)]

    def r_copy(k, us, zj, way, step):
        u0, nu = us
        sign = 1 if way == 0 else -1
        target = q + sign * (steps + 1 - step)
        if step == 1:
            src, dst = block(us, zj, target, way), ring_half.at[way, zj, pl.ds(u0, nu)]
        else:
            src, dst = block(us, zj, target), ring_full.at[way, step - 2, zj, pl.ds(u0, nu)]
        to = at.right if way == 0 else at.left
        return remote(src, dst, rs.at[k, way, step - 1, zj], rr.at[k, way, step - 1, zj], to, b)

    def z_copy(k, us, zj, way):
        u0, nu = us
        to = at.c + (pn if way == 0 else -pn)
        return remote(block(us, zj, q), line.at[way, zj, pl.ds(u0, nu)], zs.at[k, way, zj], zr.at[k, way, zj], to, b)

    def begin(k, us, sign, d):
        def go():
            for way in (0, 1):
                r_copy(k, us, zi + sign * d, way, 1).start()

        guarded(present(zi, sign, d, levels), go)

    def onward(k, us, sign, d):
        zj = zi + sign * d

        def go():
            for step in range(1, steps + 1):
                for way in (0, 1):
                    r_copy(k, us, zj, way, step).wait_recv()
                    if step < steps:
                        s = at.slot(zj, q + (1 if way == 0 else -1) * (steps - step))
                        if step == 1:
                            add(us, s, [half_at(way, zj)], way * half, half)
                        else:
                            add(us, s, [full_at(way, step, zj)], 0, rows)
                        r_copy(k, us, zj, way, step + 1).start()
            s = at.slot(zj, q)
            if steps > 1:
                add(us, s, [full_at(0, steps, zj), full_at(1, steps, zj)], 0, rows)
            else:
                add(us, s, [half_at(0, zj)], 0, half)
                add(us, s, [half_at(1, zj)], half, half)

            def passed(way):
                z_copy(k, us, zj, way).wait_recv()
                add(us, s, [line_at(way, zj)], 0, rows)

            if sign >= 0:
                pl.when(zi > 0)(lambda: passed(0))
            if sign <= 0:
                pl.when(zi < levels - 1)(lambda: passed(1))
            if sign > 0:
                z_copy(k, us, zj, 0).start()
            if sign < 0:
                z_copy(k, us, zj, 1).start()

        guarded(present(zi, sign, d, levels), go)

    def finish(k, us, sign, d):
        zj = zi + sign * d

        def go():
            for way in (0, 1):
                for step in range(1, steps + 1):
                    r_copy(k, us, zj, way, step).wait_send()
            if sign != 0:
                z_copy(k, us, zj, 0 if sign > 0 else 1).wait_send()

        guarded(present(zi, sign, d, levels), go)

    waves = [
        [(k, us, sign, d) for sign in ((0,) if d == 0 else (-1, 1))]
        for k, us in enumerate(passes)
        for d in range(levels - 1, -1, -1)
    ]
    own = at.slot(zi, q)
    if halves:
        swap = remote(acc.at[1 - member, own], swapped, ls.at[1], ls.at[2], at.partner, b)
    for group in waves[0]:
        begin(*group)
    yield
    for i, wave in enumerate(waves):
        if i + 1 < len(waves):
            for group in waves[i + 1]:
                begin(*group)
            yield
        for group in wave:
            onward(*group)
            yield
        if halves and wave[0][0] == 0 and wave[0][3] == 0:
            swap.start()

    def give(src, u):
        def one(i, carry):
            out_ref[u, pl.ds(i * 16, 16)] = src.at[pl.ds(i * 16, 16)][...]
            return carry

        lax.fori_loop(0, rows // 16, one, 0)

    if halves:
        give(acc.at[member, own], member)
        swap.wait_recv()
        give(swapped, 1 - member)
    else:
        give(acc.at[0, own], 0)
        give(acc.at[1, own], 1)
    for wave in waves:
        for group in wave:
            finish(*group)
    if halves:
        swap.wait_send()


def scatter_parts(grid, levels, rows, width):
    blocks = 2 * (2 * levels * (grid.plane // 2 + 2) + levels * grid.plane)
    parts = 1
    while blocks * rows * (width // parts) * 2 > 40 * 2**20:
        parts += 1
        while width % (128 * parts):
            parts += 1
    return parts


def in_parts(grid, levels, call, p, extra):
    parts = scatter_parts(grid, levels, p.shape[2], p.shape[3])
    if parts == 1:
        return call(p, extra)
    piece = p.shape[3] // parts
    sums, others = [], ()
    for i in range(parts):
        got = call(p[..., i * piece : (i + 1) * piece], extra if i == 0 else None)
        sums.append(got[0])
        others = got[1:] if i == 0 else others
    return (jnp.concatenate(sums, axis=-1),) + tuple(others)


def pairwise(n, c, b):
    def to(i):
        return (c + 2 * i + b) % n

    def frm(i, core):
        return (c + n - 2 * i - core) % n

    return to, frm


def middle_out(half):
    return sorted(range(1, half), key=lambda i: abs(2 * i - half))


def share_task(at, sources, views, ss, sr, fs, fr):
    n, c, b = at.n, at.c, at.b
    half = n // 2
    to, frm = pairwise(n, c, b)
    kinds = len(sources)

    def out_copy(k, i):
        return remote(sources[k](to(i)), views[k](c), ss.at[k, i], sr.at[k, i], to(i), b)

    def landed(k, i):
        return remote(sources[k](c), views[k](frm(i, b)), ss.at[k, i], sr.at[k, i], to(i), b)

    def pass_on(k, i, core):
        ref = views[k](frm(i, core))
        return at.sibling(ref, ref, fs.at[k, i], fr.at[k, i])

    def local(k):
        return pltpu.make_async_copy(sources[k](c), views[k](c), sr.at[k, 0])

    order = middle_out(half) + [0]

    def issue():
        for i in order:
            for k in range(kinds):
                if i > 0:
                    out_copy(k, i).start()
                else:
                    pl.when(b == 1)(lambda: out_copy(k, 0).start())
                    pl.when(b == 0)(lambda: local(k).start())
            yield

    def finish():
        for i in order:
            for k in range(kinds):
                if i > 0:
                    landed(k, i).wait_recv()
                else:
                    pl.when(b == 1)(lambda: landed(k, 0).wait_recv())
                    pl.when(b == 0)(lambda: local(k).wait())
                pass_on(k, i, b).start()
        for k in range(kinds):
            for i in range(half):
                pass_on(k, i, 1 - b).wait_recv()
            for i in range(half):
                pass_on(k, i, b).wait_send()
            for i in range(1, half):
                out_copy(k, i).wait_send()
            pl.when(b == 1)(lambda: out_copy(k, 0).wait_send())

    return issue(), finish


def share_sems(grid, kinds):
    return [dma(kinds, grid.n // 2) for _ in range(4)]


def tell_task(at, small_ref, all_ref, ts, tr):
    n, c, b = at.n, at.c, at.b

    def tell(off, slot):
        return remote(small_ref, all_ref.at[slot], ts.at[off], tr.at[off], (c + off) % n, b)

    keep = pltpu.make_async_copy(small_ref, all_ref.at[c], ts.at[0])

    def issue():
        keep.start()
        for off in range(1, n):
            tell(off, c).start()
        yield

    def finish():
        keep.wait()
        for off in range(1, n):
            tell(off, (c + n - off) % n).wait_recv()
        for off in range(1, n):
            tell(off, c).wait_send()

    return issue(), finish


def head_rows_task(at, x_ref, out_ref, hs, hr, fs, fr):
    c, b = at.c, at.b
    copies = at.n // HEADS
    head, rank = c % HEADS, c // HEADS
    mine = rank % 2 == b

    def out_copy(k):
        to = c // copies + HEADS * (2 * k + b)
        return to, remote(x_ref, out_ref.at[c % copies], hs.at[k], hr.at[c % copies], to, b)

    def landed(j):
        return remote(x_ref, out_ref.at[j], hs.at[0], hr.at[j], head * copies + j, b)

    def here(j):
        return pltpu.make_async_copy(x_ref, out_ref.at[j], hr.at[j])

    def pass_on(j):
        return at.sibling(out_ref.at[j], out_ref.at[j], fs.at[j], fr.at[j])

    def issue():
        for k in range(copies // 2):
            to, copy = out_copy(k)
            pl.when(to != c)(lambda: copy.start())
            pl.when(to == c)(lambda: here(c % copies).start())
            yield

    def finish():
        @pl.when(mine)
        def _():
            for j in range(copies):
                pl.when(head * copies + j != c)(lambda: landed(j).wait_recv())
                pl.when(head * copies + j == c)(lambda: here(j).wait())
                pass_on(j).start()
            for j in range(copies):
                pass_on(j).wait_send()

        @pl.when(jnp.logical_not(mine))
        def _():
            for j in range(copies):
                pass_on(j).wait_recv()

        for k in range(copies // 2):
            to, copy = out_copy(k)
            pl.when(to != c)(lambda: copy.wait_send())

    return issue(), finish


def head_rows_sems(grid):
    copies = grid.n // HEADS
    return [dma(copies), dma(copies), dma(copies), dma(copies)]


def add_rows(into, other, rows):
    step = 16 if rows % 16 == 0 else rows

    def one(r, carry):
        at = pl.ds(pl.multiple_of(r * step, step), step)
        into[at] = (into[at].astype(F32) + other[at].astype(F32)).astype(BF16)
        return carry

    lax.fori_loop(0, rows // step, one, 0)


def return_task(at, x_ref, out_ref, mine, theirs, ls, ps, pr, ss, sr, fs, fr):
    n, c, b = at.n, at.c, at.b
    half = n // 2
    to, frm = pairwise(n, c, b)
    other_to, _ = pairwise(n, c, 1 - b)

    def load(i):
        return pltpu.make_async_copy(x_ref.at[to(i)], mine.at[i], ls.at[i])

    def give(i):
        return at.sibling(x_ref.at[other_to(i)], theirs.at[i], ps.at[i], pr.at[i])

    def out_copy(i):
        return remote(mine.at[i], out_ref.at[c], ss.at[i], sr.at[i], to(i), b)

    def landed(i):
        return remote(mine.at[i], out_ref.at[frm(i, b)], ss.at[i], sr.at[i], to(i), b)

    def pass_on(i, core):
        ref = out_ref.at[frm(i, core)]
        return at.sibling(ref, ref, fs.at[i], fr.at[i])

    local = pltpu.make_async_copy(mine.at[0], out_ref.at[c], ss.at[0])
    order = middle_out(half) + [0]

    def issue():
        for i in order:
            load(i).start()
            give(i).start()
        for i in order:
            load(i).wait()
            give(i).wait_recv()
            add_rows(mine.at[i], theirs.at[i], x_ref.shape[1])
            if i > 0:
                out_copy(i).start()
            else:
                pl.when(b == 1)(lambda: out_copy(0).start())
                pl.when(b == 0)(lambda: local.start())
            yield

    def finish():
        for i in order:
            if i > 0:
                landed(i).wait_recv()
            else:
                pl.when(b == 1)(lambda: landed(0).wait_recv())
                pl.when(b == 0)(lambda: local.wait())
            pass_on(i, b).start()
        for i in range(half):
            pass_on(i, 1 - b).wait_recv()
        for i in range(half):
            give(i).wait_send()
            pass_on(i, b).wait_send()
        for i in range(1, half):
            out_copy(i).wait_send()
        pl.when(b == 1)(lambda: out_copy(0).wait_send())

    return issue(), finish


def return_scratch(grid, shape):
    blocks = (grid.n // 2,) + shape
    return [pltpu.VMEM(blocks, BF16), pltpu.VMEM(blocks, BF16)] + [dma(grid.n // 2) for _ in range(7)]


def head_return_task(at, x_ref, out_ref, mine, theirs, ls, ps, pr, hs, hr, fs, fr):
    c, b = at.c, at.b
    copies = at.n // HEADS
    head, rank = c % HEADS, c // HEADS
    taken = (c % copies) % 2 == b

    def load(k):
        return pltpu.make_async_copy(x_ref.at[2 * k + b], mine.at[k], ls.at[k])

    def give(k):
        return at.sibling(x_ref.at[2 * k + 1 - b], theirs.at[k], ps.at[k], pr.at[k])

    def out_copy(k):
        to = head * copies + 2 * k + b
        return to, remote(mine.at[k], out_ref.at[rank], hs.at[k], hr.at[rank], to, b)

    def landed(i):
        return remote(mine.at[0], out_ref.at[i], hs.at[0], hr.at[i], c // copies + HEADS * i, b)

    def here(k, i):
        return pltpu.make_async_copy(mine.at[k], out_ref.at[i], hr.at[i])

    def pass_on(i):
        return at.sibling(out_ref.at[i], out_ref.at[i], fs.at[i], fr.at[i])

    def issue():
        for k in range(copies // 2):
            load(k).start()
            give(k).start()
        for k in range(copies // 2):
            load(k).wait()
            give(k).wait_recv()
            add_rows(mine.at[k], theirs.at[k], x_ref.shape[1])
            to, copy = out_copy(k)
            pl.when(to != c)(lambda: copy.start())
            pl.when(to == c)(lambda: here(k, rank).start())
            yield

    def finish():
        @pl.when(taken)
        def _():
            for i in range(copies):
                frm = c // copies + HEADS * i
                pl.when(frm != c)(lambda: landed(i).wait_recv())
                pl.when(frm == c)(lambda: here(0, i).wait())
                pass_on(i).start()
            for i in range(copies):
                pass_on(i).wait_send()

        @pl.when(jnp.logical_not(taken))
        def _():
            for i in range(copies):
                pass_on(i).wait_recv()

        for k in range(copies // 2):
            give(k).wait_send()
            to, copy = out_copy(k)
            pl.when(to != c)(lambda: copy.wait_send())

    return issue(), finish


def head_return_scratch(grid, shape):
    copies = grid.n // HEADS
    blocks = (copies // 2,) + shape
    return [pltpu.VMEM(blocks, BF16), pltpu.VMEM(blocks, BF16)] + [dma(copies) for _ in range(7)]


def pair_task(at, x_ref, out_ref, other, sems):
    copy = at.sibling(x_ref, other, sems.at[0], sems.at[1])

    def issue():
        copy.start()
        yield

    def finish():
        copy.wait_recv()

        def one(r, carry):
            rows = pl.ds(pl.multiple_of(r * 16, 16), 16)
            out_ref[rows] = x_ref[rows].astype(F32) + other[rows].astype(F32)
            return carry

        lax.fori_loop(0, x_ref.shape[0] // 16, one, 0)
        copy.wait_send()

    return issue(), finish


class Split:
    def __init__(self, refs):
        self.refs = list(refs)

    def take(self, count):
        got, self.refs = self.refs[:count], self.refs[count:]
        return got


def together(main, *tasks):
    for _ in main:
        for issue, _finish in tasks:
            next(issue, None)
    for issue, finish in tasks:
        run(issue)
    for issue, finish in tasks:
        finish()


def open_kernel(grid, x, qkv_parts, out_codes, small, cid):
    n, levels = grid.n, grid.planes // 2
    rows_d, width = qkv_parts.shape[1:]
    flat = rows_d % 16 == 0
    copies = n // HEADS
    gs, ss, ts, hs = gather_sems(grid, levels, True), share_sems(grid, 1), [dma(n), dma(n)], head_rows_sems(grid)

    def kernel(x_ref, w_ref, o_ref, small_ref, seen_ref, codes_ref, rows_ref, all_ref, *scratch):
        at = Place(grid, levels)
        refs = Split(scratch)
        at.greet_all()

        def view(j):
            return codes_ref.at[pl.ds(j * rows_d, rows_d)] if flat else codes_ref.at[j]

        together(
            gather_steps(at, True, x_ref, seen_ref, *refs.take(len(gs))),
            tell_task(at, small_ref, all_ref, *refs.take(2)),
            share_task(at, [lambda to: w_ref.at[to % HEADS]], [view], *refs.take(len(ss))),
            head_rows_task(at, o_ref, rows_ref, *refs.take(4)),
        )

    codes_shape = (n * rows_d, width) if flat else (n, rows_d, width)
    return pl.pallas_call(
        kernel,
        out_shape=(
            jax.ShapeDtypeStruct((2, levels * grid.plane) + x.shape[1:], BF16),
            jax.ShapeDtypeStruct(codes_shape, BF16),
            jax.ShapeDtypeStruct((copies,) + out_codes.shape, BF16),
            jax.ShapeDtypeStruct((n,) + small.shape, small.dtype),
        ),
        in_specs=[INVMEM] * 4,
        out_specs=(ANY,) * 4,
        scratch_shapes=gs + ts + ss + hs,
        compiler_params=params(cid, 50),
        name="open",
    )(x, qkv_parts, out_codes, small)


def scatter_kernel(grid, levels, halves, cid, name, tasks=None):
    made, in_specs, out_shapes, out_specs, extra_scratch = tasks if tasks else (None, [], (), (), [])

    def call(p, extra):
        rows, width = p.shape[2:]
        more = () if extra is None else tuple(extra)
        own = scatter_scratch(grid, levels, halves, rows, width)

        def kernel(*refs):
            refs = Split(refs)
            (p_ref,) = refs.take(1)
            more_refs = refs.take(len(more))
            (out_ref,) = refs.take(1)
            out_refs = refs.take(len(out_shapes) if more else 0)
            mine = refs.take(len(own))
            at = Place(grid, levels)
            load = pltpu.make_async_copy(p_ref, mine[0], mine[5].at[0])
            load.start()
            if more:
                at.greet_all()
            else:
                at.greet_near(halves)
            load.wait()
            others = made(at, more_refs, out_refs, refs) if more else []
            together(scatter_steps(at, halves, out_ref, *mine), *others)

        return pl.pallas_call(
            kernel,
            out_shape=(jax.ShapeDtypeStruct((2, rows, width), BF16),) + (out_shapes if more else ()),
            in_specs=[ANY] + (in_specs if more else []),
            out_specs=(INVMEM,) + (out_specs if more else ()),
            scratch_shapes=own + (extra_scratch if more else []),
            compiler_params=params(cid + (0 if more else 20), 60),
            name=name,
        )(p, *more)

    return call


def feed_windows(grid):
    units = FF // grid.n
    window = 128 * max(-(-((c * units) % 128 + units) // 128) for c in range(grid.n))
    return units, window, lambda c: ((c * units) // 128) * 128


def attention_sums(grid, p, gate_codes, up_codes, cid):
    n, levels = grid.n, grid.planes // 2
    rows_d = gate_codes.shape[0]
    flat = rows_d % 16 == 0
    units, window, start = feed_windows(grid)
    ss = share_sems(grid, 2)

    def tasks(at, ins, outs, refs):
        def source(ref):
            return lambda to: ref.at[:, pl.ds(pl.multiple_of(start(to), 128), window)]

        def view(ref):
            return lambda j: ref.at[pl.ds(j * rows_d, rows_d)] if flat else ref.at[j]

        return [share_task(at, [source(r) for r in ins], [view(r) for r in outs], *refs.take(len(ss)))]

    shape = (n * rows_d, window) if flat else (n, rows_d, window)
    call = scatter_kernel(
        grid,
        levels,
        True,
        cid,
        "attention_sums",
        (tasks, [INVMEM, INVMEM], (jax.ShapeDtypeStruct(shape, BF16),) * 2, (ANY, ANY), ss),
    )
    return in_parts(grid, levels, call, p, (gate_codes, up_codes))


def feed_sums(grid, p, cid):
    return in_parts(grid, grid.planes, scatter_kernel(grid, grid.planes, False, cid, "feed_sums"), p, None)[0]


def feed_back_sums(grid, p, pair_grad, cid):
    rs = return_scratch(grid, pair_grad.shape[1:])

    def tasks(at, ins, outs, refs):
        return [return_task(at, ins[0], outs[0], *refs.take(len(rs)))]

    call = scatter_kernel(
        grid,
        grid.planes,
        False,
        cid,
        "feed_back_sums",
        (tasks, [ANY], (jax.ShapeDtypeStruct(pair_grad.shape, BF16),), (ANY,), rs),
    )
    return in_parts(grid, grid.planes, call, p, (pair_grad,))


def attention_back_sums(grid, p, qkv_grad, out_grad, down_grad, cid):
    n, levels = grid.n, grid.planes // 2
    rs, hs = return_scratch(grid, qkv_grad.shape[1:]), head_return_scratch(grid, out_grad.shape[1:])
    ps = [pltpu.VMEM(down_grad.shape, BF16), dma(2)]

    def tasks(at, ins, outs, refs):
        return [
            return_task(at, ins[0], outs[0], *refs.take(len(rs))),
            head_return_task(at, ins[1], outs[1], *refs.take(len(hs))),
            pair_task(at, ins[2], outs[2], *refs.take(2)),
        ]

    call = scatter_kernel(
        grid,
        levels,
        True,
        cid,
        "attention_back_sums",
        (
            tasks,
            [ANY, ANY, INVMEM],
            (
                jax.ShapeDtypeStruct(qkv_grad.shape, BF16),
                jax.ShapeDtypeStruct(out_grad.shape, BF16),
                jax.ShapeDtypeStruct(down_grad.shape, F32),
            ),
            (ANY, ANY, INVMEM),
            rs + hs + ps,
        ),
    )
    return in_parts(grid, levels, call, p, (qkv_grad, out_grad, down_grad))


def gains_kernel(grid, gains, cid):
    n = grid.n
    ss = share_sems(grid, 1)

    def kernel(x_ref, out_ref, total, other, sems, *scratch):
        at = Place(grid, grid.planes)
        at.greet_all()
        copy = at.sibling(x_ref, other, sems.at[0], sems.at[1])
        copy.start()
        copy.wait()
        total[...] = x_ref[...] + other[...]
        together((), share_task(at, [lambda to: total], [lambda j: out_ref.at[j]], *scratch))

    return pl.pallas_call(
        kernel,
        out_shape=jax.ShapeDtypeStruct((n,) + gains.shape, F32),
        in_specs=[INVMEM],
        out_specs=INVMEM,
        scratch_shapes=[pltpu.VMEM(gains.shape, F32), pltpu.VMEM(gains.shape, F32), dma(2)] + ss,
        compiler_params=params(cid),
        name="gains",
    )(gains)


def normed(value, gain):
    return value * lax.rsqrt(jnp.mean(value * value, axis=-1, keepdims=True) + 1e-06) * gain


def angles(places, head):
    freqs = 10000.0 ** (-(jnp.arange(head // 2, dtype=F32) * 2.0 / head))
    return places.astype(F32)[..., None] * freqs


def rotate(values, cosine, sine):
    half = values.shape[-1] // 2
    first = values[..., :half]
    second = values[..., half:]
    return jnp.concatenate([first * cosine - second * sine, second * cosine + first * sine], axis=-1)


def width_step(number):
    remainder = number % 3
    return jnp.where(remainder == 0, 1.0, jnp.where(remainder == 1, 16.0, 64.0)).astype(F32)


def dequantized(codes, column_scale, step):
    offset = jnp.where(step > 1.0, 0.5 * step, 0.0)
    level = jnp.floor(codes.astype(F32) / step) * step + offset
    return (level * column_scale[None, :]).astype(BF16)


def dot(left, right):
    return jnp.dot(left, right, preferred_element_type=F32)


def dot_t(left, right):
    return lax.dot_general(left, right, (((1,), (1,)), ((), ())), preferred_element_type=F32)


def t_dot(left, right):
    return lax.dot_general(left, right, (((0,), (0,)), ((), ())), preferred_element_type=F32)


def unwindowed(grid, got):
    n, rows, window = got.shape
    units = FF // n
    inner = n // HEADS
    whole = inner * units
    got = got.astype(F32).reshape(n // inner, inner, rows, window)
    total = 0.0
    for i in range(inner):
        start = i * units // 128 * 128
        total = total + jnp.pad(got[:, i], ((0, 0), (0, 0), (start, whole - start - window)))
    return jnp.transpose(total, (1, 0, 2)).reshape(rows, FF)


def on_device(
    grid,
    tokens,
    segments,
    positions,
    cotangent,
    query_codes,
    key_codes,
    value_codes,
    output_codes,
    gate_codes,
    up_codes,
    down_codes,
    query_scale,
    key_scale,
    value_scale,
    output_scale,
    gate_scale,
    up_scale,
    down_scale,
    attention_gain,
    attention_post_gain,
    feed_gain,
    feed_post_gain,
):
    n = grid.n
    group, block, _ = tokens.shape
    length = n * block
    pairs = HEADS // KV_HEADS
    scale = HEAD ** (-0.5)
    chip, core = lax.axis_index("seq"), lax.axis_index("batch")
    half = n // 2
    member = chip // half
    head = chip % HEADS
    kv_head = head // pairs
    parts = half // HEADS
    copies = n // HEADS
    asked = length // parts
    first_asked = ((chip % half) // HEADS) * asked
    steps = [width_step(core * group + m) for m in range(group)]
    step = width_step(core * group + member)
    rows_d = D // n
    units, window, _ = feed_windows(grid)

    source = tokens.astype(F32)
    first_normed = normed(source, attention_gain).astype(BF16)
    q_parts = jnp.transpose(query_codes.reshape(rows_d, HEADS, HEAD), (1, 0, 2))
    k_parts = jnp.repeat(jnp.transpose(key_codes.reshape(rows_d, KV_HEADS, HEAD), (1, 0, 2)), pairs, axis=0)
    v_parts = jnp.repeat(jnp.transpose(value_codes.reshape(rows_d, KV_HEADS, HEAD), (1, 0, 2)), pairs, axis=0)
    qkv_parts = jnp.concatenate([q_parts, k_parts, v_parts], axis=-1).astype(BF16)
    small = jnp.zeros((8, 128), jnp.int32).at[:group, :block].set(positions)
    seen, qkv_codes, out_codes, all_places = open_kernel(
        grid, first_normed, qkv_parts, output_codes.astype(BF16), small, 1
    )
    seen = seen.reshape(length, D)

    qkv_scale = jnp.concatenate(
        [
            lax.dynamic_slice_in_dim(query_scale, head * HEAD, HEAD),
            lax.dynamic_slice_in_dim(key_scale, kv_head * HEAD, HEAD),
            lax.dynamic_slice_in_dim(value_scale, kv_head * HEAD, HEAD),
        ]
    )
    qkv_matrix = dequantized(qkv_codes.reshape(D, 3 * HEAD), qkv_scale, step)
    out_matrix = dequantized(out_codes.reshape(HEAD, D), output_scale, step)

    places_all = lax.dynamic_index_in_dim(all_places[:, :group, :block], member, 1, False).reshape(length)
    turn = angles(places_all, HEAD)
    cosine, sine = jnp.cos(turn), jnp.sin(turn)
    if parts == 1:
        seen_asked, places_asked, cosine_q, sine_q = seen, places_all, cosine, sine
        projected = dot(seen, qkv_matrix)
        q_lin, kv_lin = projected[:, :HEAD], projected[:, HEAD:]
    else:
        seen_asked, places_asked, cosine_q, sine_q = [
            lax.dynamic_slice_in_dim(a, first_asked, asked) for a in (seen, places_all, cosine, sine)
        ]
        q_lin, kv_lin = dot(seen_asked, qkv_matrix[:, :HEAD]), dot(seen, qkv_matrix[:, HEAD:])
    queries = rotate(q_lin, cosine_q, sine_q).astype(BF16)
    keys = rotate(kv_lin[:, :HEAD], cosine, sine).astype(BF16)
    values = kv_lin[:, HEAD:].astype(BF16)
    q_index = first_asked + jnp.arange(asked, dtype=jnp.int32)
    key_index = jnp.arange(length, dtype=jnp.int32)
    allowed = (key_index[None, :] <= q_index[:, None]) & (key_index[None, :] >= (q_index - places_asked)[:, None])
    bent = jnp.tanh(dot_t(queries, keys) * scale / cap_limit)
    kernel = jnp.where(allowed, jnp.exp(cap_limit * bent), 0.0)
    totals = jnp.sum(kernel, axis=-1, keepdims=True)
    kernel_low = kernel.astype(BF16)
    attended = dot(kernel_low, values) / totals
    attended_low = attended.astype(BF16)

    def spread(part):
        if parts > 1:
            part = lax.dynamic_update_slice_in_dim(jnp.zeros((length, D), BF16), part, first_asked, 0)
        return part.reshape(2, half, block, D)

    attention_raw, gate_got, up_got = attention_sums(
        grid,
        spread(dot(attended_low, out_matrix).astype(BF16)),
        gate_codes.astype(BF16),
        up_codes.astype(BF16),
        2,
    )
    attention_raw = attention_raw.astype(F32)
    first_column = chip * units // 128 * 128
    inset = chip * units - first_column
    pair_scale = jnp.concatenate(
        [lax.dynamic_slice_in_dim(s, first_column, window) for s in (gate_scale, up_scale)]
    )
    feed_weights = (
        gate_got.reshape(D, window),
        up_got.reshape(D, window),
        down_codes,
        pair_scale[None],
        down_scale[None],
    )

    mixed = source + normed(attention_raw, attention_post_gain)
    second_normed = normed(mixed, feed_gain).astype(BF16)
    fed, gate_up, down_part, pair_matrices, down_matrices = feed_forward(grid, second_normed, *feed_weights, 3)
    down_raw = feed_sums(grid, down_part, 4).astype(F32)
    branch, pull_out = jax.vjp(normed, down_raw, feed_post_gain)
    output = (mixed + branch).astype(BF16)
    upstream = cotangent.astype(F32)
    grad_down_raw, grad_post_feed = pull_out(upstream)
    _, second_part, pair_grad, down_grad = feed_backward(
        grid, grad_down_raw.astype(BF16), fed, gate_up, pair_matrices, down_matrices, 9
    )
    down_grad = lax.dynamic_slice(down_grad, (inset, 0), (units, D))
    grad_second, pair_got = feed_back_sums(
        grid, second_part, pair_grad.reshape(n, rows_d, 2 * window), 5
    )
    grad_second = grad_second.astype(F32)
    gate_grad, up_grad = (unwindowed(grid, pair_got[..., i * window : (i + 1) * window]) for i in range(2))

    _, pull_feed = jax.vjp(normed, mixed, feed_gain)
    grad_mixed_part, grad_pre_feed = pull_feed(grad_second)
    grad_mixed = upstream + grad_mixed_part
    _, pull_post = jax.vjp(normed, attention_raw, attention_post_gain)
    grad_attention, grad_post_attention = pull_post(grad_mixed)
    attention_low = gather(grid, grad_attention.astype(BF16), grid.planes // 2, True, 6).reshape(length, D)
    if parts > 1:
        attention_low = lax.dynamic_slice_in_dim(attention_low, first_asked, asked)
    grad_attended = dot_t(attention_low, out_matrix)
    grad_sums = (grad_attended / totals).astype(BF16)
    offsets = jnp.sum(grad_attended * attended, axis=-1, keepdims=True) / totals
    grad_kernel = dot_t(grad_sums, values) - offsets
    grad_raw = (kernel * grad_kernel * (1.0 - bent * bent)).astype(BF16)
    grad_q = dot(grad_raw, keys) * scale
    grad_k = t_dot(grad_raw, queries) * scale
    grad_v = t_dot(kernel_low, grad_sums)
    q_low = rotate(grad_q, cosine_q, -sine_q).astype(BF16)
    kv_low = jnp.concatenate([rotate(grad_k, cosine, -sine), grad_v], axis=-1).astype(BF16)
    if parts == 1:
        qkv_low = jnp.concatenate([q_low, kv_low], axis=-1)
        first_part = dot_t(qkv_low, qkv_matrix)
        qkv_grad = t_dot(seen, qkv_low)
    else:
        first_part = dot_t(kv_low, qkv_matrix[:, HEAD:])
        q_back = dot_t(q_low, qkv_matrix[:, :HEAD])
        first_part = lax.dynamic_update_slice_in_dim(
            first_part, lax.dynamic_slice_in_dim(first_part, first_asked, asked) + q_back, first_asked, 0
        )
        qkv_grad = jnp.concatenate([t_dot(seen_asked, q_low), t_dot(seen, kv_low)], axis=-1)
    out_part = t_dot(attended_low, attention_low).astype(BF16).reshape(copies, HEAD // copies, D)
    grad_first, qkv_got, out_got, down_grad = attention_back_sums(
        grid,
        first_part.astype(BF16).reshape(2, half, block, D),
        qkv_grad.astype(BF16).reshape(n, rows_d, 3 * HEAD),
        out_part,
        down_grad,
        7,
    )
    grad_first = grad_first.astype(F32)
    _, pull_in = jax.vjp(normed, source, attention_gain)
    grad_source_part, grad_pre_attention = pull_in(grad_first)
    grad_in = (grad_mixed + grad_source_part).astype(BF16)
    qkv_got = jnp.sum(qkv_got.astype(F32).reshape(copies, HEADS, rows_d, 3 * HEAD), axis=0)
    query_grad = jnp.transpose(qkv_got[..., :HEAD], (1, 0, 2)).reshape(rows_d, HEADS * HEAD)
    kv_grad = jnp.sum(qkv_got[..., HEAD:].reshape(KV_HEADS, pairs, rows_d, 2 * HEAD), axis=1)
    key_grad = jnp.transpose(kv_grad[..., :HEAD], (1, 0, 2)).reshape(rows_d, KV_HEADS * HEAD)
    value_grad = jnp.transpose(kv_grad[..., HEAD:], (1, 0, 2)).reshape(rows_d, KV_HEADS * HEAD)
    out_grad = jnp.sum(out_got.astype(F32), axis=0)
    gains = jnp.stack([grad_pre_attention, grad_post_attention, grad_pre_feed, grad_post_feed])
    gains = jnp.sum(gains_kernel(grid, gains.reshape(8, D // 2), 8), axis=0).reshape(4, D)
    return (
        output,
        grad_in,
        query_grad,
        key_grad,
        value_grad,
        out_grad,
        gate_grad,
        up_grad,
        down_grad,
    ) + tuple(gains[i] for i in range(4))


def solution(mesh):
    rows = P("seq", None)
    return jax.shard_map(
        functools.partial(on_device, Grid(mesh.shape["seq"])),
        mesh=mesh,
        in_specs=(P("batch", "seq", None), P("batch", "seq"), P("batch", "seq"), P("batch", "seq", None))
        + (rows,) * 7
        + (P(),) * 11,
        out_specs=(P("batch", "seq", None),) * 2 + (rows,) * 7 + (P(),) * 4,
        check_vma=False,
    )
```

```python
import functools

import jax
import jax.numpy as jnp
from jax import lax
from jax.experimental import pallas as pl
from jax.experimental.pallas import tpu as pltpu
from jax.sharding import PartitionSpec as P

D = 2304
HEADS = 8
KV_HEADS = 4
HEAD = 256
FF = 9216
MESH = pl.DeviceIdType.MESH
F32 = jnp.float32
BF16 = jnp.bfloat16


cap_limit = 50.0


class Grid:
    def __init__(self, n):
        self.n = n
        self.planes = 4 if n % 8 == 0 else 2
        self.plane = n // self.planes
        wide = 1
        while wide * wide < self.plane:
            wide *= 2
        self.wide = wide

    def snake(self, p):
        y, x = p // self.wide, p % self.wide
        return y * self.wide + x + (y % 2) * (self.wide - 1 - 2 * x)


def remote(src, dst, send, recv, chip, core):
    return pltpu.make_async_remote_copy(
        src_ref=src, dst_ref=dst, send_sem=send, recv_sem=recv, device_id=(chip, core), device_id_type=MESH
    )


def greet(barrier, chip, core):
    pl.semaphore_signal(barrier, inc=1, device_id=(chip, core), device_id_type=MESH)


class Place:
    def __init__(self, grid, levels):
        self.grid, self.levels = grid, levels
        self.n, self.pn = grid.n, grid.plane
        self.steps = self.pn // 2
        self.c, self.b = lax.axis_index("seq"), lax.axis_index("batch")
        self.z, p = self.c // self.pn, self.c % self.pn
        self.q = grid.snake(p)
        self.zi = self.z % levels
        self.right = self.z * self.pn + grid.snake((self.q + 1) % self.pn)
        self.left = self.z * self.pn + grid.snake((self.q + self.pn - 1) % self.pn)
        self.member = self.c // (self.n // 2)
        self.partner = (self.c + self.n // 2) % self.n

    def slot(self, zj, qj):
        return zj * self.pn + self.grid.snake((qj + 2 * self.pn) % self.pn)

    def sibling(self, src, dst, send, recv):
        return remote(src, dst, send, recv, self.c, 1 - self.b)

    def greet_near(self, halves):
        barrier = pltpu.get_barrier_semaphore()
        zi, levels = self.zi, self.levels
        greet(barrier, self.right, self.b)
        greet(barrier, self.left, self.b)
        pl.when(zi > 0)(lambda: greet(barrier, self.c - self.pn, self.b))
        pl.when(zi < levels - 1)(lambda: greet(barrier, self.c + self.pn, self.b))
        if halves:
            greet(barrier, self.partner, self.b)
        count = 2 + jnp.where(zi > 0, 1, 0) + jnp.where(zi < levels - 1, 1, 0) + (1 if halves else 0)
        pl.semaphore_wait(barrier, count)

    def greet_all(self):
        barrier = pltpu.get_barrier_semaphore()
        greet(barrier, self.c, 1 - self.b)

        def one(off, carry):
            greet(barrier, (self.c + off) % self.n, self.b)
            return carry

        lax.fori_loop(1, self.n, one, 0)
        pl.semaphore_wait(barrier, self.n)


def present(zi, sign, d, levels):
    if d == 0:
        return None
    return (zi - d >= 0) if sign < 0 else (zi + d < levels)


def guarded(condition, action):
    if condition is None:
        action()
    else:
        pl.when(condition)(action)


def dma(*shape):
    return pltpu.SemaphoreType.DMA(shape)


ANY = pl.BlockSpec(memory_space=pl.ANY)
INVMEM = pl.BlockSpec(memory_space=pltpu.VMEM)


def params(cid, mib=None):
    if mib is None:
        return pltpu.CompilerParams(collective_id=cid, has_side_effects=True)
    return pltpu.CompilerParams(collective_id=cid, has_side_effects=True, vmem_limit_bytes=mib * 2**20)


def gather_sems(grid, levels, passes=1):
    steps = grid.plane // 2
    return [
        dma(passes, 2, levels),
        dma(passes, 2, levels),
        dma(passes, 2, steps, levels),
        dma(passes, 2, steps, levels),
        dma(3),
    ]


def gather_steps(at, x_ref, out_ref, zs, zr, rs, rr, ls, passes=((0, 2),), ready=None):
    levels, steps, zi, q, pn, b = at.levels, at.steps, at.zi, at.q, at.pn, at.b
    half = x_ref.shape[1] // 2
    own = at.slot(zi, q)

    def block(us, zj, qj, part=None):
        u0, nu = us
        if part is None:
            return out_ref.at[pl.ds(u0, nu), at.slot(zj, qj)]
        return out_ref.at[pl.ds(u0, nu), at.slot(zj, qj), pl.ds(part * half, half)]

    def z_copy(k, us, zj, sign):
        way = 0 if sign > 0 else 1
        ref = block(us, zj, q)
        return remote(ref, ref, zs.at[k, way, zj], zr.at[k, way, zj], at.c + sign * pn, b)

    def r_copy(k, us, zj, way, step, landing=False):
        away = step if landing else step - 1
        ref = block(us, zj, q - away if way == 0 else q + away, way if step == steps else None)
        to = at.right if way == 0 else at.left
        return remote(ref, ref, rs.at[k, way, step - 1, zj], rr.at[k, way, step - 1, zj], to, b)

    def arrive(k, us, sign, d):
        zj = zi + sign * d

        def go():
            if d > 0:
                z_copy(k, us, zj, -sign).wait_recv()
            if sign <= 0:
                pl.when(zi < levels - 1)(lambda: z_copy(k, us, zj, 1).start())
            if sign >= 0:
                pl.when(zi > 0)(lambda: z_copy(k, us, zj, -1).start())
            for way in (0, 1):
                r_copy(k, us, zj, way, 1).start()

        guarded(present(zi, sign, d, levels), go)

    def onward(k, us, sign, d):
        zj = zi + sign * d

        def go():
            for step in range(1, steps + 1):
                for way in (0, 1):
                    r_copy(k, us, zj, way, step, True).wait_recv()
                    if step < steps:
                        r_copy(k, us, zj, way, step + 1).start()

        guarded(present(zi, sign, d, levels), go)

    def finish(k, us, sign, d):
        zj = zi + sign * d

        def go():
            if sign <= 0:
                pl.when(zi < levels - 1)(lambda: z_copy(k, us, zj, 1).wait_send())
            if sign >= 0:
                pl.when(zi > 0)(lambda: z_copy(k, us, zj, -1).wait_send())
            for way in (0, 1):
                for step in range(1, steps + 1):
                    r_copy(k, us, zj, way, step).wait_send()

        guarded(present(zi, sign, d, levels), go)

    waves = [
        [(k, us, sign, d) for sign in ((0,) if d == 0 else (-1, 1))] for k, us in enumerate(passes) for d in range(levels)
    ]
    for i, wave in enumerate(waves):
        k, (u0, nu), _, d = wave[0]
        if d == 0:
            if ready is not None:
                ready(k)
            local = pltpu.make_async_copy(x_ref.at[pl.ds(u0, nu)], out_ref.at[pl.ds(u0, nu), own], ls.at[k])
            local.start()
            local.wait()
        for group in wave:
            arrive(*group)
            yield
        if i > 0:
            for group in waves[i - 1]:
                onward(*group)
                yield
    for group in waves[-1]:
        onward(*group)
        yield
    for wave in waves:
        for group in wave:
            finish(*group)


def run(steps):
    for _ in steps:
        pass


def gather(grid, x, levels, cid):
    count = levels * grid.plane

    def kernel(x_ref, out_ref, *sems):
        at = Place(grid, levels)
        at.greet_near(False)
        run(gather_steps(at, x_ref, out_ref, *sems))

    return pl.pallas_call(
        kernel,
        out_shape=jax.ShapeDtypeStruct((2, count) + x.shape[1:], x.dtype),
        in_specs=[INVMEM],
        out_specs=ANY,
        scratch_shapes=gather_sems(grid, levels),
        compiler_params=params(cid, 50),
        name="gather_%d" % count,
    )(x)


class LevelGather:
    def __init__(self, at, x_ref, out_ref, zs, zr, rs, rr, ls):
        self.at, self.x, self.out = at, x_ref, out_ref
        self.zs, self.zr, self.rs, self.rr, self.ls = zs, zr, rs, rr, ls
        self.half = x_ref.shape[1] // 2

    def block(self, zj, qj, part=None):
        if part is None:
            return self.out.at[:, self.at.slot(zj, qj)]
        return self.out.at[:, self.at.slot(zj, qj), pl.ds(part * self.half, self.half)]

    def z_copy(self, zj, way):
        at, ref = self.at, self.block(zj, self.at.q)
        to = at.c + (at.pn if way == 0 else -at.pn)
        return remote(ref, ref, self.zs.at[0, way, zj], self.zr.at[0, way, zj], to, at.b)

    def r_copy(self, zj, way, step, landing=False):
        at = self.at
        away = step if landing else step - 1
        ref = self.block(zj, at.q - away if way == 0 else at.q + away, way if step == at.steps else None)
        to = at.right if way == 0 else at.left
        return remote(ref, ref, self.rs.at[0, way, step - 1, zj], self.rr.at[0, way, step - 1, zj], to, at.b)

    def begin(self):
        local = pltpu.make_async_copy(self.x, self.block(self.at.zi, self.at.q), self.ls.at[0])
        local.start()
        local.wait()
        self.send(0)

    def send(self, offset):
        at = self.at
        zj = at.zi + offset
        pl.when((offset <= 0) & (at.zi < at.levels - 1))(lambda: self.z_copy(zj, 0).start())
        pl.when((offset >= 0) & (at.zi > 0))(lambda: self.z_copy(zj, 1).start())
        for way in (0, 1):
            self.r_copy(zj, way, 1).start()

    def arrive(self, sign, d):
        zj = self.at.zi + sign * d
        self.z_copy(zj, 0 if sign < 0 else 1).wait_recv()
        self.send(sign * d)

    def onward(self, sign, d):
        zj = self.at.zi + sign * d
        for step in range(1, self.at.steps):
            for way in (0, 1):
                self.r_copy(zj, way, step, True).wait_recv()
                self.r_copy(zj, way, step + 1).start()

    def landed(self, sign, d):
        zj = self.at.zi + sign * d
        for way in (0, 1):
            self.r_copy(zj, way, self.at.steps, True).wait_recv()

    def finish(self):
        at = self.at

        def one(zj, carry):
            pl.when((zj <= at.zi) & (at.zi < at.levels - 1))(lambda: self.z_copy(zj, 0).wait_send())
            pl.when((zj >= at.zi) & (at.zi > 0))(lambda: self.z_copy(zj, 1).wait_send())
            for way in (0, 1):
                for step in range(1, at.steps + 1):
                    self.r_copy(zj, way, step).wait_send()
            return carry

        lax.fori_loop(0, at.levels, one, 0)

    def run(self, compute, first=None):
        at = self.at
        zi, levels = at.zi, at.levels

        def wave(t):
            pl.when((t < levels) & (zi - t >= 0))(lambda: self.arrive(-1, t))
            pl.when((t < levels) & (zi + t < levels))(lambda: self.arrive(1, t))

        def both(d, action):
            pl.when((d < levels) & (zi - d >= 0))(lambda: action(-1, d))
            pl.when((d > 0) & (d < levels) & (zi + d < levels))(lambda: action(1, d))

        def one(t, carry):
            wave(t)
            both(t - 1, self.onward)
            if first is not None:
                pl.when(t == 2)(first)
            e = t - 2
            both(e, self.landed)

            def side(i, carry):
                zj = zi + (2 * i - 1) * e
                here = (zj >= 0) & (zj < levels) & ((e > 0) | (i == 0))
                pl.when(here)(lambda: compute(zj, e == 0))
                return carry

            lax.fori_loop(0, 2, side, 0)
            return carry

        wave(1)
        both(0, self.onward)
        lax.fori_loop(2, levels + 2, one, 0)
        self.finish()


def member_step(core, group, member):
    remainder = (core * group + member) % 3
    return jnp.where(remainder == 0, 1.0, jnp.where(remainder == 1, 16.0, 64.0)).astype(F32)


def dequantize(core, group, codes, row_scale, into, rows, first):
    def one(i, carry):
        value = codes(pl.multiple_of(i * 16, 16)).astype(F32)
        for m in range(group):
            step = member_step(core, group, m)
            offset = jnp.where(step > 1.0, 0.5 * step, 0.0)
            level = jnp.floor(value * (1.0 / step)) * step + offset
            into[m, pl.ds(pl.multiple_of(first + i * 16, 16), 16)] = (level * row_scale[...]).astype(BF16)
        return carry

    lax.fori_loop(0, rows // 16, one, 0)


GELU_A = 0.7978845608028654
GELU_B = 0.044715


class FeedWeights:
    def __init__(self, at, group, units, gate_ref, up_ref, down_ref, kept, refs):
        self.at, self.group, self.units = at, group, units
        self.sources, self.kept = (gate_ref, up_ref, down_ref), kept
        self.pair, self.down, self.codes, self.down_codes, self.sems = refs

    @staticmethod
    def scratch(group, units, window):
        return [
            pltpu.VMEM((group, D, 2 * window), BF16),
            pltpu.VMEM((group, window, D), BF16),
            pltpu.VMEM((D, 2 * window), BF16),
            pltpu.VMEM((units, D), jnp.int32),
            dma(5),
        ]

    def copies(self):
        window = self.codes.shape[1] // 2
        gate, up, down = self.sources
        copies = [pltpu.make_async_copy(down, self.down_codes, self.sems.at[2])]
        if gate is not None:
            copies += [
                pltpu.make_async_copy(gate, self.codes.at[:, pl.ds(0, window)], self.sems.at[0]),
                pltpu.make_async_copy(up, self.codes.at[:, pl.ds(window, window)], self.sems.at[1]),
            ]
        return copies

    def keeps(self):
        return [
            pltpu.make_async_copy(self.pair, self.kept[0], self.sems.at[3]),
            pltpu.make_async_copy(self.down, self.kept[1], self.sems.at[4]),
        ]

    def load(self):
        for copy in self.copies():
            copy.start()

    def make(self, pair_scale, down_scale):
        at, group, units = self.at, self.group, self.units
        window = self.down.shape[1]
        inset = (at.c * units) % 128
        for copy in self.copies():
            copy.wait()
        dequantize(at.b, group, lambda r: self.codes[pl.ds(r, 16)], pair_scale, self.pair, D, 0)

        def clear(i, carry):
            for m in range(group):
                self.down[m, pl.ds(pl.multiple_of(i * 16, 16), 16)] = jnp.zeros((16, D), BF16)
            return carry

        if window > units:
            lax.fori_loop(0, inset // 16, clear, 0)
            lax.fori_loop((inset + units) // 16, window // 16, clear, 0)
        dequantize(at.b, group, lambda r: self.down_codes[pl.ds(r, 16)], down_scale, self.down, units, inset)
        for copy in self.keeps():
            copy.start()

    def finish(self):
        for copy in self.keeps():
            copy.wait()


def feed_blocks(grid):
    return 4 if grid.plane % 4 == 0 else grid.plane


def each_chunk(grid, zj, fresh, loads, stores, compute):
    size = feed_blocks(grid)
    m = zj // (grid.planes // 2)

    def one(i, carry):
        first = zj * grid.plane + i * size
        reads, writes = loads(first), stores(first)
        for copy in reads:
            copy.start()

        @pl.when(jnp.logical_not(fresh & (i == 0)))
        def _():
            for copy in writes:
                copy.wait()

        compute(m, reads)
        for copy in writes:
            copy.start()
        return carry

    lax.fori_loop(0, grid.plane // size, one, 0)


def copies_of(blocks, pairs, sems, first):
    return [
        pltpu.make_async_copy(a.at[:, blocks] if far_a else a, b if far_a else b.at[:, blocks], sems.at[first + k])
        for k, (a, b, far_a) in enumerate(pairs)
    ]


def forward_chunks(weights, all_ref, pair_ref, part_ref, xs, gu, part, sems):
    _, size, rows, _ = xs.shape
    window = weights.down.shape[1]

    def loads(first):
        return copies_of(pl.ds(first, size), [(all_ref, xs, True)], sems, 0)

    def stores(first):
        return copies_of(pl.ds(first, size), [(gu, pair_ref, False), (part, part_ref, False)], sems, 1)

    def compute(m, reads):
        reads[0].wait()
        both = dot(xs[...].reshape(2 * size * rows, D), weights.pair[m])
        gu[...] = both.astype(BF16).reshape(gu.shape)
        gate, up = both[:, :window], both[:, window:]
        bend = jnp.tanh(GELU_A * (gate + GELU_B * gate * gate * gate))
        hidden = (0.5 * gate * (1.0 + bend) * up).astype(BF16)
        part[...] = dot(hidden, weights.down[m]).astype(BF16).reshape(part.shape)

    return loads, stores, compute


def backward_chunks(wp, wd, all_ref, pair_ref, part_ref, dgu_ref, hid_ref, ys, gu, part, dgu, hid, sems):
    _, size, rows, _ = ys.shape
    window = wd.shape[1]
    count = 2 * size * rows

    def loads(first):
        return copies_of(pl.ds(first, size), [(all_ref, ys, True), (pair_ref, gu, True)], sems, 0)

    def stores(first):
        pairs = [(part, part_ref, False), (dgu, dgu_ref, False), (hid, hid_ref, False)]
        return copies_of(pl.ds(first, size), pairs, sems, 2)

    def compute(m, reads):
        reads[0].wait()
        grad_hidden = dot_t(ys[...].reshape(count, D), wd[m])
        reads[1].wait()
        both = gu[...].reshape(count, 2 * window).astype(F32)
        gate, up = both[:, :window], both[:, window:]
        bend = jnp.tanh(GELU_A * (gate + GELU_B * gate * gate * gate))
        bell = 0.5 * gate * (1.0 + bend)
        slope = 0.5 * (1.0 + bend) + 0.5 * gate * (1.0 - bend * bend) * GELU_A * (1.0 + 3.0 * GELU_B * gate * gate)
        dgu[:, :, :, :window] = (grad_hidden * up * slope).astype(BF16).reshape(hid.shape)
        dgu[:, :, :, window:] = (grad_hidden * bell).astype(BF16).reshape(hid.shape)
        hid[...] = (bell * up).astype(BF16).reshape(hid.shape)
        part[...] = dot_t(dgu[...].reshape(count, 2 * window), wp[m]).astype(BF16).reshape(part.shape)

    return loads, stores, compute


def chunk_buffers(size, rows, *widths):
    return [pltpu.VMEM((2, size, rows, width), BF16) for width in widths]


def feed_forward(grid, x, gate_codes, up_codes, down_codes, pair_scale, down_scale, cid):
    group, rows, _ = x.shape
    n, levels = grid.n, grid.planes
    units, window, _ = feed_windows(grid)
    gs, ws = gather_sems(grid, levels), FeedWeights.scratch(group, units, window)
    size = feed_blocks(grid)

    def kernel(
        x_ref, gate_ref, up_ref, down_ref, ps_ref, ds_ref, all_ref, pair_ref, part_ref, wp_ref, wd_ref, *scratch
    ):
        refs = Split(scratch)
        at = Place(grid, levels)
        weights = FeedWeights(at, group, units, gate_ref, up_ref, down_ref, (wp_ref, wd_ref), refs.take(len(ws)))
        weights.load()
        moving = LevelGather(at, x_ref, all_ref, *refs.take(len(gs)))
        loads, stores, compute = forward_chunks(weights, all_ref, pair_ref, part_ref, *refs.take(4))
        at.greet_near(False)
        moving.begin()
        weights.make(ps_ref, ds_ref)
        moving.run(lambda zj, fresh: each_chunk(grid, zj, fresh, loads, stores, compute))
        for copy in stores(0):
            copy.wait()
        weights.finish()

    def blocks(width):
        return jax.ShapeDtypeStruct((group, n, rows, width), BF16)

    return pl.pallas_call(
        kernel,
        out_shape=(
            blocks(D),
            blocks(2 * window),
            blocks(D),
            jax.ShapeDtypeStruct((group, D, 2 * window), BF16),
            jax.ShapeDtypeStruct((group, window, D), BF16),
        ),
        in_specs=[INVMEM, ANY, ANY, ANY, INVMEM, INVMEM],
        out_specs=(ANY,) * 5,
        scratch_shapes=ws + gs + chunk_buffers(size, rows, D, 2 * window, D) + [dma(3)],
        compiler_params=params(cid, 60),
        name="feed_forward",
    )(x, gate_codes, up_codes, down_codes, pair_scale, down_scale)


def feed_backward(grid, x, pair, pair_matrices, down_matrices, cid):
    group, rows, _ = x.shape
    n, levels = grid.n, grid.planes
    _, window, _ = feed_windows(grid)
    gs = gather_sems(grid, levels)
    size = feed_blocks(grid)

    def kernel(x_ref, pair_ref, wp_ref, wd_ref, all_ref, part_ref, dgu_ref, hid_ref, *scratch):
        refs = Split(scratch)
        at = Place(grid, levels)
        moving = LevelGather(at, x_ref, all_ref, *refs.take(len(gs)))
        wp, wd, fetch_sems = refs.take(3)
        fetch = [
            pltpu.make_async_copy(wp_ref, wp, fetch_sems.at[0]),
            pltpu.make_async_copy(wd_ref, wd, fetch_sems.at[1]),
        ]
        for copy in fetch:
            copy.start()
        loads, stores, compute = backward_chunks(
            wp, wd, all_ref, pair_ref, part_ref, dgu_ref, hid_ref, *refs.take(6)
        )
        at.greet_near(False)
        moving.begin()
        for copy in fetch:
            copy.wait()
        moving.run(lambda zj, fresh: each_chunk(grid, zj, fresh, loads, stores, compute))
        for copy in stores(0):
            copy.wait()

    def blocks(width):
        return jax.ShapeDtypeStruct((group, n, rows, width), BF16)

    return pl.pallas_call(
        kernel,
        out_shape=(blocks(D), blocks(D), blocks(2 * window), blocks(window)),
        in_specs=[INVMEM] + [ANY] * 3,
        out_specs=(ANY,) * 4,
        scratch_shapes=gs
        + [pltpu.VMEM((group, D, 2 * window), BF16), pltpu.VMEM((group, window, D), BF16), dma(2)]
        + chunk_buffers(size, rows, D, 2 * window, D, 2 * window, window)
        + [dma(5)],
        compiler_params=params(cid, 62),
        name="feed_backward",
    )(x, pair, pair_matrices, down_matrices)


def scatter_scratch(grid, levels, rows, width):
    steps = grid.plane // 2
    return [
        pltpu.VMEM((2, levels * grid.plane, rows, width), BF16),
        pltpu.VMEM((2, levels, 2, rows // 2, width), BF16),
        pltpu.VMEM((2, max(steps - 1, 1), levels, 2, rows, width), BF16),
        pltpu.VMEM((2, levels, 2, rows, width), BF16),
        dma(1),
        dma(1, 2, levels),
        dma(1, 2, levels),
        dma(1, 2, steps, levels),
        dma(1, 2, steps, levels),
    ]


def scatter_steps(at, out_ref, acc, ring_half, ring_full, line, ls, zs, zr, rs, rr):
    levels, steps, zi, q, pn, b = at.levels, at.steps, at.zi, at.q, at.pn, at.b
    rows = acc.shape[2]
    half = rows // 2
    passes = [(0, 2)]

    def block(us, zj, qj, part=None):
        u0, nu = us
        if part is None:
            return acc.at[pl.ds(u0, nu), at.slot(zj, qj)]
        return acc.at[pl.ds(u0, nu), at.slot(zj, qj), pl.ds(part * half, half)]

    def add(us, s, others, lo, count):
        u0, nu = us

        def one(i, carry):
            u, r = u0 + i // (count // 16), lo + (i % (count // 16)) * 16
            total = acc[u, s, pl.ds(r, 16)].astype(F32)
            for other in others:
                total = total + other(u, r)[...].astype(F32)
            acc[u, s, pl.ds(r, 16)] = total.astype(BF16)
            return carry

        lax.fori_loop(0, nu * (count // 16), one, 0)

    def full_at(way, step, zj):
        return lambda u, r: ring_full.at[way, step - 2, zj, u, pl.ds(r, 16)]

    def half_at(way, zj):
        return lambda u, r: ring_half.at[way, zj, u, pl.ds(r - way * half, 16)]

    def line_at(way, zj):
        return lambda u, r: line.at[way, zj, u, pl.ds(r, 16)]

    def r_copy(k, us, zj, way, step):
        u0, nu = us
        sign = 1 if way == 0 else -1
        target = q + sign * (steps + 1 - step)
        if step == 1:
            src, dst = block(us, zj, target, way), ring_half.at[way, zj, pl.ds(u0, nu)]
        else:
            src, dst = block(us, zj, target), ring_full.at[way, step - 2, zj, pl.ds(u0, nu)]
        to = at.right if way == 0 else at.left
        return remote(src, dst, rs.at[k, way, step - 1, zj], rr.at[k, way, step - 1, zj], to, b)

    def z_copy(k, us, zj, way):
        u0, nu = us
        to = at.c + (pn if way == 0 else -pn)
        return remote(block(us, zj, q), line.at[way, zj, pl.ds(u0, nu)], zs.at[k, way, zj], zr.at[k, way, zj], to, b)

    def begin(k, us, sign, d):
        def go():
            for way in (0, 1):
                r_copy(k, us, zi + sign * d, way, 1).start()

        guarded(present(zi, sign, d, levels), go)

    def middle(k, us, sign, d):
        zj = zi + sign * d

        def go():
            for step in range(1, steps):
                for way in (0, 1):
                    r_copy(k, us, zj, way, step).wait_recv()
                    s = at.slot(zj, q + (1 if way == 0 else -1) * (steps - step))
                    if step == 1:
                        add(us, s, [half_at(way, zj)], way * half, half)
                    else:
                        add(us, s, [full_at(way, step, zj)], 0, rows)
                    r_copy(k, us, zj, way, step + 1).start()

        guarded(present(zi, sign, d, levels), go)

    def last(k, us, sign, d):
        zj = zi + sign * d

        def go():
            for way in (0, 1):
                r_copy(k, us, zj, way, steps).wait_recv()
            s = at.slot(zj, q)
            if steps > 1:
                add(us, s, [full_at(0, steps, zj), full_at(1, steps, zj)], 0, rows)
            else:
                add(us, s, [half_at(0, zj)], 0, half)
                add(us, s, [half_at(1, zj)], half, half)

            def passed(way):
                z_copy(k, us, zj, way).wait_recv()
                add(us, s, [line_at(way, zj)], 0, rows)

            if sign >= 0:
                pl.when(zi > 0)(lambda: passed(0))
            if sign <= 0:
                pl.when(zi < levels - 1)(lambda: passed(1))
            if sign > 0:
                z_copy(k, us, zj, 0).start()
            if sign < 0:
                z_copy(k, us, zj, 1).start()

        guarded(present(zi, sign, d, levels), go)

    def finish(k, us, sign, d):
        zj = zi + sign * d

        def go():
            for way in (0, 1):
                for step in range(1, steps + 1):
                    r_copy(k, us, zj, way, step).wait_send()
            if sign != 0:
                z_copy(k, us, zj, 0 if sign > 0 else 1).wait_send()

        guarded(present(zi, sign, d, levels), go)

    waves = [
        [(k, us, sign, d) for sign in ((0,) if d == 0 else (-1, 1))]
        for k, us in enumerate(passes)
        for d in range(levels - 1, -1, -1)
    ]
    own = at.slot(zi, q)
    def each(action, i):
        if i < len(waves):
            for group in waves[i]:
                action(*group)

    each(begin, 0)
    each(begin, 1)
    each(middle, 0)
    yield
    for i in range(len(waves)):
        each(begin, i + 2)
        each(middle, i + 1)
        yield
        each(last, i)
    yield

    def give(src, u):
        def one(i, carry):
            out_ref[u, pl.ds(i * 16, 16)] = src.at[pl.ds(i * 16, 16)][...]
            return carry

        lax.fori_loop(0, rows // 16, one, 0)

    give(acc.at[0, own], 0)
    give(acc.at[1, own], 1)
    for wave in waves:
        for group in wave:
            finish(*group)


def scatter_parts(grid, levels, rows, width):
    blocks = 2 * (2 * levels * (grid.plane // 2 + 2) + levels * grid.plane)
    parts = 1
    while blocks * rows * (width // parts) * 2 > 40 * 2**20:
        parts += 1
        while width % (128 * parts):
            parts += 1
    return parts


def in_parts(grid, levels, call, p, extra):
    parts = scatter_parts(grid, levels, p.shape[2], p.shape[3])
    if parts == 1:
        return call(p, extra)
    piece = p.shape[3] // parts
    sums, others = [], ()
    for i in range(parts):
        got = call(p[..., i * piece : (i + 1) * piece], extra if i == 0 else None)
        sums.append(got[0])
        others = got[1:] if i == 0 else others
    return (jnp.concatenate(sums, axis=-1),) + tuple(others)


def pairwise(n, c, b):
    def to(i):
        return (c + 2 * i + b) % n

    def frm(i, core):
        return (c + n - 2 * i - core) % n

    return to, frm


def middle_out(half):
    return sorted(range(1, half), key=lambda i: abs(2 * i - half))


def share_task(at, sources, views, ss, sr, fs, fr):
    n, c, b = at.n, at.c, at.b
    half = n // 2
    to, frm = pairwise(n, c, b)
    kinds = len(sources)

    def out_copy(k, i):
        return remote(sources[k](to(i)), views[k](c), ss.at[k, i], sr.at[k, i], to(i), b)

    def landed(k, i):
        return remote(sources[k](c), views[k](frm(i, b)), ss.at[k, i], sr.at[k, i], to(i), b)

    def pass_on(k, i, core):
        ref = views[k](frm(i, core))
        return at.sibling(ref, ref, fs.at[k, i], fr.at[k, i])

    def local(k):
        return pltpu.make_async_copy(sources[k](c), views[k](c), sr.at[k, 0])

    order = middle_out(half) + [0]

    def issue():
        for i in order:
            for k in range(kinds):
                if i > 0:
                    out_copy(k, i).start()
                else:
                    pl.when(b == 1)(lambda: out_copy(k, 0).start())
                    pl.when(b == 0)(lambda: local(k).start())
            yield

    def finish():
        for i in order:
            for k in range(kinds):
                if i > 0:
                    landed(k, i).wait_recv()
                else:
                    pl.when(b == 1)(lambda: landed(k, 0).wait_recv())
                    pl.when(b == 0)(lambda: local(k).wait())
                pass_on(k, i, b).start()
        for k in range(kinds):
            for i in range(half):
                pass_on(k, i, 1 - b).wait_recv()
            for i in range(half):
                pass_on(k, i, b).wait_send()
            for i in range(1, half):
                out_copy(k, i).wait_send()
            pl.when(b == 1)(lambda: out_copy(k, 0).wait_send())

    return issue(), finish


def share_sems(grid, kinds):
    return [dma(kinds, grid.n // 2) for _ in range(4)]


def tell_task(at, small_ref, all_ref, ts, tr):
    n, c, b = at.n, at.c, at.b

    def tell(off, slot):
        return remote(small_ref, all_ref.at[slot], ts.at[off], tr.at[off], (c + off) % n, b)

    keep = pltpu.make_async_copy(small_ref, all_ref.at[c], ts.at[0])

    def issue():
        keep.start()
        for off in range(1, n):
            tell(off, c).start()
        yield

    def finish():
        keep.wait()
        for off in range(1, n):
            tell(off, (c + n - off) % n).wait_recv()
        for off in range(1, n):
            tell(off, c).wait_send()

    return issue(), finish


def head_rows_task(at, x_ref, out_ref, hs, hr, fs, fr):
    c, b = at.c, at.b
    copies = at.n // HEADS
    head, rank = c % HEADS, c // HEADS
    mine = rank % 2 == b

    def out_copy(k):
        to = c // copies + HEADS * (2 * k + b)
        return to, remote(x_ref, out_ref.at[c % copies], hs.at[k], hr.at[c % copies], to, b)

    def landed(j):
        return remote(x_ref, out_ref.at[j], hs.at[0], hr.at[j], head * copies + j, b)

    def here(j):
        return pltpu.make_async_copy(x_ref, out_ref.at[j], hr.at[j])

    def pass_on(j):
        return at.sibling(out_ref.at[j], out_ref.at[j], fs.at[j], fr.at[j])

    def issue():
        for k in range(copies // 2):
            to, copy = out_copy(k)
            pl.when(to != c)(lambda: copy.start())
            pl.when(to == c)(lambda: here(c % copies).start())
            yield

    def finish():
        @pl.when(mine)
        def _():
            for j in range(copies):
                pl.when(head * copies + j != c)(lambda: landed(j).wait_recv())
                pl.when(head * copies + j == c)(lambda: here(j).wait())
                pass_on(j).start()
            for j in range(copies):
                pass_on(j).wait_send()

        @pl.when(jnp.logical_not(mine))
        def _():
            for j in range(copies):
                pass_on(j).wait_recv()

        for k in range(copies // 2):
            to, copy = out_copy(k)
            pl.when(to != c)(lambda: copy.wait_send())

    return issue(), finish


def head_rows_sems(grid):
    copies = grid.n // HEADS
    return [dma(copies), dma(copies), dma(copies), dma(copies)]


def add_rows(into, other, rows):
    step = 16 if rows % 16 == 0 else rows

    def one(r, carry):
        at = pl.ds(pl.multiple_of(r * step, step), step)
        into[at] = (into[at].astype(F32) + other[at].astype(F32)).astype(BF16)
        return carry

    lax.fori_loop(0, rows // step, one, 0)


def return_task(at, x_ref, out_ref, mine, theirs, ls, ps, pr, ss, sr, fs, fr, given=None, fill=None, prepare=None):
    n, c, b = at.n, at.c, at.b
    half = n // 2
    to, frm = pairwise(n, c, b)
    other_to, _ = pairwise(n, c, 1 - b)

    def load(i):
        return pltpu.make_async_copy(x_ref.at[to(i)], mine.at[i], ls.at[i])

    def give(i):
        source = x_ref.at[other_to(i)] if given is None else given.at[i]
        return at.sibling(source, theirs.at[i], ps.at[i], pr.at[i])

    def out_copy(i):
        return remote(mine.at[i], out_ref.at[c], ss.at[i], sr.at[i], to(i), b)

    def landed(i):
        return remote(mine.at[i], out_ref.at[frm(i, b)], ss.at[i], sr.at[i], to(i), b)

    def pass_on(i, core):
        ref = out_ref.at[frm(i, core)]
        return at.sibling(ref, ref, fs.at[i], fr.at[i])

    local = pltpu.make_async_copy(mine.at[0], out_ref.at[c], ss.at[0])
    order = middle_out(half) + [0]

    def issue():
        if prepare is not None:
            yield from prepare()
        for i in order:
            if fill is None:
                load(i).start()
            else:
                fill(i)
            give(i).start()
        for j, i in enumerate(order):
            if fill is None:
                load(i).wait()
            give(i).wait_recv()
            add_rows(mine.at[i], theirs.at[i], mine.shape[1])
            if i > 0:
                out_copy(i).start()
            else:
                pl.when(b == 1)(lambda: out_copy(0).start())
                pl.when(b == 0)(lambda: local.start())
            if j % 2 == 1:
                yield

    def finish():
        for i in order:
            if i > 0:
                landed(i).wait_recv()
            else:
                pl.when(b == 1)(lambda: landed(0).wait_recv())
                pl.when(b == 0)(lambda: local.wait())
            pass_on(i, b).start()
        for i in range(half):
            pass_on(i, 1 - b).wait_recv()
        for i in range(half):
            give(i).wait_send()
            pass_on(i, b).wait_send()
        for i in range(1, half):
            out_copy(i).wait_send()
        pl.when(b == 1)(lambda: out_copy(0).wait_send())

    return issue(), finish


def return_scratch(grid, shape):
    blocks = (grid.n // 2,) + shape
    return [pltpu.VMEM(blocks, BF16), pltpu.VMEM(blocks, BF16)] + [dma(grid.n // 2) for _ in range(7)]


def head_return_task(at, x_ref, out_ref, mine, theirs, ls, ps, pr, hs, hr, fs, fr):
    c, b = at.c, at.b
    copies = at.n // HEADS
    head, rank = c % HEADS, c // HEADS
    taken = (c % copies) % 2 == b

    def load(k):
        return pltpu.make_async_copy(x_ref.at[2 * k + b], mine.at[k], ls.at[k])

    def give(k):
        return at.sibling(x_ref.at[2 * k + 1 - b], theirs.at[k], ps.at[k], pr.at[k])

    def out_copy(k):
        to = head * copies + 2 * k + b
        return to, remote(mine.at[k], out_ref.at[rank], hs.at[k], hr.at[rank], to, b)

    def landed(i):
        return remote(mine.at[0], out_ref.at[i], hs.at[0], hr.at[i], c // copies + HEADS * i, b)

    def here(k, i):
        return pltpu.make_async_copy(mine.at[k], out_ref.at[i], hr.at[i])

    def pass_on(i):
        return at.sibling(out_ref.at[i], out_ref.at[i], fs.at[i], fr.at[i])

    def issue():
        for k in range(copies // 2):
            load(k).start()
            give(k).start()
        for k in range(copies // 2):
            load(k).wait()
            give(k).wait_recv()
            add_rows(mine.at[k], theirs.at[k], x_ref.shape[1])
            to, copy = out_copy(k)
            pl.when(to != c)(lambda: copy.start())
            pl.when(to == c)(lambda: here(k, rank).start())
            yield

    def finish():
        @pl.when(taken)
        def _():
            for i in range(copies):
                frm = c // copies + HEADS * i
                pl.when(frm != c)(lambda: landed(i).wait_recv())
                pl.when(frm == c)(lambda: here(0, i).wait())
                pass_on(i).start()
            for i in range(copies):
                pass_on(i).wait_send()

        @pl.when(jnp.logical_not(taken))
        def _():
            for i in range(copies):
                pass_on(i).wait_recv()

        for k in range(copies // 2):
            give(k).wait_send()
            to, copy = out_copy(k)
            pl.when(to != c)(lambda: copy.wait_send())

    return issue(), finish


def head_return_scratch(grid, shape):
    copies = grid.n // HEADS
    blocks = (copies // 2,) + shape
    return [pltpu.VMEM(blocks, BF16), pltpu.VMEM(blocks, BF16)] + [dma(copies) for _ in range(7)]


def pair_task(at, x_ref, out_ref, other, sems):
    copy = at.sibling(x_ref, other, sems.at[0], sems.at[1])

    def issue():
        copy.start()
        yield

    def finish():
        copy.wait_recv()

        def one(r, carry):
            rows = pl.ds(pl.multiple_of(r * 16, 16), 16)
            out_ref[rows] = (x_ref[rows].astype(F32) + other[rows].astype(F32)).astype(out_ref.dtype)
            return carry

        lax.fori_loop(0, x_ref.shape[0] // 16, one, 0)
        copy.wait_send()

    return issue(), finish


class Split:
    def __init__(self, refs):
        self.refs = list(refs)

    def take(self, count):
        got, self.refs = self.refs[:count], self.refs[count:]
        return got


def together(main, *tasks):
    for _ in main:
        for issue, _finish in tasks:
            next(issue, None)
    for issue, finish in tasks:
        run(issue)
    for issue, finish in tasks:
        finish()


def narrow_task(sources, targets, wide, low, loads, stores):
    width = wide.shape[2]
    pieces = [(k, i) for k in range(len(sources)) for i in range(sources[k].shape[1] // width)]

    def load(j):
        k, i = pieces[j]
        return pltpu.make_async_copy(sources[k].at[:, pl.ds(i * width, width)], wide.at[j % 2], loads.at[j % 2])

    def store(j):
        k, i = pieces[j]
        return pltpu.make_async_copy(low.at[j % 2], targets[k].at[:, pl.ds(i * width, width)], stores.at[j % 2])

    def issue():
        load(0).start()
        load(1).start()
        yield
        for j in range(len(pieces)):
            load(j).wait()
            if j >= 2:
                store(j - 2).wait()
            low[j % 2] = wide[j % 2].astype(F32).astype(BF16)
            store(j).start()
            if j + 2 < len(pieces):
                load(j + 2).start()
            yield

    def finish():
        for j in range(len(pieces) - 2, len(pieces)):
            store(j).wait()

    return issue(), finish


def swap_copy(at, source, target, send, recv):
    return remote(source, target.at[at.member], send, recv, at.partner, at.b)


def swap_task(at, source, target, sems):
    there = swap_copy(at, source, target, sems.at[0], sems.at[1])
    here = remote(source, target.at[1 - at.member], sems.at[0], sems.at[1], at.partner, at.b)

    def issue():
        there.start()
        yield

    def finish():
        here.wait_recv()
        there.wait_send()

    return issue(), finish


def open_kernel(grid, tokens, cotangent, gain, qkv_parts, out_codes, small, gate_codes, up_codes, cid):
    x = tokens
    n, levels = grid.n, grid.planes // 2
    rows_d, width = qkv_parts.shape[1:]
    flat = rows_d % 16 == 0
    copies = n // HEADS
    gs, ss, ts, hs = gather_sems(grid, levels, 2), share_sems(grid, 1), [dma(n), dma(n)], head_rows_sems(grid)

    piece = FF // 2
    ns = [
        pltpu.VMEM((2, rows_d, piece), jnp.int32),
        pltpu.VMEM((2, rows_d, piece), BF16),
        dma(2),
        dma(2),
    ]

    def kernel(
        x_ref, cot_ref, gain_ref, w_ref, o_ref, small_ref, gate_ref, up_ref,
        kept_ref, kept_cot_ref, seen_ref, codes_ref, rows_ref, all_ref, gl_ref, ul_ref, *scratch,
    ):
        at = Place(grid, levels)
        refs = Split(scratch)
        normed_ref, token_sems, cot_sems = refs.take(3)
        member = at.member
        at.greet_all()
        token_issue, token_finish = swap_task(at, x_ref.at[1 - member], kept_ref, token_sems)
        run(token_issue)

        def view(j):
            return codes_ref.at[pl.ds(j * rows_d, rows_d)] if flat else codes_ref.at[j]

        def ready(k):
            u = member if k == 0 else 1 - member
            if k == 1:
                token_finish()

            def one(_, r):
                if k == 0:
                    kept_ref[u, r] = x_ref[u, r]
                    kept_cot_ref[u, r] = cot_ref[u, r]
                value = kept_ref[u, r].astype(F32)
                normed_ref[u, r] = (value * inverse_rms(value) * gain_ref[...]).astype(BF16)

            each_rows(1, x_ref.shape[1], one)

        together(
            gather_steps(
                at, normed_ref, seen_ref, *refs.take(len(gs)), passes=[(member, 1), (1 - member, 1)], ready=ready
            ),
            narrow_task([gate_ref, up_ref], [gl_ref, ul_ref], *refs.take(4)),
            tell_task(at, small_ref, all_ref, *refs.take(2)),
            share_task(at, [lambda to: w_ref.at[to % HEADS]], [view], *refs.take(len(ss))),
            head_rows_task(at, o_ref, rows_ref, *refs.take(4)),
            swap_task(at, cot_ref.at[1 - member], kept_cot_ref, cot_sems),
        )

    codes_shape = (n * rows_d, width) if flat else (n, rows_d, width)
    return pl.pallas_call(
        kernel,
        out_shape=(
            jax.ShapeDtypeStruct(x.shape, BF16),
            jax.ShapeDtypeStruct(x.shape, BF16),
            jax.ShapeDtypeStruct((2, levels * grid.plane) + x.shape[1:], BF16),
            jax.ShapeDtypeStruct(codes_shape, BF16),
            jax.ShapeDtypeStruct((copies,) + out_codes.shape, BF16),
            jax.ShapeDtypeStruct((n,) + small.shape, small.dtype),
            jax.ShapeDtypeStruct(gate_codes.shape, BF16),
            jax.ShapeDtypeStruct(up_codes.shape, BF16),
        ),
        in_specs=[INVMEM] * 6 + [ANY] * 2,
        out_specs=(INVMEM, INVMEM) + (ANY,) * 6,
        scratch_shapes=[pltpu.VMEM(x.shape, BF16), dma(2), dma(2)] + gs + ns + ts + ss + hs,
        compiler_params=params(cid, 50),
        name="open",
    )(tokens, cotangent, gain, qkv_parts, out_codes, small, gate_codes, up_codes)


def scatter_kernel(grid, levels, cid, name, tasks=None, end=None):
    made, in_specs, out_shapes, out_specs, extra_scratch = tasks if tasks else (None, [], (), (), [])

    def call(p, extra):
        rows, width = p.shape[2:]
        more = () if extra is None else tuple(extra)
        own = scatter_scratch(grid, levels, rows, width)

        def kernel(*refs):
            refs = Split(refs)
            (p_ref,) = refs.take(1)
            more_refs = refs.take(len(more))
            (out_ref,) = refs.take(1)
            out_refs = refs.take(len(out_shapes) if more else 0)
            mine = refs.take(len(own))
            at = Place(grid, levels)
            load = pltpu.make_async_copy(p_ref, mine[0], mine[4].at[0])
            load.start()
            if more:
                at.greet_all()
            else:
                at.greet_near(False)
            load.wait()
            sums = refs.take(1)[0] if end else out_ref
            others = made(at, more_refs, out_refs, refs) if more else []
            if end is None:
                together(scatter_steps(at, out_ref, *mine), *others)
                return
            for _ in scatter_steps(at, sums, *mine):
                for issue, _finish in others:
                    next(issue, None)
            last = end(at, more_refs, sums, out_ref, refs)
            together((), *others)
            last()

        return pl.pallas_call(
            kernel,
            out_shape=(jax.ShapeDtypeStruct((2, rows, width), BF16),) + (out_shapes if more else ()),
            in_specs=[ANY] + (in_specs if more else []),
            out_specs=(INVMEM,) + (out_specs if more else ()),
            scratch_shapes=own + (extra_scratch if more else []),
            compiler_params=params(cid + (0 if more else 20), 60),
            name=name,
        )(p, *more)

    return call


def feed_windows(grid):
    units = FF // grid.n
    window = 128 * max(-(-((c * units) % 128 + units) // 128) for c in range(grid.n))
    return units, window, lambda c: ((c * units) // 128) * 128


def attention_sums(grid, p, gate_codes, up_codes, cid):
    n, levels = grid.n, grid.planes // 2
    rows_d = gate_codes.shape[0]
    flat = rows_d % 16 == 0
    units, window, start = feed_windows(grid)
    ss = share_sems(grid, 2)

    def tasks(at, ins, outs, refs):
        def source(ref):
            return lambda to: ref.at[:, pl.ds(pl.multiple_of(start(to), 128), window)]

        def view(ref):
            return lambda j: ref.at[pl.ds(j * rows_d, rows_d)] if flat else ref.at[j]

        return [share_task(at, [source(r) for r in ins], [view(r) for r in outs], *refs.take(len(ss)))]

    shape = (n * rows_d, window) if flat else (n, rows_d, window)
    call = scatter_kernel(
        grid,
        levels,
        cid,
        "attention_sums",
        (tasks, [INVMEM, INVMEM], (jax.ShapeDtypeStruct(shape, BF16),) * 2, (ANY, ANY), ss),
    )
    return in_parts(grid, levels, call, p, (gate_codes, up_codes))


def feed_sums(grid, p, cid):
    return in_parts(grid, grid.planes, scatter_kernel(grid, grid.planes, cid, "feed_sums"), p, None)[0]


def feed_back_sums(grid, p, pair_grad, cid):
    rs = return_scratch(grid, pair_grad.shape[1:])

    def tasks(at, ins, outs, refs):
        return [return_task(at, ins[0], outs[0], *refs.take(len(rs)))]

    call = scatter_kernel(
        grid,
        grid.planes,
        cid,
        "feed_back_sums",
        (tasks, [ANY], (jax.ShapeDtypeStruct(pair_grad.shape, BF16),), (ANY,), rs),
    )
    return in_parts(grid, grid.planes, call, p, (pair_grad,))


def attention_back_sums(grid, p, qkv_grad, out_grad, down_grad, gains, merged, cid):
    n, levels = grid.n, grid.planes // 2
    rs, hs = return_scratch(grid, qkv_grad.shape[1:]), head_return_scratch(grid, out_grad.shape[1:])
    ps = [pltpu.VMEM(down_grad.shape, BF16), dma(2)]
    gs = [pltpu.VMEM(gains.shape, F32), pltpu.VMEM(gains.shape, F32), dma(2)] + share_sems(grid, 1)
    us = assemble_scratch(grid) if merged else []
    rows, width = p.shape[2:]
    tail = [pltpu.VMEM((2, rows, width), BF16), dma(2)] if merged else []
    inputs = [qkv_grad, out_grad, down_grad, gains] + list(merged)
    in_specs = [ANY, ANY, INVMEM, INVMEM] + ([ANY] + [INVMEM] * 3 if merged else [])
    shapes = (
        jax.ShapeDtypeStruct(qkv_grad.shape, BF16),
        jax.ShapeDtypeStruct(out_grad.shape, BF16),
        jax.ShapeDtypeStruct(down_grad.shape, BF16),
        jax.ShapeDtypeStruct((n,) + gains.shape, F32),
    ) + (jax.ShapeDtypeStruct((D // n, FF), BF16),) * (2 if merged else 0)
    out_specs = (ANY, ANY, INVMEM, INVMEM) + ((ANY, ANY) if merged else ())
    sums = [pltpu.VMEM((2, rows, width), BF16)] if merged else []
    scratch = sums + rs + hs + ps + gs + us + tail

    def tasks(at, ins, outs, refs):
        made = [
            return_task(at, ins[0], outs[0], *refs.take(len(rs))),
            head_return_task(at, ins[1], outs[1], *refs.take(len(hs))),
            pair_task(at, ins[2], outs[2], *refs.take(2)),
            gains_task(at, ins[3], outs[3], *refs.take(len(gs))),
        ]
        if merged:
            made.insert(0, assemble_task(grid, ins[4], outs[4:6], *refs.take(len(us))))
        return made

    def end(at, ins, sums, out_ref, refs):
        kept, sems = refs.take(2)
        grad_ref, tokens_ref, gain_ref = ins[5:8]

        def one(u, r):
            dy, v = sums[u, r].astype(F32), tokens_ref[u, r].astype(F32)
            kept[u, r] = (grad_ref[u, r] + norm_back(v, inverse_rms(v), dy * gain_ref[...])).astype(BF16)

        each_rows(2, rows, one)
        issue, finish = swap_task(at, kept.at[1 - at.member], out_ref, sems)
        run(issue)
        out_ref[at.member] = kept[at.member]
        return finish

    call = scatter_kernel(
        grid,
        levels,
        cid,
        "attention_back_sums",
        (tasks, in_specs, shapes, out_specs, scratch),
        end if merged else None,
    )
    return in_parts(grid, levels, call, p, inputs)


def inverse_rms(v):
    return lax.rsqrt(jnp.mean(v * v, axis=-1, keepdims=True) + 1e-06)


def norm_back(v, r, weighted):
    return r * weighted - v * (r * r * r * jnp.mean(weighted * v, axis=-1, keepdims=True))


def each_rows(group, rows, step):
    def one(i, carry):
        step(i // (rows // 16), pl.ds(pl.multiple_of((i % (rows // 16)) * 16, 16), 16))
        return carry

    lax.fori_loop(0, group * (rows // 16), one, 0)


def fits(grid, rows):
    return (D // grid.n) % 16 == 0 and scatter_parts(grid, grid.planes, rows, D) == 1


def forward_kernel(
    grid, p, tokens, gate_codes, up_codes, down_codes, pair_scale, down_scale, post_gain, feed_gain, cid
):
    n, levels = grid.n, grid.planes
    group, rows, _ = tokens.shape
    rows_d = gate_codes.shape[0]
    units, window, start = feed_windows(grid)
    size = feed_blocks(grid)
    sc = scatter_scratch(grid, levels // 2, rows, D)
    ss = share_sems(grid, 2)
    ws, gs = FeedWeights.scratch(group, units, window), gather_sems(grid, levels)

    def kernel(
        p_ref, tokens_ref, gate_ref, up_ref, down_ref, ps_ref, ds_ref, pg_ref, fg_ref,
        raw_ref, mixed_ref, all_ref, pair_ref, part_ref, wp_ref, wd_ref, *scratch,
    ):
        refs = Split(scratch)
        half_at, at = Place(grid, levels // 2), Place(grid, levels)
        mine = refs.take(len(sc))
        share_refs = refs.take(len(ss))
        weights = FeedWeights(at, group, units, None, None, down_ref, (wp_ref, wd_ref), refs.take(len(ws)))
        gather_refs = refs.take(len(gs))
        (x,) = refs.take(1)
        loads, stores, compute = forward_chunks(weights, all_ref, pair_ref, part_ref, *refs.take(4))
        load = pltpu.make_async_copy(p_ref, mine[0], mine[4].at[0])
        load.start()
        weights.sources = (None, None, down_ref)
        weights.load()
        at.greet_all()
        load.wait()

        def source(ref):
            return lambda to: ref.at[:, pl.ds(pl.multiple_of(start(to), 128), window)]

        def view(k):
            return lambda j: weights.codes.at[
                pl.ds(pl.multiple_of(j * rows_d, 16), rows_d), pl.ds(k * window, window)
            ]

        issue, finish = share_task(at, [source(gate_ref), source(up_ref)], [view(0), view(1)], *share_refs)
        for _ in scatter_steps(half_at, raw_ref, *mine):
            next(issue, None)

        def norms(u, r):
            raw = raw_ref[u, r].astype(F32)
            mixed = tokens_ref[u, r].astype(F32) + raw * inverse_rms(raw) * pg_ref[...]
            mixed_ref[u, r] = mixed
            x[u, r] = (mixed * inverse_rms(mixed) * fg_ref[...]).astype(BF16)

        each_rows(group, rows, norms)
        moving = LevelGather(at, x, all_ref, *gather_refs)
        moving.begin()
        run(issue)

        def first():
            finish()
            weights.make(ps_ref, ds_ref)

        moving.run(lambda zj, fresh: each_chunk(grid, zj, fresh, loads, stores, compute), first)
        for copy in stores(0):
            copy.wait()
        weights.finish()

    def blocks(width):
        return jax.ShapeDtypeStruct((group, n, rows, width), BF16)

    return pl.pallas_call(
        kernel,
        out_shape=(
            jax.ShapeDtypeStruct(tokens.shape, BF16),
            jax.ShapeDtypeStruct(tokens.shape, F32),
            blocks(D),
            blocks(2 * window),
            blocks(D),
            jax.ShapeDtypeStruct((group, D, 2 * window), BF16),
            jax.ShapeDtypeStruct((group, window, D), BF16),
        ),
        in_specs=[ANY, INVMEM, ANY, ANY, ANY, INVMEM, INVMEM, INVMEM, INVMEM],
        out_specs=(INVMEM, INVMEM) + (ANY,) * 5,
        scratch_shapes=sc
        + ss
        + ws
        + gs
        + [pltpu.VMEM(tokens.shape, BF16)]
        + chunk_buffers(size, rows, D, 2 * window, D)
        + [dma(3)],
        compiler_params=params(cid, 62),
        name="forward",
    )(p, tokens, gate_codes, up_codes, down_codes, pair_scale, down_scale, post_gain, feed_gain)


def turn_kernel(grid, p, mixed, cotangent, pair, pair_matrices, down_matrices, post_gain, cid):
    n, levels = grid.n, grid.planes
    group, rows, _ = mixed.shape
    units, window, _ = feed_windows(grid)
    size = feed_blocks(grid)
    sc, gs = scatter_scratch(grid, levels, rows, D), gather_sems(grid, levels)

    def kernel(
        p_ref, mixed_ref, cot_ref, pair_ref, wp_ref, wd_ref, pg_ref,
        out_ref, gain_ref, all_ref, part_ref, dgu_ref, hid_ref, *scratch,
    ):
        refs = Split(scratch)
        at = Place(grid, levels)
        mine, gather_refs = refs.take(len(sc)), refs.take(len(gs))
        raw, x, kept_out, wp, wd, fetch_sems, swap_sems = refs.take(7)
        load = pltpu.make_async_copy(p_ref, mine[0], mine[4].at[0])
        load.start()
        fetch = [
            pltpu.make_async_copy(wp_ref, wp, fetch_sems.at[0]),
            pltpu.make_async_copy(wd_ref, wd, fetch_sems.at[1]),
        ]
        loads, stores, compute = backward_chunks(
            wp, wd, all_ref, pair_ref, part_ref, dgu_ref, hid_ref, *refs.take(6)
        )
        at.greet_near(True)
        load.wait()
        for copy in fetch:
            copy.start()
        run(scatter_steps(at, raw, *mine))
        gain_ref[...] = jnp.zeros_like(gain_ref)

        def norms(u, r):
            v, dy = raw[u, r].astype(F32), cot_ref[u, r].astype(F32)
            inverse, gain = inverse_rms(v), pg_ref[...]
            kept_out[u, r] = (mixed_ref[u, r] + v * inverse * gain).astype(BF16)
            x[u, r] = norm_back(v, inverse, dy * gain).astype(BF16)
            gain_ref[...] += jnp.sum(dy * v * inverse, axis=0, keepdims=True)

        each_rows(group, rows, norms)
        moving = LevelGather(at, x, all_ref, *gather_refs)
        moving.begin()
        give_out, take_out = swap_task(at, kept_out.at[1 - at.member], out_ref, swap_sems)
        run(give_out)
        out_ref[at.member] = kept_out[at.member]
        for copy in fetch:
            copy.wait()

        moving.run(lambda zj, fresh: each_chunk(grid, zj, fresh, loads, stores, compute))
        take_out()
        for copy in stores(0):
            copy.wait()

    def blocks(width):
        return jax.ShapeDtypeStruct((group, n, rows, width), BF16)

    return pl.pallas_call(
        kernel,
        out_shape=(
            jax.ShapeDtypeStruct(mixed.shape, BF16),
            jax.ShapeDtypeStruct((1, D), F32),
            blocks(D),
            blocks(D),
            blocks(2 * window),
            blocks(window),
        ),
        in_specs=[ANY, INVMEM, INVMEM, ANY, ANY, ANY, INVMEM],
        out_specs=(INVMEM, INVMEM) + (ANY,) * 4,
        scratch_shapes=sc
        + gs
        + [
            pltpu.VMEM(mixed.shape, BF16),
            pltpu.VMEM(mixed.shape, BF16),
            pltpu.VMEM(mixed.shape, BF16),
            pltpu.VMEM((group, D, 2 * window), BF16),
            pltpu.VMEM((group, window, D), BF16),
            dma(2),
            dma(2),
        ]
        + chunk_buffers(size, rows, D, 2 * window, D, 2 * window, window)
        + [dma(5)],
        compiler_params=params(cid, 62),
        name="turn",
    )(p, mixed, cotangent, pair, pair_matrices, down_matrices, post_gain)


def back_kernel(grid, p, fed, down_low, pair_low, hidden, mixed, raw, cotangent, feed_gain, post_gain, cid):
    n, levels = grid.n, grid.planes
    group, rows, _ = mixed.shape
    units, window, _ = feed_windows(grid)
    size = feed_blocks(grid)
    chunks = n // size
    count = group * size * rows
    rows_d = D // n
    half = n // 2
    tile = 256
    sc, gs = scatter_scratch(grid, levels, rows, D), gather_sems(grid, levels // 2)
    rs = return_scratch(grid, (rows_d, 2 * window))

    def kernel(
        p_ref, fed_ref, low_ref, dgu_ref, hid_ref, mixed_ref, raw_ref, cot_ref, fg_ref, pg_ref,
        grad_ref, feed_ref, post_ref, all_ref, got_ref, down_ref, *scratch,
    ):
        refs = Split(scratch)
        half_at, at = Place(grid, levels // 2), Place(grid, levels)
        mine, gather_refs, return_refs = refs.take(len(sc)), refs.take(len(gs)), refs.take(len(rs))
        raw2, x, xs, ys, dgu, hid, pair_sum, down_sum, given, down_out, sems = refs.take(11)
        load = pltpu.make_async_copy(p_ref, mine[0], mine[4].at[0])
        load.start()

        def loads(i):
            at_blocks = pl.ds(i * size, size)
            return [
                pltpu.make_async_copy(fed_ref.at[:, at_blocks], xs, sems.at[0]),
                pltpu.make_async_copy(low_ref.at[:, at_blocks], ys, sems.at[1]),
                pltpu.make_async_copy(dgu_ref.at[:, at_blocks], dgu, sems.at[2]),
                pltpu.make_async_copy(hid_ref.at[:, at_blocks], hid, sems.at[3]),
            ]

        for copy in loads(0):
            copy.start()
        at.greet_all()
        load.wait()

        def sums(i):
            def one(j, carry):
                cols = pl.ds(pl.multiple_of(j * tile, tile), tile)
                pair_term = t_dot(xs[:, :, :, cols].reshape(count, tile), dgu[...].reshape(count, 2 * window))
                down_term = t_dot(hid[...].reshape(count, window), ys[:, :, :, cols].reshape(count, tile))
                if i == 0:
                    pair_sum[cols] = pair_term
                    down_sum[:, cols] = down_term
                else:
                    pair_sum[cols] = pair_sum[cols] + pair_term
                    down_sum[:, cols] = down_sum[:, cols] + down_term
                return carry

            for copy in loads(i):
                copy.wait()
            lax.fori_loop(0, D // tile, one, 0)
            if i + 1 < chunks:
                for copy in loads(i + 1):
                    copy.start()

        to, _ = pairwise(n, at.c, at.b)
        other_to, _ = pairwise(n, at.c, 1 - at.b)
        give_down = pltpu.make_async_copy(down_out, down_ref, sems.at[4])

        def lowered(i):
            def one(r, carry):
                here = pl.ds(pl.multiple_of(r * 16, 16), 16)
                mine_at = pl.ds(pl.multiple_of(to(i) * rows_d + r * 16, 16), 16)
                other_at = pl.ds(pl.multiple_of(other_to(i) * rows_d + r * 16, 16), 16)
                return_refs[0][i, here] = pair_sum[mine_at].astype(BF16)
                given[i, here] = pair_sum[other_at].astype(BF16)
                return carry

            lax.fori_loop(0, rows_d // 16, one, 0)

        def lowered_down():
            def one(r, carry):
                here = pl.ds(pl.multiple_of(r * 16, 16), 16)
                down_out[here] = down_sum[here].astype(BF16)
                return carry

            lax.fori_loop(0, window // 16, one, 0)
            give_down.start()

        def prepare():
            for i in range(chunks):
                sums(i)
                if i % 2 == 1:
                    yield
            lowered_down()

        issue, finish = return_task(at, None, got_ref, *return_refs, given=given, fill=lowered, prepare=prepare)

        def main():
            yield from scatter_steps(at, raw2, *mine)
            feed_ref[...] = jnp.zeros_like(feed_ref)
            post_ref[...] = jnp.zeros_like(post_ref)

            def norms(u, r):
                dy, v = raw2[u, r].astype(F32), mixed_ref[u, r]
                inverse = inverse_rms(v)
                grad = cot_ref[u, r].astype(F32) + norm_back(v, inverse, dy * fg_ref[...])
                feed_ref[...] += jnp.sum(dy * v * inverse, axis=0, keepdims=True)
                grad_ref[u, r] = grad
                w = raw_ref[u, r].astype(F32)
                inverse = inverse_rms(w)
                x[u, r] = norm_back(w, inverse, grad * pg_ref[...]).astype(BF16)
                post_ref[...] += jnp.sum(grad * w * inverse, axis=0, keepdims=True)

            each_rows(group, rows, norms)
            yield from gather_steps(half_at, x, all_ref, *gather_refs)

        together(main(), (issue, finish))
        give_down.wait()

    return pl.pallas_call(
        kernel,
        out_shape=(
            jax.ShapeDtypeStruct(mixed.shape, F32),
            jax.ShapeDtypeStruct((1, D), F32),
            jax.ShapeDtypeStruct((1, D), F32),
            jax.ShapeDtypeStruct((2, half, rows, D), BF16),
            jax.ShapeDtypeStruct((n, rows_d, 2 * window), BF16),
            jax.ShapeDtypeStruct((window, D), BF16),
        ),
        in_specs=[ANY] * 5 + [INVMEM] * 5,
        out_specs=(INVMEM,) * 3 + (ANY,) * 3,
        scratch_shapes=sc
        + gs
        + rs
        + [
            pltpu.VMEM(mixed.shape, BF16),
            pltpu.VMEM(mixed.shape, BF16),
            pltpu.VMEM((group, size, rows, D), BF16),
            pltpu.VMEM((group, size, rows, D), BF16),
            pltpu.VMEM((group, size, rows, 2 * window), BF16),
            pltpu.VMEM((group, size, rows, window), BF16),
            pltpu.VMEM((D, 2 * window), F32),
            pltpu.VMEM((window, D), F32),
            pltpu.VMEM((half, rows_d, 2 * window), BF16),
            pltpu.VMEM((window, D), BF16),
            dma(5),
        ],
        compiler_params=params(cid, 63),
        name="back",
    )(p, fed, down_low, pair_low, hidden, mixed, raw, cotangent, feed_gain, post_gain)


def assemble_task(grid, got_ref, targets, wide, high, load_sem, stores):
    n = grid.n
    units, window, _ = feed_windows(grid)
    inner = n // HEADS
    whole = inner * units
    starts = [i * units // 128 * 128 for i in range(inner)]
    load = pltpu.make_async_copy(got_ref, wide, load_sem.at[0])

    def store(k):
        return pltpu.make_async_copy(high.at[k], targets[k], stores.at[k])

    def put(g, k):
        for t in range(0, whole, 128):
            total = 0.0
            for i in range(inner):
                if 0 <= t - starts[i] < window:
                    total = total + wide[g * inner + i, :, pl.ds(k * window + t - starts[i], 128)].astype(F32)
            high[k, :, pl.ds(pl.multiple_of(g * whole + t, 128), 128)] = total.astype(BF16)

    def issue():
        load.start()
        yield
        yield
        load.wait()
        for k in range(2):

            def one(g, carry):
                put(g, k)
                return carry

            lax.fori_loop(0, n // inner, one, 0)
            store(k).start()
            yield

    def finish():
        for k in range(2):
            store(k).wait()

    return issue(), finish


def assemble_scratch(grid):
    _, window, _ = feed_windows(grid)
    rows_d = D // grid.n
    return [pltpu.VMEM((grid.n, rows_d, 2 * window), BF16), pltpu.VMEM((2, rows_d, FF), BF16), dma(1), dma(2)]


def gains_task(at, x_ref, out_ref, total, other, sems, *share_refs):
    copy = at.sibling(x_ref, other, sems.at[0], sems.at[1])
    later, finish = share_task(at, [lambda to: total], [lambda j: out_ref.at[j]], *share_refs)

    def issue():
        copy.start()
        yield
        copy.wait()
        total[...] = x_ref[...] + other[...]
        yield from later

    return issue(), finish


def normed(value, gain):
    return value * lax.rsqrt(jnp.mean(value * value, axis=-1, keepdims=True) + 1e-06) * gain


def angles(places, head):
    freqs = 10000.0 ** (-(jnp.arange(head // 2, dtype=F32) * 2.0 / head))
    return places.astype(F32)[..., None] * freqs


def rotate(values, cosine, sine):
    half = values.shape[-1] // 2
    first = values[..., :half]
    second = values[..., half:]
    return jnp.concatenate([first * cosine - second * sine, second * cosine + first * sine], axis=-1)


def width_step(number):
    remainder = number % 3
    return jnp.where(remainder == 0, 1.0, jnp.where(remainder == 1, 16.0, 64.0)).astype(F32)


def dequantized(codes, column_scale, step):
    offset = jnp.where(step > 1.0, 0.5 * step, 0.0)
    level = jnp.floor(codes.astype(F32) / step) * step + offset
    return (level * column_scale[None, :]).astype(BF16)


def dot(left, right):
    return jnp.dot(left, right, preferred_element_type=F32)


def dot_t(left, right):
    return lax.dot_general(left, right, (((1,), (1,)), ((), ())), preferred_element_type=F32)


def t_dot(left, right):
    return lax.dot_general(left, right, (((0,), (0,)), ((), ())), preferred_element_type=F32)


def unwindowed(grid, got):
    n, rows, window = got.shape
    units = FF // n
    inner = n // HEADS
    whole = inner * units
    got = got.astype(F32).reshape(n // inner, inner, rows, window)
    total = 0.0
    for i in range(inner):
        start = i * units // 128 * 128
        total = total + jnp.pad(got[:, i], ((0, 0), (0, 0), (start, whole - start - window)))
    return jnp.transpose(total, (1, 0, 2)).reshape(rows, FF)


def on_device(
    grid,
    tokens,
    segments,
    positions,
    cotangent,
    query_codes,
    key_codes,
    value_codes,
    output_codes,
    gate_codes,
    up_codes,
    down_codes,
    query_scale,
    key_scale,
    value_scale,
    output_scale,
    gate_scale,
    up_scale,
    down_scale,
    attention_gain,
    attention_post_gain,
    feed_gain,
    feed_post_gain,
):
    n = grid.n
    group, block, _ = tokens.shape
    length = n * block
    pairs = HEADS // KV_HEADS
    scale = HEAD ** (-0.5)
    chip, core = lax.axis_index("seq"), lax.axis_index("batch")
    half = n // 2
    member = chip // half
    head = chip % HEADS
    kv_head = head // pairs
    parts = half // HEADS
    copies = n // HEADS
    asked = length // parts
    first_asked = ((chip % half) // HEADS) * asked
    steps = [width_step(core * group + m) for m in range(group)]
    step = width_step(core * group + member)
    rows_d = D // n
    units, window, _ = feed_windows(grid)

    q_parts = jnp.transpose(query_codes.reshape(rows_d, HEADS, HEAD), (1, 0, 2))
    k_parts = jnp.repeat(jnp.transpose(key_codes.reshape(rows_d, KV_HEADS, HEAD), (1, 0, 2)), pairs, axis=0)
    v_parts = jnp.repeat(jnp.transpose(value_codes.reshape(rows_d, KV_HEADS, HEAD), (1, 0, 2)), pairs, axis=0)
    qkv_parts = jnp.concatenate([q_parts, k_parts, v_parts], axis=-1).astype(BF16)
    small = jnp.zeros((8, 128), jnp.int32).at[:group, :block].set(positions)
    tokens, cotangent, seen, qkv_codes, out_codes, all_places, gate_low, up_low = open_kernel(
        grid,
        tokens,
        cotangent,
        attention_gain[None],
        qkv_parts,
        output_codes.astype(BF16),
        small,
        gate_codes,
        up_codes,
        1,
    )
    seen = seen.reshape(length, D)

    qkv_scale = jnp.concatenate(
        [
            lax.dynamic_slice_in_dim(query_scale, head * HEAD, HEAD),
            lax.dynamic_slice_in_dim(key_scale, kv_head * HEAD, HEAD),
            lax.dynamic_slice_in_dim(value_scale, kv_head * HEAD, HEAD),
        ]
    )
    qkv_matrix = dequantized(qkv_codes.reshape(D, 3 * HEAD), qkv_scale, step)
    out_matrix = dequantized(out_codes.reshape(HEAD, D), output_scale, step)

    places_all = lax.dynamic_index_in_dim(all_places[:, :group, :block], member, 1, False).reshape(length)
    turn = angles(places_all, HEAD)
    cosine, sine = jnp.cos(turn), jnp.sin(turn)
    if parts == 1:
        seen_asked, places_asked, cosine_q, sine_q = seen, places_all, cosine, sine
        projected = dot(seen, qkv_matrix)
        q_lin, kv_lin = projected[:, :HEAD], projected[:, HEAD:]
    else:
        seen_asked, places_asked, cosine_q, sine_q = [
            lax.dynamic_slice_in_dim(a, first_asked, asked) for a in (seen, places_all, cosine, sine)
        ]
        q_lin, kv_lin = dot(seen_asked, qkv_matrix[:, :HEAD]), dot(seen, qkv_matrix[:, HEAD:])
    queries = rotate(q_lin, cosine_q, sine_q).astype(BF16)
    keys = rotate(kv_lin[:, :HEAD], cosine, sine).astype(BF16)
    values = kv_lin[:, HEAD:].astype(BF16)
    q_index = first_asked + jnp.arange(asked, dtype=jnp.int32)
    key_index = jnp.arange(length, dtype=jnp.int32)
    allowed = (key_index[None, :] <= q_index[:, None]) & (key_index[None, :] >= (q_index - places_asked)[:, None])
    bent = jnp.tanh(dot_t(queries, keys) * scale / cap_limit)
    kernel = jnp.where(allowed, jnp.exp(cap_limit * bent), 0.0)
    totals = jnp.sum(kernel, axis=-1, keepdims=True)
    kernel_low = kernel.astype(BF16)
    attended = dot(kernel_low, values) / totals
    attended_low = attended.astype(BF16)

    def swapped_back(kept):
        own, other = (lax.dynamic_index_in_dim(kept, u, 0, False) for u in (member, 1 - member))
        other = lax.ppermute(other, "seq", [(c, (c + half) % n) for c in range(n)])
        return jnp.where(member == 0, jnp.stack([own, other]), jnp.stack([other, own]))

    def spread(part):
        if parts > 1:
            part = lax.dynamic_update_slice_in_dim(jnp.zeros((length, D), BF16), part, first_asked, 0)
        return part.reshape(2, half, block, D)

    out_part = spread(dot(attended_low, out_matrix).astype(BF16))
    first_column = chip * units // 128 * 128
    inset = chip * units - first_column
    pair_scale = jnp.concatenate(
        [lax.dynamic_slice_in_dim(s, first_column, window) for s in (gate_scale, up_scale)]
    )[None]
    if fits(grid, block):
        attention_raw, mixed, fed, gate_up, down_part, pair_matrices, down_matrices = forward_kernel(
            grid,
            out_part,
            tokens,
            gate_low,
            up_low,
            down_codes,
            pair_scale,
            down_scale[None],
            attention_post_gain[None],
            feed_gain[None],
            2,
        )
        output, grad_post_feed, down_low, second_part, pair_low, hidden = turn_kernel(
            grid, down_part, mixed, cotangent, gate_up, pair_matrices, down_matrices, feed_post_gain[None], 3
        )
        grad_mixed, grad_pre_feed, grad_post_attention, attention_low, pair_got, down_grad = back_kernel(
            grid,
            second_part,
            fed,
            down_low,
            pair_low,
            hidden,
            mixed,
            attention_raw,
            cotangent,
            feed_gain[None],
            attention_post_gain[None],
            4,
        )
    else:
        attention_raw, gate_got, up_got = attention_sums(grid, out_part, gate_low, up_low, 2)
        attention_raw = attention_raw.astype(F32)
        feed_weights = (
            gate_got.reshape(D, window),
            up_got.reshape(D, window),
            down_codes,
            pair_scale,
            down_scale[None],
        )
        mixed = tokens.astype(F32) + normed(attention_raw, attention_post_gain)
        second_normed = normed(mixed, feed_gain).astype(BF16)
        fed, gate_up, down_part, pair_matrices, down_matrices = feed_forward(grid, second_normed, *feed_weights, 3)
        down_raw = feed_sums(grid, down_part, 4).astype(F32)
        branch, pull_out = jax.vjp(normed, down_raw, feed_post_gain)
        output = swapped_back((mixed + branch).astype(BF16))
        upstream = cotangent.astype(F32)
        grad_down_raw, grad_post_feed = pull_out(upstream)
        down_low, second_part, pair_low, hidden = feed_backward(
            grid, grad_down_raw.astype(BF16), gate_up, pair_matrices, down_matrices, 9
        )
        count = group * length
        pair_grad = t_dot(fed.reshape(count, D), pair_low.reshape(count, 2 * window)).astype(BF16)
        down_grad = t_dot(hidden.reshape(count, window), down_low.reshape(count, D)).astype(BF16)
        grad_second, pair_got = feed_back_sums(grid, second_part, pair_grad.reshape(n, rows_d, 2 * window), 5)
        gate_grad, up_grad = (unwindowed(grid, pair_got[..., i * window : (i + 1) * window]) for i in range(2))
        _, pull_feed = jax.vjp(normed, mixed, feed_gain)
        grad_mixed_part, grad_pre_feed = pull_feed(grad_second.astype(F32))
        grad_mixed = upstream + grad_mixed_part
        _, pull_post = jax.vjp(normed, attention_raw, attention_post_gain)
        grad_attention, grad_post_attention = pull_post(grad_mixed)
        attention_low = gather(grid, grad_attention.astype(BF16), grid.planes // 2, 6)
    down_grad = lax.dynamic_slice(down_grad, (inset, 0), (units, D))

    attention_low = attention_low.reshape(length, D)
    if parts > 1:
        attention_low = lax.dynamic_slice_in_dim(attention_low, first_asked, asked)
    grad_attended = dot_t(attention_low, out_matrix)
    grad_sums = (grad_attended / totals).astype(BF16)
    offsets = jnp.sum(grad_attended * attended, axis=-1, keepdims=True) / totals
    grad_kernel = dot_t(grad_sums, values) - offsets
    grad_raw = (kernel * grad_kernel * (1.0 - bent * bent)).astype(BF16)
    grad_q = dot(grad_raw, keys) * scale
    grad_k = t_dot(grad_raw, queries) * scale
    grad_v = t_dot(kernel_low, grad_sums)
    q_low = rotate(grad_q, cosine_q, -sine_q).astype(BF16)
    kv_low = jnp.concatenate([rotate(grad_k, cosine, -sine), grad_v], axis=-1).astype(BF16)
    if parts == 1:
        qkv_low = jnp.concatenate([q_low, kv_low], axis=-1)
        first_part = dot_t(qkv_low, qkv_matrix)
        qkv_grad = t_dot(seen, qkv_low)
    else:
        first_part = dot_t(kv_low, qkv_matrix[:, HEAD:])
        q_back = dot_t(q_low, qkv_matrix[:, :HEAD])
        first_part = lax.dynamic_update_slice_in_dim(
            first_part, lax.dynamic_slice_in_dim(first_part, first_asked, asked) + q_back, first_asked, 0
        )
        qkv_grad = jnp.concatenate([t_dot(seen_asked, q_low), t_dot(seen, kv_low)], axis=-1)
    first_part = first_part.astype(BF16)
    grad_pre_attention = jnp.sum(first_part.astype(F32) * seen.astype(F32), axis=0) / attention_gain
    gains = jnp.stack(
        [g.reshape(D) for g in (grad_pre_attention, grad_post_attention, grad_pre_feed, grad_post_feed)]
    )
    out_part = t_dot(attended_low, attention_low).astype(BF16).reshape(copies, HEAD // copies, D)
    merged = (pair_got, grad_mixed, tokens, attention_gain[None]) if fits(grid, block) else ()
    grad_in, qkv_got, out_got, down_grad, gains, *assembled = attention_back_sums(
        grid,
        first_part.reshape(2, half, block, D),
        qkv_grad.astype(BF16).reshape(n, rows_d, 3 * HEAD),
        out_part,
        down_grad,
        gains.reshape(8, D // 2),
        merged,
        7,
    )
    if merged:
        gate_grad, up_grad = (a.astype(F32) for a in assembled)
    else:
        _, pull_in = jax.vjp(lambda value: normed(value, attention_gain), tokens.astype(F32))
        (grad_source_part,) = pull_in(grad_in.astype(F32))
        grad_in = swapped_back((grad_mixed + grad_source_part).astype(BF16))
    down_grad = down_grad.astype(F32)
    qkv_got = jnp.sum(qkv_got.astype(F32).reshape(copies, HEADS, rows_d, 3 * HEAD), axis=0)
    query_grad = jnp.transpose(qkv_got[..., :HEAD], (1, 0, 2)).reshape(rows_d, HEADS * HEAD)
    kv_grad = jnp.sum(qkv_got[..., HEAD:].reshape(KV_HEADS, pairs, rows_d, 2 * HEAD), axis=1)
    key_grad = jnp.transpose(kv_grad[..., :HEAD], (1, 0, 2)).reshape(rows_d, KV_HEADS * HEAD)
    value_grad = jnp.transpose(kv_grad[..., HEAD:], (1, 0, 2)).reshape(rows_d, KV_HEADS * HEAD)
    out_grad = jnp.sum(out_got.astype(F32), axis=0)
    gains = jnp.sum(gains, axis=0).reshape(4, D)
    return (
        output,
        grad_in,
        query_grad,
        key_grad,
        value_grad,
        out_grad,
        gate_grad,
        up_grad,
        down_grad,
    ) + tuple(gains[i] for i in range(4))


def solution(mesh):
    rows = P("seq", None)
    return jax.shard_map(
        functools.partial(on_device, Grid(mesh.shape["seq"])),
        mesh=mesh,
        in_specs=(P("batch", "seq", None), P("batch", "seq"), P("batch", "seq"), P("batch", "seq", None))
        + (rows,) * 7
        + (P(),) * 11,
        out_specs=(P("batch", "seq", None),) * 2 + (rows,) * 7 + (P(),) * 4,
        check_vma=False,
    )
```

```python
import functools

import jax
import jax.numpy as jnp
from jax import lax
from jax.experimental import pallas as pl
from jax.experimental.pallas import tpu as pltpu
from jax.sharding import PartitionSpec as P

D = 2304
HEADS = 8
KV_HEADS = 4
HEAD = 256
FF = 9216
MESH = pl.DeviceIdType.MESH
F32 = jnp.float32
BF16 = jnp.bfloat16


cap_limit = 50.0


class Grid:
    def __init__(self, n):
        self.n = n
        self.planes = 4 if n % 8 == 0 else 2
        self.plane = n // self.planes
        wide = 1
        while wide * wide < self.plane:
            wide *= 2
        self.wide = wide

    def snake(self, p):
        y, x = p // self.wide, p % self.wide
        return y * self.wide + x + (y % 2) * (self.wide - 1 - 2 * x)


def remote(src, dst, send, recv, chip, core):
    return pltpu.make_async_remote_copy(
        src_ref=src, dst_ref=dst, send_sem=send, recv_sem=recv, device_id=(chip, core), device_id_type=MESH
    )


def greet(barrier, chip, core):
    pl.semaphore_signal(barrier, inc=1, device_id=(chip, core), device_id_type=MESH)


class Place:
    def __init__(self, grid, levels):
        self.grid, self.levels = grid, levels
        self.n, self.pn = grid.n, grid.plane
        self.steps = self.pn // 2
        self.c, self.b = lax.axis_index("seq"), lax.axis_index("batch")
        self.z, p = self.c // self.pn, self.c % self.pn
        self.q = grid.snake(p)
        self.zi = self.z % levels
        self.right = self.z * self.pn + grid.snake((self.q + 1) % self.pn)
        self.left = self.z * self.pn + grid.snake((self.q + self.pn - 1) % self.pn)
        self.member = self.c // (self.n // 2)
        self.partner = (self.c + self.n // 2) % self.n

    def slot(self, zj, qj):
        return zj * self.pn + self.grid.snake((qj + 2 * self.pn) % self.pn)

    def sibling(self, src, dst, send, recv):
        return remote(src, dst, send, recv, self.c, 1 - self.b)

    def greet_near(self, halves):
        barrier = pltpu.get_barrier_semaphore()
        zi, levels = self.zi, self.levels
        greet(barrier, self.right, self.b)
        greet(barrier, self.left, self.b)
        pl.when(zi > 0)(lambda: greet(barrier, self.c - self.pn, self.b))
        pl.when(zi < levels - 1)(lambda: greet(barrier, self.c + self.pn, self.b))
        if halves:
            greet(barrier, self.partner, self.b)
        count = 2 + jnp.where(zi > 0, 1, 0) + jnp.where(zi < levels - 1, 1, 0) + (1 if halves else 0)
        pl.semaphore_wait(barrier, count)

    def greet_all(self):
        barrier = pltpu.get_barrier_semaphore()
        greet(barrier, self.c, 1 - self.b)

        def one(off, carry):
            greet(barrier, (self.c + off) % self.n, self.b)
            return carry

        lax.fori_loop(1, self.n, one, 0)
        pl.semaphore_wait(barrier, self.n)


def present(zi, sign, d, levels):
    if d == 0:
        return None
    return (zi - d >= 0) if sign < 0 else (zi + d < levels)


def guarded(condition, action):
    if condition is None:
        action()
    else:
        pl.when(condition)(action)


def dma(*shape):
    return pltpu.SemaphoreType.DMA(shape)


ANY = pl.BlockSpec(memory_space=pl.ANY)
INVMEM = pl.BlockSpec(memory_space=pltpu.VMEM)


def params(cid, mib=None):
    if mib is None:
        return pltpu.CompilerParams(collective_id=cid, has_side_effects=True)
    return pltpu.CompilerParams(collective_id=cid, has_side_effects=True, vmem_limit_bytes=mib * 2**20)


def gather_sems(grid, levels, passes=1):
    steps = grid.plane // 2
    return [
        dma(passes, 2, levels),
        dma(passes, 2, levels),
        dma(passes, 2, steps, levels),
        dma(passes, 2, steps, levels),
        dma(3),
    ]


def gather_steps(at, x_ref, out_ref, zs, zr, rs, rr, ls, passes=((0, 2),), ready=None):
    levels, steps, zi, q, pn, b = at.levels, at.steps, at.zi, at.q, at.pn, at.b
    half = x_ref.shape[1] // 2
    own = at.slot(zi, q)

    def block(us, zj, qj, part=None):
        u0, nu = us
        if part is None:
            return out_ref.at[pl.ds(u0, nu), at.slot(zj, qj)]
        return out_ref.at[pl.ds(u0, nu), at.slot(zj, qj), pl.ds(part * half, half)]

    def z_copy(k, us, zj, sign):
        way = 0 if sign > 0 else 1
        ref = block(us, zj, q)
        return remote(ref, ref, zs.at[k, way, zj], zr.at[k, way, zj], at.c + sign * pn, b)

    def r_copy(k, us, zj, way, step, landing=False):
        away = step if landing else step - 1
        ref = block(us, zj, q - away if way == 0 else q + away, way if step == steps else None)
        to = at.right if way == 0 else at.left
        return remote(ref, ref, rs.at[k, way, step - 1, zj], rr.at[k, way, step - 1, zj], to, b)

    def arrive(k, us, sign, d):
        zj = zi + sign * d

        def go():
            if d > 0:
                z_copy(k, us, zj, -sign).wait_recv()
            if sign <= 0:
                pl.when(zi < levels - 1)(lambda: z_copy(k, us, zj, 1).start())
            if sign >= 0:
                pl.when(zi > 0)(lambda: z_copy(k, us, zj, -1).start())
            for way in (0, 1):
                r_copy(k, us, zj, way, 1).start()

        guarded(present(zi, sign, d, levels), go)

    def onward(k, us, sign, d):
        zj = zi + sign * d

        def go():
            for step in range(1, steps + 1):
                for way in (0, 1):
                    r_copy(k, us, zj, way, step, True).wait_recv()
                    if step < steps:
                        r_copy(k, us, zj, way, step + 1).start()

        guarded(present(zi, sign, d, levels), go)

    def finish(k, us, sign, d):
        zj = zi + sign * d

        def go():
            if sign <= 0:
                pl.when(zi < levels - 1)(lambda: z_copy(k, us, zj, 1).wait_send())
            if sign >= 0:
                pl.when(zi > 0)(lambda: z_copy(k, us, zj, -1).wait_send())
            for way in (0, 1):
                for step in range(1, steps + 1):
                    r_copy(k, us, zj, way, step).wait_send()

        guarded(present(zi, sign, d, levels), go)

    waves = [
        [(k, us, sign, d) for sign in ((0,) if d == 0 else (-1, 1))] for k, us in enumerate(passes) for d in range(levels)
    ]
    for i, wave in enumerate(waves):
        k, (u0, nu), _, d = wave[0]
        if d == 0:
            if ready is not None:
                ready(k)
            local = pltpu.make_async_copy(x_ref.at[pl.ds(u0, nu)], out_ref.at[pl.ds(u0, nu), own], ls.at[k])
            local.start()
            local.wait()
        for group in wave:
            arrive(*group)
            yield
        if i > 0:
            for group in waves[i - 1]:
                onward(*group)
                yield
    for group in waves[-1]:
        onward(*group)
        yield
    for wave in waves:
        for group in wave:
            finish(*group)


def run(steps):
    for _ in steps:
        pass


def gather(grid, x, levels, cid):
    count = levels * grid.plane

    def kernel(x_ref, out_ref, *sems):
        at = Place(grid, levels)
        at.greet_near(False)
        run(gather_steps(at, x_ref, out_ref, *sems))

    return pl.pallas_call(
        kernel,
        out_shape=jax.ShapeDtypeStruct((2, count) + x.shape[1:], x.dtype),
        in_specs=[INVMEM],
        out_specs=ANY,
        scratch_shapes=gather_sems(grid, levels),
        compiler_params=params(cid, 50),
        name="gather_%d" % count,
    )(x)


def level_sems(grid, levels):
    steps = grid.plane // 2
    return gather_sems(grid, levels) + [dma(2, levels), dma(2, levels), dma(2, steps), dma(2, steps)]


class LevelGather:
    def __init__(self, split, at, x_ref, out_ref, zs, zr, rs, rr, ls, lzs, lzr, lrs, lrr):
        self.at, self.x, self.out = at, x_ref, out_ref
        self.zs, self.zr, self.rs, self.rr, self.ls = zs, zr, rs, rr, ls
        self.lzs, self.lzr, self.lrs, self.lrr = lzs, lzr, lrs, lrr
        rows = x_ref.shape[1]
        cut = rows * 3 // 4 // 16 * 16 if split else rows
        self.split, self.first, self.last = split, pl.ds(0, cut), pl.ds(cut, rows - cut)

    def block(self, zj, qj, part, rows):
        which = pl.ds(0, 2) if part is None else pl.ds(part, 1)
        return self.out.at[which, self.at.slot(zj, qj), rows]

    def z_copy(self, zj, way):
        at, ref = self.at, self.block(zj, self.at.q, None, self.first)
        to = at.c + (at.pn if way == 0 else -at.pn)
        return remote(ref, ref, self.zs.at[0, way, zj], self.zr.at[0, way, zj], to, at.b)

    def ring_copy(self, zj, way, step, landing, rows, send, recv):
        at = self.at
        away = step if landing else step - 1
        ref = self.block(zj, at.q - away if way == 0 else at.q + away, way if step == at.steps else None, rows)
        return remote(ref, ref, send, recv, at.right if way == 0 else at.left, at.b)

    def r_copy(self, zj, way, step, landing=False):
        sems = self.rs.at[0, way, step - 1, zj], self.rr.at[0, way, step - 1, zj]
        return self.ring_copy(zj, way, step, landing, self.first, *sems)

    def low_copy(self, way, step, landing=False):
        sems = self.lrs.at[way, step - 1], self.lrr.at[way, step - 1]
        return self.ring_copy(self.at.zi, way, step, landing, self.last, *sems)

    def low_z_copy(self, zj, way):
        at = self.at
        ref = self.out.at[:, pl.ds(zj * at.pn, at.pn), self.last]
        to = at.c + (at.pn if way == 0 else -at.pn)
        return remote(ref, ref, self.lzs.at[way, zj], self.lzr.at[way, zj], to, at.b)

    def begin(self):
        at = self.at
        local = pltpu.make_async_copy(self.x, self.out.at[:, at.slot(at.zi, at.q)], self.ls.at[0])
        local.start()
        local.wait()
        self.send(0)
        if self.split:
            for way in (0, 1):
                self.low_copy(way, 1).start()

    def along(self, offset, copy):
        at = self.at
        zj = at.zi + offset
        pl.when((offset <= 0) & (at.zi < at.levels - 1))(lambda: copy(zj, 0).start())
        pl.when((offset >= 0) & (at.zi > 0))(lambda: copy(zj, 1).start())

    def send(self, offset):
        self.along(offset, self.z_copy)
        for way in (0, 1):
            self.r_copy(self.at.zi + offset, way, 1).start()

    def arrive(self, sign, d):
        self.z_copy(self.at.zi + sign * d, 0 if sign < 0 else 1).wait_recv()
        self.send(sign * d)

    def low_arrive(self, sign, d):
        self.low_z_copy(self.at.zi + sign * d, 0 if sign < 0 else 1).wait_recv()
        self.along(sign * d, self.low_z_copy)

    def onward(self, sign, d):
        zj = self.at.zi + sign * d
        for step in range(1, self.at.steps):
            for way in (0, 1):
                self.r_copy(zj, way, step, True).wait_recv()
                self.r_copy(zj, way, step + 1).start()

    def low_onward(self):
        for step in range(1, self.at.steps):
            for way in (0, 1):
                self.low_copy(way, step, True).wait_recv()
                self.low_copy(way, step + 1).start()

    def low_landed(self):
        for way in (0, 1):
            self.low_copy(way, self.at.steps, True).wait_recv()
        self.along(0, self.low_z_copy)

    def landed(self, sign, d):
        zj = self.at.zi + sign * d
        for way in (0, 1):
            self.r_copy(zj, way, self.at.steps, True).wait_recv()

    def finish(self):
        at = self.at

        def one(zj, carry):
            for copy in (self.z_copy, self.low_z_copy)[: 2 if self.split else 1]:
                pl.when((zj <= at.zi) & (at.zi < at.levels - 1))(lambda: copy(zj, 0).wait_send())
                pl.when((zj >= at.zi) & (at.zi > 0))(lambda: copy(zj, 1).wait_send())
            for way in (0, 1):
                for step in range(1, at.steps + 1):
                    self.r_copy(zj, way, step).wait_send()
            return carry

        lax.fori_loop(0, at.levels, one, 0)
        for way in (0, 1) if self.split else ():
            for step in range(1, at.steps + 1):
                self.low_copy(way, step).wait_send()

    def run(self, compute, first=None):
        at = self.at
        zi, levels = at.zi, at.levels

        def wave(t):
            pl.when((t < levels) & (zi - t >= 0))(lambda: self.arrive(-1, t))
            pl.when((t < levels) & (zi + t < levels))(lambda: self.arrive(1, t))

        def both(d, action, least=0):
            pl.when((d >= least) & (d < levels) & (zi - d >= 0))(lambda: action(-1, d))
            pl.when((d > 0) & (d < levels) & (zi + d < levels))(lambda: action(1, d))

        def one(t, carry):
            wave(t)
            if self.split:
                pl.when(t == 2)(self.low_landed)
            both(t - 1, self.onward)
            if first is not None:
                pl.when(t == 2)(first)
            e = t - 2
            if self.split:
                both(e, self.low_arrive, 1)
            both(e, self.landed)

            def side(i, carry):
                zj = zi + (2 * i - 1) * e
                here = (zj >= 0) & (zj < levels) & ((e > 0) | (i == 0))
                pl.when(here)(lambda: compute(zj, e == 0))
                return carry

            lax.fori_loop(0, 2, side, 0)
            return carry

        wave(1)
        both(0, self.onward)
        if self.split:
            self.low_onward()
        lax.fori_loop(2, levels + 2, one, 0)
        self.finish()


def member_step(core, group, member):
    remainder = (core * group + member) % 3
    return jnp.where(remainder == 0, 1.0, jnp.where(remainder == 1, 16.0, 64.0)).astype(F32)


def dequantize(core, group, codes, row_scale, into, rows, first):
    def one(i, carry):
        value = codes(pl.multiple_of(i * 16, 16)).astype(F32)
        for m in range(group):
            step = member_step(core, group, m)
            offset = jnp.where(step > 1.0, 0.5 * step, 0.0)
            level = jnp.floor(value * (1.0 / step)) * step + offset
            into[m, pl.ds(pl.multiple_of(first + i * 16, 16), 16)] = (level * row_scale[...]).astype(BF16)
        return carry

    lax.fori_loop(0, rows // 16, one, 0)


GELU_A = 0.7978845608028654
GELU_B = 0.044715


EARLY = 4


class FeedWeights:
    def __init__(self, at, group, units, gate_ref, up_ref, down_ref, kept, refs):
        self.at, self.group, self.units = at, group, units
        self.sources, self.kept = (gate_ref, up_ref, down_ref), kept
        self.pair, self.down, self.codes, self.down_codes, self.sems = refs

    @staticmethod
    def scratch(group, units, window):
        return [
            pltpu.VMEM((group, D, 2 * window), BF16),
            pltpu.VMEM((group, window, D), BF16),
            pltpu.VMEM((D, 2 * window), BF16),
            pltpu.VMEM((units, D), jnp.int32),
            dma(5),
        ]

    def copies(self):
        window = self.codes.shape[1] // 2
        gate, up, down = self.sources
        copies = [pltpu.make_async_copy(down, self.down_codes, self.sems.at[2])]
        if gate is not None:
            copies += [
                pltpu.make_async_copy(gate, self.codes.at[:, pl.ds(0, window)], self.sems.at[0]),
                pltpu.make_async_copy(up, self.codes.at[:, pl.ds(window, window)], self.sems.at[1]),
            ]
        return copies

    def keeps(self):
        return [
            pltpu.make_async_copy(self.pair, self.kept[0], self.sems.at[3]),
            pltpu.make_async_copy(self.down, self.kept[1], self.sems.at[4]),
        ]

    def load(self):
        for copy in self.copies():
            copy.start()

    def make(self, pair_scale, down_scale):
        at, group, units = self.at, self.group, self.units
        window = self.down.shape[1]
        inset = (at.c * units) % 128
        for copy in self.copies():
            copy.wait()
        dequantize(at.b, group, lambda r: self.codes[pl.ds(r, 16)], pair_scale, self.pair, D, 0)

        def clear(i, carry):
            for m in range(group):
                self.down[m, pl.ds(pl.multiple_of(i * 16, 16), 16)] = jnp.zeros((16, D), BF16)
            return carry

        if window > units:
            lax.fori_loop(0, inset // 16, clear, 0)
            lax.fori_loop((inset + units) // 16, window // 16, clear, 0)
        dequantize(at.b, group, lambda r: self.down_codes[pl.ds(r, 16)], down_scale, self.down, units, inset)
        for copy in self.keeps():
            copy.start()

    def finish(self):
        for copy in self.keeps():
            copy.wait()


def feed_blocks(grid):
    return 4 if grid.plane % 4 == 0 else grid.plane


def each_chunk(grid, zj, fresh, loads, stores, compute):
    size = feed_blocks(grid)
    m = zj // (grid.planes // 2)

    def one(i, carry):
        first = zj * grid.plane + i * size
        reads, writes = loads(first), stores(first)
        for copy in reads:
            copy.start()

        @pl.when(jnp.logical_not(fresh & (i == 0)))
        def _():
            for copy in writes:
                copy.wait()

        compute(m, reads)
        for copy in writes:
            copy.start()
        return carry

    lax.fori_loop(0, grid.plane // size, one, 0)


def copies_of(blocks, pairs, sems, first):
    return [
        pltpu.make_async_copy(a.at[:, blocks] if far_a else a, b if far_a else b.at[:, blocks], sems.at[first + k])
        for k, (a, b, far_a) in enumerate(pairs)
    ]


def forward_chunks(weights, all_ref, pair_ref, part_ref, xs, gu, part, sems):
    _, size, rows, _ = gu.shape
    window = weights.down.shape[1]

    def loads(first):
        return copies_of(pl.ds(first, size), [(all_ref, xs, True)], sems, 0)

    def stores(first):
        return copies_of(pl.ds(first, size), [(gu, pair_ref, False), (part, part_ref, False)], sems, 1)

    def compute(m, reads):
        reads[0].wait()
        both = dot(xs[...].reshape(2 * size * rows, D), weights.pair[m])
        gu[...] = both.astype(BF16).reshape(gu.shape)
        gate, up = both[:, :window], both[:, window:]
        bend = jnp.tanh(GELU_A * (gate + GELU_B * gate * gate * gate))
        hidden = (0.5 * gate * (1.0 + bend) * up).astype(BF16)
        part[...] = dot(hidden, weights.down[m]).astype(BF16).reshape(part.shape)

    return loads, stores, compute


def backward_chunks(wp, wd, all_ref, pair_ref, part_ref, dgu_ref, hid_ref, ys, gu, part, dgu, hid, sems):
    _, size, rows, _ = ys.shape
    window = wd.shape[1]
    count = 2 * size * rows

    def loads(first):
        return copies_of(pl.ds(first, size), [(all_ref, ys, True), (pair_ref, gu, True)], sems, 0)

    def stores(first):
        pairs = [(part, part_ref, False), (dgu, dgu_ref, False), (hid, hid_ref, False)]
        return copies_of(pl.ds(first, size), pairs, sems, 2)

    def compute(m, reads):
        reads[0].wait()
        grad_hidden = dot_t(ys[...].reshape(count, D), wd[m])
        reads[1].wait()
        both = gu[...].reshape(count, 2 * window).astype(F32)
        gate, up = both[:, :window], both[:, window:]
        bend = jnp.tanh(GELU_A * (gate + GELU_B * gate * gate * gate))
        bell = 0.5 * gate * (1.0 + bend)
        slope = 0.5 * (1.0 + bend) + 0.5 * gate * (1.0 - bend * bend) * GELU_A * (1.0 + 3.0 * GELU_B * gate * gate)
        dgu[:, :, :, :window] = (grad_hidden * up * slope).astype(BF16).reshape(hid.shape)
        dgu[:, :, :, window:] = (grad_hidden * bell).astype(BF16).reshape(hid.shape)
        hid[...] = (bell * up).astype(BF16).reshape(hid.shape)
        part[...] = dot_t(dgu[...].reshape(count, 2 * window), wp[m]).astype(BF16).reshape(part.shape)

    return loads, stores, compute


def chunk_buffers(size, rows, *widths):
    return [pltpu.VMEM((2, size, rows, width), BF16) for width in widths]


def feed_forward(grid, x, gate_codes, up_codes, down_codes, pair_scale, down_scale, cid):
    group, rows, _ = x.shape
    n, levels = grid.n, grid.planes
    units, window, _ = feed_windows(grid)
    gs, ws = level_sems(grid, levels), FeedWeights.scratch(group, units, window)
    size = feed_blocks(grid)

    def kernel(
        x_ref, gate_ref, up_ref, down_ref, ps_ref, ds_ref, all_ref, pair_ref, part_ref, wp_ref, wd_ref, *scratch
    ):
        refs = Split(scratch)
        at = Place(grid, levels)
        weights = FeedWeights(at, group, units, gate_ref, up_ref, down_ref, (wp_ref, wd_ref), refs.take(len(ws)))
        weights.load()
        moving = LevelGather(True, at, x_ref, all_ref, *refs.take(len(gs)))
        loads, stores, compute = forward_chunks(weights, all_ref, pair_ref, part_ref, *refs.take(4))
        at.greet_near(False)
        moving.begin()
        weights.make(ps_ref, ds_ref)
        moving.run(lambda zj, fresh: each_chunk(grid, zj, fresh, loads, stores, compute))
        for copy in stores(0):
            copy.wait()
        weights.finish()

    def blocks(width):
        return jax.ShapeDtypeStruct((group, n, rows, width), BF16)

    return pl.pallas_call(
        kernel,
        out_shape=(
            blocks(D),
            blocks(2 * window),
            blocks(D),
            jax.ShapeDtypeStruct((group, D, 2 * window), BF16),
            jax.ShapeDtypeStruct((group, window, D), BF16),
        ),
        in_specs=[INVMEM, ANY, ANY, ANY, INVMEM, INVMEM],
        out_specs=(ANY,) * 5,
        scratch_shapes=ws + gs + chunk_buffers(size, rows, D, 2 * window, D) + [dma(3)],
        compiler_params=params(cid, 60),
        name="feed_forward",
    )(x, gate_codes, up_codes, down_codes, pair_scale, down_scale)


def feed_backward(grid, x, pair, pair_matrices, down_matrices, cid):
    group, rows, _ = x.shape
    n, levels = grid.n, grid.planes
    _, window, _ = feed_windows(grid)
    gs = level_sems(grid, levels)
    size = feed_blocks(grid)

    def kernel(x_ref, pair_ref, wp_ref, wd_ref, all_ref, part_ref, dgu_ref, hid_ref, *scratch):
        refs = Split(scratch)
        at = Place(grid, levels)
        moving = LevelGather(True, at, x_ref, all_ref, *refs.take(len(gs)))
        wp, wd, fetch_sems = refs.take(3)
        fetch = [
            pltpu.make_async_copy(wp_ref, wp, fetch_sems.at[0]),
            pltpu.make_async_copy(wd_ref, wd, fetch_sems.at[1]),
        ]
        for copy in fetch:
            copy.start()
        loads, stores, compute = backward_chunks(
            wp, wd, all_ref, pair_ref, part_ref, dgu_ref, hid_ref, *refs.take(6)
        )
        at.greet_near(False)
        moving.begin()
        for copy in fetch:
            copy.wait()
        moving.run(lambda zj, fresh: each_chunk(grid, zj, fresh, loads, stores, compute))
        for copy in stores(0):
            copy.wait()

    def blocks(width):
        return jax.ShapeDtypeStruct((group, n, rows, width), BF16)

    return pl.pallas_call(
        kernel,
        out_shape=(blocks(D), blocks(D), blocks(2 * window), blocks(window)),
        in_specs=[INVMEM] + [ANY] * 3,
        out_specs=(ANY,) * 4,
        scratch_shapes=gs
        + [pltpu.VMEM((group, D, 2 * window), BF16), pltpu.VMEM((group, window, D), BF16), dma(2)]
        + chunk_buffers(size, rows, D, 2 * window, D, 2 * window, window)
        + [dma(5)],
        compiler_params=params(cid, 62),
        name="feed_backward",
    )(x, pair, pair_matrices, down_matrices)


def scatter_scratch(grid, levels, rows, width):
    steps = grid.plane // 2
    return [
        pltpu.VMEM((2, levels * grid.plane, rows, width), BF16),
        pltpu.VMEM((2, levels, 2, rows // 2, width), BF16),
        pltpu.VMEM((2, max(steps - 1, 1), levels, 2, rows, width), BF16),
        pltpu.VMEM((2, levels, 2, rows, width), BF16),
        dma(1),
        dma(1, 2, levels),
        dma(1, 2, levels),
        dma(1, 2, steps, levels),
        dma(1, 2, steps, levels),
    ]


def scatter_steps(at, out_ref, acc, ring_half, ring_full, line, ls, zs, zr, rs, rr):
    levels, steps, zi, q, pn, b = at.levels, at.steps, at.zi, at.q, at.pn, at.b
    rows = acc.shape[2]
    half = rows // 2
    passes = [(0, 2)]

    def block(us, zj, qj, part=None):
        u0, nu = us
        if part is None:
            return acc.at[pl.ds(u0, nu), at.slot(zj, qj)]
        return acc.at[pl.ds(u0, nu), at.slot(zj, qj), pl.ds(part * half, half)]

    def add(us, s, others, lo, count):
        u0, nu = us

        def one(i, carry):
            u, r = u0 + i // (count // 16), lo + (i % (count // 16)) * 16
            total = acc[u, s, pl.ds(r, 16)].astype(F32)
            for other in others:
                total = total + other(u, r)[...].astype(F32)
            acc[u, s, pl.ds(r, 16)] = total.astype(BF16)
            return carry

        lax.fori_loop(0, nu * (count // 16), one, 0)

    def full_at(way, step, zj):
        return lambda u, r: ring_full.at[way, step - 2, zj, u, pl.ds(r, 16)]

    def half_at(way, zj):
        return lambda u, r: ring_half.at[way, zj, u, pl.ds(r - way * half, 16)]

    def line_at(way, zj):
        return lambda u, r: line.at[way, zj, u, pl.ds(r, 16)]

    def r_copy(k, us, zj, way, step):
        u0, nu = us
        sign = 1 if way == 0 else -1
        target = q + sign * (steps + 1 - step)
        if step == 1:
            src, dst = block(us, zj, target, way), ring_half.at[way, zj, pl.ds(u0, nu)]
        else:
            src, dst = block(us, zj, target), ring_full.at[way, step - 2, zj, pl.ds(u0, nu)]
        to = at.right if way == 0 else at.left
        return remote(src, dst, rs.at[k, way, step - 1, zj], rr.at[k, way, step - 1, zj], to, b)

    def z_copy(k, us, zj, way):
        u0, nu = us
        to = at.c + (pn if way == 0 else -pn)
        return remote(block(us, zj, q), line.at[way, zj, pl.ds(u0, nu)], zs.at[k, way, zj], zr.at[k, way, zj], to, b)

    def begin(k, us, sign, d):
        def go():
            for way in (0, 1):
                r_copy(k, us, zi + sign * d, way, 1).start()

        guarded(present(zi, sign, d, levels), go)

    def middle(k, us, sign, d):
        zj = zi + sign * d

        def go():
            for step in range(1, steps):
                for way in (0, 1):
                    r_copy(k, us, zj, way, step).wait_recv()
                    s = at.slot(zj, q + (1 if way == 0 else -1) * (steps - step))
                    if step == 1:
                        add(us, s, [half_at(way, zj)], way * half, half)
                    else:
                        add(us, s, [full_at(way, step, zj)], 0, rows)
                    r_copy(k, us, zj, way, step + 1).start()

        guarded(present(zi, sign, d, levels), go)

    def last(k, us, sign, d):
        zj = zi + sign * d

        def go():
            for way in (0, 1):
                r_copy(k, us, zj, way, steps).wait_recv()
            s = at.slot(zj, q)
            if steps > 1:
                add(us, s, [full_at(0, steps, zj), full_at(1, steps, zj)], 0, rows)
            else:
                add(us, s, [half_at(0, zj)], 0, half)
                add(us, s, [half_at(1, zj)], half, half)

            def passed(way):
                z_copy(k, us, zj, way).wait_recv()
                add(us, s, [line_at(way, zj)], 0, rows)

            if sign >= 0:
                pl.when(zi > 0)(lambda: passed(0))
            if sign <= 0:
                pl.when(zi < levels - 1)(lambda: passed(1))
            if sign > 0:
                z_copy(k, us, zj, 0).start()
            if sign < 0:
                z_copy(k, us, zj, 1).start()

        guarded(present(zi, sign, d, levels), go)

    def finish(k, us, sign, d):
        zj = zi + sign * d

        def go():
            for way in (0, 1):
                for step in range(1, steps + 1):
                    r_copy(k, us, zj, way, step).wait_send()
            if sign != 0:
                z_copy(k, us, zj, 0 if sign > 0 else 1).wait_send()

        guarded(present(zi, sign, d, levels), go)

    waves = [
        [(k, us, sign, d) for sign in ((0,) if d == 0 else (-1, 1))]
        for k, us in enumerate(passes)
        for d in range(levels - 1, -1, -1)
    ]
    own = at.slot(zi, q)
    def each(action, i):
        if i < len(waves):
            for group in waves[i]:
                action(*group)

    each(begin, 0)
    each(begin, 1)
    each(middle, 0)
    yield
    for i in range(len(waves)):
        each(begin, i + 2)
        each(middle, i + 1)
        yield
        each(last, i)
    yield

    def give(src, u):
        def one(i, carry):
            out_ref[u, pl.ds(i * 16, 16)] = src.at[pl.ds(i * 16, 16)][...]
            return carry

        lax.fori_loop(0, rows // 16, one, 0)

    give(acc.at[0, own], 0)
    give(acc.at[1, own], 1)
    for wave in waves:
        for group in wave:
            finish(*group)


def scatter_parts(grid, levels, rows, width):
    blocks = 2 * (2 * levels * (grid.plane // 2 + 2) + levels * grid.plane)
    parts = 1
    while blocks * rows * (width // parts) * 2 > 40 * 2**20:
        parts += 1
        while width % (128 * parts):
            parts += 1
    return parts


def in_parts(grid, levels, call, p, extra):
    parts = scatter_parts(grid, levels, p.shape[2], p.shape[3])
    if parts == 1:
        return call(p, extra)
    piece = p.shape[3] // parts
    sums, others = [], ()
    for i in range(parts):
        got = call(p[..., i * piece : (i + 1) * piece], extra if i == 0 else None)
        sums.append(got[0])
        others = got[1:] if i == 0 else others
    return (jnp.concatenate(sums, axis=-1),) + tuple(others)


def pairwise(n, c, b):
    def to(i):
        return (c + 2 * i + b) % n

    def frm(i, core):
        return (c + n - 2 * i - core) % n

    return to, frm


def middle_out(half):
    return sorted(range(1, half), key=lambda i: abs(2 * i - half))


def share_task(at, sources, views, ss, sr, fs, fr):
    n, c, b = at.n, at.c, at.b
    half = n // 2
    to, frm = pairwise(n, c, b)
    kinds = len(sources)

    def out_copy(k, i):
        return remote(sources[k](to(i)), views[k](c), ss.at[k, i], sr.at[k, i], to(i), b)

    def landed(k, i):
        return remote(sources[k](c), views[k](frm(i, b)), ss.at[k, i], sr.at[k, i], to(i), b)

    def pass_on(k, i, core):
        ref = views[k](frm(i, core))
        return at.sibling(ref, ref, fs.at[k, i], fr.at[k, i])

    def local(k):
        return pltpu.make_async_copy(sources[k](c), views[k](c), sr.at[k, 0])

    order = middle_out(half) + [0]

    def issue():
        for i in order:
            for k in range(kinds):
                if i > 0:
                    out_copy(k, i).start()
                else:
                    pl.when(b == 1)(lambda: out_copy(k, 0).start())
                    pl.when(b == 0)(lambda: local(k).start())
            yield

    def finish():
        for i in order:
            for k in range(kinds):
                if i > 0:
                    landed(k, i).wait_recv()
                else:
                    pl.when(b == 1)(lambda: landed(k, 0).wait_recv())
                    pl.when(b == 0)(lambda: local(k).wait())
                pass_on(k, i, b).start()
        for k in range(kinds):
            for i in range(half):
                pass_on(k, i, 1 - b).wait_recv()
            for i in range(half):
                pass_on(k, i, b).wait_send()
            for i in range(1, half):
                out_copy(k, i).wait_send()
            pl.when(b == 1)(lambda: out_copy(k, 0).wait_send())

    return issue(), finish


def share_sems(grid, kinds):
    return [dma(kinds, grid.n // 2) for _ in range(4)]


def tell_task(at, small_ref, all_ref, ts, tr):
    n, c, b = at.n, at.c, at.b

    def tell(off, slot):
        return remote(small_ref, all_ref.at[slot], ts.at[off], tr.at[off], (c + off) % n, b)

    keep = pltpu.make_async_copy(small_ref, all_ref.at[c], ts.at[0])

    def issue():
        keep.start()
        for off in range(1, n):
            tell(off, c).start()
        yield

    def finish():
        keep.wait()
        for off in range(1, n):
            tell(off, (c + n - off) % n).wait_recv()
        for off in range(1, n):
            tell(off, c).wait_send()

    return issue(), finish


def head_rows_task(at, x_ref, out_ref, hs, hr, fs, fr):
    c, b = at.c, at.b
    copies = at.n // HEADS
    head, rank = c % HEADS, c // HEADS
    mine = rank % 2 == b

    def out_copy(k):
        to = c // copies + HEADS * (2 * k + b)
        return to, remote(x_ref, out_ref.at[c % copies], hs.at[k], hr.at[c % copies], to, b)

    def landed(j):
        return remote(x_ref, out_ref.at[j], hs.at[0], hr.at[j], head * copies + j, b)

    def here(j):
        return pltpu.make_async_copy(x_ref, out_ref.at[j], hr.at[j])

    def pass_on(j):
        return at.sibling(out_ref.at[j], out_ref.at[j], fs.at[j], fr.at[j])

    def issue():
        for k in range(copies // 2):
            to, copy = out_copy(k)
            pl.when(to != c)(lambda: copy.start())
            pl.when(to == c)(lambda: here(c % copies).start())
            yield

    def finish():
        @pl.when(mine)
        def _():
            for j in range(copies):
                pl.when(head * copies + j != c)(lambda: landed(j).wait_recv())
                pl.when(head * copies + j == c)(lambda: here(j).wait())
                pass_on(j).start()
            for j in range(copies):
                pass_on(j).wait_send()

        @pl.when(jnp.logical_not(mine))
        def _():
            for j in range(copies):
                pass_on(j).wait_recv()

        for k in range(copies // 2):
            to, copy = out_copy(k)
            pl.when(to != c)(lambda: copy.wait_send())

    return issue(), finish


def head_rows_sems(grid):
    copies = grid.n // HEADS
    return [dma(copies), dma(copies), dma(copies), dma(copies)]


def add_rows(into, other, rows):
    step = 16 if rows % 16 == 0 else rows

    def one(r, carry):
        at = pl.ds(pl.multiple_of(r * step, step), step)
        into[at] = (into[at].astype(F32) + other[at].astype(F32)).astype(BF16)
        return carry

    lax.fori_loop(0, rows // step, one, 0)


def return_task(at, x_ref, out_ref, mine, theirs, ls, ps, pr, ss, sr, fs, fr, given=None, fill=None, prepare=None):
    n, c, b = at.n, at.c, at.b
    half = n // 2
    to, frm = pairwise(n, c, b)
    other_to, _ = pairwise(n, c, 1 - b)

    def load(i):
        return pltpu.make_async_copy(x_ref.at[to(i)], mine.at[i], ls.at[i])

    def give(i):
        source = x_ref.at[other_to(i)] if given is None else given.at[i]
        return at.sibling(source, theirs.at[i], ps.at[i], pr.at[i])

    def out_copy(i):
        return remote(mine.at[i], out_ref.at[c], ss.at[i], sr.at[i], to(i), b)

    def landed(i):
        return remote(mine.at[i], out_ref.at[frm(i, b)], ss.at[i], sr.at[i], to(i), b)

    def pass_on(i, core):
        ref = out_ref.at[frm(i, core)]
        return at.sibling(ref, ref, fs.at[i], fr.at[i])

    local = pltpu.make_async_copy(mine.at[0], out_ref.at[c], ss.at[0])
    order = middle_out(half) + [0]

    def issue():
        if prepare is not None:
            yield from prepare()
        for i in order:
            if fill is None:
                load(i).start()
            else:
                fill(i)
            give(i).start()
        for j, i in enumerate(order):
            if fill is None:
                load(i).wait()
            give(i).wait_recv()
            add_rows(mine.at[i], theirs.at[i], mine.shape[1])
            if i > 0:
                out_copy(i).start()
            else:
                pl.when(b == 1)(lambda: out_copy(0).start())
                pl.when(b == 0)(lambda: local.start())
            if j % 2 == 1:
                yield

    def finish():
        for i in order:
            if i > 0:
                landed(i).wait_recv()
            else:
                pl.when(b == 1)(lambda: landed(0).wait_recv())
                pl.when(b == 0)(lambda: local.wait())
            pass_on(i, b).start()
        for i in range(half):
            pass_on(i, 1 - b).wait_recv()
        for i in range(half):
            give(i).wait_send()
            pass_on(i, b).wait_send()
        for i in range(1, half):
            out_copy(i).wait_send()
        pl.when(b == 1)(lambda: out_copy(0).wait_send())

    return issue(), finish


def return_scratch(grid, shape):
    blocks = (grid.n // 2,) + shape
    return [pltpu.VMEM(blocks, BF16), pltpu.VMEM(blocks, BF16)] + [dma(grid.n // 2) for _ in range(7)]


def head_return_task(at, x_ref, out_ref, mine, theirs, ls, ps, pr, hs, hr, fs, fr):
    c, b = at.c, at.b
    copies = at.n // HEADS
    head, rank = c % HEADS, c // HEADS
    taken = (c % copies) % 2 == b

    def load(k):
        return pltpu.make_async_copy(x_ref.at[2 * k + b], mine.at[k], ls.at[k])

    def give(k):
        return at.sibling(x_ref.at[2 * k + 1 - b], theirs.at[k], ps.at[k], pr.at[k])

    def out_copy(k):
        to = head * copies + 2 * k + b
        return to, remote(mine.at[k], out_ref.at[rank], hs.at[k], hr.at[rank], to, b)

    def landed(i):
        return remote(mine.at[0], out_ref.at[i], hs.at[0], hr.at[i], c // copies + HEADS * i, b)

    def here(k, i):
        return pltpu.make_async_copy(mine.at[k], out_ref.at[i], hr.at[i])

    def pass_on(i):
        return at.sibling(out_ref.at[i], out_ref.at[i], fs.at[i], fr.at[i])

    def issue():
        for k in range(copies // 2):
            load(k).start()
            give(k).start()
        for k in range(copies // 2):
            load(k).wait()
            give(k).wait_recv()
            add_rows(mine.at[k], theirs.at[k], x_ref.shape[1])
            to, copy = out_copy(k)
            pl.when(to != c)(lambda: copy.start())
            pl.when(to == c)(lambda: here(k, rank).start())
            yield

    def finish():
        @pl.when(taken)
        def _():
            for i in range(copies):
                frm = c // copies + HEADS * i
                pl.when(frm != c)(lambda: landed(i).wait_recv())
                pl.when(frm == c)(lambda: here(0, i).wait())
                pass_on(i).start()
            for i in range(copies):
                pass_on(i).wait_send()

        @pl.when(jnp.logical_not(taken))
        def _():
            for i in range(copies):
                pass_on(i).wait_recv()

        for k in range(copies // 2):
            give(k).wait_send()
            to, copy = out_copy(k)
            pl.when(to != c)(lambda: copy.wait_send())

    return issue(), finish


def head_return_scratch(grid, shape):
    copies = grid.n // HEADS
    blocks = (copies // 2,) + shape
    return [pltpu.VMEM(blocks, BF16), pltpu.VMEM(blocks, BF16)] + [dma(copies) for _ in range(7)]


def pair_task(at, x_ref, out_ref, other, sems):
    copy = at.sibling(x_ref, other, sems.at[0], sems.at[1])

    def issue():
        copy.start()
        yield

    def finish():
        copy.wait_recv()

        def one(r, carry):
            rows = pl.ds(pl.multiple_of(r * 16, 16), 16)
            out_ref[rows] = (x_ref[rows].astype(F32) + other[rows].astype(F32)).astype(out_ref.dtype)
            return carry

        lax.fori_loop(0, x_ref.shape[0] // 16, one, 0)
        copy.wait_send()

    return issue(), finish


class Split:
    def __init__(self, refs):
        self.refs = list(refs)

    def take(self, count):
        got, self.refs = self.refs[:count], self.refs[count:]
        return got


def together(main, *tasks):
    for _ in main:
        for issue, _finish in tasks:
            next(issue, None)
    for issue, finish in tasks:
        run(issue)
    for issue, finish in tasks:
        finish()


def narrow_task(sources, targets, wide, low, loads, stores):
    width = wide.shape[2]
    pieces = [(k, i) for k in range(len(sources)) for i in range(sources[k].shape[1] // width)]

    def load(j):
        k, i = pieces[j]
        return pltpu.make_async_copy(sources[k].at[:, pl.ds(i * width, width)], wide.at[j % 2], loads.at[j % 2])

    def store(j):
        k, i = pieces[j]
        return pltpu.make_async_copy(low.at[j % 2], targets[k].at[:, pl.ds(i * width, width)], stores.at[j % 2])

    def issue():
        load(0).start()
        load(1).start()
        yield
        for j in range(len(pieces)):
            load(j).wait()
            if j >= 2:
                store(j - 2).wait()
            low[j % 2] = wide[j % 2].astype(F32).astype(BF16)
            store(j).start()
            if j + 2 < len(pieces):
                load(j + 2).start()
            yield

    def finish():
        for j in range(len(pieces) - 2, len(pieces)):
            store(j).wait()

    return issue(), finish


def swap_copy(at, source, target, send, recv):
    return remote(source, target.at[at.member], send, recv, at.partner, at.b)


def swap_task(at, source, target, sems):
    there = swap_copy(at, source, target, sems.at[0], sems.at[1])
    here = remote(source, target.at[1 - at.member], sems.at[0], sems.at[1], at.partner, at.b)

    def issue():
        there.start()
        yield

    def finish():
        here.wait_recv()
        there.wait_send()

    return issue(), finish


def open_kernel(grid, tokens, gain, qkv_parts, out_codes, small, gate_codes, up_codes, cid):
    x = tokens
    n, levels = grid.n, grid.planes // 2
    rows_d, width = qkv_parts.shape[1:]
    flat = rows_d % 16 == 0
    copies = n // HEADS
    gs, ss, ts, hs = gather_sems(grid, levels, 2), share_sems(grid, 1), [dma(n), dma(n)], head_rows_sems(grid)

    piece = FF // 2
    ns = [
        pltpu.VMEM((2, rows_d, piece), jnp.int32),
        pltpu.VMEM((2, rows_d, piece), BF16),
        dma(2),
        dma(2),
    ]

    def kernel(
        x_ref, gain_ref, w_ref, o_ref, small_ref, gate_ref, up_ref,
        kept_ref, seen_ref, codes_ref, rows_ref, all_ref, gl_ref, ul_ref, *scratch,
    ):
        at = Place(grid, levels)
        refs = Split(scratch)
        normed_ref, token_sems = refs.take(2)
        member = at.member
        at.greet_all()
        token_issue, token_finish = swap_task(at, x_ref.at[1 - member], kept_ref, token_sems)
        run(token_issue)

        def view(j):
            return codes_ref.at[pl.ds(j * rows_d, rows_d)] if flat else codes_ref.at[j]

        def ready(k):
            u = member if k == 0 else 1 - member
            if k == 1:
                token_finish()

            def one(_, r):
                if k == 0:
                    kept_ref[u, r] = x_ref[u, r]
                value = kept_ref[u, r].astype(F32)
                normed_ref[u, r] = (value * inverse_rms(value) * gain_ref[0:1]).astype(BF16)

            each_rows(1, x_ref.shape[1], one)

        together(
            gather_steps(
                at, normed_ref, seen_ref, *refs.take(len(gs)), passes=[(member, 1), (1 - member, 1)], ready=ready
            ),
            narrow_task([gate_ref, up_ref], [gl_ref, ul_ref], *refs.take(4)),
            tell_task(at, small_ref, all_ref, *refs.take(2)),
            share_task(at, [lambda to: w_ref.at[to % HEADS]], [view], *refs.take(len(ss))),
            head_rows_task(at, o_ref, rows_ref, *refs.take(4)),
        )

    codes_shape = (n * rows_d, width) if flat else (n, rows_d, width)
    return pl.pallas_call(
        kernel,
        out_shape=(
            jax.ShapeDtypeStruct(x.shape, BF16),
            jax.ShapeDtypeStruct((2, levels * grid.plane) + x.shape[1:], BF16),
            jax.ShapeDtypeStruct(codes_shape, BF16),
            jax.ShapeDtypeStruct((copies,) + out_codes.shape, BF16),
            jax.ShapeDtypeStruct((n,) + small.shape, small.dtype),
            jax.ShapeDtypeStruct(gate_codes.shape, BF16),
            jax.ShapeDtypeStruct(up_codes.shape, BF16),
        ),
        in_specs=[INVMEM] * 5 + [ANY] * 2,
        out_specs=(INVMEM,) + (ANY,) * 6,
        scratch_shapes=[pltpu.VMEM(x.shape, BF16), dma(2)] + gs + ns + ts + ss + hs,
        compiler_params=params(cid, 50),
        name="open",
    )(tokens, gain, qkv_parts, out_codes, small, gate_codes, up_codes)


def scatter_kernel(grid, levels, cid, name, tasks=None, end=None):
    made, in_specs, out_shapes, out_specs, extra_scratch = tasks if tasks else (None, [], (), (), [])

    def call(p, extra):
        rows, width = p.shape[2:]
        more = () if extra is None else tuple(extra)
        own = scatter_scratch(grid, levels, rows, width)

        def kernel(*refs):
            refs = Split(refs)
            (p_ref,) = refs.take(1)
            more_refs = refs.take(len(more))
            (out_ref,) = refs.take(1)
            out_refs = refs.take(len(out_shapes) if more else 0)
            mine = refs.take(len(own))
            at = Place(grid, levels)
            load = pltpu.make_async_copy(p_ref, mine[0], mine[4].at[0])
            load.start()
            if more:
                at.greet_all()
            else:
                at.greet_near(False)
            load.wait()
            sums = refs.take(1)[0] if end else out_ref
            others = made(at, more_refs, out_refs, refs) if more else []
            if end is None:
                together(scatter_steps(at, out_ref, *mine), *others)
                return
            for _ in scatter_steps(at, sums, *mine):
                for issue, _finish in others:
                    next(issue, None)
            last = end(at, more_refs, sums, out_ref, refs)
            together((), *others)
            last()

        return pl.pallas_call(
            kernel,
            out_shape=(jax.ShapeDtypeStruct((2, rows, width), BF16),) + (out_shapes if more else ()),
            in_specs=[ANY] + (in_specs if more else []),
            out_specs=(INVMEM,) + (out_specs if more else ()),
            scratch_shapes=own + (extra_scratch if more else []),
            compiler_params=params(cid + (0 if more else 20), 60),
            name=name,
        )(p, *more)

    return call


def feed_windows(grid):
    units = FF // grid.n
    window = 128 * max(-(-((c * units) % 128 + units) // 128) for c in range(grid.n))
    return units, window, lambda c: ((c * units) // 128) * 128


def attention_sums(grid, p, gate_codes, up_codes, cid):
    n, levels = grid.n, grid.planes // 2
    rows_d = gate_codes.shape[0]
    flat = rows_d % 16 == 0
    units, window, start = feed_windows(grid)
    ss = share_sems(grid, 2)

    def tasks(at, ins, outs, refs):
        def source(ref):
            return lambda to: ref.at[:, pl.ds(pl.multiple_of(start(to), 128), window)]

        def view(ref):
            return lambda j: ref.at[pl.ds(j * rows_d, rows_d)] if flat else ref.at[j]

        return [share_task(at, [source(r) for r in ins], [view(r) for r in outs], *refs.take(len(ss)))]

    shape = (n * rows_d, window) if flat else (n, rows_d, window)
    call = scatter_kernel(
        grid,
        levels,
        cid,
        "attention_sums",
        (tasks, [INVMEM, INVMEM], (jax.ShapeDtypeStruct(shape, BF16),) * 2, (ANY, ANY), ss),
    )
    return in_parts(grid, levels, call, p, (gate_codes, up_codes))


def feed_sums(grid, p, cid):
    return in_parts(grid, grid.planes, scatter_kernel(grid, grid.planes, cid, "feed_sums"), p, None)[0]


def feed_back_sums(grid, p, pair_grad, cid):
    rs = return_scratch(grid, pair_grad.shape[1:])

    def tasks(at, ins, outs, refs):
        return [return_task(at, ins[0], outs[0], *refs.take(len(rs)))]

    call = scatter_kernel(
        grid,
        grid.planes,
        cid,
        "feed_back_sums",
        (tasks, [ANY], (jax.ShapeDtypeStruct(pair_grad.shape, BF16),), (ANY,), rs),
    )
    return in_parts(grid, grid.planes, call, p, (pair_grad,))


def attention_back_sums(grid, p, qkv_grad, out_grad, down_grad, gains, merged, cid):
    n, levels = grid.n, grid.planes // 2
    rs, hs = return_scratch(grid, qkv_grad.shape[1:]), head_return_scratch(grid, out_grad.shape[1:])
    ps = [pltpu.VMEM(down_grad.shape, BF16), dma(2)]
    every = pltpu.VMEM((n,) + gains.shape, F32)
    gs = [pltpu.VMEM(gains.shape, F32), pltpu.VMEM(gains.shape, F32), every, dma(2)] + share_sems(grid, 1)
    us = assemble_scratch(grid) if merged else []
    rows, width = p.shape[2:]
    tail = [pltpu.VMEM((2, rows, width), BF16), dma(2)] if merged else []
    inputs = [qkv_grad, out_grad, down_grad, gains] + list(merged)
    in_specs = [ANY, ANY, INVMEM, INVMEM] + ([ANY] + [INVMEM] * 3 if merged else [])
    shapes = (
        jax.ShapeDtypeStruct(qkv_grad.shape, BF16),
        jax.ShapeDtypeStruct(out_grad.shape, BF16),
        jax.ShapeDtypeStruct(down_grad.shape, BF16),
        jax.ShapeDtypeStruct(gains.shape, F32),
    ) + (jax.ShapeDtypeStruct((D // n, FF), BF16),) * (2 if merged else 0)
    out_specs = (ANY, ANY, INVMEM, INVMEM) + ((ANY, ANY) if merged else ())
    sums = [pltpu.VMEM((2, rows, width), BF16)] if merged else []
    scratch = sums + rs + hs + ps + gs + us + tail

    def tasks(at, ins, outs, refs):
        made = [
            return_task(at, ins[0], outs[0], *refs.take(len(rs))),
            head_return_task(at, ins[1], outs[1], *refs.take(len(hs))),
            pair_task(at, ins[2], outs[2], *refs.take(2)),
            gains_task(at, ins[3], outs[3], *refs.take(len(gs))),
        ]
        if merged:
            made.insert(0, assemble_task(grid, ins[4], outs[4:6], *refs.take(len(us))))
        return made

    def end(at, ins, sums, out_ref, refs):
        kept, sems = refs.take(2)
        grad_ref, tokens_ref, gain_ref = ins[5:8]

        def one(u, r):
            dy, v = sums[u, r].astype(F32), tokens_ref[u, r].astype(F32)
            kept[u, r] = (grad_ref[u, r] + norm_back(v, inverse_rms(v), dy * gain_ref[0:1])).astype(BF16)

        each_rows(2, rows, one)
        issue, finish = swap_task(at, kept.at[1 - at.member], out_ref, sems)
        run(issue)
        out_ref[at.member] = kept[at.member]
        return finish

    call = scatter_kernel(
        grid,
        levels,
        cid,
        "attention_back_sums",
        (tasks, in_specs, shapes, out_specs, scratch),
        end if merged else None,
    )
    return in_parts(grid, levels, call, p, inputs)


SCALE = HEAD ** (-0.5)


def rotated(u, cosine, sine):
    half = u.shape[1] // 2
    first, second = u[:, :half], u[:, half:]
    return jnp.concatenate([first * cosine - second * sine, second * cosine + first * sine], axis=1)


def scores(q, k, start, first):
    bent = jnp.tanh(dot_t(q, k) * (SCALE / cap_limit))
    key = lax.broadcasted_iota(jnp.int32, bent.shape, 1)
    query = first + lax.broadcasted_iota(jnp.int32, bent.shape, 0)
    return jnp.where((key <= query) & (key >= start), jnp.exp(cap_limit * bent), 0.0), bent


def scale_rows(core, member, codes, column_scale, into, rows):
    step = member_step(core, 2, member)
    offset = jnp.where(step > 1.0, 0.5 * step, 0.0)

    def one(i, carry):
        r = pl.ds(pl.multiple_of(i * 16, 16), 16)
        level = jnp.floor(codes[r].astype(F32) * (1.0 / step)) * step + offset
        into[r] = (level * column_scale).astype(BF16)
        return carry

    lax.fori_loop(0, rows // 16, one, 0)


def attention_body(w, o, x_rows, put, cos_ref, sin_ref, start_ref, q_ref, k_ref, v_ref, a_ref, t_ref, block=256):
    length = q_ref.shape[0]
    for i in range(length // block):
        r = pl.ds(i * block, block)
        lin = dot(x_rows(i), w[...])
        q_ref[r] = rotated(lin[:, :HEAD], cos_ref[r], sin_ref[r]).astype(BF16)
        k_ref[r] = rotated(lin[:, HEAD : 2 * HEAD], cos_ref[r], sin_ref[r]).astype(BF16)
        v_ref[r] = lin[:, 2 * HEAD :].astype(BF16)
    for i in range(length // block):
        r, keys = pl.ds(i * block, block), pl.ds(0, (i + 1) * block)
        e, _ = scores(q_ref[r], k_ref[keys], start_ref[r], i * block)
        total = jnp.sum(e, axis=1, keepdims=True)
        attended = (dot(e.astype(BF16), v_ref[keys]) / total).astype(BF16)
        a_ref[r] = attended
        t_ref[r] = total
        put(i, dot(attended, o[...]).astype(BF16))


def attention_backward(seen, grad, w, o, q, k, v, attended, totals, vectors, cosine, sine, start):
    length = seen.shape[0]
    block, tile = 256, 256

    def kernel(
        x_ref, g_ref, w_ref, o_ref, q_ref, k_ref, v_ref, a_ref, t_ref, vec_ref, cos_ref, sin_ref, start_ref,
        part_ref, wg_ref, og_ref, gain_ref, xs, gs, dk, dv, low, sems,
    ):
        load_g = pltpu.make_async_copy(g_ref, gs, sems.at[0])
        load_x = pltpu.make_async_copy(x_ref, xs, sems.at[1])
        load_g.start()
        load_x.start()
        dk[...] = jnp.zeros_like(dk)
        dv[...] = jnp.zeros_like(dv)
        load_g.wait()
        for i in range(length // block):
            r, keys = pl.ds(i * block, block), pl.ds(0, (i + 1) * block)
            grad_attended = dot_t(gs[r], o_ref[...])
            total = t_ref[r]
            grad_sums = (grad_attended / total).astype(BF16)
            offset = jnp.sum(grad_attended * a_ref[r].astype(F32), axis=1, keepdims=True) / total
            e, bent = scores(q_ref[r], k_ref[keys], start_ref[r], i * block)
            grad_e = dot_t(grad_sums, v_ref[keys]) - offset
            grad_s = (e * grad_e * (1.0 - bent * bent)).astype(BF16)
            dv[keys] += t_dot(e.astype(BF16), grad_sums)
            dk[keys] += t_dot(grad_s, q_ref[r])
            low[r, :HEAD] = rotated(dot(grad_s, k_ref[keys]) * SCALE, cos_ref[r], -sin_ref[r]).astype(BF16)
        for i in range(length // block):
            r = pl.ds(i * block, block)
            low[r, HEAD : 2 * HEAD] = rotated(dk[r] * SCALE, cos_ref[r], -sin_ref[r]).astype(BF16)
            low[r, 2 * HEAD :] = dv[r].astype(BF16)
        load_x.wait()
        gain_ref[...] = jnp.zeros_like(gain_ref)

        def parts(i, carry):
            r = pl.ds(pl.multiple_of(i * block, block), block)
            term = dot_t(low[r], w_ref[...])
            part_ref[r] = term.astype(BF16)
            gain_ref[...] += jnp.sum(term * xs[r].astype(F32), axis=0, keepdims=True)
            return carry

        lax.fori_loop(0, length // block, parts, 0)
        gain_ref[...] = gain_ref[...] / vec_ref[0:1]

        def grads(j, carry):
            cols = pl.ds(pl.multiple_of(j * tile, tile), tile)
            wg_ref[cols] = t_dot(xs[:, cols], low[...]).astype(BF16)
            og_ref[:, cols] = t_dot(a_ref[...], gs[:, cols]).astype(BF16)
            return carry

        lax.fori_loop(0, D // tile, grads, 0)

    return pl.pallas_call(
        kernel,
        out_shape=(
            jax.ShapeDtypeStruct((length, D), BF16),
            jax.ShapeDtypeStruct((D, 3 * HEAD), BF16),
            jax.ShapeDtypeStruct((HEAD, D), BF16),
            jax.ShapeDtypeStruct((1, D), F32),
        ),
        in_specs=[ANY, ANY] + [INVMEM] * 11,
        out_specs=(INVMEM,) * 4,
        scratch_shapes=[
            pltpu.VMEM(seen.shape, BF16),
            pltpu.VMEM(seen.shape, BF16),
            pltpu.VMEM((length, HEAD), F32),
            pltpu.VMEM((length, HEAD), F32),
            pltpu.VMEM((length, 3 * HEAD), BF16),
            dma(2),
        ],
        compiler_params=pltpu.CompilerParams(vmem_limit_bytes=60 * 2**20),
        name="attention_backward",
    )(seen, grad, w, o, q, k, v, attended, totals, vectors, cosine, sine, start)


def inverse_rms(v):
    return lax.rsqrt(jnp.mean(v * v, axis=-1, keepdims=True) + 1e-06)


def norm_back(v, r, weighted):
    return r * weighted - v * (r * r * r * jnp.mean(weighted * v, axis=-1, keepdims=True))


def each_rows(group, rows, step):
    def one(i, carry):
        step(i // (rows // 16), pl.ds(pl.multiple_of((i % (rows // 16)) * 16, 16), 16))
        return carry

    lax.fori_loop(0, group * (rows // 16), one, 0)


def fits(grid, rows):
    return (D // grid.n) % 16 == 0 and scatter_parts(grid, grid.planes, rows, D) == 1


def forward_kernel(
    grid, seen, qkv_codes, out_codes, qkv_scale, cosine, sine, begins, tokens, cotangent, gate_codes, up_codes, down_codes,
    pair_scale, vectors, cid,
):
    n, levels = grid.n, grid.planes
    group, rows, _ = tokens.shape
    rows_d = gate_codes.shape[0]
    units, window, start = feed_windows(grid)
    size = feed_blocks(grid)
    sc = scatter_scratch(grid, levels // 2, rows, D)
    ss = share_sems(grid, 2)
    ws, gs = FeedWeights.scratch(group, units, window), level_sems(grid, levels)

    length = seen.shape[0]
    block = 256
    here = block // rows

    def kernel(
        x_ref, codes_ref, rows_ref, scale_ref, cos_ref, sin_ref, start_ref, tokens_ref, cot_ref, gate_ref, up_ref, down_ref,
        ps_ref, vec_ref,
        w_ref, o_ref, q_ref, k_ref, v_ref, a_ref, t_ref,
        kept_cot_ref, raw_ref, mixed_ref, all_ref, pair_ref, part_ref, wp_ref, wd_ref, *scratch,
    ):
        refs = Split(scratch)
        half_at, at = Place(grid, levels // 2), Place(grid, levels)
        mine = refs.take(len(sc))
        share_refs = refs.take(len(ss))
        weights = FeedWeights(at, group, units, None, None, down_ref, (wp_ref, wd_ref), refs.take(len(ws)))
        gather_refs = refs.take(len(gs))
        x, xs, head_sems, cot_sems = refs.take(4)
        loads, stores, compute = forward_chunks(weights, all_ref, pair_ref, part_ref, *refs.take(4))
        w = weights.pair.at[0, :, pl.ds(0, 3 * HEAD)]
        w_codes = weights.pair.at[1, :, pl.ds(0, 3 * HEAD)]
        o = weights.down.at[0, pl.ds(0, HEAD)]
        acc = mine[0]
        load_w = pltpu.make_async_copy(codes_ref, w_codes, head_sems.at[0])
        load_x = pltpu.make_async_copy(x_ref, xs, head_sems.at[1])
        load_w.start()
        load_x.start()
        weights.sources = (None, None, down_ref)
        weights.load()
        at.greet_all()

        def source(ref):
            return lambda to: ref.at[:, pl.ds(pl.multiple_of(start(to), 128), window)]

        def view(k):
            return lambda j: weights.codes.at[
                pl.ds(pl.multiple_of(j * rows_d, 16), rows_d), pl.ds(k * window, window)
            ]

        issue, finish = share_task(at, [source(gate_ref), source(up_ref)], [view(0), view(1)], *share_refs)
        for _ in range(EARLY):
            next(issue, None)
        scale_rows(at.b, at.member, rows_ref, vec_ref[4:5], o, HEAD)
        load_w.wait()
        scale_rows(at.b, at.member, w_codes, scale_ref[...], w, D)
        keep_w = pltpu.make_async_copy(w, w_ref, head_sems.at[2])
        keep_o = pltpu.make_async_copy(o, o_ref, head_sems.at[3])
        keep_w.start()
        keep_o.start()
        load_x.wait()

        def put(i, value):
            first = i * here
            half = grid.n // 2
            acc[first // half, pl.ds(first % half, here)] = value.reshape(here, rows, D)

        attention_body(
            w,
            o,
            lambda i: xs[pl.ds(i * block, block)],
            put,
            cos_ref,
            sin_ref,
            start_ref,
            q_ref,
            k_ref,
            v_ref,
            a_ref,
            t_ref,
        )
        for _ in scatter_steps(half_at, raw_ref, *mine):
            next(issue, None)

        def norms(u, r):
            raw = raw_ref[u, r].astype(F32)
            mixed = tokens_ref[u, r].astype(F32) + raw * inverse_rms(raw) * vec_ref[1:2]
            mixed_ref[u, r] = mixed
            x[u, r] = (mixed * inverse_rms(mixed) * vec_ref[2:3]).astype(BF16)

        each_rows(group, rows, norms)
        moving = LevelGather(False, at, x, all_ref, *gather_refs)
        moving.begin()
        run(issue)
        give_cot, take_cot = swap_task(at, cot_ref.at[1 - at.member], kept_cot_ref, cot_sems)
        run(give_cot)
        kept_cot_ref[at.member] = cot_ref[at.member]

        def first():
            finish()
            keep_w.wait()
            keep_o.wait()
            weights.make(ps_ref, vec_ref.at[5:6])

        moving.run(lambda zj, fresh: each_chunk(grid, zj, fresh, loads, stores, compute), first)
        for copy in stores(0):
            copy.wait()
        weights.finish()
        take_cot()

    def blocks(width):
        return jax.ShapeDtypeStruct((group, n, rows, width), BF16)

    head = jax.ShapeDtypeStruct((length, HEAD), BF16)
    return pl.pallas_call(
        kernel,
        out_shape=(
            jax.ShapeDtypeStruct((D, 3 * HEAD), BF16),
            jax.ShapeDtypeStruct((HEAD, D), BF16),
            head,
            head,
            head,
            head,
            jax.ShapeDtypeStruct((length, 1), F32),
            jax.ShapeDtypeStruct(tokens.shape, BF16),
            jax.ShapeDtypeStruct(tokens.shape, BF16),
            jax.ShapeDtypeStruct(tokens.shape, F32),
            blocks(D),
            blocks(2 * window),
            blocks(D),
            jax.ShapeDtypeStruct((group, D, 2 * window), BF16),
            jax.ShapeDtypeStruct((group, window, D), BF16),
        ),
        in_specs=[ANY, ANY] + [INVMEM] * 7 + [ANY] * 3 + [INVMEM] * 2,
        out_specs=(ANY, ANY) + (INVMEM,) * 8 + (ANY,) * 5,
        scratch_shapes=sc
        + ss
        + ws
        + gs
        + [pltpu.VMEM(tokens.shape, BF16), pltpu.VMEM(seen.shape, BF16), dma(4), dma(2)]
        + chunk_buffers(size, rows, D, 2 * window, D)
        + [dma(3)],
        compiler_params=params(cid, 62),
        name="forward",
    )(
        seen, qkv_codes, out_codes, qkv_scale, cosine, sine, begins, tokens, cotangent, gate_codes, up_codes, down_codes,
        pair_scale, vectors,
    )


def turn_kernel(grid, p, mixed, cotangent, pair, pair_matrices, down_matrices, vectors, cid):
    n, levels = grid.n, grid.planes
    group, rows, _ = mixed.shape
    units, window, _ = feed_windows(grid)
    size = feed_blocks(grid)
    sc, gs = scatter_scratch(grid, levels, rows, D), level_sems(grid, levels)

    def kernel(
        p_ref, mixed_ref, cot_ref, pair_ref, wp_ref, wd_ref, vec_ref,
        out_ref, gain_ref, all_ref, part_ref, dgu_ref, hid_ref, *scratch,
    ):
        refs = Split(scratch)
        at = Place(grid, levels)
        mine, gather_refs = refs.take(len(sc)), refs.take(len(gs))
        raw, x, kept_out, wp, wd, fetch_sems, swap_sems = refs.take(7)
        load = pltpu.make_async_copy(p_ref, mine[0], mine[4].at[0])
        load.start()
        fetch = [
            pltpu.make_async_copy(wp_ref, wp, fetch_sems.at[0]),
            pltpu.make_async_copy(wd_ref, wd, fetch_sems.at[1]),
        ]
        loads, stores, compute = backward_chunks(
            wp, wd, all_ref, pair_ref, part_ref, dgu_ref, hid_ref, *refs.take(6)
        )
        at.greet_near(True)
        load.wait()
        for copy in fetch:
            copy.start()
        run(scatter_steps(at, raw, *mine))
        gain_ref[...] = jnp.zeros_like(gain_ref)

        def norms(u, r):
            v, dy = raw[u, r].astype(F32), cot_ref[u, r].astype(F32)
            inverse, gain = inverse_rms(v), vec_ref[3:4]
            kept_out[u, r] = (mixed_ref[u, r] + v * inverse * gain).astype(BF16)
            x[u, r] = norm_back(v, inverse, dy * gain).astype(BF16)
            gain_ref[...] += jnp.sum(dy * v * inverse, axis=0, keepdims=True)

        each_rows(group, rows, norms)
        moving = LevelGather(True, at, x, all_ref, *gather_refs)
        moving.begin()
        give_out, take_out = swap_task(at, kept_out.at[1 - at.member], out_ref, swap_sems)
        run(give_out)
        out_ref[at.member] = kept_out[at.member]
        for copy in fetch:
            copy.wait()

        moving.run(lambda zj, fresh: each_chunk(grid, zj, fresh, loads, stores, compute))
        take_out()
        for copy in stores(0):
            copy.wait()

    def blocks(width):
        return jax.ShapeDtypeStruct((group, n, rows, width), BF16)

    return pl.pallas_call(
        kernel,
        out_shape=(
            jax.ShapeDtypeStruct(mixed.shape, BF16),
            jax.ShapeDtypeStruct((1, D), F32),
            blocks(D),
            blocks(D),
            blocks(2 * window),
            blocks(window),
        ),
        in_specs=[ANY, INVMEM, INVMEM, ANY, ANY, ANY, INVMEM],
        out_specs=(INVMEM, INVMEM) + (ANY,) * 4,
        scratch_shapes=sc
        + gs
        + [
            pltpu.VMEM(mixed.shape, BF16),
            pltpu.VMEM(mixed.shape, BF16),
            pltpu.VMEM(mixed.shape, BF16),
            pltpu.VMEM((group, D, 2 * window), BF16),
            pltpu.VMEM((group, window, D), BF16),
            dma(2),
            dma(2),
        ]
        + chunk_buffers(size, rows, D, 2 * window, D, 2 * window, window)
        + [dma(5)],
        compiler_params=params(cid, 62),
        name="turn",
    )(p, mixed, cotangent, pair, pair_matrices, down_matrices, vectors)


def back_kernel(grid, p, fed, down_low, pair_low, hidden, mixed, raw, cotangent, vectors, cid):
    n, levels = grid.n, grid.planes
    group, rows, _ = mixed.shape
    units, window, _ = feed_windows(grid)
    size = feed_blocks(grid)
    chunks = n // size
    count = group * size * rows
    rows_d = D // n
    half = n // 2
    tile = 256
    sc, gs = scatter_scratch(grid, levels, rows, D), gather_sems(grid, levels // 2)
    rs = return_scratch(grid, (rows_d, 2 * window))

    def kernel(
        p_ref, fed_ref, low_ref, dgu_ref, hid_ref, mixed_ref, raw_ref, cot_ref, vec_ref,
        grad_ref, feed_ref, post_ref, all_ref, got_ref, down_ref, *scratch,
    ):
        refs = Split(scratch)
        half_at, at = Place(grid, levels // 2), Place(grid, levels)
        mine, gather_refs, return_refs = refs.take(len(sc)), refs.take(len(gs)), refs.take(len(rs))
        raw2, x, xs, ys, dgu, hid, pair_sum, down_sum, given, down_out, sems = refs.take(11)
        load = pltpu.make_async_copy(p_ref, mine[0], mine[4].at[0])
        load.start()

        def loads(i):
            at_blocks = pl.ds(i * size, size)
            return [
                pltpu.make_async_copy(fed_ref.at[:, at_blocks], xs, sems.at[0]),
                pltpu.make_async_copy(low_ref.at[:, at_blocks], ys, sems.at[1]),
                pltpu.make_async_copy(dgu_ref.at[:, at_blocks], dgu, sems.at[2]),
                pltpu.make_async_copy(hid_ref.at[:, at_blocks], hid, sems.at[3]),
            ]

        for copy in loads(0):
            copy.start()
        at.greet_all()
        load.wait()

        def sums(i):
            def one(j, carry):
                cols = pl.ds(pl.multiple_of(j * tile, tile), tile)
                pair_term = t_dot(xs[:, :, :, cols].reshape(count, tile), dgu[...].reshape(count, 2 * window))
                down_term = t_dot(hid[...].reshape(count, window), ys[:, :, :, cols].reshape(count, tile))
                if i == 0:
                    pair_sum[cols] = pair_term
                    down_sum[:, cols] = down_term
                else:
                    pair_sum[cols] = pair_sum[cols] + pair_term
                    down_sum[:, cols] = down_sum[:, cols] + down_term
                return carry

            for copy in loads(i):
                copy.wait()
            lax.fori_loop(0, D // tile, one, 0)
            if i + 1 < chunks:
                for copy in loads(i + 1):
                    copy.start()

        to, _ = pairwise(n, at.c, at.b)
        other_to, _ = pairwise(n, at.c, 1 - at.b)
        give_down = pltpu.make_async_copy(down_out, down_ref, sems.at[4])

        def lowered(i):
            def one(r, carry):
                here = pl.ds(pl.multiple_of(r * 16, 16), 16)
                mine_at = pl.ds(pl.multiple_of(to(i) * rows_d + r * 16, 16), 16)
                other_at = pl.ds(pl.multiple_of(other_to(i) * rows_d + r * 16, 16), 16)
                return_refs[0][i, here] = pair_sum[mine_at].astype(BF16)
                given[i, here] = pair_sum[other_at].astype(BF16)
                return carry

            lax.fori_loop(0, rows_d // 16, one, 0)

        def lowered_down():
            def one(r, carry):
                here = pl.ds(pl.multiple_of(r * 16, 16), 16)
                down_out[here] = down_sum[here].astype(BF16)
                return carry

            lax.fori_loop(0, window // 16, one, 0)
            give_down.start()

        def prepare():
            for i in range(chunks):
                sums(i)
                if i % 2 == 1:
                    yield
            lowered_down()

        issue, finish = return_task(at, None, got_ref, *return_refs, given=given, fill=lowered, prepare=prepare)

        def main():
            yield from scatter_steps(at, raw2, *mine)
            feed_ref[...] = jnp.zeros_like(feed_ref)
            post_ref[...] = jnp.zeros_like(post_ref)

            def norms(u, r):
                dy, v = raw2[u, r].astype(F32), mixed_ref[u, r]
                inverse = inverse_rms(v)
                grad = cot_ref[u, r].astype(F32) + norm_back(v, inverse, dy * vec_ref[2:3])
                feed_ref[...] += jnp.sum(dy * v * inverse, axis=0, keepdims=True)
                grad_ref[u, r] = grad
                w = raw_ref[u, r].astype(F32)
                inverse = inverse_rms(w)
                x[u, r] = norm_back(w, inverse, grad * vec_ref[1:2]).astype(BF16)
                post_ref[...] += jnp.sum(grad * w * inverse, axis=0, keepdims=True)

            each_rows(group, rows, norms)
            yield from gather_steps(half_at, x, all_ref, *gather_refs)

        together(main(), (issue, finish))
        give_down.wait()

    return pl.pallas_call(
        kernel,
        out_shape=(
            jax.ShapeDtypeStruct(mixed.shape, F32),
            jax.ShapeDtypeStruct((1, D), F32),
            jax.ShapeDtypeStruct((1, D), F32),
            jax.ShapeDtypeStruct((2, half, rows, D), BF16),
            jax.ShapeDtypeStruct((n, rows_d, 2 * window), BF16),
            jax.ShapeDtypeStruct((window, D), BF16),
        ),
        in_specs=[ANY] * 5 + [INVMEM] * 4,
        out_specs=(INVMEM,) * 3 + (ANY,) * 3,
        scratch_shapes=sc
        + gs
        + rs
        + [
            pltpu.VMEM(mixed.shape, BF16),
            pltpu.VMEM(mixed.shape, BF16),
            pltpu.VMEM((group, size, rows, D), BF16),
            pltpu.VMEM((group, size, rows, D), BF16),
            pltpu.VMEM((group, size, rows, 2 * window), BF16),
            pltpu.VMEM((group, size, rows, window), BF16),
            pltpu.VMEM((D, 2 * window), F32),
            pltpu.VMEM((window, D), F32),
            pltpu.VMEM((half, rows_d, 2 * window), BF16),
            pltpu.VMEM((window, D), BF16),
            dma(5),
        ],
        compiler_params=params(cid, 63),
        name="back",
    )(p, fed, down_low, pair_low, hidden, mixed, raw, cotangent, vectors)


def assemble_task(grid, got_ref, targets, wide, high, load_sem, stores):
    n = grid.n
    units, window, _ = feed_windows(grid)
    inner = n // HEADS
    whole = inner * units
    starts = [i * units // 128 * 128 for i in range(inner)]
    load = pltpu.make_async_copy(got_ref, wide, load_sem.at[0])

    def store(k):
        return pltpu.make_async_copy(high.at[k], targets[k], stores.at[k])

    def put(g, k):
        for t in range(0, whole, 128):
            total = 0.0
            for i in range(inner):
                if 0 <= t - starts[i] < window:
                    total = total + wide[g * inner + i, :, pl.ds(k * window + t - starts[i], 128)].astype(F32)
            high[k, :, pl.ds(pl.multiple_of(g * whole + t, 128), 128)] = total.astype(BF16)

    def issue():
        load.start()
        yield
        yield
        load.wait()
        for k in range(2):

            def one(g, carry):
                put(g, k)
                return carry

            lax.fori_loop(0, n // inner, one, 0)
            store(k).start()
            yield

    def finish():
        for k in range(2):
            store(k).wait()

    return issue(), finish


def assemble_scratch(grid):
    _, window, _ = feed_windows(grid)
    rows_d = D // grid.n
    return [pltpu.VMEM((grid.n, rows_d, 2 * window), BF16), pltpu.VMEM((2, rows_d, FF), BF16), dma(1), dma(2)]


def gains_task(at, x_ref, out_ref, total, other, every, sems, *share_refs):
    copy = at.sibling(x_ref, other, sems.at[0], sems.at[1])
    later, end = share_task(at, [lambda to: total], [lambda j: every.at[j]], *share_refs)

    def issue():
        copy.start()
        yield
        copy.wait()
        total[...] = x_ref[...] + other[...]
        yield from later

    def finish():
        end()
        out_ref[...] = jnp.sum(every[...], axis=0)

    return issue(), finish


def normed(value, gain):
    return value * lax.rsqrt(jnp.mean(value * value, axis=-1, keepdims=True) + 1e-06) * gain


def angles(places, head):
    freqs = 10000.0 ** (-(jnp.arange(head // 2, dtype=F32) * 2.0 / head))
    return places.astype(F32)[..., None] * freqs


def rotate(values, cosine, sine):
    half = values.shape[-1] // 2
    first = values[..., :half]
    second = values[..., half:]
    return jnp.concatenate([first * cosine - second * sine, second * cosine + first * sine], axis=-1)


def width_step(number):
    remainder = number % 3
    return jnp.where(remainder == 0, 1.0, jnp.where(remainder == 1, 16.0, 64.0)).astype(F32)


def dequantized(codes, column_scale, step):
    offset = jnp.where(step > 1.0, 0.5 * step, 0.0)
    level = jnp.floor(codes.astype(F32) / step) * step + offset
    return (level * column_scale[None, :]).astype(BF16)


def dot(left, right):
    return jnp.dot(left, right, preferred_element_type=F32)


def dot_t(left, right):
    return lax.dot_general(left, right, (((1,), (1,)), ((), ())), preferred_element_type=F32)


def t_dot(left, right):
    return lax.dot_general(left, right, (((0,), (0,)), ((), ())), preferred_element_type=F32)


def unwindowed(grid, got):
    n, rows, window = got.shape
    units = FF // n
    inner = n // HEADS
    whole = inner * units
    got = got.astype(F32).reshape(n // inner, inner, rows, window)
    total = 0.0
    for i in range(inner):
        start = i * units // 128 * 128
        total = total + jnp.pad(got[:, i], ((0, 0), (0, 0), (start, whole - start - window)))
    return jnp.transpose(total, (1, 0, 2)).reshape(rows, FF)


def on_device(
    grid,
    tokens,
    segments,
    positions,
    cotangent,
    query_codes,
    key_codes,
    value_codes,
    output_codes,
    gate_codes,
    up_codes,
    down_codes,
    query_scale,
    key_scale,
    value_scale,
    output_scale,
    gate_scale,
    up_scale,
    down_scale,
    attention_gain,
    attention_post_gain,
    feed_gain,
    feed_post_gain,
):
    n = grid.n
    group, block, _ = tokens.shape
    length = n * block
    pairs = HEADS // KV_HEADS
    scale = HEAD ** (-0.5)
    chip, core = lax.axis_index("seq"), lax.axis_index("batch")
    half = n // 2
    member = chip // half
    head = chip % HEADS
    kv_head = head // pairs
    parts = half // HEADS
    copies = n // HEADS
    asked = length // parts
    first_asked = ((chip % half) // HEADS) * asked
    steps = [width_step(core * group + m) for m in range(group)]
    step = width_step(core * group + member)
    rows_d = D // n
    units, window, _ = feed_windows(grid)

    vectors = jnp.stack(
        [attention_gain, attention_post_gain, feed_gain, feed_post_gain, output_scale, down_scale]
    )

    q_parts = jnp.transpose(query_codes.reshape(rows_d, HEADS, HEAD), (1, 0, 2))
    k_parts = jnp.repeat(jnp.transpose(key_codes.reshape(rows_d, KV_HEADS, HEAD), (1, 0, 2)), pairs, axis=0)
    v_parts = jnp.repeat(jnp.transpose(value_codes.reshape(rows_d, KV_HEADS, HEAD), (1, 0, 2)), pairs, axis=0)
    qkv_parts = jnp.concatenate([q_parts, k_parts, v_parts], axis=-1).astype(BF16)
    small = jnp.zeros((8, 128), jnp.int32).at[:group, :block].set(positions)
    tokens, seen, qkv_codes, out_codes, all_places, gate_low, up_low = open_kernel(
        grid,
        tokens,
        vectors,
        qkv_parts,
        output_codes.astype(BF16),
        small,
        gate_codes,
        up_codes,
        1,
    )
    seen = seen.reshape(length, D)

    qkv_scale = jnp.concatenate(
        [
            lax.dynamic_slice_in_dim(query_scale, head * HEAD, HEAD),
            lax.dynamic_slice_in_dim(key_scale, kv_head * HEAD, HEAD),
            lax.dynamic_slice_in_dim(value_scale, kv_head * HEAD, HEAD),
        ]
    )
    def swapped_back(kept):
        own, other = (lax.dynamic_index_in_dim(kept, u, 0, False) for u in (member, 1 - member))
        other = lax.ppermute(other, "seq", [(c, (c + half) % n) for c in range(n)])
        return jnp.where(member == 0, jnp.stack([own, other]), jnp.stack([other, own]))

    def spread(part):
        if parts > 1:
            part = lax.dynamic_update_slice_in_dim(jnp.zeros((length, D), BF16), part, first_asked, 0)
        return part.reshape(2, half, block, D)

    places_all = lax.dynamic_index_in_dim(all_places[:, :group, :block], member, 1, False).reshape(length)
    turn = angles(places_all, HEAD)
    cosine, sine = jnp.cos(turn), jnp.sin(turn)
    q_index = first_asked + jnp.arange(asked, dtype=jnp.int32)
    whole = fits(grid, block) and parts == 1
    pair_scale = jnp.concatenate(
        [lax.dynamic_slice_in_dim(s, chip * units // 128 * 128, window) for s in (gate_scale, up_scale)]
    )[None]
    if whole:
        start = (q_index - places_all)[:, None]
        (
            *kept_heads, cotangent, attention_raw, mixed, fed, gate_up, down_part, pair_matrices, down_matrices,
        ) = forward_kernel(
            grid,
            seen,
            qkv_codes.reshape(D, 3 * HEAD),
            out_codes.reshape(HEAD, D),
            qkv_scale[None],
            cosine,
            sine,
            start,
            tokens,
            cotangent,
            gate_low,
            up_low,
            down_codes,
            pair_scale,
            vectors,
            2,
        )
    else:
        qkv_matrix = dequantized(qkv_codes.reshape(D, 3 * HEAD), qkv_scale, step)
        out_matrix = dequantized(out_codes.reshape(HEAD, D), output_scale, step)
        if parts == 1:
            seen_asked, places_asked, cosine_q, sine_q = seen, places_all, cosine, sine
            projected = dot(seen, qkv_matrix)
            q_lin, kv_lin = projected[:, :HEAD], projected[:, HEAD:]
        else:
            seen_asked, places_asked, cosine_q, sine_q = [
                lax.dynamic_slice_in_dim(a, first_asked, asked) for a in (seen, places_all, cosine, sine)
            ]
            q_lin, kv_lin = dot(seen_asked, qkv_matrix[:, :HEAD]), dot(seen, qkv_matrix[:, HEAD:])
        queries = rotate(q_lin, cosine_q, sine_q).astype(BF16)
        keys = rotate(kv_lin[:, :HEAD], cosine, sine).astype(BF16)
        values = kv_lin[:, HEAD:].astype(BF16)
        key_index = jnp.arange(length, dtype=jnp.int32)
        allowed = (key_index[None, :] <= q_index[:, None]) & (key_index[None, :] >= (q_index - places_asked)[:, None])
        bent = jnp.tanh(dot_t(queries, keys) * scale / cap_limit)
        kernel = jnp.where(allowed, jnp.exp(cap_limit * bent), 0.0)
        totals = jnp.sum(kernel, axis=-1, keepdims=True)
        kernel_low = kernel.astype(BF16)
        attended = dot(kernel_low, values) / totals
        attended_low = attended.astype(BF16)

        out_part = spread(dot(attended_low, out_matrix).astype(BF16))
    first_column = chip * units // 128 * 128
    inset = chip * units - first_column
    if whole:
        output, grad_post_feed, down_low, second_part, pair_low, hidden = turn_kernel(
            grid, down_part, mixed, cotangent, gate_up, pair_matrices, down_matrices, vectors, 3
        )
        grad_mixed, grad_pre_feed, grad_post_attention, attention_low, pair_got, down_grad = back_kernel(
            grid,
            second_part,
            fed,
            down_low,
            pair_low,
            hidden,
            mixed,
            attention_raw,
            cotangent,
            vectors,
            4,
        )
    else:
        cotangent = swapped_back(cotangent)
        attention_raw, gate_got, up_got = attention_sums(grid, out_part, gate_low, up_low, 2)
        attention_raw = attention_raw.astype(F32)
        feed_weights = (
            gate_got.reshape(D, window),
            up_got.reshape(D, window),
            down_codes,
            pair_scale,
            down_scale[None],
        )
        mixed = tokens.astype(F32) + normed(attention_raw, attention_post_gain)
        second_normed = normed(mixed, feed_gain).astype(BF16)
        fed, gate_up, down_part, pair_matrices, down_matrices = feed_forward(grid, second_normed, *feed_weights, 3)
        down_raw = feed_sums(grid, down_part, 4).astype(F32)
        branch, pull_out = jax.vjp(normed, down_raw, feed_post_gain)
        output = swapped_back((mixed + branch).astype(BF16))
        upstream = cotangent.astype(F32)
        grad_down_raw, grad_post_feed = pull_out(upstream)
        down_low, second_part, pair_low, hidden = feed_backward(
            grid, grad_down_raw.astype(BF16), gate_up, pair_matrices, down_matrices, 9
        )
        count = group * length
        pair_grad = t_dot(fed.reshape(count, D), pair_low.reshape(count, 2 * window)).astype(BF16)
        down_grad = t_dot(hidden.reshape(count, window), down_low.reshape(count, D)).astype(BF16)
        grad_second, pair_got = feed_back_sums(grid, second_part, pair_grad.reshape(n, rows_d, 2 * window), 5)
        gate_grad, up_grad = (unwindowed(grid, pair_got[..., i * window : (i + 1) * window]) for i in range(2))
        _, pull_feed = jax.vjp(normed, mixed, feed_gain)
        grad_mixed_part, grad_pre_feed = pull_feed(grad_second.astype(F32))
        grad_mixed = upstream + grad_mixed_part
        _, pull_post = jax.vjp(normed, attention_raw, attention_post_gain)
        grad_attention, grad_post_attention = pull_post(grad_mixed)
        attention_low = gather(grid, grad_attention.astype(BF16), grid.planes // 2, 6)
    down_grad = lax.dynamic_slice(down_grad, (inset, 0), (units, D))

    attention_low = attention_low.reshape(length, D)
    if whole:
        first_part, qkv_grad, out_part, grad_pre_attention = attention_backward(
            seen, attention_low, *kept_heads, vectors, cosine, sine, start
        )
    else:
        if parts > 1:
            attention_low = lax.dynamic_slice_in_dim(attention_low, first_asked, asked)
        grad_attended = dot_t(attention_low, out_matrix)
        grad_sums = (grad_attended / totals).astype(BF16)
        offsets = jnp.sum(grad_attended * attended, axis=-1, keepdims=True) / totals
        grad_kernel = dot_t(grad_sums, values) - offsets
        grad_raw = (kernel * grad_kernel * (1.0 - bent * bent)).astype(BF16)
        grad_q = dot(grad_raw, keys) * scale
        grad_k = t_dot(grad_raw, queries) * scale
        grad_v = t_dot(kernel_low, grad_sums)
        q_low = rotate(grad_q, cosine_q, -sine_q).astype(BF16)
        kv_low = jnp.concatenate([rotate(grad_k, cosine, -sine), grad_v], axis=-1).astype(BF16)
        if parts == 1:
            qkv_low = jnp.concatenate([q_low, kv_low], axis=-1)
            first_part = dot_t(qkv_low, qkv_matrix)
            qkv_grad = t_dot(seen, qkv_low)
        else:
            first_part = dot_t(kv_low, qkv_matrix[:, HEAD:])
            q_back = dot_t(q_low, qkv_matrix[:, :HEAD])
            first_part = lax.dynamic_update_slice_in_dim(
                first_part, lax.dynamic_slice_in_dim(first_part, first_asked, asked) + q_back, first_asked, 0
            )
            qkv_grad = jnp.concatenate([t_dot(seen_asked, q_low), t_dot(seen, kv_low)], axis=-1)
        first_part = first_part.astype(BF16)
        grad_pre_attention = jnp.sum(first_part.astype(F32) * seen.astype(F32), axis=0) / attention_gain
        out_part = t_dot(attended_low, attention_low).astype(BF16)
    gains = jnp.stack(
        [g.reshape(D) for g in (grad_pre_attention, grad_post_attention, grad_pre_feed, grad_post_feed)]
    )
    out_part = out_part.reshape(copies, HEAD // copies, D)
    merged = (pair_got, grad_mixed, tokens, vectors) if whole else ()
    grad_in, qkv_got, out_got, down_grad, gains, *assembled = attention_back_sums(
        grid,
        first_part.reshape(2, half, block, D),
        qkv_grad.astype(BF16).reshape(n, rows_d, 3 * HEAD),
        out_part,
        down_grad,
        gains,
        merged,
        7,
    )
    if merged:
        gate_grad, up_grad = (a.astype(F32) for a in assembled)
    else:
        _, pull_in = jax.vjp(lambda value: normed(value, attention_gain), tokens.astype(F32))
        (grad_source_part,) = pull_in(grad_in.astype(F32))
        grad_in = swapped_back((grad_mixed + grad_source_part).astype(BF16))
    down_grad = down_grad.astype(F32)
    qkv_got = jnp.sum(qkv_got.astype(F32).reshape(copies, HEADS, rows_d, 3 * HEAD), axis=0)
    query_grad = jnp.transpose(qkv_got[..., :HEAD], (1, 0, 2)).reshape(rows_d, HEADS * HEAD)
    kv_grad = jnp.sum(qkv_got[..., HEAD:].reshape(KV_HEADS, pairs, rows_d, 2 * HEAD), axis=1)
    key_grad = jnp.transpose(kv_grad[..., :HEAD], (1, 0, 2)).reshape(rows_d, KV_HEADS * HEAD)
    value_grad = jnp.transpose(kv_grad[..., HEAD:], (1, 0, 2)).reshape(rows_d, KV_HEADS * HEAD)
    out_grad = jnp.sum(out_got.astype(F32), axis=0)
    return (
        output,
        grad_in,
        query_grad,
        key_grad,
        value_grad,
        out_grad,
        gate_grad,
        up_grad,
        down_grad,
    ) + tuple(gains[i] for i in range(4))


def solution(mesh):
    rows = P("seq", None)
    return jax.shard_map(
        functools.partial(on_device, Grid(mesh.shape["seq"])),
        mesh=mesh,
        in_specs=(P("batch", "seq", None), P("batch", "seq"), P("batch", "seq"), P("batch", "seq", None))
        + (rows,) * 7
        + (P(),) * 11,
        out_specs=(P("batch", "seq", None),) * 2 + (rows,) * 7 + (P(),) * 4,
        check_vma=False,
    )
```

```python
import functools

import jax
import jax.numpy as jnp
from jax import lax
from jax.experimental import pallas as pl
from jax.experimental.pallas import tpu as pltpu
from jax.sharding import PartitionSpec as P

D = 2304
HEADS = 8
KV_HEADS = 4
HEAD = 256
FF = 9216
MESH = pl.DeviceIdType.MESH
F32 = jnp.float32
BF16 = jnp.bfloat16


cap_limit = 50.0


class Grid:
    def __init__(self, n):
        self.n = n
        self.planes = 4 if n % 8 == 0 else 2
        self.plane = n // self.planes
        wide = 1
        while wide * wide < self.plane:
            wide *= 2
        self.wide = wide

    def snake(self, p):
        y, x = p // self.wide, p % self.wide
        return y * self.wide + x + (y % 2) * (self.wide - 1 - 2 * x)


def remote(src, dst, send, recv, chip, core):
    return pltpu.make_async_remote_copy(
        src_ref=src, dst_ref=dst, send_sem=send, recv_sem=recv, device_id=(chip, core), device_id_type=MESH
    )


def greet(barrier, chip, core):
    pl.semaphore_signal(barrier, inc=1, device_id=(chip, core), device_id_type=MESH)


class Place:
    def __init__(self, grid, levels):
        self.grid, self.levels = grid, levels
        self.n, self.pn = grid.n, grid.plane
        self.steps = self.pn // 2
        self.c, self.b = lax.axis_index("seq"), lax.axis_index("batch")
        self.z, p = self.c // self.pn, self.c % self.pn
        self.q = grid.snake(p)
        self.zi = self.z % levels
        self.right = self.z * self.pn + grid.snake((self.q + 1) % self.pn)
        self.left = self.z * self.pn + grid.snake((self.q + self.pn - 1) % self.pn)
        self.member = self.c // (self.n // 2)
        self.partner = (self.c + self.n // 2) % self.n

    def slot(self, zj, qj):
        return zj * self.pn + self.grid.snake((qj + 2 * self.pn) % self.pn)

    def sibling(self, src, dst, send, recv):
        return remote(src, dst, send, recv, self.c, 1 - self.b)

    def greet_near(self, halves):
        barrier = pltpu.get_barrier_semaphore()
        zi, levels = self.zi, self.levels
        greet(barrier, self.right, self.b)
        greet(barrier, self.left, self.b)
        pl.when(zi > 0)(lambda: greet(barrier, self.c - self.pn, self.b))
        pl.when(zi < levels - 1)(lambda: greet(barrier, self.c + self.pn, self.b))
        if halves:
            greet(barrier, self.partner, self.b)
        count = 2 + jnp.where(zi > 0, 1, 0) + jnp.where(zi < levels - 1, 1, 0) + (1 if halves else 0)
        pl.semaphore_wait(barrier, count)

    def greet_all(self):
        barrier = pltpu.get_barrier_semaphore()
        greet(barrier, self.c, 1 - self.b)

        def one(off, carry):
            greet(barrier, (self.c + off) % self.n, self.b)
            return carry

        lax.fori_loop(1, self.n, one, 0)
        pl.semaphore_wait(barrier, self.n)


def present(zi, sign, d, levels):
    if d == 0:
        return None
    return (zi - d >= 0) if sign < 0 else (zi + d < levels)


def guarded(condition, action):
    if condition is None:
        action()
    else:
        pl.when(condition)(action)


def dma(*shape):
    return pltpu.SemaphoreType.DMA(shape)


ANY = pl.BlockSpec(memory_space=pl.ANY)
INVMEM = pl.BlockSpec(memory_space=pltpu.VMEM)


def params(cid, mib=None):
    if mib is None:
        return pltpu.CompilerParams(collective_id=cid, has_side_effects=True)
    return pltpu.CompilerParams(collective_id=cid, has_side_effects=True, vmem_limit_bytes=mib * 2**20)


def gather_sems(grid, levels, passes=1):
    steps = grid.plane // 2
    return [
        dma(passes, 2, levels),
        dma(passes, 2, levels),
        dma(passes, 2, steps, levels),
        dma(passes, 2, steps, levels),
        dma(3),
    ]


def gather_steps(at, x_ref, out_ref, zs, zr, rs, rr, ls, passes=((0, 2),), ready=None):
    levels, steps, zi, q, pn, b = at.levels, at.steps, at.zi, at.q, at.pn, at.b
    half = x_ref.shape[1] // 2
    own = at.slot(zi, q)

    def block(us, zj, qj, part=None):
        u0, nu = us
        if part is None:
            return out_ref.at[pl.ds(u0, nu), at.slot(zj, qj)]
        return out_ref.at[pl.ds(u0, nu), at.slot(zj, qj), pl.ds(part * half, half)]

    def z_copy(k, us, zj, sign):
        way = 0 if sign > 0 else 1
        ref = block(us, zj, q)
        return remote(ref, ref, zs.at[k, way, zj], zr.at[k, way, zj], at.c + sign * pn, b)

    def r_copy(k, us, zj, way, step, landing=False):
        away = step if landing else step - 1
        ref = block(us, zj, q - away if way == 0 else q + away, way if step == steps else None)
        to = at.right if way == 0 else at.left
        return remote(ref, ref, rs.at[k, way, step - 1, zj], rr.at[k, way, step - 1, zj], to, b)

    def arrive(k, us, sign, d):
        zj = zi + sign * d

        def go():
            if d > 0:
                z_copy(k, us, zj, -sign).wait_recv()
            if sign <= 0:
                pl.when(zi < levels - 1)(lambda: z_copy(k, us, zj, 1).start())
            if sign >= 0:
                pl.when(zi > 0)(lambda: z_copy(k, us, zj, -1).start())
            for way in (0, 1):
                r_copy(k, us, zj, way, 1).start()

        guarded(present(zi, sign, d, levels), go)

    def onward(k, us, sign, d):
        zj = zi + sign * d

        def go():
            for step in range(1, steps + 1):
                for way in (0, 1):
                    r_copy(k, us, zj, way, step, True).wait_recv()
                    if step < steps:
                        r_copy(k, us, zj, way, step + 1).start()

        guarded(present(zi, sign, d, levels), go)

    def finish(k, us, sign, d):
        zj = zi + sign * d

        def go():
            if sign <= 0:
                pl.when(zi < levels - 1)(lambda: z_copy(k, us, zj, 1).wait_send())
            if sign >= 0:
                pl.when(zi > 0)(lambda: z_copy(k, us, zj, -1).wait_send())
            for way in (0, 1):
                for step in range(1, steps + 1):
                    r_copy(k, us, zj, way, step).wait_send()

        guarded(present(zi, sign, d, levels), go)

    waves = [
        [(k, us, sign, d) for sign in ((0,) if d == 0 else (-1, 1))] for k, us in enumerate(passes) for d in range(levels)
    ]
    for i, wave in enumerate(waves):
        k, (u0, nu), _, d = wave[0]
        if d == 0:
            if ready is not None:
                ready(k)
            local = pltpu.make_async_copy(x_ref.at[pl.ds(u0, nu)], out_ref.at[pl.ds(u0, nu), own], ls.at[k])
            local.start()
            local.wait()
        for group in wave:
            arrive(*group)
            yield
        if i > 0:
            for group in waves[i - 1]:
                onward(*group)
                yield
    for group in waves[-1]:
        onward(*group)
        yield
    for wave in waves:
        for group in wave:
            finish(*group)


def run(steps):
    for _ in steps:
        pass


def gather(grid, x, levels, cid):
    count = levels * grid.plane

    def kernel(x_ref, out_ref, *sems):
        at = Place(grid, levels)
        at.greet_near(False)
        run(gather_steps(at, x_ref, out_ref, *sems))

    return pl.pallas_call(
        kernel,
        out_shape=jax.ShapeDtypeStruct((2, count) + x.shape[1:], x.dtype),
        in_specs=[INVMEM],
        out_specs=ANY,
        scratch_shapes=gather_sems(grid, levels),
        compiler_params=params(cid, 50),
        name="gather_%d" % count,
    )(x)


def level_sems(grid, levels):
    steps = grid.plane // 2
    return gather_sems(grid, levels) + [dma(2, levels), dma(2, levels), dma(2, steps), dma(2, steps)]


class LevelGather:
    def __init__(self, split, at, x_ref, out_ref, zs, zr, rs, rr, ls, lzs, lzr, lrs, lrr):
        self.at, self.x, self.out = at, x_ref, out_ref
        self.zs, self.zr, self.rs, self.rr, self.ls = zs, zr, rs, rr, ls
        self.lzs, self.lzr, self.lrs, self.lrr = lzs, lzr, lrs, lrr
        rows = x_ref.shape[1]
        cut = rows * 3 // 4 // 16 * 16 if split else rows
        self.split, self.first, self.last = split, pl.ds(0, cut), pl.ds(cut, rows - cut)

    def block(self, zj, qj, part, rows):
        which = pl.ds(0, 2) if part is None else pl.ds(part, 1)
        return self.out.at[which, self.at.slot(zj, qj), rows]

    def z_copy(self, zj, way):
        at, ref = self.at, self.block(zj, self.at.q, None, self.first)
        to = at.c + (at.pn if way == 0 else -at.pn)
        return remote(ref, ref, self.zs.at[0, way, zj], self.zr.at[0, way, zj], to, at.b)

    def ring_copy(self, zj, way, step, landing, rows, send, recv):
        at = self.at
        away = step if landing else step - 1
        ref = self.block(zj, at.q - away if way == 0 else at.q + away, way if step == at.steps else None, rows)
        return remote(ref, ref, send, recv, at.right if way == 0 else at.left, at.b)

    def r_copy(self, zj, way, step, landing=False):
        sems = self.rs.at[0, way, step - 1, zj], self.rr.at[0, way, step - 1, zj]
        return self.ring_copy(zj, way, step, landing, self.first, *sems)

    def low_copy(self, way, step, landing=False):
        sems = self.lrs.at[way, step - 1], self.lrr.at[way, step - 1]
        return self.ring_copy(self.at.zi, way, step, landing, self.last, *sems)

    def low_z_copy(self, zj, way):
        at = self.at
        ref = self.out.at[:, pl.ds(zj * at.pn, at.pn), self.last]
        to = at.c + (at.pn if way == 0 else -at.pn)
        return remote(ref, ref, self.lzs.at[way, zj], self.lzr.at[way, zj], to, at.b)

    def begin(self):
        at = self.at
        local = pltpu.make_async_copy(self.x, self.out.at[:, at.slot(at.zi, at.q)], self.ls.at[0])
        local.start()
        local.wait()
        self.send(0)
        if self.split:
            for way in (0, 1):
                self.low_copy(way, 1).start()

    def along(self, offset, copy):
        at = self.at
        zj = at.zi + offset
        pl.when((offset <= 0) & (at.zi < at.levels - 1))(lambda: copy(zj, 0).start())
        pl.when((offset >= 0) & (at.zi > 0))(lambda: copy(zj, 1).start())

    def send(self, offset):
        self.along(offset, self.z_copy)
        for way in (0, 1):
            self.r_copy(self.at.zi + offset, way, 1).start()

    def arrive(self, sign, d):
        self.z_copy(self.at.zi + sign * d, 0 if sign < 0 else 1).wait_recv()
        self.send(sign * d)

    def low_arrive(self, sign, d):
        self.low_z_copy(self.at.zi + sign * d, 0 if sign < 0 else 1).wait_recv()
        self.along(sign * d, self.low_z_copy)

    def onward(self, sign, d):
        zj = self.at.zi + sign * d
        for step in range(1, self.at.steps):
            for way in (0, 1):
                self.r_copy(zj, way, step, True).wait_recv()
                self.r_copy(zj, way, step + 1).start()

    def low_onward(self):
        for step in range(1, self.at.steps):
            for way in (0, 1):
                self.low_copy(way, step, True).wait_recv()
                self.low_copy(way, step + 1).start()

    def low_landed(self):
        for way in (0, 1):
            self.low_copy(way, self.at.steps, True).wait_recv()
        self.along(0, self.low_z_copy)

    def landed(self, sign, d):
        zj = self.at.zi + sign * d
        for way in (0, 1):
            self.r_copy(zj, way, self.at.steps, True).wait_recv()

    def finish(self):
        at = self.at

        def one(zj, carry):
            for copy in (self.z_copy, self.low_z_copy)[: 2 if self.split else 1]:
                pl.when((zj <= at.zi) & (at.zi < at.levels - 1))(lambda: copy(zj, 0).wait_send())
                pl.when((zj >= at.zi) & (at.zi > 0))(lambda: copy(zj, 1).wait_send())
            for way in (0, 1):
                for step in range(1, at.steps + 1):
                    self.r_copy(zj, way, step).wait_send()
            return carry

        lax.fori_loop(0, at.levels, one, 0)
        for way in (0, 1) if self.split else ():
            for step in range(1, at.steps + 1):
                self.low_copy(way, step).wait_send()

    def run(self, compute, first=None):
        at = self.at
        zi, levels = at.zi, at.levels

        def wave(t):
            pl.when((t < levels) & (zi - t >= 0))(lambda: self.arrive(-1, t))
            pl.when((t < levels) & (zi + t < levels))(lambda: self.arrive(1, t))

        def both(d, action, least=0):
            pl.when((d >= least) & (d < levels) & (zi - d >= 0))(lambda: action(-1, d))
            pl.when((d > 0) & (d < levels) & (zi + d < levels))(lambda: action(1, d))

        def one(t, carry):
            wave(t)
            if self.split:
                pl.when(t == 2)(self.low_landed)
            both(t - 1, self.onward)
            if first is not None:
                pl.when(t == 2)(first)
            e = t - 2
            if self.split:
                both(e, self.low_arrive, 1)
            both(e, self.landed)

            def side(i, carry):
                zj = zi + (2 * i - 1) * e
                here = (zj >= 0) & (zj < levels) & ((e > 0) | (i == 0))
                pl.when(here)(lambda: compute(zj, e == 0))
                return carry

            lax.fori_loop(0, 2, side, 0)
            return carry

        wave(1)
        both(0, self.onward)
        if self.split:
            self.low_onward()
        lax.fori_loop(2, levels + 2, one, 0)
        self.finish()


def member_step(core, group, member):
    remainder = (core * group + member) % 3
    return jnp.where(remainder == 0, 1.0, jnp.where(remainder == 1, 16.0, 64.0)).astype(F32)


def dequantize(core, group, codes, row_scale, into, rows, first):
    def one(i, carry):
        value = codes(pl.multiple_of(i * 16, 16)).astype(F32)
        for m in range(group):
            step = member_step(core, group, m)
            offset = jnp.where(step > 1.0, 0.5 * step, 0.0)
            level = jnp.floor(value * (1.0 / step)) * step + offset
            into[m, pl.ds(pl.multiple_of(first + i * 16, 16), 16)] = (level * row_scale[...]).astype(BF16)
        return carry

    lax.fori_loop(0, rows // 16, one, 0)


GELU_A = 0.7978845608028654
GELU_B = 0.044715


EARLY = 4
PER = 4


class FeedWeights:
    def __init__(self, at, group, units, gate_ref, up_ref, down_ref, kept, refs):
        self.at, self.group, self.units = at, group, units
        self.sources, self.kept = (gate_ref, up_ref, down_ref), kept
        self.pair, self.down, self.codes, self.down_codes, self.sems = refs

    @staticmethod
    def scratch(group, units, window):
        return [
            pltpu.VMEM((group, D, 2 * window), BF16),
            pltpu.VMEM((group, window, D), BF16),
            pltpu.VMEM((D, 2 * window), BF16),
            pltpu.VMEM((units, D), jnp.int32),
            dma(5),
        ]

    def copies(self):
        window = self.codes.shape[1] // 2
        gate, up, down = self.sources
        copies = [pltpu.make_async_copy(down, self.down_codes, self.sems.at[2])]
        if gate is not None:
            copies += [
                pltpu.make_async_copy(gate, self.codes.at[:, pl.ds(0, window)], self.sems.at[0]),
                pltpu.make_async_copy(up, self.codes.at[:, pl.ds(window, window)], self.sems.at[1]),
            ]
        return copies

    def keeps(self):
        return [
            pltpu.make_async_copy(self.pair, self.kept[0], self.sems.at[3]),
            pltpu.make_async_copy(self.down, self.kept[1], self.sems.at[4]),
        ]

    def load(self):
        for copy in self.copies():
            copy.start()

    def make(self, pair_scale, down_scale):
        at, group, units = self.at, self.group, self.units
        window = self.down.shape[1]
        inset = (at.c * units) % 128
        for copy in self.copies():
            copy.wait()
        dequantize(at.b, group, lambda r: self.codes[pl.ds(r, 16)], pair_scale, self.pair, D, 0)

        def clear(i, carry):
            for m in range(group):
                self.down[m, pl.ds(pl.multiple_of(i * 16, 16), 16)] = jnp.zeros((16, D), BF16)
            return carry

        if window > units:
            lax.fori_loop(0, inset // 16, clear, 0)
            lax.fori_loop((inset + units) // 16, window // 16, clear, 0)
        dequantize(at.b, group, lambda r: self.down_codes[pl.ds(r, 16)], down_scale, self.down, units, inset)
        for copy in self.keeps():
            copy.start()

    def finish(self):
        for copy in self.keeps():
            copy.wait()


def feed_blocks(grid):
    return 4 if grid.plane % 4 == 0 else grid.plane


def each_chunk(grid, zj, fresh, loads, stores, compute):
    size = feed_blocks(grid)
    m = zj // (grid.planes // 2)

    def one(i, carry):
        first = zj * grid.plane + i * size
        reads, writes = loads(first), stores(first)
        for copy in reads:
            copy.start()

        @pl.when(jnp.logical_not(fresh & (i == 0)))
        def _():
            for copy in writes:
                copy.wait()

        compute(m, reads)
        for copy in writes:
            copy.start()
        return carry

    lax.fori_loop(0, grid.plane // size, one, 0)


def copies_of(blocks, pairs, sems, first):
    return [
        pltpu.make_async_copy(a.at[:, blocks] if far_a else a, b if far_a else b.at[:, blocks], sems.at[first + k])
        for k, (a, b, far_a) in enumerate(pairs)
    ]


def forward_chunks(weights, all_ref, pair_ref, part_ref, xs, gu, part, sems):
    _, size, rows, _ = gu.shape
    window = weights.down.shape[1]

    def loads(first):
        return copies_of(pl.ds(first, size), [(all_ref, xs, True)], sems, 0)

    def stores(first):
        return copies_of(pl.ds(first, size), [(gu, pair_ref, False), (part, part_ref, False)], sems, 1)

    def compute(m, reads):
        reads[0].wait()
        both = dot(xs[...].reshape(2 * size * rows, D), weights.pair[m])
        gu[...] = both.astype(BF16).reshape(gu.shape)
        gate, up = both[:, :window], both[:, window:]
        bend = jnp.tanh(GELU_A * (gate + GELU_B * gate * gate * gate))
        hidden = (0.5 * gate * (1.0 + bend) * up).astype(BF16)
        part[...] = dot(hidden, weights.down[m]).astype(BF16).reshape(part.shape)

    return loads, stores, compute


def backward_chunks(wp, wd, all_ref, pair_ref, part_ref, dgu_ref, hid_ref, ys, gu, part, dgu, hid, sems):
    _, size, rows, _ = ys.shape
    window = wd.shape[1]
    count = 2 * size * rows

    def loads(first):
        return copies_of(pl.ds(first, size), [(all_ref, ys, True), (pair_ref, gu, True)], sems, 0)

    def stores(first):
        pairs = [(part, part_ref, False), (dgu, dgu_ref, False), (hid, hid_ref, False)]
        return copies_of(pl.ds(first, size), pairs, sems, 2)

    def compute(m, reads):
        reads[0].wait()
        grad_hidden = dot_t(ys[...].reshape(count, D), wd[m])
        reads[1].wait()
        both = gu[...].reshape(count, 2 * window).astype(F32)
        gate, up = both[:, :window], both[:, window:]
        bend = jnp.tanh(GELU_A * (gate + GELU_B * gate * gate * gate))
        bell = 0.5 * gate * (1.0 + bend)
        slope = 0.5 * (1.0 + bend) + 0.5 * gate * (1.0 - bend * bend) * GELU_A * (1.0 + 3.0 * GELU_B * gate * gate)
        dgu[:, :, :, :window] = (grad_hidden * up * slope).astype(BF16).reshape(hid.shape)
        dgu[:, :, :, window:] = (grad_hidden * bell).astype(BF16).reshape(hid.shape)
        hid[...] = (bell * up).astype(BF16).reshape(hid.shape)
        part[...] = dot_t(dgu[...].reshape(count, 2 * window), wp[m]).astype(BF16).reshape(part.shape)

    return loads, stores, compute


def chunk_buffers(size, rows, *widths):
    return [pltpu.VMEM((2, size, rows, width), BF16) for width in widths]


def feed_forward(grid, x, gate_codes, up_codes, down_codes, pair_scale, down_scale, cid):
    group, rows, _ = x.shape
    n, levels = grid.n, grid.planes
    units, window, _ = feed_windows(grid)
    gs, ws = level_sems(grid, levels), FeedWeights.scratch(group, units, window)
    size = feed_blocks(grid)

    def kernel(
        x_ref, gate_ref, up_ref, down_ref, ps_ref, ds_ref, all_ref, pair_ref, part_ref, wp_ref, wd_ref, *scratch
    ):
        refs = Split(scratch)
        at = Place(grid, levels)
        weights = FeedWeights(at, group, units, gate_ref, up_ref, down_ref, (wp_ref, wd_ref), refs.take(len(ws)))
        weights.load()
        moving = LevelGather(True, at, x_ref, all_ref, *refs.take(len(gs)))
        loads, stores, compute = forward_chunks(weights, all_ref, pair_ref, part_ref, *refs.take(4))
        at.greet_near(False)
        moving.begin()
        weights.make(ps_ref, ds_ref)
        moving.run(lambda zj, fresh: each_chunk(grid, zj, fresh, loads, stores, compute))
        for copy in stores(0):
            copy.wait()
        weights.finish()

    def blocks(width):
        return jax.ShapeDtypeStruct((group, n, rows, width), BF16)

    return pl.pallas_call(
        kernel,
        out_shape=(
            blocks(D),
            blocks(2 * window),
            blocks(D),
            jax.ShapeDtypeStruct((group, D, 2 * window), BF16),
            jax.ShapeDtypeStruct((group, window, D), BF16),
        ),
        in_specs=[INVMEM, ANY, ANY, ANY, INVMEM, INVMEM],
        out_specs=(ANY,) * 5,
        scratch_shapes=ws + gs + chunk_buffers(size, rows, D, 2 * window, D) + [dma(3)],
        compiler_params=params(cid, 60),
        name="feed_forward",
    )(x, gate_codes, up_codes, down_codes, pair_scale, down_scale)


def feed_backward(grid, x, pair, pair_matrices, down_matrices, cid):
    group, rows, _ = x.shape
    n, levels = grid.n, grid.planes
    _, window, _ = feed_windows(grid)
    gs = level_sems(grid, levels)
    size = feed_blocks(grid)

    def kernel(x_ref, pair_ref, wp_ref, wd_ref, all_ref, part_ref, dgu_ref, hid_ref, *scratch):
        refs = Split(scratch)
        at = Place(grid, levels)
        moving = LevelGather(True, at, x_ref, all_ref, *refs.take(len(gs)))
        wp, wd, fetch_sems = refs.take(3)
        fetch = [
            pltpu.make_async_copy(wp_ref, wp, fetch_sems.at[0]),
            pltpu.make_async_copy(wd_ref, wd, fetch_sems.at[1]),
        ]
        for copy in fetch:
            copy.start()
        loads, stores, compute = backward_chunks(
            wp, wd, all_ref, pair_ref, part_ref, dgu_ref, hid_ref, *refs.take(6)
        )
        at.greet_near(False)
        moving.begin()
        for copy in fetch:
            copy.wait()
        moving.run(lambda zj, fresh: each_chunk(grid, zj, fresh, loads, stores, compute))
        for copy in stores(0):
            copy.wait()

    def blocks(width):
        return jax.ShapeDtypeStruct((group, n, rows, width), BF16)

    return pl.pallas_call(
        kernel,
        out_shape=(blocks(D), blocks(D), blocks(2 * window), blocks(window)),
        in_specs=[INVMEM] + [ANY] * 3,
        out_specs=(ANY,) * 4,
        scratch_shapes=gs
        + [pltpu.VMEM((group, D, 2 * window), BF16), pltpu.VMEM((group, window, D), BF16), dma(2)]
        + chunk_buffers(size, rows, D, 2 * window, D, 2 * window, window)
        + [dma(5)],
        compiler_params=params(cid, 62),
        name="feed_backward",
    )(x, pair, pair_matrices, down_matrices)


def scatter_scratch(grid, levels, rows, width):
    steps = grid.plane // 2
    return [
        pltpu.VMEM((2, levels * grid.plane, rows, width), BF16),
        pltpu.VMEM((2, levels, 2, rows // 2, width), BF16),
        pltpu.VMEM((2, max(steps - 1, 1), levels, 2, rows, width), BF16),
        pltpu.VMEM((2, levels, 2, rows, width), BF16),
        dma(1),
        dma(1, 2, levels),
        dma(1, 2, levels),
        dma(1, 2, steps, levels),
        dma(1, 2, steps, levels),
    ]


def scatter_steps(at, out_ref, acc, ring_half, ring_full, line, ls, zs, zr, rs, rr):
    levels, steps, zi, q, pn, b = at.levels, at.steps, at.zi, at.q, at.pn, at.b
    rows = acc.shape[2]
    half = rows // 2
    passes = [(0, 2)]

    def block(us, zj, qj, part=None):
        u0, nu = us
        if part is None:
            return acc.at[pl.ds(u0, nu), at.slot(zj, qj)]
        return acc.at[pl.ds(u0, nu), at.slot(zj, qj), pl.ds(part * half, half)]

    def add(us, s, others, lo, count):
        u0, nu = us

        def one(i, carry):
            u, r = u0 + i // (count // 16), lo + (i % (count // 16)) * 16
            total = acc[u, s, pl.ds(r, 16)].astype(F32)
            for other in others:
                total = total + other(u, r)[...].astype(F32)
            acc[u, s, pl.ds(r, 16)] = total.astype(BF16)
            return carry

        lax.fori_loop(0, nu * (count // 16), one, 0)

    def full_at(way, step, zj):
        return lambda u, r: ring_full.at[way, step - 2, zj, u, pl.ds(r, 16)]

    def half_at(way, zj):
        return lambda u, r: ring_half.at[way, zj, u, pl.ds(r - way * half, 16)]

    def line_at(way, zj):
        return lambda u, r: line.at[way, zj, u, pl.ds(r, 16)]

    def r_copy(k, us, zj, way, step):
        u0, nu = us
        sign = 1 if way == 0 else -1
        target = q + sign * (steps + 1 - step)
        if step == 1:
            src, dst = block(us, zj, target, way), ring_half.at[way, zj, pl.ds(u0, nu)]
        else:
            src, dst = block(us, zj, target), ring_full.at[way, step - 2, zj, pl.ds(u0, nu)]
        to = at.right if way == 0 else at.left
        return remote(src, dst, rs.at[k, way, step - 1, zj], rr.at[k, way, step - 1, zj], to, b)

    def z_copy(k, us, zj, way):
        u0, nu = us
        to = at.c + (pn if way == 0 else -pn)
        return remote(block(us, zj, q), line.at[way, zj, pl.ds(u0, nu)], zs.at[k, way, zj], zr.at[k, way, zj], to, b)

    def begin(k, us, sign, d):
        def go():
            for way in (0, 1):
                r_copy(k, us, zi + sign * d, way, 1).start()

        guarded(present(zi, sign, d, levels), go)

    def middle(k, us, sign, d):
        zj = zi + sign * d

        def go():
            for step in range(1, steps):
                for way in (0, 1):
                    r_copy(k, us, zj, way, step).wait_recv()
                    s = at.slot(zj, q + (1 if way == 0 else -1) * (steps - step))
                    if step == 1:
                        add(us, s, [half_at(way, zj)], way * half, half)
                    else:
                        add(us, s, [full_at(way, step, zj)], 0, rows)
                    r_copy(k, us, zj, way, step + 1).start()

        guarded(present(zi, sign, d, levels), go)

    def last(k, us, sign, d):
        zj = zi + sign * d

        def go():
            for way in (0, 1):
                r_copy(k, us, zj, way, steps).wait_recv()
            s = at.slot(zj, q)
            if steps > 1:
                add(us, s, [full_at(0, steps, zj), full_at(1, steps, zj)], 0, rows)
            else:
                add(us, s, [half_at(0, zj)], 0, half)
                add(us, s, [half_at(1, zj)], half, half)

            def passed(way):
                z_copy(k, us, zj, way).wait_recv()
                add(us, s, [line_at(way, zj)], 0, rows)

            if sign >= 0:
                pl.when(zi > 0)(lambda: passed(0))
            if sign <= 0:
                pl.when(zi < levels - 1)(lambda: passed(1))
            if sign > 0:
                z_copy(k, us, zj, 0).start()
            if sign < 0:
                z_copy(k, us, zj, 1).start()

        guarded(present(zi, sign, d, levels), go)

    def finish(k, us, sign, d):
        zj = zi + sign * d

        def go():
            for way in (0, 1):
                for step in range(1, steps + 1):
                    r_copy(k, us, zj, way, step).wait_send()
            if sign != 0:
                z_copy(k, us, zj, 0 if sign > 0 else 1).wait_send()

        guarded(present(zi, sign, d, levels), go)

    waves = [
        [(k, us, sign, d) for sign in ((0,) if d == 0 else (-1, 1))]
        for k, us in enumerate(passes)
        for d in range(levels - 1, -1, -1)
    ]
    own = at.slot(zi, q)
    def each(action, i):
        if i < len(waves):
            for group in waves[i]:
                action(*group)

    each(begin, 0)
    each(begin, 1)
    each(middle, 0)
    yield
    for i in range(len(waves)):
        each(begin, i + 2)
        each(middle, i + 1)
        yield
        each(last, i)
    yield

    def give(src, u):
        def one(i, carry):
            out_ref[u, pl.ds(i * 16, 16)] = src.at[pl.ds(i * 16, 16)][...]
            return carry

        lax.fori_loop(0, rows // 16, one, 0)

    give(acc.at[0, own], 0)
    give(acc.at[1, own], 1)
    for wave in waves:
        for group in wave:
            finish(*group)


def split_scratch(grid, levels, rows, width):
    steps, pn = grid.plane // 2, grid.plane
    cut = rows * 3 // 4 // 16 * 16
    more = max(steps - 1, 1)
    return [
        pltpu.VMEM((2, levels * pn, rows, width), BF16),
        pltpu.VMEM((2, levels, cut, width), BF16),
        pltpu.VMEM((2, more, levels, 2, cut, width), BF16),
        pltpu.VMEM((2, levels, 2, cut, width), BF16),
        pltpu.VMEM((2, rows - cut, width), BF16),
        pltpu.VMEM((2, more, 2, rows - cut, width), BF16),
        pltpu.VMEM((2, levels, 2, pn, rows - cut, width), BF16),
        dma(1),
        dma(2, levels),
        dma(2, levels),
        dma(2, steps, levels),
        dma(2, steps, levels),
        dma(2, levels),
        dma(2, levels),
        dma(2, steps),
        dma(2, steps),
    ]


def split_scatter_steps(
    at, out_ref, acc, half_ref, full_ref, line_ref, low_half, low_full, low_line,
    ls, zs, zr, rs, rr, lzs, lzr, lrs, lrr,
):
    levels, steps, zi, q, pn, b = at.levels, at.steps, at.zi, at.q, at.pn, at.b
    rows = acc.shape[2]
    cut = half_ref.shape[2]
    upper, lower = pl.ds(0, cut), pl.ds(cut, rows - cut)

    def add(target, others, pieces):
        def one(i, carry):
            total = target(i)[...].astype(F32)
            for other in others:
                total = total + other(i)[...].astype(F32)
            target(i)[...] = total.astype(BF16)
            return carry

        lax.fori_loop(0, pieces, one, 0)

    def spans(ref, first, count):
        per = count // 16
        return lambda i: ref.at[i // per, pl.ds(pl.multiple_of(first + (i % per) * 16, 16), 16)]

    def along(way):
        return at.c + (pn if way == 0 else -pn)

    def r_copy(zj, way, step):
        target = at.slot(zj, q + (1 if way == 0 else -1) * (steps + 1 - step))
        if step == 1:
            src, dst = acc.at[way, target, upper], half_ref.at[way, zj]
        else:
            src, dst = acc.at[:, target, upper], full_ref.at[way, step - 2, zj]
        to = at.right if way == 0 else at.left
        return remote(src, dst, rs.at[way, step - 1, zj], rr.at[way, step - 1, zj], to, b)

    def z_copy(zj, way):
        return remote(
            acc.at[:, at.slot(zj, q), upper], line_ref.at[way, zj], zs.at[way, zj], zr.at[way, zj], along(way), b
        )

    def begin(sign, d):
        for way in (0, 1):
            r_copy(zi + sign * d, way, 1).start()

    def middle(sign, d):
        zj = zi + sign * d
        for step in range(1, steps):
            for way in (0, 1):
                r_copy(zj, way, step).wait_recv()
                s = at.slot(zj, q + (1 if way == 0 else -1) * (steps - step))
                if step == 1:
                    add(
                        lambda i: acc.at[way, s, pl.ds(pl.multiple_of(i * 16, 16), 16)],
                        [lambda i: half_ref.at[way, zj, pl.ds(pl.multiple_of(i * 16, 16), 16)]],
                        cut // 16,
                    )
                else:
                    add(spans(acc.at[:, s], 0, cut), [spans(full_ref.at[way, step - 2, zj], 0, cut)], 2 * cut // 16)
                r_copy(zj, way, step + 1).start()

    def last(sign, d):
        zj = zi + sign * d
        for way in (0, 1):
            r_copy(zj, way, steps).wait_recv()
        s = at.slot(zj, q)
        mine = spans(acc.at[:, s], 0, cut)
        add(mine, [spans(full_ref.at[way, steps - 2, zj], 0, cut) for way in (0, 1)], 2 * cut // 16)

        def passed(way):
            z_copy(zj, way).wait_recv()
            add(mine, [spans(line_ref.at[way, zj], 0, cut)], 2 * cut // 16)

        if sign >= 0:
            pl.when(zi > 0)(lambda: passed(0))
        if sign <= 0:
            pl.when(zi < levels - 1)(lambda: passed(1))
        if sign != 0:
            z_copy(zj, 0 if sign > 0 else 1).start()

    def done(sign, d):
        zj = zi + sign * d
        for way in (0, 1):
            for step in range(1, steps + 1):
                r_copy(zj, way, step).wait_send()
        if sign != 0:
            z_copy(zj, 0 if sign > 0 else 1).wait_send()

    def low_z_copy(zj, way):
        ref = acc.at[:, pl.ds(zj * pn, pn), lower]
        return remote(ref, low_line.at[way, zj], lzs.at[way, zj], lzr.at[way, zj], along(way), b)

    def low_passed(zj, way):
        low_z_copy(zj, way).wait_recv()
        per = (rows - cut) // 16

        def piece(i):
            return i // (pn * per), (i // per) % pn, (i % per) * 16

        def into(i):
            u, j, r = piece(i)
            return acc.at[u, zj * pn + j, pl.ds(pl.multiple_of(cut + r, 16), 16)]

        def come(i):
            u, j, r = piece(i)
            return low_line.at[way, zj, u, j, pl.ds(pl.multiple_of(r, 16), 16)]

        add(into, [come], 2 * pn * per)

    def low_start():
        for zj in range(levels - 1, 0, -1):
            pl.when(zi == 0)(lambda: low_z_copy(zj, 0).start())
        for zj in range(levels - 1):
            pl.when(zi == levels - 1)(lambda: low_z_copy(zj, 1).start())

    def low_stage(a):
        up, down = zi + levels - 1 - a, a - (levels - 1 - zi)

        def from_below():
            low_passed(up, 0)
            pl.when(up > zi)(lambda: low_z_copy(up, 0).start())

        def from_above():
            low_passed(down, 1)
            pl.when(down < zi)(lambda: low_z_copy(down, 1).start())

        pl.when((zi > 0) & (up >= zi) & (up < levels))(from_below)
        pl.when((zi < levels - 1) & (down >= 0) & (down <= zi))(from_above)

    def low_r_copy(way, step):
        target = at.slot(zi, q + (1 if way == 0 else -1) * (steps + 1 - step))
        if step == 1:
            src, dst = acc.at[way, target, lower], low_half.at[way]
        else:
            src, dst = acc.at[:, target, lower], low_full.at[way, step - 2]
        to = at.right if way == 0 else at.left
        return remote(src, dst, lrs.at[way, step - 1], lrr.at[way, step - 1], to, b)

    def low_middle():
        for step in range(1, steps):
            for way in (0, 1):
                low_r_copy(way, step).wait_recv()
                s = at.slot(zi, q + (1 if way == 0 else -1) * (steps - step))
                if step == 1:
                    add(
                        lambda i: acc.at[way, s, pl.ds(pl.multiple_of(cut + i * 16, 16), 16)],
                        [lambda i: low_half.at[way, pl.ds(pl.multiple_of(i * 16, 16), 16)]],
                        (rows - cut) // 16,
                    )
                else:
                    add(
                        spans(acc.at[:, s], cut, rows - cut),
                        [spans(low_full.at[way, step - 2], 0, rows - cut)],
                        2 * (rows - cut) // 16,
                    )
                low_r_copy(way, step + 1).start()

    def low_last():
        for way in (0, 1):
            low_r_copy(way, steps).wait_recv()
        add(
            spans(acc.at[:, at.slot(zi, q)], cut, rows - cut),
            [spans(low_full.at[way, steps - 2], 0, rows - cut) for way in (0, 1)],
            2 * (rows - cut) // 16,
        )

    def each(action, d):
        if d >= 0:
            for sign in (0,) if d == 0 else (-1, 1):
                guarded(present(zi, sign, d, levels), lambda: action(sign, d))

    far = levels - 1
    each(begin, far)
    low_start()
    each(begin, far - 1)
    each(middle, far)
    yield
    for a in range(1, levels):
        low_stage(a)
        d = far - a
        each(begin, d - 1)
        each(middle, d)
        yield
        each(last, d + 1)
    for way in (0, 1):
        low_r_copy(way, 1).start()
    low_middle()
    each(last, 0)
    low_last()
    yield

    def give(i, carry):
        r = pl.ds(pl.multiple_of((i % (rows // 16)) * 16, 16), 16)
        out_ref[i // (rows // 16), r] = acc[i // (rows // 16), at.slot(zi, q), r]
        return carry

    lax.fori_loop(0, 2 * (rows // 16), give, 0)
    for d in range(levels):
        each(done, d)
    for zj in range(levels):
        pl.when(zj > zi)(lambda: low_z_copy(zj, 0).wait_send())
        pl.when(zj < zi)(lambda: low_z_copy(zj, 1).wait_send())
    for way in (0, 1):
        for step in range(1, steps + 1):
            low_r_copy(way, step).wait_send()


def scatter_parts(grid, levels, rows, width):
    blocks = 2 * (2 * levels * (grid.plane // 2 + 2) + levels * grid.plane)
    parts = 1
    while blocks * rows * (width // parts) * 2 > 40 * 2**20:
        parts += 1
        while width % (128 * parts):
            parts += 1
    return parts


def in_parts(grid, levels, call, p, extra):
    parts = scatter_parts(grid, levels, p.shape[2], p.shape[3])
    if parts == 1:
        return call(p, extra)
    piece = p.shape[3] // parts
    sums, others = [], ()
    for i in range(parts):
        got = call(p[..., i * piece : (i + 1) * piece], extra if i == 0 else None)
        sums.append(got[0])
        others = got[1:] if i == 0 else others
    return (jnp.concatenate(sums, axis=-1),) + tuple(others)


def pairwise(n, c, b):
    def to(i):
        return (c + 2 * i + b) % n

    def frm(i, core):
        return (c + n - 2 * i - core) % n

    return to, frm


def middle_out(half):
    return sorted(range(1, half), key=lambda i: abs(2 * i - half))


def share_task(at, sources, views, ss, sr, fs, fr):
    n, c, b = at.n, at.c, at.b
    half = n // 2
    to, frm = pairwise(n, c, b)
    kinds = len(sources)

    def out_copy(k, i):
        return remote(sources[k](to(i)), views[k](c), ss.at[k, i], sr.at[k, i], to(i), b)

    def landed(k, i):
        return remote(sources[k](c), views[k](frm(i, b)), ss.at[k, i], sr.at[k, i], to(i), b)

    def pass_on(k, i, core):
        ref = views[k](frm(i, core))
        return at.sibling(ref, ref, fs.at[k, i], fr.at[k, i])

    def local(k):
        return pltpu.make_async_copy(sources[k](c), views[k](c), sr.at[k, 0])

    order = middle_out(half) + [0]

    def issue():
        for i in order:
            for k in range(kinds):
                if i > 0:
                    out_copy(k, i).start()
                else:
                    pl.when(b == 1)(lambda: out_copy(k, 0).start())
                    pl.when(b == 0)(lambda: local(k).start())
            yield

    def finish():
        for i in order:
            for k in range(kinds):
                if i > 0:
                    landed(k, i).wait_recv()
                else:
                    pl.when(b == 1)(lambda: landed(k, 0).wait_recv())
                    pl.when(b == 0)(lambda: local(k).wait())
                pass_on(k, i, b).start()
        for k in range(kinds):
            for i in range(half):
                pass_on(k, i, 1 - b).wait_recv()
            for i in range(half):
                pass_on(k, i, b).wait_send()
            for i in range(1, half):
                out_copy(k, i).wait_send()
            pl.when(b == 1)(lambda: out_copy(k, 0).wait_send())

    return issue(), finish


def share_sems(grid, kinds):
    return [dma(kinds, grid.n // 2) for _ in range(4)]


def tell_task(at, small_ref, all_ref, ts, tr):
    n, c, b = at.n, at.c, at.b

    def tell(off, slot):
        return remote(small_ref, all_ref.at[slot], ts.at[off], tr.at[off], (c + off) % n, b)

    keep = pltpu.make_async_copy(small_ref, all_ref.at[c], ts.at[0])

    def issue():
        keep.start()
        for off in range(1, n):
            tell(off, c).start()
        yield

    def finish():
        keep.wait()
        for off in range(1, n):
            tell(off, (c + n - off) % n).wait_recv()
        for off in range(1, n):
            tell(off, c).wait_send()

    return issue(), finish


def head_rows_task(at, x_ref, out_ref, hs, hr, fs, fr):
    c, b = at.c, at.b
    copies = at.n // HEADS
    head, rank = c % HEADS, c // HEADS
    mine = rank % 2 == b

    def out_copy(k):
        to = c // copies + HEADS * (2 * k + b)
        return to, remote(x_ref, out_ref.at[c % copies], hs.at[k], hr.at[c % copies], to, b)

    def landed(j):
        return remote(x_ref, out_ref.at[j], hs.at[0], hr.at[j], head * copies + j, b)

    def here(j):
        return pltpu.make_async_copy(x_ref, out_ref.at[j], hr.at[j])

    def pass_on(j):
        return at.sibling(out_ref.at[j], out_ref.at[j], fs.at[j], fr.at[j])

    def issue():
        for k in range(copies // 2):
            to, copy = out_copy(k)
            pl.when(to != c)(lambda: copy.start())
            pl.when(to == c)(lambda: here(c % copies).start())
            yield

    def finish():
        @pl.when(mine)
        def _():
            for j in range(copies):
                pl.when(head * copies + j != c)(lambda: landed(j).wait_recv())
                pl.when(head * copies + j == c)(lambda: here(j).wait())
                pass_on(j).start()
            for j in range(copies):
                pass_on(j).wait_send()

        @pl.when(jnp.logical_not(mine))
        def _():
            for j in range(copies):
                pass_on(j).wait_recv()

        for k in range(copies // 2):
            to, copy = out_copy(k)
            pl.when(to != c)(lambda: copy.wait_send())

    return issue(), finish


def head_rows_sems(grid):
    copies = grid.n // HEADS
    return [dma(copies), dma(copies), dma(copies), dma(copies)]


def add_rows(into, other, rows):
    step = 16 if rows % 16 == 0 else rows

    def one(r, carry):
        at = pl.ds(pl.multiple_of(r * step, step), step)
        into[at] = (into[at].astype(F32) + other[at].astype(F32)).astype(BF16)
        return carry

    lax.fori_loop(0, rows // step, one, 0)


def return_task(at, x_ref, out_ref, mine, theirs, ls, ps, pr, ss, sr, fs, fr, given=None, fill=None, prepare=None, per=2):
    n, c, b = at.n, at.c, at.b
    half = n // 2
    to, frm = pairwise(n, c, b)
    other_to, _ = pairwise(n, c, 1 - b)

    def load(i):
        return pltpu.make_async_copy(x_ref.at[to(i)], mine.at[i], ls.at[i])

    def give(i):
        source = x_ref.at[other_to(i)] if given is None else given.at[i]
        return at.sibling(source, theirs.at[i], ps.at[i], pr.at[i])

    def out_copy(i):
        return remote(mine.at[i], out_ref.at[c], ss.at[i], sr.at[i], to(i), b)

    def landed(i):
        return remote(mine.at[i], out_ref.at[frm(i, b)], ss.at[i], sr.at[i], to(i), b)

    def pass_on(i, core):
        ref = out_ref.at[frm(i, core)]
        return at.sibling(ref, ref, fs.at[i], fr.at[i])

    local = pltpu.make_async_copy(mine.at[0], out_ref.at[c], ss.at[0])
    order = middle_out(half) + [0]

    def issue():
        if prepare is not None:
            yield from prepare()
        for i in order:
            if fill is None:
                load(i).start()
            else:
                fill(i)
            give(i).start()
        for j, i in enumerate(order):
            if fill is None:
                load(i).wait()
            give(i).wait_recv()
            add_rows(mine.at[i], theirs.at[i], mine.shape[1])
            if i > 0:
                out_copy(i).start()
            else:
                pl.when(b == 1)(lambda: out_copy(0).start())
                pl.when(b == 0)(lambda: local.start())
            if j % per == per - 1:
                yield

    def finish():
        for i in order:
            if i > 0:
                landed(i).wait_recv()
            else:
                pl.when(b == 1)(lambda: landed(0).wait_recv())
                pl.when(b == 0)(lambda: local.wait())
            pass_on(i, b).start()
        for i in range(half):
            pass_on(i, 1 - b).wait_recv()
        for i in range(half):
            give(i).wait_send()
            pass_on(i, b).wait_send()
        for i in range(1, half):
            out_copy(i).wait_send()
        pl.when(b == 1)(lambda: out_copy(0).wait_send())

    return issue(), finish


def return_scratch(grid, shape):
    blocks = (grid.n // 2,) + shape
    return [pltpu.VMEM(blocks, BF16), pltpu.VMEM(blocks, BF16)] + [dma(grid.n // 2) for _ in range(7)]


def head_return_task(at, x_ref, out_ref, mine, theirs, ls, ps, pr, hs, hr, fs, fr):
    c, b = at.c, at.b
    copies = at.n // HEADS
    head, rank = c % HEADS, c // HEADS
    taken = (c % copies) % 2 == b

    def load(k):
        return pltpu.make_async_copy(x_ref.at[2 * k + b], mine.at[k], ls.at[k])

    def give(k):
        return at.sibling(x_ref.at[2 * k + 1 - b], theirs.at[k], ps.at[k], pr.at[k])

    def out_copy(k):
        to = head * copies + 2 * k + b
        return to, remote(mine.at[k], out_ref.at[rank], hs.at[k], hr.at[rank], to, b)

    def landed(i):
        return remote(mine.at[0], out_ref.at[i], hs.at[0], hr.at[i], c // copies + HEADS * i, b)

    def here(k, i):
        return pltpu.make_async_copy(mine.at[k], out_ref.at[i], hr.at[i])

    def pass_on(i):
        return at.sibling(out_ref.at[i], out_ref.at[i], fs.at[i], fr.at[i])

    def issue():
        for k in range(copies // 2):
            load(k).start()
            give(k).start()
        for k in range(copies // 2):
            load(k).wait()
            give(k).wait_recv()
            add_rows(mine.at[k], theirs.at[k], x_ref.shape[1])
            to, copy = out_copy(k)
            pl.when(to != c)(lambda: copy.start())
            pl.when(to == c)(lambda: here(k, rank).start())
            yield

    def finish():
        @pl.when(taken)
        def _():
            for i in range(copies):
                frm = c // copies + HEADS * i
                pl.when(frm != c)(lambda: landed(i).wait_recv())
                pl.when(frm == c)(lambda: here(0, i).wait())
                pass_on(i).start()
            for i in range(copies):
                pass_on(i).wait_send()

        @pl.when(jnp.logical_not(taken))
        def _():
            for i in range(copies):
                pass_on(i).wait_recv()

        for k in range(copies // 2):
            give(k).wait_send()
            to, copy = out_copy(k)
            pl.when(to != c)(lambda: copy.wait_send())

    return issue(), finish


def head_return_scratch(grid, shape):
    copies = grid.n // HEADS
    blocks = (copies // 2,) + shape
    return [pltpu.VMEM(blocks, BF16), pltpu.VMEM(blocks, BF16)] + [dma(copies) for _ in range(7)]


def pair_task(at, x_ref, out_ref, other, sems):
    copy = at.sibling(x_ref, other, sems.at[0], sems.at[1])

    def issue():
        copy.start()
        yield

    def finish():
        copy.wait_recv()

        def one(r, carry):
            rows = pl.ds(pl.multiple_of(r * 16, 16), 16)
            out_ref[rows] = (x_ref[rows].astype(F32) + other[rows].astype(F32)).astype(out_ref.dtype)
            return carry

        lax.fori_loop(0, x_ref.shape[0] // 16, one, 0)
        copy.wait_send()

    return issue(), finish


class Split:
    def __init__(self, refs):
        self.refs = list(refs)

    def take(self, count):
        got, self.refs = self.refs[:count], self.refs[count:]
        return got


def together(main, *tasks):
    for _ in main:
        for issue, _finish in tasks:
            next(issue, None)
    for issue, finish in tasks:
        run(issue)
    for issue, finish in tasks:
        finish()


def narrow_task(sources, targets, wide, low, loads, stores):
    width = wide.shape[2]
    pieces = [(k, i) for k in range(len(sources)) for i in range(sources[k].shape[1] // width)]

    def load(j):
        k, i = pieces[j]
        return pltpu.make_async_copy(sources[k].at[:, pl.ds(i * width, width)], wide.at[j % 2], loads.at[j % 2])

    def store(j):
        k, i = pieces[j]
        return pltpu.make_async_copy(low.at[j % 2], targets[k].at[:, pl.ds(i * width, width)], stores.at[j % 2])

    def issue():
        load(0).start()
        load(1).start()
        yield
        for j in range(len(pieces)):
            load(j).wait()
            if j >= 2:
                store(j - 2).wait()
            low[j % 2] = wide[j % 2].astype(F32).astype(BF16)
            store(j).start()
            if j + 2 < len(pieces):
                load(j + 2).start()
            yield

    def finish():
        for j in range(len(pieces) - 2, len(pieces)):
            store(j).wait()

    return issue(), finish


def swap_copy(at, source, target, send, recv):
    return remote(source, target.at[at.member], send, recv, at.partner, at.b)


def swap_task(at, source, target, sems):
    there = swap_copy(at, source, target, sems.at[0], sems.at[1])
    here = remote(source, target.at[1 - at.member], sems.at[0], sems.at[1], at.partner, at.b)

    def issue():
        there.start()
        yield

    def finish():
        here.wait_recv()
        there.wait_send()

    return issue(), finish


def open_kernel(grid, tokens, gain, qkv_parts, out_codes, small, gate_codes, up_codes, rows_too, cid):
    x = tokens
    n, levels = grid.n, grid.planes // 2
    rows_d, width = qkv_parts.shape[1:]
    flat = rows_d % 16 == 0
    copies = n // HEADS
    gs, ss, ts, hs = gather_sems(grid, levels, 2), share_sems(grid, 1), [dma(n), dma(n)], head_rows_sems(grid)

    piece = FF // 2
    ns = [
        pltpu.VMEM((2, rows_d, piece), jnp.int32),
        pltpu.VMEM((2, rows_d, piece), BF16),
        dma(2),
        dma(2),
    ]

    def kernel(
        x_ref, gain_ref, w_ref, o_ref, small_ref, gate_ref, up_ref,
        kept_ref, seen_ref, codes_ref, rows_ref, all_ref, gl_ref, ul_ref, *scratch,
    ):
        at = Place(grid, levels)
        refs = Split(scratch)
        normed_ref, token_sems = refs.take(2)
        member = at.member
        at.greet_all()
        token_issue, token_finish = swap_task(at, x_ref.at[1 - member], kept_ref, token_sems)
        run(token_issue)

        def view(j):
            return codes_ref.at[pl.ds(j * rows_d, rows_d)] if flat else codes_ref.at[j]

        def ready(k):
            u = member if k == 0 else 1 - member
            if k == 1:
                token_finish()

            def one(_, r):
                if k == 0:
                    kept_ref[u, r] = x_ref[u, r]
                value = kept_ref[u, r].astype(F32)
                normed_ref[u, r] = (value * inverse_rms(value) * gain_ref[0:1]).astype(BF16)

            each_rows(1, x_ref.shape[1], one)

        together(
            gather_steps(
                at, normed_ref, seen_ref, *refs.take(len(gs)), passes=[(member, 1), (1 - member, 1)], ready=ready
            ),
            narrow_task([gate_ref, up_ref], [gl_ref, ul_ref], *refs.take(4)),
            tell_task(at, small_ref, all_ref, *refs.take(2)),
            share_task(at, [lambda to: w_ref.at[to % HEADS]], [view], *refs.take(len(ss))),
            *([head_rows_task(at, o_ref, rows_ref, *refs.take(4))] if rows_too else []),
        )
        if not rows_too:
            rows_ref[...] = o_ref[...]

    codes_shape = (n * rows_d, width) if flat else (n, rows_d, width)
    return pl.pallas_call(
        kernel,
        out_shape=(
            jax.ShapeDtypeStruct(x.shape, BF16),
            jax.ShapeDtypeStruct((2, levels * grid.plane) + x.shape[1:], BF16),
            jax.ShapeDtypeStruct(codes_shape, BF16),
            jax.ShapeDtypeStruct((copies,) + out_codes.shape if rows_too else out_codes.shape, BF16),
            jax.ShapeDtypeStruct((n,) + small.shape, small.dtype),
            jax.ShapeDtypeStruct(gate_codes.shape, BF16),
            jax.ShapeDtypeStruct(up_codes.shape, BF16),
        ),
        in_specs=[INVMEM] * 5 + [ANY] * 2,
        out_specs=(INVMEM, ANY, ANY, ANY if rows_too else INVMEM) + (ANY,) * 3,
        scratch_shapes=[pltpu.VMEM(x.shape, BF16), dma(2)] + gs + ns + ts + ss + hs,
        compiler_params=params(cid, 50),
        name="open",
    )(tokens, gain, qkv_parts, out_codes, small, gate_codes, up_codes)


def scatter_kernel(grid, levels, cid, name, tasks=None, end=None):
    made, in_specs, out_shapes, out_specs, extra_scratch = tasks if tasks else (None, [], (), (), [])

    def call(p, extra):
        rows, width = p.shape[2:]
        more = () if extra is None else tuple(extra)
        own = scatter_scratch(grid, levels, rows, width)

        def kernel(*refs):
            refs = Split(refs)
            (p_ref,) = refs.take(1)
            more_refs = refs.take(len(more))
            (out_ref,) = refs.take(1)
            out_refs = refs.take(len(out_shapes) if more else 0)
            mine = refs.take(len(own))
            at = Place(grid, levels)
            load = pltpu.make_async_copy(p_ref, mine[0], mine[4].at[0])
            load.start()
            if more:
                at.greet_all()
            else:
                at.greet_near(False)
            load.wait()
            sums = refs.take(1)[0] if end else out_ref
            others = made(at, more_refs, out_refs, refs) if more else []
            if end is None:
                together(scatter_steps(at, out_ref, *mine), *others)
                return
            for _ in scatter_steps(at, sums, *mine):
                for issue, _finish in others:
                    next(issue, None)
            last = end(at, more_refs, sums, out_ref, refs)
            together((), *others)
            last()

        return pl.pallas_call(
            kernel,
            out_shape=(jax.ShapeDtypeStruct((2, rows, width), BF16),) + (out_shapes if more else ()),
            in_specs=[ANY] + (in_specs if more else []),
            out_specs=(INVMEM,) + (out_specs if more else ()),
            scratch_shapes=own + (extra_scratch if more else []),
            compiler_params=params(cid + (0 if more else 20), 60),
            name=name,
        )(p, *more)

    return call


def feed_windows(grid):
    units = FF // grid.n
    window = 128 * max(-(-((c * units) % 128 + units) // 128) for c in range(grid.n))
    return units, window, lambda c: ((c * units) // 128) * 128


def attention_sums(grid, p, gate_codes, up_codes, cid):
    n, levels = grid.n, grid.planes // 2
    rows_d = gate_codes.shape[0]
    flat = rows_d % 16 == 0
    units, window, start = feed_windows(grid)
    ss = share_sems(grid, 2)

    def tasks(at, ins, outs, refs):
        def source(ref):
            return lambda to: ref.at[:, pl.ds(pl.multiple_of(start(to), 128), window)]

        def view(ref):
            return lambda j: ref.at[pl.ds(j * rows_d, rows_d)] if flat else ref.at[j]

        return [share_task(at, [source(r) for r in ins], [view(r) for r in outs], *refs.take(len(ss)))]

    shape = (n * rows_d, window) if flat else (n, rows_d, window)
    call = scatter_kernel(
        grid,
        levels,
        cid,
        "attention_sums",
        (tasks, [INVMEM, INVMEM], (jax.ShapeDtypeStruct(shape, BF16),) * 2, (ANY, ANY), ss),
    )
    return in_parts(grid, levels, call, p, (gate_codes, up_codes))


def feed_sums(grid, p, cid):
    return in_parts(grid, grid.planes, scatter_kernel(grid, grid.planes, cid, "feed_sums"), p, None)[0]


def feed_back_sums(grid, p, pair_grad, cid):
    rs = return_scratch(grid, pair_grad.shape[1:])

    def tasks(at, ins, outs, refs):
        return [return_task(at, ins[0], outs[0], *refs.take(len(rs)))]

    call = scatter_kernel(
        grid,
        grid.planes,
        cid,
        "feed_back_sums",
        (tasks, [ANY], (jax.ShapeDtypeStruct(pair_grad.shape, BF16),), (ANY,), rs),
    )
    return in_parts(grid, grid.planes, call, p, (pair_grad,))


def attention_back_sums(grid, p, qkv_grad, out_grad, down_grad, gains, merged, cid):
    n, levels = grid.n, grid.planes // 2
    rs, hs = return_scratch(grid, qkv_grad.shape[1:]), head_return_scratch(grid, out_grad.shape[1:])
    ps = [pltpu.VMEM(down_grad.shape, BF16), dma(2)]
    every = pltpu.VMEM((n,) + gains.shape, F32)
    gs = [pltpu.VMEM(gains.shape, F32), pltpu.VMEM(gains.shape, F32), every, dma(2)] + share_sems(grid, 1)
    us = assemble_scratch(grid) if merged else []
    rows, width = p.shape[2:]
    tail = [pltpu.VMEM((2, rows, width), BF16), dma(2)] if merged else []
    inputs = [qkv_grad, out_grad, down_grad, gains] + list(merged)
    in_specs = [ANY, ANY, INVMEM, INVMEM] + ([ANY] + [INVMEM] * 3 if merged else [])
    shapes = (
        jax.ShapeDtypeStruct(qkv_grad.shape, BF16),
        jax.ShapeDtypeStruct(out_grad.shape, BF16),
        jax.ShapeDtypeStruct(down_grad.shape, BF16),
        jax.ShapeDtypeStruct(gains.shape, F32),
    ) + (jax.ShapeDtypeStruct((D // n, FF), BF16),) * (2 if merged else 0)
    out_specs = (ANY, ANY, INVMEM, INVMEM) + ((ANY, ANY) if merged else ())
    sums = [pltpu.VMEM((2, rows, width), BF16)] if merged else []
    scratch = sums + rs + hs + ps + gs + us + tail

    def tasks(at, ins, outs, refs):
        made = [
            return_task(at, ins[0], outs[0], *refs.take(len(rs)), per=PER),
            head_return_task(at, ins[1], outs[1], *refs.take(len(hs))),
            pair_task(at, ins[2], outs[2], *refs.take(2)),
            gains_task(at, ins[3], outs[3], *refs.take(len(gs))),
        ]
        if merged:
            made.insert(0, assemble_task(grid, ins[4], outs[4:6], *refs.take(len(us))))
        return made

    def end(at, ins, sums, out_ref, refs):
        kept, sems = refs.take(2)
        grad_ref, tokens_ref, gain_ref = ins[5:8]

        def one(u, r):
            dy, v = sums[u, r].astype(F32), tokens_ref[u, r].astype(F32)
            kept[u, r] = (grad_ref[u, r] + norm_back(v, inverse_rms(v), dy * gain_ref[0:1])).astype(BF16)

        each_rows(2, rows, one)
        issue, finish = swap_task(at, kept.at[1 - at.member], out_ref, sems)
        run(issue)
        out_ref[at.member] = kept[at.member]
        return finish

    call = scatter_kernel(
        grid,
        levels,
        cid,
        "attention_back_sums",
        (tasks, in_specs, shapes, out_specs, scratch),
        end if merged else None,
    )
    return in_parts(grid, levels, call, p, inputs)


SCALE = HEAD ** (-0.5)


def rotated(u, cosine, sine):
    half = u.shape[1] // 2
    first, second = u[:, :half], u[:, half:]
    return jnp.concatenate([first * cosine - second * sine, second * cosine + first * sine], axis=1)


def scores(q, k, start, first):
    bent = jnp.tanh(dot_t(q, k) * (SCALE / cap_limit))
    key = lax.broadcasted_iota(jnp.int32, bent.shape, 1)
    query = first + lax.broadcasted_iota(jnp.int32, bent.shape, 0)
    return jnp.where((key <= query) & (key >= start), jnp.exp(cap_limit * bent), 0.0), bent


def scale_rows(core, member, codes, column_scale, into, rows):
    step = member_step(core, 2, member)
    offset = jnp.where(step > 1.0, 0.5 * step, 0.0)

    def one(i, carry):
        r = pl.ds(pl.multiple_of(i * 16, 16), 16)
        level = jnp.floor(codes[r].astype(F32) * (1.0 / step)) * step + offset
        into[r] = (level * column_scale).astype(BF16)
        return carry

    lax.fori_loop(0, rows // 16, one, 0)


def attention_body(w, o, x_rows, put, ready, cos_ref, sin_ref, start_ref, q_ref, k_ref, v_ref, a_ref, t_ref, block=256):
    length = q_ref.shape[0]
    for i in range(length // block):
        r = pl.ds(i * block, block)
        lin = dot(x_rows(i), w[...])
        q_ref[r] = rotated(lin[:, :HEAD], cos_ref[r], sin_ref[r]).astype(BF16)
        k_ref[r] = rotated(lin[:, HEAD : 2 * HEAD], cos_ref[r], sin_ref[r]).astype(BF16)
        v_ref[r] = lin[:, 2 * HEAD :].astype(BF16)
    ready()
    for i in range(length // block):
        r, keys = pl.ds(i * block, block), pl.ds(0, (i + 1) * block)
        e, _ = scores(q_ref[r], k_ref[keys], start_ref[r], i * block)
        total = jnp.sum(e, axis=1, keepdims=True)
        attended = (dot(e.astype(BF16), v_ref[keys]) / total).astype(BF16)
        a_ref[r] = attended
        t_ref[r] = total
        put(i, dot(attended, o[...]).astype(BF16))


def attention_backward(seen, grad, w, o, q, k, v, attended, totals, vectors, cosine, sine, start):
    length = seen.shape[0]
    block, tile = 256, 256

    def kernel(
        x_ref, g_ref, w_ref, o_ref, q_ref, k_ref, v_ref, a_ref, t_ref, vec_ref, cos_ref, sin_ref, start_ref,
        part_ref, wg_ref, og_ref, gain_ref, xs, gs, dk, dv, low, sems,
    ):
        load_g = pltpu.make_async_copy(g_ref, gs, sems.at[0])
        load_x = pltpu.make_async_copy(x_ref, xs, sems.at[1])
        load_g.start()
        load_x.start()
        dk[...] = jnp.zeros_like(dk)
        dv[...] = jnp.zeros_like(dv)
        load_g.wait()
        for i in range(length // block):
            r, keys = pl.ds(i * block, block), pl.ds(0, (i + 1) * block)
            grad_attended = dot_t(gs[r], o_ref[...])
            total = t_ref[r]
            grad_sums = (grad_attended / total).astype(BF16)
            offset = jnp.sum(grad_attended * a_ref[r].astype(F32), axis=1, keepdims=True) / total
            e, bent = scores(q_ref[r], k_ref[keys], start_ref[r], i * block)
            grad_e = dot_t(grad_sums, v_ref[keys]) - offset
            grad_s = (e * grad_e * (1.0 - bent * bent)).astype(BF16)
            dv[keys] += t_dot(e.astype(BF16), grad_sums)
            dk[keys] += t_dot(grad_s, q_ref[r])
            low[r, :HEAD] = rotated(dot(grad_s, k_ref[keys]) * SCALE, cos_ref[r], -sin_ref[r]).astype(BF16)
        for i in range(length // block):
            r = pl.ds(i * block, block)
            low[r, HEAD : 2 * HEAD] = rotated(dk[r] * SCALE, cos_ref[r], -sin_ref[r]).astype(BF16)
            low[r, 2 * HEAD :] = dv[r].astype(BF16)
        load_x.wait()
        gain_ref[...] = jnp.zeros_like(gain_ref)

        def parts(i, carry):
            r = pl.ds(pl.multiple_of(i * block, block), block)
            term = dot_t(low[r], w_ref[...])
            part_ref[r] = term.astype(BF16)
            gain_ref[...] += jnp.sum(term * xs[r].astype(F32), axis=0, keepdims=True)
            return carry

        lax.fori_loop(0, length // block, parts, 0)
        gain_ref[...] = gain_ref[...] / vec_ref[0:1]

        def grads(j, carry):
            cols = pl.ds(pl.multiple_of(j * tile, tile), tile)
            wg_ref[cols] = t_dot(xs[:, cols], low[...]).astype(BF16)
            og_ref[:, cols] = t_dot(a_ref[...], gs[:, cols]).astype(BF16)
            return carry

        lax.fori_loop(0, D // tile, grads, 0)

    return pl.pallas_call(
        kernel,
        out_shape=(
            jax.ShapeDtypeStruct((length, D), BF16),
            jax.ShapeDtypeStruct((D, 3 * HEAD), BF16),
            jax.ShapeDtypeStruct((HEAD, D), BF16),
            jax.ShapeDtypeStruct((1, D), F32),
        ),
        in_specs=[ANY, ANY] + [INVMEM] * 11,
        out_specs=(INVMEM,) * 4,
        scratch_shapes=[
            pltpu.VMEM(seen.shape, BF16),
            pltpu.VMEM(seen.shape, BF16),
            pltpu.VMEM((length, HEAD), F32),
            pltpu.VMEM((length, HEAD), F32),
            pltpu.VMEM((length, 3 * HEAD), BF16),
            dma(2),
        ],
        compiler_params=pltpu.CompilerParams(vmem_limit_bytes=60 * 2**20),
        name="attention_backward",
    )(seen, grad, w, o, q, k, v, attended, totals, vectors, cosine, sine, start)


def inverse_rms(v):
    return lax.rsqrt(jnp.mean(v * v, axis=-1, keepdims=True) + 1e-06)


def norm_back(v, r, weighted):
    return r * weighted - v * (r * r * r * jnp.mean(weighted * v, axis=-1, keepdims=True))


def each_rows(group, rows, step):
    def one(i, carry):
        step(i // (rows // 16), pl.ds(pl.multiple_of((i % (rows // 16)) * 16, 16), 16))
        return carry

    lax.fori_loop(0, group * (rows // 16), one, 0)


def fits(grid, rows):
    return (D // grid.n) % 16 == 0 and scatter_parts(grid, grid.planes, rows, D) == 1


def forward_kernel(
    grid, seen, qkv_codes, out_codes, qkv_scale, cosine, sine, begins, tokens, cotangent, gate_codes, up_codes, down_codes,
    pair_scale, vectors, cid,
):
    n, levels = grid.n, grid.planes
    group, rows, _ = tokens.shape
    rows_d = gate_codes.shape[0]
    units, window, start = feed_windows(grid)
    size = feed_blocks(grid)
    sc = scatter_scratch(grid, levels // 2, rows, D)
    ss = share_sems(grid, 2)
    ws, gs = FeedWeights.scratch(group, units, window), level_sems(grid, levels)

    length = seen.shape[0]
    block = 256
    here = block // rows
    hs = head_rows_sems(grid)

    def kernel(
        x_ref, codes_ref, rows_ref, scale_ref, cos_ref, sin_ref, start_ref, tokens_ref, cot_ref, gate_ref, up_ref, down_ref,
        ps_ref, vec_ref,
        w_ref, o_ref, q_ref, k_ref, v_ref, a_ref, t_ref,
        kept_cot_ref, raw_ref, mixed_ref, all_ref, pair_ref, part_ref, wp_ref, wd_ref, *scratch,
    ):
        refs = Split(scratch)
        half_at, at = Place(grid, levels // 2), Place(grid, levels)
        mine = refs.take(len(sc))
        share_refs = refs.take(len(ss))
        weights = FeedWeights(at, group, units, None, None, down_ref, (wp_ref, wd_ref), refs.take(len(ws)))
        gather_refs = refs.take(len(gs))
        x, xs, o_codes, head_sems, cot_sems = refs.take(5)
        head_refs = refs.take(len(hs))
        loads, stores, compute = forward_chunks(weights, all_ref, pair_ref, part_ref, *refs.take(4))
        w = weights.pair.at[0, :, pl.ds(0, 3 * HEAD)]
        w_codes = weights.pair.at[1, :, pl.ds(0, 3 * HEAD)]
        o = weights.down.at[0, pl.ds(0, HEAD)]
        acc = mine[0]
        load_w = pltpu.make_async_copy(codes_ref, w_codes, head_sems.at[0])
        load_x = pltpu.make_async_copy(x_ref, xs, head_sems.at[1])
        load_w.start()
        load_x.start()
        weights.sources = (None, None, down_ref)
        weights.load()
        at.greet_all()

        def source(ref):
            return lambda to: ref.at[:, pl.ds(pl.multiple_of(start(to), 128), window)]

        def view(k):
            return lambda j: weights.codes.at[
                pl.ds(pl.multiple_of(j * rows_d, 16), rows_d), pl.ds(k * window, window)
            ]

        heads, heads_finish = head_rows_task(at, rows_ref, o_codes, *head_refs)
        run(heads)
        issue, finish = share_task(at, [source(gate_ref), source(up_ref)], [view(0), view(1)], *share_refs)
        load_w.wait()
        scale_rows(at.b, at.member, w_codes, scale_ref[...], w, D)
        keep_w = pltpu.make_async_copy(w, w_ref, head_sems.at[2])
        keep_o = pltpu.make_async_copy(o, o_ref, head_sems.at[3])
        keep_w.start()
        load_x.wait()

        def ready():
            heads_finish()
            for _ in range(EARLY):
                next(issue, None)
            each = o_codes.shape[1]
            for j in range(o_codes.shape[0]):
                scale_rows(at.b, at.member, o_codes.at[j], vec_ref[4:5], o.at[pl.ds(j * each, each)], each)
            keep_o.start()

        def put(i, value):
            first = i * here
            half = grid.n // 2
            acc[first // half, pl.ds(first % half, here)] = value.reshape(here, rows, D)

        attention_body(
            w,
            o,
            lambda i: xs[pl.ds(i * block, block)],
            put,
            ready,
            cos_ref,
            sin_ref,
            start_ref,
            q_ref,
            k_ref,
            v_ref,
            a_ref,
            t_ref,
        )
        for _ in scatter_steps(half_at, raw_ref, *mine):
            next(issue, None)

        def norms(u, r):
            raw = raw_ref[u, r].astype(F32)
            mixed = tokens_ref[u, r].astype(F32) + raw * inverse_rms(raw) * vec_ref[1:2]
            mixed_ref[u, r] = mixed
            x[u, r] = (mixed * inverse_rms(mixed) * vec_ref[2:3]).astype(BF16)

        each_rows(group, rows, norms)
        moving = LevelGather(False, at, x, all_ref, *gather_refs)
        moving.begin()
        run(issue)
        give_cot, take_cot = swap_task(at, cot_ref.at[1 - at.member], kept_cot_ref, cot_sems)
        run(give_cot)
        kept_cot_ref[at.member] = cot_ref[at.member]

        def first():
            finish()
            keep_w.wait()
            keep_o.wait()
            weights.make(ps_ref, vec_ref.at[5:6])

        moving.run(lambda zj, fresh: each_chunk(grid, zj, fresh, loads, stores, compute), first)
        for copy in stores(0):
            copy.wait()
        weights.finish()
        take_cot()

    def blocks(width):
        return jax.ShapeDtypeStruct((group, n, rows, width), BF16)

    head = jax.ShapeDtypeStruct((length, HEAD), BF16)
    return pl.pallas_call(
        kernel,
        out_shape=(
            jax.ShapeDtypeStruct((D, 3 * HEAD), BF16),
            jax.ShapeDtypeStruct((HEAD, D), BF16),
            head,
            head,
            head,
            head,
            jax.ShapeDtypeStruct((length, 1), F32),
            jax.ShapeDtypeStruct(tokens.shape, BF16),
            jax.ShapeDtypeStruct(tokens.shape, BF16),
            jax.ShapeDtypeStruct(tokens.shape, F32),
            blocks(D),
            blocks(2 * window),
            blocks(D),
            jax.ShapeDtypeStruct((group, D, 2 * window), BF16),
            jax.ShapeDtypeStruct((group, window, D), BF16),
        ),
        in_specs=[ANY, ANY] + [INVMEM] * 7 + [ANY] * 3 + [INVMEM] * 2,
        out_specs=(ANY, ANY) + (INVMEM,) * 8 + (ANY,) * 5,
        scratch_shapes=sc
        + ss
        + ws
        + gs
        + [
            pltpu.VMEM(tokens.shape, BF16),
            pltpu.VMEM(seen.shape, BF16),
            pltpu.VMEM((n // HEADS,) + out_codes.shape, BF16),
            dma(4),
            dma(2),
        ]
        + hs
        + chunk_buffers(size, rows, D, 2 * window, D)
        + [dma(3)],
        compiler_params=params(cid, 62),
        name="forward",
    )(
        seen, qkv_codes, out_codes, qkv_scale, cosine, sine, begins, tokens, cotangent, gate_codes, up_codes, down_codes,
        pair_scale, vectors,
    )


def turn_kernel(grid, p, mixed, cotangent, pair, pair_matrices, down_matrices, vectors, cid):
    n, levels = grid.n, grid.planes
    group, rows, _ = mixed.shape
    units, window, _ = feed_windows(grid)
    size = feed_blocks(grid)
    sc, gs = split_scratch(grid, levels, rows, D), level_sems(grid, levels)

    def kernel(
        p_ref, mixed_ref, cot_ref, pair_ref, wp_ref, wd_ref, vec_ref,
        out_ref, gain_ref, all_ref, part_ref, dgu_ref, hid_ref, *scratch,
    ):
        refs = Split(scratch)
        at = Place(grid, levels)
        mine, gather_refs = refs.take(len(sc)), refs.take(len(gs))
        raw, x, kept_out, wp, wd, fetch_sems, swap_sems = refs.take(7)
        load = pltpu.make_async_copy(p_ref, mine[0], mine[7].at[0])
        load.start()
        fetch = [
            pltpu.make_async_copy(wp_ref, wp, fetch_sems.at[0]),
            pltpu.make_async_copy(wd_ref, wd, fetch_sems.at[1]),
        ]
        loads, stores, compute = backward_chunks(
            wp, wd, all_ref, pair_ref, part_ref, dgu_ref, hid_ref, *refs.take(6)
        )
        at.greet_near(True)
        load.wait()
        for copy in fetch:
            copy.start()
        run(split_scatter_steps(at, raw, *mine))
        gain_ref[...] = jnp.zeros_like(gain_ref)

        def norms(u, r):
            v, dy = raw[u, r].astype(F32), cot_ref[u, r].astype(F32)
            inverse, gain = inverse_rms(v), vec_ref[3:4]
            kept_out[u, r] = (mixed_ref[u, r] + v * inverse * gain).astype(BF16)
            x[u, r] = norm_back(v, inverse, dy * gain).astype(BF16)
            gain_ref[...] += jnp.sum(dy * v * inverse, axis=0, keepdims=True)

        each_rows(group, rows, norms)
        moving = LevelGather(True, at, x, all_ref, *gather_refs)
        moving.begin()
        give_out, take_out = swap_task(at, kept_out.at[1 - at.member], out_ref, swap_sems)
        run(give_out)
        out_ref[at.member] = kept_out[at.member]
        for copy in fetch:
            copy.wait()

        moving.run(lambda zj, fresh: each_chunk(grid, zj, fresh, loads, stores, compute))
        take_out()
        for copy in stores(0):
            copy.wait()

    def blocks(width):
        return jax.ShapeDtypeStruct((group, n, rows, width), BF16)

    return pl.pallas_call(
        kernel,
        out_shape=(
            jax.ShapeDtypeStruct(mixed.shape, BF16),
            jax.ShapeDtypeStruct((1, D), F32),
            blocks(D),
            blocks(D),
            blocks(2 * window),
            blocks(window),
        ),
        in_specs=[ANY, INVMEM, INVMEM, ANY, ANY, ANY, INVMEM],
        out_specs=(INVMEM, INVMEM) + (ANY,) * 4,
        scratch_shapes=sc
        + gs
        + [
            pltpu.VMEM(mixed.shape, BF16),
            pltpu.VMEM(mixed.shape, BF16),
            pltpu.VMEM(mixed.shape, BF16),
            pltpu.VMEM((group, D, 2 * window), BF16),
            pltpu.VMEM((group, window, D), BF16),
            dma(2),
            dma(2),
        ]
        + chunk_buffers(size, rows, D, 2 * window, D, 2 * window, window)
        + [dma(5)],
        compiler_params=params(cid, 62),
        name="turn",
    )(p, mixed, cotangent, pair, pair_matrices, down_matrices, vectors)


def back_kernel(grid, p, fed, down_low, pair_low, hidden, mixed, raw, cotangent, vectors, cid):
    n, levels = grid.n, grid.planes
    group, rows, _ = mixed.shape
    units, window, _ = feed_windows(grid)
    size = feed_blocks(grid)
    chunks = n // size
    count = group * size * rows
    rows_d = D // n
    half = n // 2
    tile = 256
    sc, gs = scatter_scratch(grid, levels, rows, D), gather_sems(grid, levels // 2)
    rs = return_scratch(grid, (rows_d, 2 * window))

    def kernel(
        p_ref, fed_ref, low_ref, dgu_ref, hid_ref, mixed_ref, raw_ref, cot_ref, vec_ref,
        grad_ref, feed_ref, post_ref, all_ref, got_ref, down_ref, *scratch,
    ):
        refs = Split(scratch)
        half_at, at = Place(grid, levels // 2), Place(grid, levels)
        mine, gather_refs, return_refs = refs.take(len(sc)), refs.take(len(gs)), refs.take(len(rs))
        raw2, x, xs, ys, dgu, hid, pair_sum, down_sum, given, down_out, sems = refs.take(11)
        load = pltpu.make_async_copy(p_ref, mine[0], mine[4].at[0])
        load.start()

        def loads(i):
            at_blocks = pl.ds(i * size, size)
            return [
                pltpu.make_async_copy(fed_ref.at[:, at_blocks], xs, sems.at[0]),
                pltpu.make_async_copy(low_ref.at[:, at_blocks], ys, sems.at[1]),
                pltpu.make_async_copy(dgu_ref.at[:, at_blocks], dgu, sems.at[2]),
                pltpu.make_async_copy(hid_ref.at[:, at_blocks], hid, sems.at[3]),
            ]

        for copy in loads(0):
            copy.start()
        at.greet_all()
        load.wait()

        def sums(i):
            def one(j, carry):
                cols = pl.ds(pl.multiple_of(j * tile, tile), tile)
                pair_term = t_dot(xs[:, :, :, cols].reshape(count, tile), dgu[...].reshape(count, 2 * window))
                down_term = t_dot(hid[...].reshape(count, window), ys[:, :, :, cols].reshape(count, tile))
                if i == 0:
                    pair_sum[cols] = pair_term
                    down_sum[:, cols] = down_term
                else:
                    pair_sum[cols] = pair_sum[cols] + pair_term
                    down_sum[:, cols] = down_sum[:, cols] + down_term
                return carry

            for copy in loads(i):
                copy.wait()
            lax.fori_loop(0, D // tile, one, 0)
            if i + 1 < chunks:
                for copy in loads(i + 1):
                    copy.start()

        to, _ = pairwise(n, at.c, at.b)
        other_to, _ = pairwise(n, at.c, 1 - at.b)
        give_down = pltpu.make_async_copy(down_out, down_ref, sems.at[4])

        def lowered(i):
            def one(r, carry):
                here = pl.ds(pl.multiple_of(r * 16, 16), 16)
                mine_at = pl.ds(pl.multiple_of(to(i) * rows_d + r * 16, 16), 16)
                other_at = pl.ds(pl.multiple_of(other_to(i) * rows_d + r * 16, 16), 16)
                return_refs[0][i, here] = pair_sum[mine_at].astype(BF16)
                given[i, here] = pair_sum[other_at].astype(BF16)
                return carry

            lax.fori_loop(0, rows_d // 16, one, 0)

        def lowered_down():
            def one(r, carry):
                here = pl.ds(pl.multiple_of(r * 16, 16), 16)
                down_out[here] = down_sum[here].astype(BF16)
                return carry

            lax.fori_loop(0, window // 16, one, 0)
            give_down.start()

        def prepare():
            for i in range(chunks):
                sums(i)
                if i % 2 == 1:
                    yield
            lowered_down()

        issue, finish = return_task(at, None, got_ref, *return_refs, given=given, fill=lowered, prepare=prepare)

        def main():
            yield from scatter_steps(at, raw2, *mine)
            feed_ref[...] = jnp.zeros_like(feed_ref)
            post_ref[...] = jnp.zeros_like(post_ref)

            def norms(u, r):
                dy, v = raw2[u, r].astype(F32), mixed_ref[u, r]
                inverse = inverse_rms(v)
                grad = cot_ref[u, r].astype(F32) + norm_back(v, inverse, dy * vec_ref[2:3])
                feed_ref[...] += jnp.sum(dy * v * inverse, axis=0, keepdims=True)
                grad_ref[u, r] = grad
                w = raw_ref[u, r].astype(F32)
                inverse = inverse_rms(w)
                x[u, r] = norm_back(w, inverse, grad * vec_ref[1:2]).astype(BF16)
                post_ref[...] += jnp.sum(grad * w * inverse, axis=0, keepdims=True)

            each_rows(group, rows, norms)
            yield from gather_steps(half_at, x, all_ref, *gather_refs)

        together(main(), (issue, finish))
        give_down.wait()

    return pl.pallas_call(
        kernel,
        out_shape=(
            jax.ShapeDtypeStruct(mixed.shape, F32),
            jax.ShapeDtypeStruct((1, D), F32),
            jax.ShapeDtypeStruct((1, D), F32),
            jax.ShapeDtypeStruct((2, half, rows, D), BF16),
            jax.ShapeDtypeStruct((n, rows_d, 2 * window), BF16),
            jax.ShapeDtypeStruct((window, D), BF16),
        ),
        in_specs=[ANY] * 5 + [INVMEM] * 4,
        out_specs=(INVMEM,) * 3 + (ANY,) * 3,
        scratch_shapes=sc
        + gs
        + rs
        + [
            pltpu.VMEM(mixed.shape, BF16),
            pltpu.VMEM(mixed.shape, BF16),
            pltpu.VMEM((group, size, rows, D), BF16),
            pltpu.VMEM((group, size, rows, D), BF16),
            pltpu.VMEM((group, size, rows, 2 * window), BF16),
            pltpu.VMEM((group, size, rows, window), BF16),
            pltpu.VMEM((D, 2 * window), F32),
            pltpu.VMEM((window, D), F32),
            pltpu.VMEM((half, rows_d, 2 * window), BF16),
            pltpu.VMEM((window, D), BF16),
            dma(5),
        ],
        compiler_params=params(cid, 63),
        name="back",
    )(p, fed, down_low, pair_low, hidden, mixed, raw, cotangent, vectors)


def assemble_task(grid, got_ref, targets, wide, high, load_sem, stores):
    n = grid.n
    units, window, _ = feed_windows(grid)
    inner = n // HEADS
    whole = inner * units
    starts = [i * units // 128 * 128 for i in range(inner)]
    load = pltpu.make_async_copy(got_ref, wide, load_sem.at[0])

    def store(k):
        return pltpu.make_async_copy(high.at[k], targets[k], stores.at[k])

    def put(g, k):
        for t in range(0, whole, 128):
            total = 0.0
            for i in range(inner):
                if 0 <= t - starts[i] < window:
                    total = total + wide[g * inner + i, :, pl.ds(k * window + t - starts[i], 128)].astype(F32)
            high[k, :, pl.ds(pl.multiple_of(g * whole + t, 128), 128)] = total.astype(BF16)

    def issue():
        load.start()
        yield
        yield
        load.wait()
        for k in range(2):

            def one(g, carry):
                put(g, k)
                return carry

            lax.fori_loop(0, n // inner, one, 0)
            store(k).start()
            yield

    def finish():
        for k in range(2):
            store(k).wait()

    return issue(), finish


def assemble_scratch(grid):
    _, window, _ = feed_windows(grid)
    rows_d = D // grid.n
    return [pltpu.VMEM((grid.n, rows_d, 2 * window), BF16), pltpu.VMEM((2, rows_d, FF), BF16), dma(1), dma(2)]


def gains_task(at, x_ref, out_ref, total, other, every, sems, *share_refs):
    copy = at.sibling(x_ref, other, sems.at[0], sems.at[1])
    later, end = share_task(at, [lambda to: total], [lambda j: every.at[j]], *share_refs)

    def issue():
        copy.start()
        yield
        copy.wait()
        total[...] = x_ref[...] + other[...]
        yield from later

    def finish():
        end()
        out_ref[...] = jnp.sum(every[...], axis=0)

    return issue(), finish


def normed(value, gain):
    return value * lax.rsqrt(jnp.mean(value * value, axis=-1, keepdims=True) + 1e-06) * gain


def angles(places, head):
    freqs = 10000.0 ** (-(jnp.arange(head // 2, dtype=F32) * 2.0 / head))
    return places.astype(F32)[..., None] * freqs


def rotate(values, cosine, sine):
    half = values.shape[-1] // 2
    first = values[..., :half]
    second = values[..., half:]
    return jnp.concatenate([first * cosine - second * sine, second * cosine + first * sine], axis=-1)


def width_step(number):
    remainder = number % 3
    return jnp.where(remainder == 0, 1.0, jnp.where(remainder == 1, 16.0, 64.0)).astype(F32)


def dequantized(codes, column_scale, step):
    offset = jnp.where(step > 1.0, 0.5 * step, 0.0)
    level = jnp.floor(codes.astype(F32) / step) * step + offset
    return (level * column_scale[None, :]).astype(BF16)


def dot(left, right):
    return jnp.dot(left, right, preferred_element_type=F32)


def dot_t(left, right):
    return lax.dot_general(left, right, (((1,), (1,)), ((), ())), preferred_element_type=F32)


def t_dot(left, right):
    return lax.dot_general(left, right, (((0,), (0,)), ((), ())), preferred_element_type=F32)


def unwindowed(grid, got):
    n, rows, window = got.shape
    units = FF // n
    inner = n // HEADS
    whole = inner * units
    got = got.astype(F32).reshape(n // inner, inner, rows, window)
    total = 0.0
    for i in range(inner):
        start = i * units // 128 * 128
        total = total + jnp.pad(got[:, i], ((0, 0), (0, 0), (start, whole - start - window)))
    return jnp.transpose(total, (1, 0, 2)).reshape(rows, FF)


def on_device(
    grid,
    tokens,
    segments,
    positions,
    cotangent,
    query_codes,
    key_codes,
    value_codes,
    output_codes,
    gate_codes,
    up_codes,
    down_codes,
    query_scale,
    key_scale,
    value_scale,
    output_scale,
    gate_scale,
    up_scale,
    down_scale,
    attention_gain,
    attention_post_gain,
    feed_gain,
    feed_post_gain,
):
    n = grid.n
    group, block, _ = tokens.shape
    length = n * block
    pairs = HEADS // KV_HEADS
    scale = HEAD ** (-0.5)
    chip, core = lax.axis_index("seq"), lax.axis_index("batch")
    half = n // 2
    member = chip // half
    head = chip % HEADS
    kv_head = head // pairs
    parts = half // HEADS
    copies = n // HEADS
    asked = length // parts
    first_asked = ((chip % half) // HEADS) * asked
    steps = [width_step(core * group + m) for m in range(group)]
    step = width_step(core * group + member)
    rows_d = D // n
    units, window, _ = feed_windows(grid)

    whole = fits(grid, block) and parts == 1
    vectors = jnp.stack(
        [attention_gain, attention_post_gain, feed_gain, feed_post_gain, output_scale, down_scale]
    )

    q_parts = jnp.transpose(query_codes.reshape(rows_d, HEADS, HEAD), (1, 0, 2))
    k_parts = jnp.repeat(jnp.transpose(key_codes.reshape(rows_d, KV_HEADS, HEAD), (1, 0, 2)), pairs, axis=0)
    v_parts = jnp.repeat(jnp.transpose(value_codes.reshape(rows_d, KV_HEADS, HEAD), (1, 0, 2)), pairs, axis=0)
    qkv_parts = jnp.concatenate([q_parts, k_parts, v_parts], axis=-1).astype(BF16)
    small = jnp.zeros((8, 128), jnp.int32).at[:group, :block].set(positions)
    tokens, seen, qkv_codes, out_codes, all_places, gate_low, up_low = open_kernel(
        grid,
        tokens,
        vectors,
        qkv_parts,
        output_codes.astype(BF16),
        small,
        gate_codes,
        up_codes,
        not whole,
        1,
    )
    seen = seen.reshape(length, D)

    qkv_scale = jnp.concatenate(
        [
            lax.dynamic_slice_in_dim(query_scale, head * HEAD, HEAD),
            lax.dynamic_slice_in_dim(key_scale, kv_head * HEAD, HEAD),
            lax.dynamic_slice_in_dim(value_scale, kv_head * HEAD, HEAD),
        ]
    )
    def swapped_back(kept):
        own, other = (lax.dynamic_index_in_dim(kept, u, 0, False) for u in (member, 1 - member))
        other = lax.ppermute(other, "seq", [(c, (c + half) % n) for c in range(n)])
        return jnp.where(member == 0, jnp.stack([own, other]), jnp.stack([other, own]))

    def spread(part):
        if parts > 1:
            part = lax.dynamic_update_slice_in_dim(jnp.zeros((length, D), BF16), part, first_asked, 0)
        return part.reshape(2, half, block, D)

    places_all = lax.dynamic_index_in_dim(all_places[:, :group, :block], member, 1, False).reshape(length)
    turn = angles(places_all, HEAD)
    cosine, sine = jnp.cos(turn), jnp.sin(turn)
    q_index = first_asked + jnp.arange(asked, dtype=jnp.int32)
    pair_scale = jnp.concatenate(
        [lax.dynamic_slice_in_dim(s, chip * units // 128 * 128, window) for s in (gate_scale, up_scale)]
    )[None]
    if whole:
        start = (q_index - places_all)[:, None]
        (
            *kept_heads, cotangent, attention_raw, mixed, fed, gate_up, down_part, pair_matrices, down_matrices,
        ) = forward_kernel(
            grid,
            seen,
            qkv_codes.reshape(D, 3 * HEAD),
            out_codes,
            qkv_scale[None],
            cosine,
            sine,
            start,
            tokens,
            cotangent,
            gate_low,
            up_low,
            down_codes,
            pair_scale,
            vectors,
            2,
        )
    else:
        qkv_matrix = dequantized(qkv_codes.reshape(D, 3 * HEAD), qkv_scale, step)
        out_matrix = dequantized(out_codes.reshape(HEAD, D), output_scale, step)
        if parts == 1:
            seen_asked, places_asked, cosine_q, sine_q = seen, places_all, cosine, sine
            projected = dot(seen, qkv_matrix)
            q_lin, kv_lin = projected[:, :HEAD], projected[:, HEAD:]
        else:
            seen_asked, places_asked, cosine_q, sine_q = [
                lax.dynamic_slice_in_dim(a, first_asked, asked) for a in (seen, places_all, cosine, sine)
            ]
            q_lin, kv_lin = dot(seen_asked, qkv_matrix[:, :HEAD]), dot(seen, qkv_matrix[:, HEAD:])
        queries = rotate(q_lin, cosine_q, sine_q).astype(BF16)
        keys = rotate(kv_lin[:, :HEAD], cosine, sine).astype(BF16)
        values = kv_lin[:, HEAD:].astype(BF16)
        key_index = jnp.arange(length, dtype=jnp.int32)
        allowed = (key_index[None, :] <= q_index[:, None]) & (key_index[None, :] >= (q_index - places_asked)[:, None])
        bent = jnp.tanh(dot_t(queries, keys) * scale / cap_limit)
        kernel = jnp.where(allowed, jnp.exp(cap_limit * bent), 0.0)
        totals = jnp.sum(kernel, axis=-1, keepdims=True)
        kernel_low = kernel.astype(BF16)
        attended = dot(kernel_low, values) / totals
        attended_low = attended.astype(BF16)

        out_part = spread(dot(attended_low, out_matrix).astype(BF16))
    first_column = chip * units // 128 * 128
    inset = chip * units - first_column
    if whole:
        output, grad_post_feed, down_low, second_part, pair_low, hidden = turn_kernel(
            grid, down_part, mixed, cotangent, gate_up, pair_matrices, down_matrices, vectors, 3
        )
        grad_mixed, grad_pre_feed, grad_post_attention, attention_low, pair_got, down_grad = back_kernel(
            grid,
            second_part,
            fed,
            down_low,
            pair_low,
            hidden,
            mixed,
            attention_raw,
            cotangent,
            vectors,
            4,
        )
    else:
        cotangent = swapped_back(cotangent)
        attention_raw, gate_got, up_got = attention_sums(grid, out_part, gate_low, up_low, 2)
        attention_raw = attention_raw.astype(F32)
        feed_weights = (
            gate_got.reshape(D, window),
            up_got.reshape(D, window),
            down_codes,
            pair_scale,
            down_scale[None],
        )
        mixed = tokens.astype(F32) + normed(attention_raw, attention_post_gain)
        second_normed = normed(mixed, feed_gain).astype(BF16)
        fed, gate_up, down_part, pair_matrices, down_matrices = feed_forward(grid, second_normed, *feed_weights, 3)
        down_raw = feed_sums(grid, down_part, 4).astype(F32)
        branch, pull_out = jax.vjp(normed, down_raw, feed_post_gain)
        output = swapped_back((mixed + branch).astype(BF16))
        upstream = cotangent.astype(F32)
        grad_down_raw, grad_post_feed = pull_out(upstream)
        down_low, second_part, pair_low, hidden = feed_backward(
            grid, grad_down_raw.astype(BF16), gate_up, pair_matrices, down_matrices, 9
        )
        count = group * length
        pair_grad = t_dot(fed.reshape(count, D), pair_low.reshape(count, 2 * window)).astype(BF16)
        down_grad = t_dot(hidden.reshape(count, window), down_low.reshape(count, D)).astype(BF16)
        grad_second, pair_got = feed_back_sums(grid, second_part, pair_grad.reshape(n, rows_d, 2 * window), 5)
        gate_grad, up_grad = (unwindowed(grid, pair_got[..., i * window : (i + 1) * window]) for i in range(2))
        _, pull_feed = jax.vjp(normed, mixed, feed_gain)
        grad_mixed_part, grad_pre_feed = pull_feed(grad_second.astype(F32))
        grad_mixed = upstream + grad_mixed_part
        _, pull_post = jax.vjp(normed, attention_raw, attention_post_gain)
        grad_attention, grad_post_attention = pull_post(grad_mixed)
        attention_low = gather(grid, grad_attention.astype(BF16), grid.planes // 2, 6)
    down_grad = lax.dynamic_slice(down_grad, (inset, 0), (units, D))

    attention_low = attention_low.reshape(length, D)
    if whole:
        first_part, qkv_grad, out_part, grad_pre_attention = attention_backward(
            seen, attention_low, *kept_heads, vectors, cosine, sine, start
        )
    else:
        if parts > 1:
            attention_low = lax.dynamic_slice_in_dim(attention_low, first_asked, asked)
        grad_attended = dot_t(attention_low, out_matrix)
        grad_sums = (grad_attended / totals).astype(BF16)
        offsets = jnp.sum(grad_attended * attended, axis=-1, keepdims=True) / totals
        grad_kernel = dot_t(grad_sums, values) - offsets
        grad_raw = (kernel * grad_kernel * (1.0 - bent * bent)).astype(BF16)
        grad_q = dot(grad_raw, keys) * scale
        grad_k = t_dot(grad_raw, queries) * scale
        grad_v = t_dot(kernel_low, grad_sums)
        q_low = rotate(grad_q, cosine_q, -sine_q).astype(BF16)
        kv_low = jnp.concatenate([rotate(grad_k, cosine, -sine), grad_v], axis=-1).astype(BF16)
        if parts == 1:
            qkv_low = jnp.concatenate([q_low, kv_low], axis=-1)
            first_part = dot_t(qkv_low, qkv_matrix)
            qkv_grad = t_dot(seen, qkv_low)
        else:
            first_part = dot_t(kv_low, qkv_matrix[:, HEAD:])
            q_back = dot_t(q_low, qkv_matrix[:, :HEAD])
            first_part = lax.dynamic_update_slice_in_dim(
                first_part, lax.dynamic_slice_in_dim(first_part, first_asked, asked) + q_back, first_asked, 0
            )
            qkv_grad = jnp.concatenate([t_dot(seen_asked, q_low), t_dot(seen, kv_low)], axis=-1)
        first_part = first_part.astype(BF16)
        grad_pre_attention = jnp.sum(first_part.astype(F32) * seen.astype(F32), axis=0) / attention_gain
        out_part = t_dot(attended_low, attention_low).astype(BF16)
    gains = jnp.stack(
        [g.reshape(D) for g in (grad_pre_attention, grad_post_attention, grad_pre_feed, grad_post_feed)]
    )
    out_part = out_part.reshape(copies, HEAD // copies, D)
    merged = (pair_got, grad_mixed, tokens, vectors) if whole else ()
    grad_in, qkv_got, out_got, down_grad, gains, *assembled = attention_back_sums(
        grid,
        first_part.reshape(2, half, block, D),
        qkv_grad.astype(BF16).reshape(n, rows_d, 3 * HEAD),
        out_part,
        down_grad,
        gains,
        merged,
        7,
    )
    if merged:
        gate_grad, up_grad = (a.astype(F32) for a in assembled)
    else:
        _, pull_in = jax.vjp(lambda value: normed(value, attention_gain), tokens.astype(F32))
        (grad_source_part,) = pull_in(grad_in.astype(F32))
        grad_in = swapped_back((grad_mixed + grad_source_part).astype(BF16))
    down_grad = down_grad.astype(F32)
    qkv_got = jnp.sum(qkv_got.astype(F32).reshape(copies, HEADS, rows_d, 3 * HEAD), axis=0)
    query_grad = jnp.transpose(qkv_got[..., :HEAD], (1, 0, 2)).reshape(rows_d, HEADS * HEAD)
    kv_grad = jnp.sum(qkv_got[..., HEAD:].reshape(KV_HEADS, pairs, rows_d, 2 * HEAD), axis=1)
    key_grad = jnp.transpose(kv_grad[..., :HEAD], (1, 0, 2)).reshape(rows_d, KV_HEADS * HEAD)
    value_grad = jnp.transpose(kv_grad[..., HEAD:], (1, 0, 2)).reshape(rows_d, KV_HEADS * HEAD)
    out_grad = jnp.sum(out_got.astype(F32), axis=0)
    return (
        output,
        grad_in,
        query_grad,
        key_grad,
        value_grad,
        out_grad,
        gate_grad,
        up_grad,
        down_grad,
    ) + tuple(gains[i] for i in range(4))


def solution(mesh):
    rows = P("seq", None)
    return jax.shard_map(
        functools.partial(on_device, Grid(mesh.shape["seq"])),
        mesh=mesh,
        in_specs=(P("batch", "seq", None), P("batch", "seq"), P("batch", "seq"), P("batch", "seq", None))
        + (rows,) * 7
        + (P(),) * 11,
        out_specs=(P("batch", "seq", None),) * 2 + (rows,) * 7 + (P(),) * 4,
        check_vma=False,
    )
```

```python
import functools

import jax
import jax.numpy as jnp
from jax import lax
from jax.experimental import pallas as pl
from jax.experimental.pallas import tpu as pltpu
from jax.sharding import PartitionSpec as P

D = 2304
HEADS = 8
KV_HEADS = 4
HEAD = 256
FF = 9216
MESH = pl.DeviceIdType.MESH
F32 = jnp.float32
BF16 = jnp.bfloat16


cap_limit = 50.0


class Grid:
    def __init__(self, n):
        self.n = n
        self.planes = 4 if n % 8 == 0 else 2
        self.plane = n // self.planes
        wide = 1
        while wide * wide < self.plane:
            wide *= 2
        self.wide = wide

    def snake(self, p):
        y, x = p // self.wide, p % self.wide
        return y * self.wide + x + (y % 2) * (self.wide - 1 - 2 * x)


def remote(src, dst, send, recv, chip, core):
    return pltpu.make_async_remote_copy(
        src_ref=src, dst_ref=dst, send_sem=send, recv_sem=recv, device_id=(chip, core), device_id_type=MESH
    )


def greet(barrier, chip, core):
    pl.semaphore_signal(barrier, inc=1, device_id=(chip, core), device_id_type=MESH)


class Place:
    def __init__(self, grid, levels):
        self.grid, self.levels = grid, levels
        self.n, self.pn = grid.n, grid.plane
        self.steps = self.pn // 2
        self.c, self.b = lax.axis_index("seq"), lax.axis_index("batch")
        self.z, p = self.c // self.pn, self.c % self.pn
        self.q = grid.snake(p)
        self.zi = self.z % levels
        self.right = self.z * self.pn + grid.snake((self.q + 1) % self.pn)
        self.left = self.z * self.pn + grid.snake((self.q + self.pn - 1) % self.pn)
        self.member = self.c // (self.n // 2)
        self.partner = (self.c + self.n // 2) % self.n

    def slot(self, zj, qj):
        return zj * self.pn + self.grid.snake((qj + 2 * self.pn) % self.pn)

    def sibling(self, src, dst, send, recv):
        return remote(src, dst, send, recv, self.c, 1 - self.b)

    def greet_near(self, halves):
        barrier = pltpu.get_barrier_semaphore()
        zi, levels = self.zi, self.levels
        greet(barrier, self.right, self.b)
        greet(barrier, self.left, self.b)
        pl.when(zi > 0)(lambda: greet(barrier, self.c - self.pn, self.b))
        pl.when(zi < levels - 1)(lambda: greet(barrier, self.c + self.pn, self.b))
        if halves:
            greet(barrier, self.partner, self.b)
        count = 2 + jnp.where(zi > 0, 1, 0) + jnp.where(zi < levels - 1, 1, 0) + (1 if halves else 0)
        pl.semaphore_wait(barrier, count)

    def greet_all(self):
        barrier = pltpu.get_barrier_semaphore()
        greet(barrier, self.c, 1 - self.b)

        def one(off, carry):
            greet(barrier, (self.c + off) % self.n, self.b)
            return carry

        lax.fori_loop(1, self.n, one, 0)
        pl.semaphore_wait(barrier, self.n)


def present(zi, sign, d, levels):
    if d == 0:
        return None
    return (zi - d >= 0) if sign < 0 else (zi + d < levels)


def guarded(condition, action):
    if condition is None:
        action()
    else:
        pl.when(condition)(action)


def dma(*shape):
    return pltpu.SemaphoreType.DMA(shape)


ANY = pl.BlockSpec(memory_space=pl.ANY)
INVMEM = pl.BlockSpec(memory_space=pltpu.VMEM)


def params(cid, mib=None):
    if mib is None:
        return pltpu.CompilerParams(collective_id=cid, has_side_effects=True)
    return pltpu.CompilerParams(collective_id=cid, has_side_effects=True, vmem_limit_bytes=mib * 2**20)


def gather_sems(grid, levels, passes=1):
    steps = grid.plane // 2
    return [
        dma(passes, 2, levels),
        dma(passes, 2, levels),
        dma(passes, 2, steps, levels),
        dma(passes, 2, steps, levels),
        dma(3),
    ]


def gather_steps(at, x_ref, out_ref, zs, zr, rs, rr, ls, passes=((0, 2),), ready=None):
    levels, steps, zi, q, pn, b = at.levels, at.steps, at.zi, at.q, at.pn, at.b
    half = x_ref.shape[1] // 2
    own = at.slot(zi, q)

    def block(us, zj, qj, part=None):
        u0, nu = us
        if part is None:
            return out_ref.at[pl.ds(u0, nu), at.slot(zj, qj)]
        return out_ref.at[pl.ds(u0, nu), at.slot(zj, qj), pl.ds(part * half, half)]

    def z_copy(k, us, zj, sign):
        way = 0 if sign > 0 else 1
        ref = block(us, zj, q)
        return remote(ref, ref, zs.at[k, way, zj], zr.at[k, way, zj], (at.c + at.n + sign * pn) % at.n, b)

    def r_copy(k, us, zj, way, step, landing=False):
        away = step if landing else step - 1
        ref = block(us, zj, q - away if way == 0 else q + away, way if step == steps else None)
        to = at.right if way == 0 else at.left
        return remote(ref, ref, rs.at[k, way, step - 1, zj], rr.at[k, way, step - 1, zj], to, b)

    def arrive(k, us, sign, d):
        zj = zi + sign * d

        def go():
            if d > 0:
                z_copy(k, us, zj, -sign).wait_recv()
            if sign <= 0:
                pl.when(zi < levels - 1)(lambda: z_copy(k, us, zj, 1).start())
            if sign >= 0:
                pl.when(zi > 0)(lambda: z_copy(k, us, zj, -1).start())
            for way in (0, 1):
                r_copy(k, us, zj, way, 1).start()

        guarded(present(zi, sign, d, levels), go)

    def onward(k, us, sign, d):
        zj = zi + sign * d

        def go():
            for step in range(1, steps + 1):
                for way in (0, 1):
                    r_copy(k, us, zj, way, step, True).wait_recv()
                    if step < steps:
                        r_copy(k, us, zj, way, step + 1).start()

        guarded(present(zi, sign, d, levels), go)

    def finish(k, us, sign, d):
        zj = zi + sign * d

        def go():
            if sign <= 0:
                pl.when(zi < levels - 1)(lambda: z_copy(k, us, zj, 1).wait_send())
            if sign >= 0:
                pl.when(zi > 0)(lambda: z_copy(k, us, zj, -1).wait_send())
            for way in (0, 1):
                for step in range(1, steps + 1):
                    r_copy(k, us, zj, way, step).wait_send()

        guarded(present(zi, sign, d, levels), go)

    waves = [
        [(k, us, sign, d) for sign in ((0,) if d == 0 else (-1, 1))] for k, us in enumerate(passes) for d in range(levels)
    ]
    for i, wave in enumerate(waves):
        k, (u0, nu), _, d = wave[0]
        if d == 0:
            if ready is not None:
                ready(k)
            local = pltpu.make_async_copy(x_ref.at[pl.ds(u0, nu)], out_ref.at[pl.ds(u0, nu), own], ls.at[k])
            local.start()
            local.wait()
        for group in wave:
            arrive(*group)
            yield
        if i > 0:
            for group in waves[i - 1]:
                onward(*group)
                yield
    for group in waves[-1]:
        onward(*group)
        yield
    for wave in waves:
        for group in wave:
            finish(*group)


def run(steps):
    for _ in steps:
        pass


def gather(grid, x, levels, cid):
    count = levels * grid.plane

    def kernel(x_ref, out_ref, *sems):
        at = Place(grid, levels)
        at.greet_near(False)
        run(gather_steps(at, x_ref, out_ref, *sems))

    return pl.pallas_call(
        kernel,
        out_shape=jax.ShapeDtypeStruct((2, count) + x.shape[1:], x.dtype),
        in_specs=[INVMEM],
        out_specs=ANY,
        scratch_shapes=gather_sems(grid, levels),
        compiler_params=params(cid, 50),
        name="gather_%d" % count,
    )(x)


def level_sems(grid, levels):
    steps = grid.plane // 2
    return gather_sems(grid, levels) + [dma(2, levels), dma(2, levels), dma(2, steps), dma(2, steps)]


class LevelGather:
    def __init__(self, split, at, x_ref, out_ref, zs, zr, rs, rr, ls, lzs, lzr, lrs, lrr):
        self.at, self.x, self.out = at, x_ref, out_ref
        self.zs, self.zr, self.rs, self.rr, self.ls = zs, zr, rs, rr, ls
        self.lzs, self.lzr, self.lrs, self.lrr = lzs, lzr, lrs, lrr
        rows = x_ref.shape[1]
        cut = rows * 3 // 4 // 16 * 16 if split else rows
        self.split, self.first, self.last = split, pl.ds(0, cut), pl.ds(cut, rows - cut)

    def block(self, zj, qj, part, rows):
        which = pl.ds(0, 2) if part is None else pl.ds(part, 1)
        return self.out.at[which, self.at.slot(zj, qj), rows]

    def z_copy(self, zj, way):
        at, ref = self.at, self.block(zj, self.at.q, None, self.first)
        to = (at.c + at.n + (at.pn if way == 0 else -at.pn)) % at.n
        return remote(ref, ref, self.zs.at[0, way, zj], self.zr.at[0, way, zj], to, at.b)

    def ring_copy(self, zj, way, step, landing, rows, send, recv):
        at = self.at
        away = step if landing else step - 1
        ref = self.block(zj, at.q - away if way == 0 else at.q + away, way if step == at.steps else None, rows)
        return remote(ref, ref, send, recv, at.right if way == 0 else at.left, at.b)

    def r_copy(self, zj, way, step, landing=False):
        sems = self.rs.at[0, way, step - 1, zj], self.rr.at[0, way, step - 1, zj]
        return self.ring_copy(zj, way, step, landing, self.first, *sems)

    def low_copy(self, way, step, landing=False):
        sems = self.lrs.at[way, step - 1], self.lrr.at[way, step - 1]
        return self.ring_copy(self.at.zi, way, step, landing, self.last, *sems)

    def low_z_copy(self, zj, way):
        at = self.at
        ref = self.out.at[:, pl.ds(zj * at.pn, at.pn), self.last]
        to = (at.c + at.n + (at.pn if way == 0 else -at.pn)) % at.n
        return remote(ref, ref, self.lzs.at[way, zj], self.lzr.at[way, zj], to, at.b)

    def begin(self):
        at = self.at
        local = pltpu.make_async_copy(self.x, self.out.at[:, at.slot(at.zi, at.q)], self.ls.at[0])
        local.start()
        local.wait()
        self.send(0)
        if self.split:
            for way in (0, 1):
                self.low_copy(way, 1).start()

    def along(self, offset, copy):
        at = self.at
        zj = at.zi + offset
        pl.when((offset <= 0) & (at.zi < at.levels - 1))(lambda: copy(zj, 0).start())
        pl.when((offset >= 0) & (at.zi > 0))(lambda: copy(zj, 1).start())

    def send(self, offset):
        self.along(offset, self.z_copy)
        for way in (0, 1):
            self.r_copy(self.at.zi + offset, way, 1).start()

    def arrive(self, sign, d):
        self.z_copy(self.at.zi + sign * d, 0 if sign < 0 else 1).wait_recv()
        self.send(sign * d)

    def low_arrive(self, sign, d):
        self.low_z_copy(self.at.zi + sign * d, 0 if sign < 0 else 1).wait_recv()
        self.along(sign * d, self.low_z_copy)

    def onward(self, sign, d):
        zj = self.at.zi + sign * d
        for step in range(1, self.at.steps):
            for way in (0, 1):
                self.r_copy(zj, way, step, True).wait_recv()
                self.r_copy(zj, way, step + 1).start()

    def low_onward(self):
        for step in range(1, self.at.steps):
            for way in (0, 1):
                self.low_copy(way, step, True).wait_recv()
                self.low_copy(way, step + 1).start()

    def low_landed(self):
        for way in (0, 1):
            self.low_copy(way, self.at.steps, True).wait_recv()
        self.along(0, self.low_z_copy)

    def landed(self, sign, d):
        zj = self.at.zi + sign * d
        for way in (0, 1):
            self.r_copy(zj, way, self.at.steps, True).wait_recv()

    def finish(self):
        at = self.at

        def one(zj, carry):
            for copy in (self.z_copy, self.low_z_copy)[: 2 if self.split else 1]:
                pl.when((zj <= at.zi) & (at.zi < at.levels - 1))(lambda: copy(zj, 0).wait_send())
                pl.when((zj >= at.zi) & (at.zi > 0))(lambda: copy(zj, 1).wait_send())
            for way in (0, 1):
                for step in range(1, at.steps + 1):
                    self.r_copy(zj, way, step).wait_send()
            return carry

        lax.fori_loop(0, at.levels, one, 0)
        for way in (0, 1) if self.split else ():
            for step in range(1, at.steps + 1):
                self.low_copy(way, step).wait_send()

    def run(self, compute, first=None):
        at = self.at
        zi, levels = at.zi, at.levels

        def wave(t):
            pl.when((t < levels) & (zi - t >= 0))(lambda: self.arrive(-1, t))
            pl.when((t < levels) & (zi + t < levels))(lambda: self.arrive(1, t))

        def both(d, action, least=0):
            pl.when((d >= least) & (d < levels) & (zi - d >= 0))(lambda: action(-1, d))
            pl.when((d > 0) & (d < levels) & (zi + d < levels))(lambda: action(1, d))

        def one(t, carry):
            wave(t)
            if self.split:
                pl.when(t == 2)(self.low_landed)
            both(t - 1, self.onward)
            if first is not None:
                pl.when(t == 2)(first)
            e = t - 2
            if self.split:
                both(e, self.low_arrive, 1)
            both(e, self.landed)

            def side(i, carry):
                zj = zi + (2 * i - 1) * e
                here = (zj >= 0) & (zj < levels) & ((e > 0) | (i == 0))
                pl.when(here)(lambda: compute(zj, e == 0))
                return carry

            lax.fori_loop(0, 2, side, 0)
            return carry

        wave(1)
        both(0, self.onward)
        if self.split:
            self.low_onward()
        lax.fori_loop(2, levels + 2, one, 0)
        self.finish()


def member_step(core, group, member):
    remainder = (core * group + member) % 3
    return jnp.where(remainder == 0, 1.0, jnp.where(remainder == 1, 16.0, 64.0)).astype(F32)


def dequantize(core, group, codes, row_scale, into, rows, first):
    def one(i, carry):
        value = codes(pl.multiple_of(i * 16, 16)).astype(F32)
        for m in range(group):
            step = member_step(core, group, m)
            offset = jnp.where(step > 1.0, 0.5 * step, 0.0)
            level = jnp.floor(value * (1.0 / step)) * step + offset
            into[m, pl.ds(pl.multiple_of(first + i * 16, 16), 16)] = (level * row_scale[...]).astype(BF16)
        return carry

    lax.fori_loop(0, rows // 16, one, 0)


GELU_A = 0.7978845608028654
GELU_B = 0.044715


EARLY = 4
PER = 4


class FeedWeights:
    def __init__(self, at, group, units, gate_ref, up_ref, down_ref, kept, refs):
        self.at, self.group, self.units = at, group, units
        self.sources, self.kept = (gate_ref, up_ref, down_ref), kept
        self.pair, self.down, self.codes, self.down_codes, self.sems = refs

    @staticmethod
    def scratch(group, units, window):
        return [
            pltpu.VMEM((group, D, 2 * window), BF16),
            pltpu.VMEM((group, window, D), BF16),
            pltpu.VMEM((D, 2 * window), BF16),
            pltpu.VMEM((units, D), jnp.int32),
            dma(5),
        ]

    def copies(self):
        window = self.codes.shape[1] // 2
        gate, up, down = self.sources
        copies = [pltpu.make_async_copy(down, self.down_codes, self.sems.at[2])]
        if gate is not None:
            copies += [
                pltpu.make_async_copy(gate, self.codes.at[:, pl.ds(0, window)], self.sems.at[0]),
                pltpu.make_async_copy(up, self.codes.at[:, pl.ds(window, window)], self.sems.at[1]),
            ]
        return copies

    def keeps(self):
        return [
            pltpu.make_async_copy(self.pair, self.kept[0], self.sems.at[3]),
            pltpu.make_async_copy(self.down, self.kept[1], self.sems.at[4]),
        ]

    def load(self):
        for copy in self.copies():
            copy.start()

    def make(self, pair_scale, down_scale):
        at, group, units = self.at, self.group, self.units
        window = self.down.shape[1]
        inset = (at.c * units) % 128
        for copy in self.copies():
            copy.wait()
        dequantize(at.b, group, lambda r: self.codes[pl.ds(r, 16)], pair_scale, self.pair, D, 0)

        def clear(i, carry):
            for m in range(group):
                self.down[m, pl.ds(pl.multiple_of(i * 16, 16), 16)] = jnp.zeros((16, D), BF16)
            return carry

        if window > units:
            lax.fori_loop(0, inset // 16, clear, 0)
            lax.fori_loop((inset + units) // 16, window // 16, clear, 0)
        dequantize(at.b, group, lambda r: self.down_codes[pl.ds(r, 16)], down_scale, self.down, units, inset)
        for copy in self.keeps():
            copy.start()

    def finish(self):
        for copy in self.keeps():
            copy.wait()


def feed_blocks(grid):
    return 4 if grid.plane % 4 == 0 else grid.plane


def each_chunk(grid, zj, fresh, loads, stores, compute):
    size = feed_blocks(grid)
    m = zj // (grid.planes // 2)

    def one(i, carry):
        first = zj * grid.plane + i * size
        reads, writes = loads(first), stores(first)
        for copy in reads:
            copy.start()

        @pl.when(jnp.logical_not(fresh & (i == 0)))
        def _():
            for copy in writes:
                copy.wait()

        compute(m, reads)
        for copy in writes:
            copy.start()
        return carry

    lax.fori_loop(0, grid.plane // size, one, 0)


def copies_of(blocks, pairs, sems, first):
    return [
        pltpu.make_async_copy(a.at[:, blocks] if far_a else a, b if far_a else b.at[:, blocks], sems.at[first + k])
        for k, (a, b, far_a) in enumerate(pairs)
    ]


def forward_chunks(weights, all_ref, pair_ref, part_ref, xs, gu, part, sems):
    _, size, rows, _ = gu.shape
    window = weights.down.shape[1]

    def loads(first):
        return copies_of(pl.ds(first, size), [(all_ref, xs, True)], sems, 0)

    def stores(first):
        return copies_of(pl.ds(first, size), [(gu, pair_ref, False), (part, part_ref, False)], sems, 1)

    def compute(m, reads):
        reads[0].wait()
        both = dot(xs[...].reshape(2 * size * rows, D), weights.pair[m])
        gu[...] = both.astype(BF16).reshape(gu.shape)
        gate, up = both[:, :window], both[:, window:]
        bend = jnp.tanh(GELU_A * (gate + GELU_B * gate * gate * gate))
        hidden = (0.5 * gate * (1.0 + bend) * up).astype(BF16)
        part[...] = dot(hidden, weights.down[m]).astype(BF16).reshape(part.shape)

    return loads, stores, compute


def backward_chunks(wp, wd, all_ref, pair_ref, part_ref, dgu_ref, hid_ref, ys, gu, part, dgu, hid, sems):
    _, size, rows, _ = ys.shape
    window = wd.shape[1]
    count = 2 * size * rows

    def loads(first):
        return copies_of(pl.ds(first, size), [(all_ref, ys, True), (pair_ref, gu, True)], sems, 0)

    def stores(first):
        pairs = [(part, part_ref, False), (dgu, dgu_ref, False), (hid, hid_ref, False)]
        return copies_of(pl.ds(first, size), pairs, sems, 2)

    def compute(m, reads):
        reads[0].wait()
        grad_hidden = dot_t(ys[...].reshape(count, D), wd[m])
        reads[1].wait()
        both = gu[...].reshape(count, 2 * window).astype(F32)
        gate, up = both[:, :window], both[:, window:]
        bend = jnp.tanh(GELU_A * (gate + GELU_B * gate * gate * gate))
        bell = 0.5 * gate * (1.0 + bend)
        slope = 0.5 * (1.0 + bend) + 0.5 * gate * (1.0 - bend * bend) * GELU_A * (1.0 + 3.0 * GELU_B * gate * gate)
        dgu[:, :, :, :window] = (grad_hidden * up * slope).astype(BF16).reshape(hid.shape)
        dgu[:, :, :, window:] = (grad_hidden * bell).astype(BF16).reshape(hid.shape)
        hid[...] = (bell * up).astype(BF16).reshape(hid.shape)
        part[...] = dot_t(dgu[...].reshape(count, 2 * window), wp[m]).astype(BF16).reshape(part.shape)

    return loads, stores, compute


def chunk_buffers(size, rows, *widths):
    return [pltpu.VMEM((2, size, rows, width), BF16) for width in widths]


def feed_forward(grid, x, gate_codes, up_codes, down_codes, pair_scale, down_scale, cid):
    group, rows, _ = x.shape
    n, levels = grid.n, grid.planes
    units, window, _ = feed_windows(grid)
    gs, ws = level_sems(grid, levels), FeedWeights.scratch(group, units, window)
    size = feed_blocks(grid)

    def kernel(
        x_ref, gate_ref, up_ref, down_ref, ps_ref, ds_ref, all_ref, pair_ref, part_ref, wp_ref, wd_ref, *scratch
    ):
        refs = Split(scratch)
        at = Place(grid, levels)
        weights = FeedWeights(at, group, units, gate_ref, up_ref, down_ref, (wp_ref, wd_ref), refs.take(len(ws)))
        weights.load()
        moving = LevelGather(True, at, x_ref, all_ref, *refs.take(len(gs)))
        loads, stores, compute = forward_chunks(weights, all_ref, pair_ref, part_ref, *refs.take(4))
        at.greet_near(False)
        moving.begin()
        weights.make(ps_ref, ds_ref)
        moving.run(lambda zj, fresh: each_chunk(grid, zj, fresh, loads, stores, compute))
        for copy in stores(0):
            copy.wait()
        weights.finish()

    def blocks(width):
        return jax.ShapeDtypeStruct((group, n, rows, width), BF16)

    return pl.pallas_call(
        kernel,
        out_shape=(
            blocks(D),
            blocks(2 * window),
            blocks(D),
            jax.ShapeDtypeStruct((group, D, 2 * window), BF16),
            jax.ShapeDtypeStruct((group, window, D), BF16),
        ),
        in_specs=[INVMEM, ANY, ANY, ANY, INVMEM, INVMEM],
        out_specs=(ANY,) * 5,
        scratch_shapes=ws + gs + chunk_buffers(size, rows, D, 2 * window, D) + [dma(3)],
        compiler_params=params(cid, 60),
        name="feed_forward",
    )(x, gate_codes, up_codes, down_codes, pair_scale, down_scale)


def feed_backward(grid, x, pair, pair_matrices, down_matrices, cid):
    group, rows, _ = x.shape
    n, levels = grid.n, grid.planes
    _, window, _ = feed_windows(grid)
    gs = level_sems(grid, levels)
    size = feed_blocks(grid)

    def kernel(x_ref, pair_ref, wp_ref, wd_ref, all_ref, part_ref, dgu_ref, hid_ref, *scratch):
        refs = Split(scratch)
        at = Place(grid, levels)
        moving = LevelGather(True, at, x_ref, all_ref, *refs.take(len(gs)))
        wp, wd, fetch_sems = refs.take(3)
        fetch = [
            pltpu.make_async_copy(wp_ref, wp, fetch_sems.at[0]),
            pltpu.make_async_copy(wd_ref, wd, fetch_sems.at[1]),
        ]
        for copy in fetch:
            copy.start()
        loads, stores, compute = backward_chunks(
            wp, wd, all_ref, pair_ref, part_ref, dgu_ref, hid_ref, *refs.take(6)
        )
        at.greet_near(False)
        moving.begin()
        for copy in fetch:
            copy.wait()
        moving.run(lambda zj, fresh: each_chunk(grid, zj, fresh, loads, stores, compute))
        for copy in stores(0):
            copy.wait()

    def blocks(width):
        return jax.ShapeDtypeStruct((group, n, rows, width), BF16)

    return pl.pallas_call(
        kernel,
        out_shape=(blocks(D), blocks(D), blocks(2 * window), blocks(window)),
        in_specs=[INVMEM] + [ANY] * 3,
        out_specs=(ANY,) * 4,
        scratch_shapes=gs
        + [pltpu.VMEM((group, D, 2 * window), BF16), pltpu.VMEM((group, window, D), BF16), dma(2)]
        + chunk_buffers(size, rows, D, 2 * window, D, 2 * window, window)
        + [dma(5)],
        compiler_params=params(cid, 62),
        name="feed_backward",
    )(x, pair, pair_matrices, down_matrices)


def scatter_scratch(grid, levels, rows, width):
    steps = grid.plane // 2
    return [
        pltpu.VMEM((2, levels * grid.plane, rows, width), BF16),
        pltpu.VMEM((2, levels, 2, rows // 2, width), BF16),
        pltpu.VMEM((2, max(steps - 1, 1), levels, 2, rows, width), BF16),
        pltpu.VMEM((2, levels, 2, rows, width), BF16),
        dma(1),
        dma(1, 2, levels),
        dma(1, 2, levels),
        dma(1, 2, steps, levels),
        dma(1, 2, steps, levels),
    ]


def scatter_steps(at, out_ref, acc, ring_half, ring_full, line, ls, zs, zr, rs, rr):
    levels, steps, zi, q, pn, b = at.levels, at.steps, at.zi, at.q, at.pn, at.b
    rows = acc.shape[2]
    half = rows // 2
    passes = [(0, 2)]

    def block(us, zj, qj, part=None):
        u0, nu = us
        if part is None:
            return acc.at[pl.ds(u0, nu), at.slot(zj, qj)]
        return acc.at[pl.ds(u0, nu), at.slot(zj, qj), pl.ds(part * half, half)]

    def add(us, s, others, lo, count):
        u0, nu = us

        def one(i, carry):
            u, r = u0 + i // (count // 16), lo + (i % (count // 16)) * 16
            total = acc[u, s, pl.ds(r, 16)].astype(F32)
            for other in others:
                total = total + other(u, r)[...].astype(F32)
            acc[u, s, pl.ds(r, 16)] = total.astype(BF16)
            return carry

        lax.fori_loop(0, nu * (count // 16), one, 0)

    def full_at(way, step, zj):
        return lambda u, r: ring_full.at[way, step - 2, zj, u, pl.ds(r, 16)]

    def half_at(way, zj):
        return lambda u, r: ring_half.at[way, zj, u, pl.ds(r - way * half, 16)]

    def line_at(way, zj):
        return lambda u, r: line.at[way, zj, u, pl.ds(r, 16)]

    def r_copy(k, us, zj, way, step):
        u0, nu = us
        sign = 1 if way == 0 else -1
        target = q + sign * (steps + 1 - step)
        if step == 1:
            src, dst = block(us, zj, target, way), ring_half.at[way, zj, pl.ds(u0, nu)]
        else:
            src, dst = block(us, zj, target), ring_full.at[way, step - 2, zj, pl.ds(u0, nu)]
        to = at.right if way == 0 else at.left
        return remote(src, dst, rs.at[k, way, step - 1, zj], rr.at[k, way, step - 1, zj], to, b)

    def z_copy(k, us, zj, way):
        u0, nu = us
        to = (at.c + at.n + (pn if way == 0 else -pn)) % at.n
        return remote(block(us, zj, q), line.at[way, zj, pl.ds(u0, nu)], zs.at[k, way, zj], zr.at[k, way, zj], to, b)

    def begin(k, us, sign, d):
        def go():
            for way in (0, 1):
                r_copy(k, us, zi + sign * d, way, 1).start()

        guarded(present(zi, sign, d, levels), go)

    def middle(k, us, sign, d):
        zj = zi + sign * d

        def go():
            for step in range(1, steps):
                for way in (0, 1):
                    r_copy(k, us, zj, way, step).wait_recv()
                    s = at.slot(zj, q + (1 if way == 0 else -1) * (steps - step))
                    if step == 1:
                        add(us, s, [half_at(way, zj)], way * half, half)
                    else:
                        add(us, s, [full_at(way, step, zj)], 0, rows)
                    r_copy(k, us, zj, way, step + 1).start()

        guarded(present(zi, sign, d, levels), go)

    def last(k, us, sign, d):
        zj = zi + sign * d

        def go():
            for way in (0, 1):
                r_copy(k, us, zj, way, steps).wait_recv()
            s = at.slot(zj, q)
            if steps > 1:
                add(us, s, [full_at(0, steps, zj), full_at(1, steps, zj)], 0, rows)
            else:
                add(us, s, [half_at(0, zj)], 0, half)
                add(us, s, [half_at(1, zj)], half, half)

            def passed(way):
                z_copy(k, us, zj, way).wait_recv()
                add(us, s, [line_at(way, zj)], 0, rows)

            if sign >= 0:
                pl.when(zi > 0)(lambda: passed(0))
            if sign <= 0:
                pl.when(zi < levels - 1)(lambda: passed(1))
            if sign > 0:
                z_copy(k, us, zj, 0).start()
            if sign < 0:
                z_copy(k, us, zj, 1).start()

        guarded(present(zi, sign, d, levels), go)

    def finish(k, us, sign, d):
        zj = zi + sign * d

        def go():
            for way in (0, 1):
                for step in range(1, steps + 1):
                    r_copy(k, us, zj, way, step).wait_send()
            if sign != 0:
                z_copy(k, us, zj, 0 if sign > 0 else 1).wait_send()

        guarded(present(zi, sign, d, levels), go)

    waves = [
        [(k, us, sign, d) for sign in ((0,) if d == 0 else (-1, 1))]
        for k, us in enumerate(passes)
        for d in range(levels - 1, -1, -1)
    ]
    own = at.slot(zi, q)
    def each(action, i):
        if i < len(waves):
            for group in waves[i]:
                action(*group)

    each(begin, 0)
    each(begin, 1)
    each(middle, 0)
    yield
    for i in range(len(waves)):
        each(begin, i + 2)
        each(middle, i + 1)
        yield
        each(last, i)
    yield

    def give(src, u):
        def one(i, carry):
            out_ref[u, pl.ds(i * 16, 16)] = src.at[pl.ds(i * 16, 16)][...]
            return carry

        lax.fori_loop(0, rows // 16, one, 0)

    give(acc.at[0, own], 0)
    give(acc.at[1, own], 1)
    for wave in waves:
        for group in wave:
            finish(*group)


def split_scratch(grid, levels, rows, width):
    steps, pn = grid.plane // 2, grid.plane
    cut = rows * 3 // 4 // 16 * 16
    more = max(steps - 1, 1)
    return [
        pltpu.VMEM((2, levels * pn, rows, width), BF16),
        pltpu.VMEM((2, levels, cut, width), BF16),
        pltpu.VMEM((2, more, levels, 2, cut, width), BF16),
        pltpu.VMEM((2, levels, 2, cut, width), BF16),
        pltpu.VMEM((2, rows - cut, width), BF16),
        pltpu.VMEM((2, more, 2, rows - cut, width), BF16),
        pltpu.VMEM((2, levels, 2, pn, rows - cut, width), BF16),
        dma(1),
        dma(2, levels),
        dma(2, levels),
        dma(2, steps, levels),
        dma(2, steps, levels),
        dma(2, levels),
        dma(2, levels),
        dma(2, steps),
        dma(2, steps),
    ]


def split_scatter_steps(
    at, out_ref, acc, half_ref, full_ref, line_ref, low_half, low_full, low_line,
    ls, zs, zr, rs, rr, lzs, lzr, lrs, lrr,
):
    levels, steps, zi, q, pn, b = at.levels, at.steps, at.zi, at.q, at.pn, at.b
    rows = acc.shape[2]
    cut = half_ref.shape[2]
    upper, lower = pl.ds(0, cut), pl.ds(cut, rows - cut)

    def add(target, others, pieces):
        def one(i, carry):
            total = target(i)[...].astype(F32)
            for other in others:
                total = total + other(i)[...].astype(F32)
            target(i)[...] = total.astype(BF16)
            return carry

        lax.fori_loop(0, pieces, one, 0)

    def spans(ref, first, count):
        per = count // 16
        return lambda i: ref.at[i // per, pl.ds(pl.multiple_of(first + (i % per) * 16, 16), 16)]

    def along(way):
        return (at.c + at.n + (pn if way == 0 else -pn)) % at.n

    def r_copy(zj, way, step):
        target = at.slot(zj, q + (1 if way == 0 else -1) * (steps + 1 - step))
        if step == 1:
            src, dst = acc.at[way, target, upper], half_ref.at[way, zj]
        else:
            src, dst = acc.at[:, target, upper], full_ref.at[way, step - 2, zj]
        to = at.right if way == 0 else at.left
        return remote(src, dst, rs.at[way, step - 1, zj], rr.at[way, step - 1, zj], to, b)

    def z_copy(zj, way):
        return remote(
            acc.at[:, at.slot(zj, q), upper], line_ref.at[way, zj], zs.at[way, zj], zr.at[way, zj], along(way), b
        )

    def begin(sign, d):
        for way in (0, 1):
            r_copy(zi + sign * d, way, 1).start()

    def middle(sign, d):
        zj = zi + sign * d
        for step in range(1, steps):
            for way in (0, 1):
                r_copy(zj, way, step).wait_recv()
                s = at.slot(zj, q + (1 if way == 0 else -1) * (steps - step))
                if step == 1:
                    add(
                        lambda i: acc.at[way, s, pl.ds(pl.multiple_of(i * 16, 16), 16)],
                        [lambda i: half_ref.at[way, zj, pl.ds(pl.multiple_of(i * 16, 16), 16)]],
                        cut // 16,
                    )
                else:
                    add(spans(acc.at[:, s], 0, cut), [spans(full_ref.at[way, step - 2, zj], 0, cut)], 2 * cut // 16)
                r_copy(zj, way, step + 1).start()

    def last(sign, d):
        zj = zi + sign * d
        for way in (0, 1):
            r_copy(zj, way, steps).wait_recv()
        s = at.slot(zj, q)
        mine = spans(acc.at[:, s], 0, cut)
        add(mine, [spans(full_ref.at[way, steps - 2, zj], 0, cut) for way in (0, 1)], 2 * cut // 16)

        def passed(way):
            z_copy(zj, way).wait_recv()
            add(mine, [spans(line_ref.at[way, zj], 0, cut)], 2 * cut // 16)

        if sign >= 0:
            pl.when(zi > 0)(lambda: passed(0))
        if sign <= 0:
            pl.when(zi < levels - 1)(lambda: passed(1))
        if sign != 0:
            z_copy(zj, 0 if sign > 0 else 1).start()

    def done(sign, d):
        zj = zi + sign * d
        for way in (0, 1):
            for step in range(1, steps + 1):
                r_copy(zj, way, step).wait_send()
        if sign != 0:
            z_copy(zj, 0 if sign > 0 else 1).wait_send()

    def low_z_copy(zj, way):
        ref = acc.at[:, pl.ds(zj * pn, pn), lower]
        return remote(ref, low_line.at[way, zj], lzs.at[way, zj], lzr.at[way, zj], along(way), b)

    def low_passed(zj, way):
        low_z_copy(zj, way).wait_recv()
        per = (rows - cut) // 16

        def piece(i):
            return i // (pn * per), (i // per) % pn, (i % per) * 16

        def into(i):
            u, j, r = piece(i)
            return acc.at[u, zj * pn + j, pl.ds(pl.multiple_of(cut + r, 16), 16)]

        def come(i):
            u, j, r = piece(i)
            return low_line.at[way, zj, u, j, pl.ds(pl.multiple_of(r, 16), 16)]

        add(into, [come], 2 * pn * per)

    def low_start():
        for zj in range(levels - 1, 0, -1):
            pl.when(zi == 0)(lambda: low_z_copy(zj, 0).start())
        for zj in range(levels - 1):
            pl.when(zi == levels - 1)(lambda: low_z_copy(zj, 1).start())

    def low_stage(a):
        up, down = zi + levels - 1 - a, a - (levels - 1 - zi)

        def from_below():
            low_passed(up, 0)
            pl.when(up > zi)(lambda: low_z_copy(up, 0).start())

        def from_above():
            low_passed(down, 1)
            pl.when(down < zi)(lambda: low_z_copy(down, 1).start())

        pl.when((zi > 0) & (up >= zi) & (up < levels))(from_below)
        pl.when((zi < levels - 1) & (down >= 0) & (down <= zi))(from_above)

    def low_r_copy(way, step):
        target = at.slot(zi, q + (1 if way == 0 else -1) * (steps + 1 - step))
        if step == 1:
            src, dst = acc.at[way, target, lower], low_half.at[way]
        else:
            src, dst = acc.at[:, target, lower], low_full.at[way, step - 2]
        to = at.right if way == 0 else at.left
        return remote(src, dst, lrs.at[way, step - 1], lrr.at[way, step - 1], to, b)

    def low_middle():
        for step in range(1, steps):
            for way in (0, 1):
                low_r_copy(way, step).wait_recv()
                s = at.slot(zi, q + (1 if way == 0 else -1) * (steps - step))
                if step == 1:
                    add(
                        lambda i: acc.at[way, s, pl.ds(pl.multiple_of(cut + i * 16, 16), 16)],
                        [lambda i: low_half.at[way, pl.ds(pl.multiple_of(i * 16, 16), 16)]],
                        (rows - cut) // 16,
                    )
                else:
                    add(
                        spans(acc.at[:, s], cut, rows - cut),
                        [spans(low_full.at[way, step - 2], 0, rows - cut)],
                        2 * (rows - cut) // 16,
                    )
                low_r_copy(way, step + 1).start()

    def low_last():
        for way in (0, 1):
            low_r_copy(way, steps).wait_recv()
        add(
            spans(acc.at[:, at.slot(zi, q)], cut, rows - cut),
            [spans(low_full.at[way, steps - 2], 0, rows - cut) for way in (0, 1)],
            2 * (rows - cut) // 16,
        )

    def each(action, d):
        if d >= 0:
            for sign in (0,) if d == 0 else (-1, 1):
                guarded(present(zi, sign, d, levels), lambda: action(sign, d))

    far = levels - 1
    each(begin, far)
    low_start()
    each(begin, far - 1)
    each(middle, far)
    yield
    for a in range(1, levels):
        low_stage(a)
        d = far - a
        each(begin, d - 1)
        each(middle, d)
        yield
        each(last, d + 1)
    for way in (0, 1):
        low_r_copy(way, 1).start()
    low_middle()
    each(last, 0)
    low_last()
    yield

    def give(i, carry):
        r = pl.ds(pl.multiple_of((i % (rows // 16)) * 16, 16), 16)
        out_ref[i // (rows // 16), r] = acc[i // (rows // 16), at.slot(zi, q), r]
        return carry

    lax.fori_loop(0, 2 * (rows // 16), give, 0)
    for d in range(levels):
        each(done, d)
    for zj in range(levels):
        pl.when(zj > zi)(lambda: low_z_copy(zj, 0).wait_send())
        pl.when(zj < zi)(lambda: low_z_copy(zj, 1).wait_send())
    for way in (0, 1):
        for step in range(1, steps + 1):
            low_r_copy(way, step).wait_send()


def scatter_parts(grid, levels, rows, width):
    blocks = 2 * (2 * levels * (grid.plane // 2 + 2) + levels * grid.plane)
    parts = 1
    while blocks * rows * (width // parts) * 2 > 40 * 2**20:
        parts += 1
        while width % (128 * parts):
            parts += 1
    return parts


def in_parts(grid, levels, call, p, extra):
    parts = scatter_parts(grid, levels, p.shape[2], p.shape[3])
    if parts == 1:
        return call(p, extra)
    piece = p.shape[3] // parts
    sums, others = [], ()
    for i in range(parts):
        got = call(p[..., i * piece : (i + 1) * piece], extra if i == 0 else None)
        sums.append(got[0])
        others = got[1:] if i == 0 else others
    return (jnp.concatenate(sums, axis=-1),) + tuple(others)


def pairwise(n, c, b):
    def to(i):
        return (c + 2 * i + b) % n

    def frm(i, core):
        return (c + n - 2 * i - core) % n

    return to, frm


def middle_out(half):
    return sorted(range(1, half), key=lambda i: abs(2 * i - half))


def share_task(at, sources, views, ss, sr, fs, fr):
    n, c, b = at.n, at.c, at.b
    half = n // 2
    to, frm = pairwise(n, c, b)
    kinds = len(sources)

    def out_copy(k, i):
        return remote(sources[k](to(i)), views[k](c), ss.at[k, i], sr.at[k, i], to(i), b)

    def landed(k, i):
        return remote(sources[k](c), views[k](frm(i, b)), ss.at[k, i], sr.at[k, i], to(i), b)

    def pass_on(k, i, core):
        ref = views[k](frm(i, core))
        return at.sibling(ref, ref, fs.at[k, i], fr.at[k, i])

    def local(k):
        return pltpu.make_async_copy(sources[k](c), views[k](c), sr.at[k, 0])

    order = middle_out(half) + [0]

    def issue():
        for i in order:
            for k in range(kinds):
                if i > 0:
                    out_copy(k, i).start()
                else:
                    pl.when(b == 1)(lambda: out_copy(k, 0).start())
                    pl.when(b == 0)(lambda: local(k).start())
            yield

    def finish():
        for i in order:
            for k in range(kinds):
                if i > 0:
                    landed(k, i).wait_recv()
                else:
                    pl.when(b == 1)(lambda: landed(k, 0).wait_recv())
                    pl.when(b == 0)(lambda: local(k).wait())
                pass_on(k, i, b).start()
        for k in range(kinds):
            for i in range(half):
                pass_on(k, i, 1 - b).wait_recv()
            for i in range(half):
                pass_on(k, i, b).wait_send()
            for i in range(1, half):
                out_copy(k, i).wait_send()
            pl.when(b == 1)(lambda: out_copy(k, 0).wait_send())

    return issue(), finish


def share_sems(grid, kinds):
    return [dma(kinds, grid.n // 2) for _ in range(4)]


def tell_task(at, small_ref, all_ref, ts, tr):
    n, c, b = at.n, at.c, at.b

    def tell(off, slot):
        return remote(small_ref, all_ref.at[slot], ts.at[off], tr.at[off], (c + off) % n, b)

    keep = pltpu.make_async_copy(small_ref, all_ref.at[c], ts.at[0])

    def issue():
        keep.start()
        for off in range(1, n):
            tell(off, c).start()
        yield

    def finish():
        keep.wait()
        for off in range(1, n):
            tell(off, (c + n - off) % n).wait_recv()
        for off in range(1, n):
            tell(off, c).wait_send()

    return issue(), finish


def head_rows_task(at, x_ref, out_ref, hs, hr, fs, fr):
    c, b = at.c, at.b
    copies = at.n // HEADS
    head, rank = c % HEADS, c // HEADS
    mine = rank % 2 == b

    def out_copy(k):
        to = c // copies + HEADS * (2 * k + b)
        return to, remote(x_ref, out_ref.at[c % copies], hs.at[k], hr.at[c % copies], to, b)

    def landed(j):
        return remote(x_ref, out_ref.at[j], hs.at[0], hr.at[j], head * copies + j, b)

    def here(j):
        return pltpu.make_async_copy(x_ref, out_ref.at[j], hr.at[j])

    def pass_on(j):
        return at.sibling(out_ref.at[j], out_ref.at[j], fs.at[j], fr.at[j])

    def issue():
        for k in range(copies // 2):
            to, copy = out_copy(k)
            pl.when(to != c)(lambda: copy.start())
            pl.when(to == c)(lambda: here(c % copies).start())
            yield

    def finish():
        @pl.when(mine)
        def _():
            for j in range(copies):
                pl.when(head * copies + j != c)(lambda: landed(j).wait_recv())
                pl.when(head * copies + j == c)(lambda: here(j).wait())
                pass_on(j).start()
            for j in range(copies):
                pass_on(j).wait_send()

        @pl.when(jnp.logical_not(mine))
        def _():
            for j in range(copies):
                pass_on(j).wait_recv()

        for k in range(copies // 2):
            to, copy = out_copy(k)
            pl.when(to != c)(lambda: copy.wait_send())

    return issue(), finish


def head_rows_sems(grid):
    copies = grid.n // HEADS
    return [dma(copies), dma(copies), dma(copies), dma(copies)]


def add_rows(into, other, rows):
    step = 16 if rows % 16 == 0 else rows

    def one(r, carry):
        at = pl.ds(pl.multiple_of(r * step, step), step)
        into[at] = (into[at].astype(F32) + other[at].astype(F32)).astype(BF16)
        return carry

    lax.fori_loop(0, rows // step, one, 0)


def return_task(at, x_ref, out_ref, mine, theirs, ls, ps, pr, ss, sr, fs, fr, given=None, fill=None, prepare=None, per=2):
    n, c, b = at.n, at.c, at.b
    half = n // 2
    to, frm = pairwise(n, c, b)
    other_to, _ = pairwise(n, c, 1 - b)

    def load(i):
        return pltpu.make_async_copy(x_ref.at[to(i)], mine.at[i], ls.at[i])

    def give(i):
        source = x_ref.at[other_to(i)] if given is None else given.at[i]
        return at.sibling(source, theirs.at[i], ps.at[i], pr.at[i])

    def out_copy(i):
        return remote(mine.at[i], out_ref.at[c], ss.at[i], sr.at[i], to(i), b)

    def landed(i):
        return remote(mine.at[i], out_ref.at[frm(i, b)], ss.at[i], sr.at[i], to(i), b)

    def pass_on(i, core):
        ref = out_ref.at[frm(i, core)]
        return at.sibling(ref, ref, fs.at[i], fr.at[i])

    local = pltpu.make_async_copy(mine.at[0], out_ref.at[c], ss.at[0])
    order = middle_out(half) + [0]

    def issue():
        if prepare is not None:
            yield from prepare()
        for i in order:
            if fill is None:
                load(i).start()
            else:
                fill(i)
            give(i).start()
        for j, i in enumerate(order):
            if fill is None:
                load(i).wait()
            give(i).wait_recv()
            add_rows(mine.at[i], theirs.at[i], mine.shape[1])
            if i > 0:
                out_copy(i).start()
            else:
                pl.when(b == 1)(lambda: out_copy(0).start())
                pl.when(b == 0)(lambda: local.start())
            if j % per == per - 1:
                yield

    def finish():
        for i in order:
            if i > 0:
                landed(i).wait_recv()
            else:
                pl.when(b == 1)(lambda: landed(0).wait_recv())
                pl.when(b == 0)(lambda: local.wait())
            pass_on(i, b).start()
        for i in range(half):
            pass_on(i, 1 - b).wait_recv()
        for i in range(half):
            give(i).wait_send()
            pass_on(i, b).wait_send()
        for i in range(1, half):
            out_copy(i).wait_send()
        pl.when(b == 1)(lambda: out_copy(0).wait_send())

    return issue(), finish


def return_scratch(grid, shape):
    blocks = (grid.n // 2,) + shape
    return [pltpu.VMEM(blocks, BF16), pltpu.VMEM(blocks, BF16)] + [dma(grid.n // 2) for _ in range(7)]


def head_return_task(at, x_ref, out_ref, mine, theirs, ls, ps, pr, hs, hr, fs, fr):
    c, b = at.c, at.b
    copies = at.n // HEADS
    head, rank = c % HEADS, c // HEADS
    taken = (c % copies) % 2 == b

    def load(k):
        return pltpu.make_async_copy(x_ref.at[2 * k + b], mine.at[k], ls.at[k])

    def give(k):
        return at.sibling(x_ref.at[2 * k + 1 - b], theirs.at[k], ps.at[k], pr.at[k])

    def out_copy(k):
        to = head * copies + 2 * k + b
        return to, remote(mine.at[k], out_ref.at[rank], hs.at[k], hr.at[rank], to, b)

    def landed(i):
        return remote(mine.at[0], out_ref.at[i], hs.at[0], hr.at[i], c // copies + HEADS * i, b)

    def here(k, i):
        return pltpu.make_async_copy(mine.at[k], out_ref.at[i], hr.at[i])

    def pass_on(i):
        return at.sibling(out_ref.at[i], out_ref.at[i], fs.at[i], fr.at[i])

    def issue():
        for k in range(copies // 2):
            load(k).start()
            give(k).start()
        for k in range(copies // 2):
            load(k).wait()
            give(k).wait_recv()
            add_rows(mine.at[k], theirs.at[k], x_ref.shape[1])
            to, copy = out_copy(k)
            pl.when(to != c)(lambda: copy.start())
            pl.when(to == c)(lambda: here(k, rank).start())
            yield

    def finish():
        @pl.when(taken)
        def _():
            for i in range(copies):
                frm = c // copies + HEADS * i
                pl.when(frm != c)(lambda: landed(i).wait_recv())
                pl.when(frm == c)(lambda: here(0, i).wait())
                pass_on(i).start()
            for i in range(copies):
                pass_on(i).wait_send()

        @pl.when(jnp.logical_not(taken))
        def _():
            for i in range(copies):
                pass_on(i).wait_recv()

        for k in range(copies // 2):
            give(k).wait_send()
            to, copy = out_copy(k)
            pl.when(to != c)(lambda: copy.wait_send())

    return issue(), finish


def head_return_scratch(grid, shape):
    copies = grid.n // HEADS
    blocks = (copies // 2,) + shape
    return [pltpu.VMEM(blocks, BF16), pltpu.VMEM(blocks, BF16)] + [dma(copies) for _ in range(7)]


def pair_task(at, x_ref, first, out_ref, other, sems):
    count = out_ref.shape[0]
    copy = at.sibling(x_ref.at[pl.ds(pl.multiple_of(first, 16), count)], other, sems.at[0], sems.at[1])

    def issue():
        copy.start()
        yield

    def finish():
        copy.wait_recv()

        def one(r, carry):
            rows = pl.ds(pl.multiple_of(r * 16, 16), 16)
            mine = x_ref[pl.ds(pl.multiple_of(first + r * 16, 16), 16)]
            out_ref[rows] = (mine.astype(F32) + other[rows].astype(F32)).astype(out_ref.dtype)
            return carry

        lax.fori_loop(0, count // 16, one, 0)
        copy.wait_send()

    return issue(), finish


class Split:
    def __init__(self, refs):
        self.refs = list(refs)

    def take(self, count):
        got, self.refs = self.refs[:count], self.refs[count:]
        return got


def together(main, *tasks):
    for _ in main:
        for issue, _finish in tasks:
            next(issue, None)
    for issue, finish in tasks:
        run(issue)
    for issue, finish in tasks:
        finish()


def narrow_task(sources, targets, wide, low, loads, stores):
    width = wide.shape[2]
    pieces = [(k, i) for k in range(len(sources)) for i in range(sources[k].shape[1] // width)]

    def load(j):
        k, i = pieces[j]
        return pltpu.make_async_copy(sources[k].at[:, pl.ds(i * width, width)], wide.at[j % 2], loads.at[j % 2])

    def store(j):
        k, i = pieces[j]
        return pltpu.make_async_copy(low.at[j % 2], targets[k].at[:, pl.ds(i * width, width)], stores.at[j % 2])

    def issue():
        load(0).start()
        load(1).start()
        yield
        for j in range(len(pieces)):
            load(j).wait()
            if j >= 2:
                store(j - 2).wait()
            low[j % 2] = wide[j % 2].astype(F32).astype(BF16)
            store(j).start()
            if j + 2 < len(pieces):
                load(j + 2).start()
            yield

    def finish():
        for j in range(len(pieces) - 2, len(pieces)):
            store(j).wait()

    return issue(), finish


def swap_copy(at, source, target, send, recv):
    return remote(source, target.at[at.member], send, recv, at.partner, at.b)


def swap_task(at, source, target, sems):
    there = swap_copy(at, source, target, sems.at[0], sems.at[1])
    here = remote(source, target.at[1 - at.member], sems.at[0], sems.at[1], at.partner, at.b)

    def issue():
        there.start()
        yield

    def finish():
        here.wait_recv()
        there.wait_send()

    return issue(), finish


def open_kernel(grid, tokens, gain, qkv_parts, out_codes, small, gate_codes, up_codes, rows_too, cid):
    x = tokens
    n, levels = grid.n, grid.planes // 2
    rows_d, width = qkv_parts.shape[1:]
    flat = rows_d % 16 == 0
    copies = n // HEADS
    gs, ss, ts, hs = gather_sems(grid, levels, 2), share_sems(grid, 1), [dma(n), dma(n)], head_rows_sems(grid)

    piece = FF // 2
    ns = [
        pltpu.VMEM((2, rows_d, piece), jnp.int32),
        pltpu.VMEM((2, rows_d, piece), BF16),
        dma(2),
        dma(2),
    ]

    def kernel(
        x_ref, gain_ref, w_ref, o_ref, small_ref, gate_ref, up_ref,
        kept_ref, seen_ref, codes_ref, rows_ref, all_ref, gl_ref, ul_ref, *scratch,
    ):
        at = Place(grid, levels)
        refs = Split(scratch)
        normed_ref, token_sems = refs.take(2)
        member = at.member
        at.greet_all()
        token_issue, token_finish = swap_task(at, x_ref.at[1 - member], kept_ref, token_sems)
        run(token_issue)

        def view(j):
            return codes_ref.at[pl.ds(j * rows_d, rows_d)] if flat else codes_ref.at[j]

        def ready(k):
            u = member if k == 0 else 1 - member
            if k == 1:
                token_finish()

            def one(_, r):
                if k == 0:
                    kept_ref[u, r] = x_ref[u, r]
                value = kept_ref[u, r].astype(F32)
                normed_ref[u, r] = (value * inverse_rms(value) * gain_ref[0:1]).astype(BF16)

            each_rows(1, x_ref.shape[1], one)

        together(
            gather_steps(
                at, normed_ref, seen_ref, *refs.take(len(gs)), passes=[(member, 1), (1 - member, 1)], ready=ready
            ),
            narrow_task([gate_ref, up_ref], [gl_ref, ul_ref], *refs.take(4)),
            tell_task(at, small_ref, all_ref, *refs.take(2)),
            share_task(at, [lambda to: w_ref.at[to % HEADS]], [view], *refs.take(len(ss))),
            *([head_rows_task(at, o_ref, rows_ref, *refs.take(4))] if rows_too else []),
        )
        if not rows_too:
            rows_ref[...] = o_ref[...]

    codes_shape = (n * rows_d, width) if flat else (n, rows_d, width)
    return pl.pallas_call(
        kernel,
        out_shape=(
            jax.ShapeDtypeStruct(x.shape, BF16),
            jax.ShapeDtypeStruct((2, levels * grid.plane) + x.shape[1:], BF16),
            jax.ShapeDtypeStruct(codes_shape, BF16),
            jax.ShapeDtypeStruct((copies,) + out_codes.shape if rows_too else out_codes.shape, BF16),
            jax.ShapeDtypeStruct((n,) + small.shape, small.dtype),
            jax.ShapeDtypeStruct(gate_codes.shape, BF16),
            jax.ShapeDtypeStruct(up_codes.shape, BF16),
        ),
        in_specs=[INVMEM] * 5 + [ANY] * 2,
        out_specs=(INVMEM, ANY, ANY, ANY if rows_too else INVMEM) + (ANY,) * 3,
        scratch_shapes=[pltpu.VMEM(x.shape, BF16), dma(2)] + gs + ns + ts + ss + hs,
        compiler_params=params(cid, 50),
        name="open",
    )(tokens, gain, qkv_parts, out_codes, small, gate_codes, up_codes)


def scatter_kernel(grid, levels, cid, name, tasks=None, end=None):
    made, in_specs, out_shapes, out_specs, extra_scratch = tasks if tasks else (None, [], (), (), [])

    def call(p, extra):
        rows, width = p.shape[2:]
        more = () if extra is None else tuple(extra)
        own = scatter_scratch(grid, levels, rows, width)

        def kernel(*refs):
            refs = Split(refs)
            (p_ref,) = refs.take(1)
            more_refs = refs.take(len(more))
            (out_ref,) = refs.take(1)
            out_refs = refs.take(len(out_shapes) if more else 0)
            mine = refs.take(len(own))
            at = Place(grid, levels)
            load = pltpu.make_async_copy(p_ref, mine[0], mine[4].at[0])
            load.start()
            if more:
                at.greet_all()
            else:
                at.greet_near(False)
            load.wait()
            sums = refs.take(1)[0] if end else out_ref
            others = made(at, more_refs, out_refs, refs) if more else []
            if end is None:
                together(scatter_steps(at, out_ref, *mine), *others)
                return
            for _ in scatter_steps(at, sums, *mine):
                for issue, _finish in others:
                    next(issue, None)
            last = end(at, more_refs, sums, out_ref, refs)
            together((), *others)
            last()

        return pl.pallas_call(
            kernel,
            out_shape=(jax.ShapeDtypeStruct((2, rows, width), BF16),) + (out_shapes if more else ()),
            in_specs=[ANY] + (in_specs if more else []),
            out_specs=(INVMEM,) + (out_specs if more else ()),
            scratch_shapes=own + (extra_scratch if more else []),
            compiler_params=params(cid + (0 if more else 20), 60),
            name=name,
        )(p, *more)

    return call


def feed_windows(grid):
    units = FF // grid.n
    window = 128 * max(-(-((c * units) % 128 + units) // 128) for c in range(grid.n))
    return units, window, lambda c: ((c * units) // 128) * 128


def attention_sums(grid, p, gate_codes, up_codes, cid):
    n, levels = grid.n, grid.planes // 2
    rows_d = gate_codes.shape[0]
    flat = rows_d % 16 == 0
    units, window, start = feed_windows(grid)
    ss = share_sems(grid, 2)

    def tasks(at, ins, outs, refs):
        def source(ref):
            return lambda to: ref.at[:, pl.ds(pl.multiple_of(start(to), 128), window)]

        def view(ref):
            return lambda j: ref.at[pl.ds(j * rows_d, rows_d)] if flat else ref.at[j]

        return [share_task(at, [source(r) for r in ins], [view(r) for r in outs], *refs.take(len(ss)))]

    shape = (n * rows_d, window) if flat else (n, rows_d, window)
    call = scatter_kernel(
        grid,
        levels,
        cid,
        "attention_sums",
        (tasks, [INVMEM, INVMEM], (jax.ShapeDtypeStruct(shape, BF16),) * 2, (ANY, ANY), ss),
    )
    return in_parts(grid, levels, call, p, (gate_codes, up_codes))


def feed_sums(grid, p, cid):
    return in_parts(grid, grid.planes, scatter_kernel(grid, grid.planes, cid, "feed_sums"), p, None)[0]


def feed_back_sums(grid, p, pair_grad, cid):
    rs = return_scratch(grid, pair_grad.shape[1:])

    def tasks(at, ins, outs, refs):
        return [return_task(at, ins[0], outs[0], *refs.take(len(rs)))]

    call = scatter_kernel(
        grid,
        grid.planes,
        cid,
        "feed_back_sums",
        (tasks, [ANY], (jax.ShapeDtypeStruct(pair_grad.shape, BF16),), (ANY,), rs),
    )
    return in_parts(grid, grid.planes, call, p, (pair_grad,))


def attention_back_sums(grid, p, qkv_grad, out_grad, down_grad, gains, merged, cid):
    n, levels = grid.n, grid.planes // 2
    rs, hs = return_scratch(grid, qkv_grad.shape[1:]), head_return_scratch(grid, out_grad.shape[1:])
    units, _, _ = feed_windows(grid)
    ps = [pltpu.VMEM((units, D), BF16), dma(2)]
    every = pltpu.VMEM((n,) + gains.shape, F32)
    gs = [pltpu.VMEM(gains.shape, F32), pltpu.VMEM(gains.shape, F32), every, dma(2)] + share_sems(grid, 1)
    us = assemble_scratch(grid) if merged else []
    rows, width = p.shape[2:]
    tail = [pltpu.VMEM((2, rows, width), BF16), dma(2)] if merged else []
    inputs = [qkv_grad, out_grad, down_grad, gains] + list(merged)
    in_specs = [ANY, ANY, INVMEM, INVMEM] + ([ANY] + [INVMEM] * 3 if merged else [])
    shapes = (
        jax.ShapeDtypeStruct(qkv_grad.shape, BF16),
        jax.ShapeDtypeStruct(out_grad.shape, BF16),
        jax.ShapeDtypeStruct((units, D), BF16),
        jax.ShapeDtypeStruct(gains.shape, F32),
    ) + (jax.ShapeDtypeStruct((D // n, FF), BF16),) * (2 if merged else 0)
    out_specs = (ANY, ANY, INVMEM, INVMEM) + ((ANY, ANY) if merged else ())
    sums = [pltpu.VMEM((2, rows, width), BF16)] if merged else []
    scratch = sums + rs + hs + ps + gs + us + tail

    def tasks(at, ins, outs, refs):
        made = [
            return_task(at, ins[0], outs[0], *refs.take(len(rs)), per=PER),
            head_return_task(at, ins[1], outs[1], *refs.take(len(hs))),
            pair_task(at, ins[2], (at.c * units) % 128, outs[2], *refs.take(2)),
            gains_task(at, ins[3], outs[3], *refs.take(len(gs))),
        ]
        if merged:
            made.insert(0, assemble_task(grid, ins[4], outs[4:6], *refs.take(len(us))))
        return made

    def end(at, ins, sums, out_ref, refs):
        kept, sems = refs.take(2)
        grad_ref, tokens_ref, gain_ref = ins[5:8]

        def one(u, r):
            dy, v = sums[u, r].astype(F32), tokens_ref[u, r].astype(F32)
            kept[u, r] = (grad_ref[u, r] + norm_back(v, inverse_rms(v), dy * gain_ref[0:1])).astype(BF16)

        each_rows(2, rows, one)
        issue, finish = swap_task(at, kept.at[1 - at.member], out_ref, sems)
        run(issue)
        out_ref[at.member] = kept[at.member]
        return finish

    call = scatter_kernel(
        grid,
        levels,
        cid,
        "attention_back_sums",
        (tasks, in_specs, shapes, out_specs, scratch),
        end if merged else None,
    )
    return in_parts(grid, levels, call, p, inputs)


SCALE = HEAD ** (-0.5)


def rotated(u, cosine, sine):
    half = u.shape[1] // 2
    first, second = u[:, :half], u[:, half:]
    return jnp.concatenate([first * cosine - second * sine, second * cosine + first * sine], axis=1)


def scores(q, k, start, first):
    bent = jnp.tanh(dot_t(q, k) * (SCALE / cap_limit))
    key = lax.broadcasted_iota(jnp.int32, bent.shape, 1)
    query = first + lax.broadcasted_iota(jnp.int32, bent.shape, 0)
    return jnp.where((key <= query) & (key >= start), jnp.exp(cap_limit * bent), 0.0), bent


def scale_rows(core, member, codes, column_scale, into, rows):
    step = member_step(core, 2, member)
    offset = jnp.where(step > 1.0, 0.5 * step, 0.0)

    def one(i, carry):
        r = pl.ds(pl.multiple_of(i * 16, 16), 16)
        level = jnp.floor(codes[r].astype(F32) * (1.0 / step)) * step + offset
        into[r] = (level * column_scale).astype(BF16)
        return carry

    lax.fori_loop(0, rows // 16, one, 0)


def attention_body(w, o, x_rows, put, ready, cos_ref, sin_ref, start_ref, q_ref, k_ref, v_ref, a_ref, t_ref, block=256):
    length = q_ref.shape[0]
    for i in range(length // block):
        r = pl.ds(i * block, block)
        lin = dot(x_rows(i), w[...])
        q_ref[r] = rotated(lin[:, :HEAD], cos_ref[r], sin_ref[r]).astype(BF16)
        k_ref[r] = rotated(lin[:, HEAD : 2 * HEAD], cos_ref[r], sin_ref[r]).astype(BF16)
        v_ref[r] = lin[:, 2 * HEAD :].astype(BF16)
    ready()
    for i in range(length // block):
        r, keys = pl.ds(i * block, block), pl.ds(0, (i + 1) * block)
        e, _ = scores(q_ref[r], k_ref[keys], start_ref[r], i * block)
        total = jnp.sum(e, axis=1, keepdims=True)
        attended = (dot(e.astype(BF16), v_ref[keys]) / total).astype(BF16)
        a_ref[r] = attended
        t_ref[r] = total
        put(i, dot(attended, o[...]).astype(BF16))


def attention_backward(seen, grad, w, o, q, k, v, attended, totals, vectors, cosine, sine, start):
    length = seen.shape[0]
    block, tile = 256, 256

    def kernel(
        x_ref, g_ref, w_ref, o_ref, q_ref, k_ref, v_ref, a_ref, t_ref, vec_ref, cos_ref, sin_ref, start_ref,
        part_ref, wg_ref, og_ref, gain_ref, xs, gs, w, part, wg, dk, dv, low, sems, out_sems,
    ):
        load_w = pltpu.make_async_copy(w_ref, w, sems.at[2])
        give_part = pltpu.make_async_copy(part, part_ref, sems.at[3])

        def give_rows(j):
            rows = pl.ds(pl.multiple_of(j * tile, tile), tile)
            return pltpu.make_async_copy(wg.at[rows], wg_ref.at[rows], out_sems.at[j])

        load_g = pltpu.make_async_copy(g_ref, gs, sems.at[0])
        load_x = pltpu.make_async_copy(x_ref, xs, sems.at[1])
        load_g.start()
        load_x.start()
        load_w.start()
        dk[...] = jnp.zeros_like(dk)
        dv[...] = jnp.zeros_like(dv)
        load_g.wait()
        for i in range(length // block):
            r, keys = pl.ds(i * block, block), pl.ds(0, (i + 1) * block)
            grad_attended = dot_t(gs[r], o_ref[...])
            total = t_ref[r]
            grad_sums = (grad_attended / total).astype(BF16)
            offset = jnp.sum(grad_attended * a_ref[r].astype(F32), axis=1, keepdims=True) / total
            e, bent = scores(q_ref[r], k_ref[keys], start_ref[r], i * block)
            grad_e = dot_t(grad_sums, v_ref[keys]) - offset
            grad_s = (e * grad_e * (1.0 - bent * bent)).astype(BF16)
            dv[keys] += t_dot(e.astype(BF16), grad_sums)
            dk[keys] += t_dot(grad_s, q_ref[r])
            low[r, :HEAD] = rotated(dot(grad_s, k_ref[keys]) * SCALE, cos_ref[r], -sin_ref[r]).astype(BF16)
        for i in range(length // block):
            r = pl.ds(i * block, block)
            low[r, HEAD : 2 * HEAD] = rotated(dk[r] * SCALE, cos_ref[r], -sin_ref[r]).astype(BF16)
            low[r, 2 * HEAD :] = dv[r].astype(BF16)
        load_x.wait()
        load_w.wait()
        gain_ref[...] = jnp.zeros_like(gain_ref)

        def parts(i, carry):
            r = pl.ds(pl.multiple_of(i * block, block), block)
            term = dot_t(low[r], w[...])
            part[r] = term.astype(BF16)
            gain_ref[...] += jnp.sum(term * xs[r].astype(F32), axis=0, keepdims=True)
            return carry

        lax.fori_loop(0, length // block, parts, 0)
        give_part.start()
        gain_ref[...] = gain_ref[...] / vec_ref[0:1]

        def grads(j, carry):
            cols = pl.ds(pl.multiple_of(j * tile, tile), tile)
            wg[cols] = t_dot(xs[:, cols], low[...]).astype(BF16)
            give_rows(j).start()
            og_ref[:, cols] = t_dot(a_ref[...], gs[:, cols]).astype(BF16)
            return carry

        lax.fori_loop(0, D // tile, grads, 0)
        give_part.wait()
        for j in range(D // tile):
            give_rows(j).wait()

    return pl.pallas_call(
        kernel,
        out_shape=(
            jax.ShapeDtypeStruct((length, D), BF16),
            jax.ShapeDtypeStruct((D, 3 * HEAD), BF16),
            jax.ShapeDtypeStruct((HEAD, D), BF16),
            jax.ShapeDtypeStruct((1, D), F32),
        ),
        in_specs=[ANY, ANY, ANY] + [INVMEM] * 10,
        out_specs=(ANY, ANY, INVMEM, INVMEM),
        scratch_shapes=[
            pltpu.VMEM(seen.shape, BF16),
            pltpu.VMEM(seen.shape, BF16),
            pltpu.VMEM((D, 3 * HEAD), BF16),
            pltpu.VMEM((length, D), BF16),
            pltpu.VMEM((D, 3 * HEAD), BF16),
            pltpu.VMEM((length, HEAD), F32),
            pltpu.VMEM((length, HEAD), F32),
            pltpu.VMEM((length, 3 * HEAD), BF16),
            dma(4),
            dma(D // tile),
        ],
        compiler_params=pltpu.CompilerParams(vmem_limit_bytes=60 * 2**20),
        name="attention_backward",
    )(seen, grad, w, o, q, k, v, attended, totals, vectors, cosine, sine, start)


def inverse_rms(v):
    return lax.rsqrt(jnp.mean(v * v, axis=-1, keepdims=True) + 1e-06)


def norm_back(v, r, weighted):
    return r * weighted - v * (r * r * r * jnp.mean(weighted * v, axis=-1, keepdims=True))


def each_rows(group, rows, step):
    def one(i, carry):
        step(i // (rows // 16), pl.ds(pl.multiple_of((i % (rows // 16)) * 16, 16), 16))
        return carry

    lax.fori_loop(0, group * (rows // 16), one, 0)


def fits(grid, rows):
    return (D // grid.n) % 16 == 0 and scatter_parts(grid, grid.planes, rows, D) == 1


def forward_kernel(
    grid, seen, qkv_codes, out_codes, qkv_scale, cosine, sine, begins, tokens, cotangent, gate_codes, up_codes, down_codes,
    pair_scale, vectors, cid,
):
    n, levels = grid.n, grid.planes
    group, rows, _ = tokens.shape
    rows_d = gate_codes.shape[0]
    units, window, start = feed_windows(grid)
    size = feed_blocks(grid)
    sc = scatter_scratch(grid, levels // 2, rows, D)
    ss = share_sems(grid, 2)
    ws, gs = FeedWeights.scratch(group, units, window), level_sems(grid, levels)

    length = seen.shape[0]
    block = 256
    here = block // rows
    hs = head_rows_sems(grid)

    def kernel(
        x_ref, codes_ref, rows_ref, scale_ref, cos_ref, sin_ref, start_ref, tokens_ref, cot_ref, gate_ref, up_ref, down_ref,
        ps_ref, vec_ref,
        w_ref, o_ref, q_ref, k_ref, v_ref, a_ref, t_ref,
        kept_cot_ref, raw_ref, mixed_ref, all_ref, pair_ref, part_ref, wp_ref, wd_ref, *scratch,
    ):
        refs = Split(scratch)
        half_at, at = Place(grid, levels // 2), Place(grid, levels)
        mine = refs.take(len(sc))
        share_refs = refs.take(len(ss))
        weights = FeedWeights(at, group, units, None, None, down_ref, (wp_ref, wd_ref), refs.take(len(ws)))
        gather_refs = refs.take(len(gs))
        x, xs, o_codes, head_sems, cot_sems = refs.take(5)
        head_refs = refs.take(len(hs))
        loads, stores, compute = forward_chunks(weights, all_ref, pair_ref, part_ref, *refs.take(4))
        w = weights.pair.at[0, :, pl.ds(0, 3 * HEAD)]
        w_codes = weights.pair.at[1, :, pl.ds(0, 3 * HEAD)]
        o = weights.down.at[0, pl.ds(0, HEAD)]
        acc = mine[0]
        load_w = pltpu.make_async_copy(codes_ref, w_codes, head_sems.at[0])
        load_x = pltpu.make_async_copy(x_ref, xs, head_sems.at[1])
        load_w.start()
        load_x.start()
        weights.sources = (None, None, down_ref)
        weights.load()
        at.greet_all()

        def source(ref):
            return lambda to: ref.at[:, pl.ds(pl.multiple_of(start(to), 128), window)]

        def view(k):
            return lambda j: weights.codes.at[
                pl.ds(pl.multiple_of(j * rows_d, 16), rows_d), pl.ds(k * window, window)
            ]

        heads, heads_finish = head_rows_task(at, rows_ref, o_codes, *head_refs)
        run(heads)
        issue, finish = share_task(at, [source(gate_ref), source(up_ref)], [view(0), view(1)], *share_refs)
        load_w.wait()
        scale_rows(at.b, at.member, w_codes, scale_ref[...], w, D)
        keep_w = pltpu.make_async_copy(w, w_ref, head_sems.at[2])
        keep_o = pltpu.make_async_copy(o, o_ref, head_sems.at[3])
        keep_w.start()
        load_x.wait()

        def ready():
            heads_finish()
            for _ in range(EARLY):
                next(issue, None)
            each = o_codes.shape[1]
            for j in range(o_codes.shape[0]):
                scale_rows(at.b, at.member, o_codes.at[j], vec_ref[4:5], o.at[pl.ds(j * each, each)], each)
            keep_o.start()

        def put(i, value):
            first = i * here
            half = grid.n // 2
            acc[first // half, pl.ds(first % half, here)] = value.reshape(here, rows, D)

        attention_body(
            w,
            o,
            lambda i: xs[pl.ds(i * block, block)],
            put,
            ready,
            cos_ref,
            sin_ref,
            start_ref,
            q_ref,
            k_ref,
            v_ref,
            a_ref,
            t_ref,
        )
        for _ in scatter_steps(half_at, raw_ref, *mine):
            next(issue, None)

        def norms(u, r):
            raw = raw_ref[u, r].astype(F32)
            mixed = tokens_ref[u, r].astype(F32) + raw * inverse_rms(raw) * vec_ref[1:2]
            mixed_ref[u, r] = mixed
            x[u, r] = (mixed * inverse_rms(mixed) * vec_ref[2:3]).astype(BF16)

        each_rows(group, rows, norms)
        moving = LevelGather(False, at, x, all_ref, *gather_refs)
        moving.begin()
        run(issue)
        give_cot, take_cot = swap_task(at, cot_ref.at[1 - at.member], kept_cot_ref, cot_sems)
        run(give_cot)
        kept_cot_ref[at.member] = cot_ref[at.member]

        def first():
            finish()
            keep_w.wait()
            keep_o.wait()
            weights.make(ps_ref, vec_ref.at[5:6])

        moving.run(lambda zj, fresh: each_chunk(grid, zj, fresh, loads, stores, compute), first)
        for copy in stores(0):
            copy.wait()
        weights.finish()
        take_cot()

    def blocks(width):
        return jax.ShapeDtypeStruct((group, n, rows, width), BF16)

    head = jax.ShapeDtypeStruct((length, HEAD), BF16)
    return pl.pallas_call(
        kernel,
        out_shape=(
            jax.ShapeDtypeStruct((D, 3 * HEAD), BF16),
            jax.ShapeDtypeStruct((HEAD, D), BF16),
            head,
            head,
            head,
            head,
            jax.ShapeDtypeStruct((length, 1), F32),
            jax.ShapeDtypeStruct(tokens.shape, BF16),
            jax.ShapeDtypeStruct(tokens.shape, BF16),
            jax.ShapeDtypeStruct(tokens.shape, F32),
            blocks(D),
            blocks(2 * window),
            blocks(D),
            jax.ShapeDtypeStruct((group, D, 2 * window), BF16),
            jax.ShapeDtypeStruct((group, window, D), BF16),
        ),
        in_specs=[ANY, ANY] + [INVMEM] * 7 + [ANY] * 3 + [INVMEM] * 2,
        out_specs=(ANY, ANY) + (INVMEM,) * 8 + (ANY,) * 5,
        scratch_shapes=sc
        + ss
        + ws
        + gs
        + [
            pltpu.VMEM(tokens.shape, BF16),
            pltpu.VMEM(seen.shape, BF16),
            pltpu.VMEM((n // HEADS,) + out_codes.shape, BF16),
            dma(4),
            dma(2),
        ]
        + hs
        + chunk_buffers(size, rows, D, 2 * window, D)
        + [dma(3)],
        compiler_params=params(cid, 62),
        name="forward",
    )(
        seen, qkv_codes, out_codes, qkv_scale, cosine, sine, begins, tokens, cotangent, gate_codes, up_codes, down_codes,
        pair_scale, vectors,
    )


def turn_kernel(grid, p, mixed, cotangent, pair, pair_matrices, down_matrices, vectors, cid):
    n, levels = grid.n, grid.planes
    group, rows, _ = mixed.shape
    units, window, _ = feed_windows(grid)
    size = feed_blocks(grid)
    sc, gs = split_scratch(grid, levels, rows, D), level_sems(grid, levels)

    def kernel(
        p_ref, mixed_ref, cot_ref, pair_ref, wp_ref, wd_ref, vec_ref,
        out_ref, gain_ref, all_ref, part_ref, dgu_ref, hid_ref, *scratch,
    ):
        refs = Split(scratch)
        at = Place(grid, levels)
        mine, gather_refs = refs.take(len(sc)), refs.take(len(gs))
        raw, x, kept_out, wp, wd, fetch_sems, swap_sems = refs.take(7)
        load = pltpu.make_async_copy(p_ref, mine[0], mine[7].at[0])
        load.start()
        fetch = [
            pltpu.make_async_copy(wp_ref, wp, fetch_sems.at[0]),
            pltpu.make_async_copy(wd_ref, wd, fetch_sems.at[1]),
        ]
        loads, stores, compute = backward_chunks(
            wp, wd, all_ref, pair_ref, part_ref, dgu_ref, hid_ref, *refs.take(6)
        )
        at.greet_near(True)
        load.wait()
        for copy in fetch:
            copy.start()
        run(split_scatter_steps(at, raw, *mine))
        gain_ref[...] = jnp.zeros_like(gain_ref)

        def norms(u, r):
            v, dy = raw[u, r].astype(F32), cot_ref[u, r].astype(F32)
            inverse, gain = inverse_rms(v), vec_ref[3:4]
            kept_out[u, r] = (mixed_ref[u, r] + v * inverse * gain).astype(BF16)
            x[u, r] = norm_back(v, inverse, dy * gain).astype(BF16)
            gain_ref[...] += jnp.sum(dy * v * inverse, axis=0, keepdims=True)

        each_rows(group, rows, norms)
        moving = LevelGather(True, at, x, all_ref, *gather_refs)
        moving.begin()
        give_out, take_out = swap_task(at, kept_out.at[1 - at.member], out_ref, swap_sems)
        run(give_out)
        out_ref[at.member] = kept_out[at.member]
        for copy in fetch:
            copy.wait()

        moving.run(lambda zj, fresh: each_chunk(grid, zj, fresh, loads, stores, compute))
        take_out()
        for copy in stores(0):
            copy.wait()

    def blocks(width):
        return jax.ShapeDtypeStruct((group, n, rows, width), BF16)

    return pl.pallas_call(
        kernel,
        out_shape=(
            jax.ShapeDtypeStruct(mixed.shape, BF16),
            jax.ShapeDtypeStruct((1, D), F32),
            blocks(D),
            blocks(D),
            blocks(2 * window),
            blocks(window),
        ),
        in_specs=[ANY, INVMEM, INVMEM, ANY, ANY, ANY, INVMEM],
        out_specs=(INVMEM, INVMEM) + (ANY,) * 4,
        scratch_shapes=sc
        + gs
        + [
            pltpu.VMEM(mixed.shape, BF16),
            pltpu.VMEM(mixed.shape, BF16),
            pltpu.VMEM(mixed.shape, BF16),
            pltpu.VMEM((group, D, 2 * window), BF16),
            pltpu.VMEM((group, window, D), BF16),
            dma(2),
            dma(2),
        ]
        + chunk_buffers(size, rows, D, 2 * window, D, 2 * window, window)
        + [dma(5)],
        compiler_params=params(cid, 62),
        name="turn",
    )(p, mixed, cotangent, pair, pair_matrices, down_matrices, vectors)


def back_kernel(grid, p, fed, down_low, pair_low, hidden, mixed, raw, cotangent, vectors, cid):
    n, levels = grid.n, grid.planes
    group, rows, _ = mixed.shape
    units, window, _ = feed_windows(grid)
    size = feed_blocks(grid)
    chunks = n // size
    count = group * size * rows
    rows_d = D // n
    half = n // 2
    tile = 256
    sc, gs = scatter_scratch(grid, levels, rows, D), gather_sems(grid, levels // 2)
    rs = return_scratch(grid, (rows_d, 2 * window))

    def kernel(
        p_ref, fed_ref, low_ref, dgu_ref, hid_ref, mixed_ref, raw_ref, cot_ref, vec_ref,
        grad_ref, feed_ref, post_ref, all_ref, got_ref, down_ref, *scratch,
    ):
        refs = Split(scratch)
        half_at, at = Place(grid, levels // 2), Place(grid, levels)
        mine, gather_refs, return_refs = refs.take(len(sc)), refs.take(len(gs)), refs.take(len(rs))
        raw2, x, xs, ys, dgu, hid, pair_sum, down_sum, given, down_out, sems = refs.take(11)
        load = pltpu.make_async_copy(p_ref, mine[0], mine[4].at[0])
        load.start()

        def loads(i):
            at_blocks = pl.ds(i * size, size)
            return [
                pltpu.make_async_copy(fed_ref.at[:, at_blocks], xs, sems.at[0]),
                pltpu.make_async_copy(low_ref.at[:, at_blocks], ys, sems.at[1]),
                pltpu.make_async_copy(dgu_ref.at[:, at_blocks], dgu, sems.at[2]),
                pltpu.make_async_copy(hid_ref.at[:, at_blocks], hid, sems.at[3]),
            ]

        for copy in loads(0):
            copy.start()
        at.greet_all()
        load.wait()

        def sums(i):
            def one(j, carry):
                cols = pl.ds(pl.multiple_of(j * tile, tile), tile)
                pair_term = t_dot(xs[:, :, :, cols].reshape(count, tile), dgu[...].reshape(count, 2 * window))
                down_term = t_dot(hid[...].reshape(count, window), ys[:, :, :, cols].reshape(count, tile))
                if i == 0:
                    pair_sum[cols] = pair_term
                    down_sum[:, cols] = down_term
                else:
                    pair_sum[cols] = pair_sum[cols] + pair_term
                    down_sum[:, cols] = down_sum[:, cols] + down_term
                return carry

            for copy in loads(i):
                copy.wait()
            lax.fori_loop(0, D // tile, one, 0)
            if i + 1 < chunks:
                for copy in loads(i + 1):
                    copy.start()

        to, _ = pairwise(n, at.c, at.b)
        other_to, _ = pairwise(n, at.c, 1 - at.b)
        give_down = pltpu.make_async_copy(down_out, down_ref, sems.at[4])

        def lowered(i):
            def one(r, carry):
                here = pl.ds(pl.multiple_of(r * 16, 16), 16)
                mine_at = pl.ds(pl.multiple_of(to(i) * rows_d + r * 16, 16), 16)
                other_at = pl.ds(pl.multiple_of(other_to(i) * rows_d + r * 16, 16), 16)
                return_refs[0][i, here] = pair_sum[mine_at].astype(BF16)
                given[i, here] = pair_sum[other_at].astype(BF16)
                return carry

            lax.fori_loop(0, rows_d // 16, one, 0)

        def lowered_down():
            def one(r, carry):
                here = pl.ds(pl.multiple_of(r * 16, 16), 16)
                down_out[here] = down_sum[here].astype(BF16)
                return carry

            lax.fori_loop(0, window // 16, one, 0)
            give_down.start()

        def prepare():
            for i in range(chunks):
                sums(i)
                if i % 2 == 1:
                    yield
            lowered_down()

        issue, finish = return_task(at, None, got_ref, *return_refs, given=given, fill=lowered, prepare=prepare)

        def main():
            yield from scatter_steps(at, raw2, *mine)
            feed_ref[...] = jnp.zeros_like(feed_ref)
            post_ref[...] = jnp.zeros_like(post_ref)

            def norms(u, r):
                dy, v = raw2[u, r].astype(F32), mixed_ref[u, r]
                inverse = inverse_rms(v)
                grad = cot_ref[u, r].astype(F32) + norm_back(v, inverse, dy * vec_ref[2:3])
                feed_ref[...] += jnp.sum(dy * v * inverse, axis=0, keepdims=True)
                grad_ref[u, r] = grad
                w = raw_ref[u, r].astype(F32)
                inverse = inverse_rms(w)
                x[u, r] = norm_back(w, inverse, grad * vec_ref[1:2]).astype(BF16)
                post_ref[...] += jnp.sum(grad * w * inverse, axis=0, keepdims=True)

            each_rows(group, rows, norms)
            yield from gather_steps(half_at, x, all_ref, *gather_refs)

        together(main(), (issue, finish))
        give_down.wait()

    return pl.pallas_call(
        kernel,
        out_shape=(
            jax.ShapeDtypeStruct(mixed.shape, F32),
            jax.ShapeDtypeStruct((1, D), F32),
            jax.ShapeDtypeStruct((1, D), F32),
            jax.ShapeDtypeStruct((2, half, rows, D), BF16),
            jax.ShapeDtypeStruct((n, rows_d, 2 * window), BF16),
            jax.ShapeDtypeStruct((window, D), BF16),
        ),
        in_specs=[ANY] * 5 + [INVMEM] * 4,
        out_specs=(INVMEM,) * 3 + (ANY,) * 3,
        scratch_shapes=sc
        + gs
        + rs
        + [
            pltpu.VMEM(mixed.shape, BF16),
            pltpu.VMEM(mixed.shape, BF16),
            pltpu.VMEM((group, size, rows, D), BF16),
            pltpu.VMEM((group, size, rows, D), BF16),
            pltpu.VMEM((group, size, rows, 2 * window), BF16),
            pltpu.VMEM((group, size, rows, window), BF16),
            pltpu.VMEM((D, 2 * window), F32),
            pltpu.VMEM((window, D), F32),
            pltpu.VMEM((half, rows_d, 2 * window), BF16),
            pltpu.VMEM((window, D), BF16),
            dma(5),
        ],
        compiler_params=params(cid, 63),
        name="back",
    )(p, fed, down_low, pair_low, hidden, mixed, raw, cotangent, vectors)


def assemble_task(grid, got_ref, targets, wide, high, load_sem, stores):
    n = grid.n
    units, window, _ = feed_windows(grid)
    inner = n // HEADS
    whole = inner * units
    starts = [i * units // 128 * 128 for i in range(inner)]
    load = pltpu.make_async_copy(got_ref, wide, load_sem.at[0])

    def store(k):
        return pltpu.make_async_copy(high.at[k], targets[k], stores.at[k])

    def put(g, k):
        for t in range(0, whole, 128):
            total = 0.0
            for i in range(inner):
                if 0 <= t - starts[i] < window:
                    total = total + wide[g * inner + i, :, pl.ds(k * window + t - starts[i], 128)].astype(F32)
            high[k, :, pl.ds(pl.multiple_of(g * whole + t, 128), 128)] = total.astype(BF16)

    def issue():
        load.start()
        yield
        yield
        load.wait()
        for k in range(2):

            def one(g, carry):
                put(g, k)
                return carry

            lax.fori_loop(0, n // inner, one, 0)
            store(k).start()
            yield

    def finish():
        for k in range(2):
            store(k).wait()

    return issue(), finish


def assemble_scratch(grid):
    _, window, _ = feed_windows(grid)
    rows_d = D // grid.n
    return [pltpu.VMEM((grid.n, rows_d, 2 * window), BF16), pltpu.VMEM((2, rows_d, FF), BF16), dma(1), dma(2)]


def gains_task(at, x_ref, out_ref, total, other, every, sems, *share_refs):
    copy = at.sibling(x_ref, other, sems.at[0], sems.at[1])
    later, end = share_task(at, [lambda to: total], [lambda j: every.at[j]], *share_refs)

    def issue():
        copy.start()
        yield
        copy.wait()
        total[...] = x_ref[...] + other[...]
        yield from later

    def finish():
        end()
        out_ref[...] = jnp.sum(every[...], axis=0)

    return issue(), finish


def normed(value, gain):
    return value * lax.rsqrt(jnp.mean(value * value, axis=-1, keepdims=True) + 1e-06) * gain


def angles(places, head):
    freqs = 10000.0 ** (-(jnp.arange(head // 2, dtype=F32) * 2.0 / head))
    return places.astype(F32)[..., None] * freqs


def rotate(values, cosine, sine):
    half = values.shape[-1] // 2
    first = values[..., :half]
    second = values[..., half:]
    return jnp.concatenate([first * cosine - second * sine, second * cosine + first * sine], axis=-1)


def width_step(number):
    remainder = number % 3
    return jnp.where(remainder == 0, 1.0, jnp.where(remainder == 1, 16.0, 64.0)).astype(F32)


def dequantized(codes, column_scale, step):
    offset = jnp.where(step > 1.0, 0.5 * step, 0.0)
    level = jnp.floor(codes.astype(F32) / step) * step + offset
    return (level * column_scale[None, :]).astype(BF16)


def dot(left, right):
    return jnp.dot(left, right, preferred_element_type=F32)


def dot_t(left, right):
    return lax.dot_general(left, right, (((1,), (1,)), ((), ())), preferred_element_type=F32)


def t_dot(left, right):
    return lax.dot_general(left, right, (((0,), (0,)), ((), ())), preferred_element_type=F32)


def unwindowed(grid, got):
    n, rows, window = got.shape
    units = FF // n
    inner = n // HEADS
    whole = inner * units
    got = got.astype(F32).reshape(n // inner, inner, rows, window)
    total = 0.0
    for i in range(inner):
        start = i * units // 128 * 128
        total = total + jnp.pad(got[:, i], ((0, 0), (0, 0), (start, whole - start - window)))
    return jnp.transpose(total, (1, 0, 2)).reshape(rows, FF)


def on_device(
    grid,
    tokens,
    segments,
    positions,
    cotangent,
    query_codes,
    key_codes,
    value_codes,
    output_codes,
    gate_codes,
    up_codes,
    down_codes,
    query_scale,
    key_scale,
    value_scale,
    output_scale,
    gate_scale,
    up_scale,
    down_scale,
    attention_gain,
    attention_post_gain,
    feed_gain,
    feed_post_gain,
):
    n = grid.n
    group, block, _ = tokens.shape
    length = n * block
    pairs = HEADS // KV_HEADS
    scale = HEAD ** (-0.5)
    chip, core = lax.axis_index("seq"), lax.axis_index("batch")
    half = n // 2
    member = chip // half
    head = chip % HEADS
    kv_head = head // pairs
    parts = half // HEADS
    copies = n // HEADS
    asked = length // parts
    first_asked = ((chip % half) // HEADS) * asked
    steps = [width_step(core * group + m) for m in range(group)]
    step = width_step(core * group + member)
    rows_d = D // n
    units, window, _ = feed_windows(grid)

    whole = fits(grid, block) and parts == 1
    vectors = jnp.stack(
        [attention_gain, attention_post_gain, feed_gain, feed_post_gain, output_scale, down_scale]
    )

    q_parts = jnp.transpose(query_codes.reshape(rows_d, HEADS, HEAD), (1, 0, 2))
    k_parts = jnp.repeat(jnp.transpose(key_codes.reshape(rows_d, KV_HEADS, HEAD), (1, 0, 2)), pairs, axis=0)
    v_parts = jnp.repeat(jnp.transpose(value_codes.reshape(rows_d, KV_HEADS, HEAD), (1, 0, 2)), pairs, axis=0)
    qkv_parts = jnp.concatenate([q_parts, k_parts, v_parts], axis=-1).astype(BF16)
    small = jnp.zeros((8, 128), jnp.int32).at[:group, :block].set(positions)
    tokens, seen, qkv_codes, out_codes, all_places, gate_low, up_low = open_kernel(
        grid,
        tokens,
        vectors,
        qkv_parts,
        output_codes.astype(BF16),
        small,
        gate_codes,
        up_codes,
        not whole,
        1,
    )
    seen = seen.reshape(length, D)

    qkv_scale = jnp.concatenate(
        [
            lax.dynamic_slice_in_dim(query_scale, head * HEAD, HEAD),
            lax.dynamic_slice_in_dim(key_scale, kv_head * HEAD, HEAD),
            lax.dynamic_slice_in_dim(value_scale, kv_head * HEAD, HEAD),
        ]
    )
    def swapped_back(kept):
        own, other = (lax.dynamic_index_in_dim(kept, u, 0, False) for u in (member, 1 - member))
        other = lax.ppermute(other, "seq", [(c, (c + half) % n) for c in range(n)])
        return jnp.where(member == 0, jnp.stack([own, other]), jnp.stack([other, own]))

    def spread(part):
        if parts > 1:
            part = lax.dynamic_update_slice_in_dim(jnp.zeros((length, D), BF16), part, first_asked, 0)
        return part.reshape(2, half, block, D)

    places_all = lax.dynamic_index_in_dim(all_places[:, :group, :block], member, 1, False).reshape(length)
    turn = angles(places_all, HEAD)
    cosine, sine = jnp.cos(turn), jnp.sin(turn)
    q_index = first_asked + jnp.arange(asked, dtype=jnp.int32)
    pair_scale = jnp.concatenate(
        [lax.dynamic_slice_in_dim(s, chip * units // 128 * 128, window) for s in (gate_scale, up_scale)]
    )[None]
    if whole:
        start = (q_index - places_all)[:, None]
        (
            *kept_heads, cotangent, attention_raw, mixed, fed, gate_up, down_part, pair_matrices, down_matrices,
        ) = forward_kernel(
            grid,
            seen,
            qkv_codes.reshape(D, 3 * HEAD),
            out_codes,
            qkv_scale[None],
            cosine,
            sine,
            start,
            tokens,
            cotangent,
            gate_low,
            up_low,
            down_codes,
            pair_scale,
            vectors,
            2,
        )
    else:
        qkv_matrix = dequantized(qkv_codes.reshape(D, 3 * HEAD), qkv_scale, step)
        out_matrix = dequantized(out_codes.reshape(HEAD, D), output_scale, step)
        if parts == 1:
            seen_asked, places_asked, cosine_q, sine_q = seen, places_all, cosine, sine
            projected = dot(seen, qkv_matrix)
            q_lin, kv_lin = projected[:, :HEAD], projected[:, HEAD:]
        else:
            seen_asked, places_asked, cosine_q, sine_q = [
                lax.dynamic_slice_in_dim(a, first_asked, asked) for a in (seen, places_all, cosine, sine)
            ]
            q_lin, kv_lin = dot(seen_asked, qkv_matrix[:, :HEAD]), dot(seen, qkv_matrix[:, HEAD:])
        queries = rotate(q_lin, cosine_q, sine_q).astype(BF16)
        keys = rotate(kv_lin[:, :HEAD], cosine, sine).astype(BF16)
        values = kv_lin[:, HEAD:].astype(BF16)
        key_index = jnp.arange(length, dtype=jnp.int32)
        allowed = (key_index[None, :] <= q_index[:, None]) & (key_index[None, :] >= (q_index - places_asked)[:, None])
        bent = jnp.tanh(dot_t(queries, keys) * scale / cap_limit)
        kernel = jnp.where(allowed, jnp.exp(cap_limit * bent), 0.0)
        totals = jnp.sum(kernel, axis=-1, keepdims=True)
        kernel_low = kernel.astype(BF16)
        attended = dot(kernel_low, values) / totals
        attended_low = attended.astype(BF16)

        out_part = spread(dot(attended_low, out_matrix).astype(BF16))
    first_column = chip * units // 128 * 128
    if whole:
        output, grad_post_feed, down_low, second_part, pair_low, hidden = turn_kernel(
            grid, down_part, mixed, cotangent, gate_up, pair_matrices, down_matrices, vectors, 3
        )
        grad_mixed, grad_pre_feed, grad_post_attention, attention_low, pair_got, down_grad = back_kernel(
            grid,
            second_part,
            fed,
            down_low,
            pair_low,
            hidden,
            mixed,
            attention_raw,
            cotangent,
            vectors,
            4,
        )
    else:
        cotangent = swapped_back(cotangent)
        attention_raw, gate_got, up_got = attention_sums(grid, out_part, gate_low, up_low, 2)
        attention_raw = attention_raw.astype(F32)
        feed_weights = (
            gate_got.reshape(D, window),
            up_got.reshape(D, window),
            down_codes,
            pair_scale,
            down_scale[None],
        )
        mixed = tokens.astype(F32) + normed(attention_raw, attention_post_gain)
        second_normed = normed(mixed, feed_gain).astype(BF16)
        fed, gate_up, down_part, pair_matrices, down_matrices = feed_forward(grid, second_normed, *feed_weights, 3)
        down_raw = feed_sums(grid, down_part, 4).astype(F32)
        branch, pull_out = jax.vjp(normed, down_raw, feed_post_gain)
        output = swapped_back((mixed + branch).astype(BF16))
        upstream = cotangent.astype(F32)
        grad_down_raw, grad_post_feed = pull_out(upstream)
        down_low, second_part, pair_low, hidden = feed_backward(
            grid, grad_down_raw.astype(BF16), gate_up, pair_matrices, down_matrices, 9
        )
        count = group * length
        pair_grad = t_dot(fed.reshape(count, D), pair_low.reshape(count, 2 * window)).astype(BF16)
        down_grad = t_dot(hidden.reshape(count, window), down_low.reshape(count, D)).astype(BF16)
        grad_second, pair_got = feed_back_sums(grid, second_part, pair_grad.reshape(n, rows_d, 2 * window), 5)
        gate_grad, up_grad = (unwindowed(grid, pair_got[..., i * window : (i + 1) * window]) for i in range(2))
        _, pull_feed = jax.vjp(normed, mixed, feed_gain)
        grad_mixed_part, grad_pre_feed = pull_feed(grad_second.astype(F32))
        grad_mixed = upstream + grad_mixed_part
        _, pull_post = jax.vjp(normed, attention_raw, attention_post_gain)
        grad_attention, grad_post_attention = pull_post(grad_mixed)
        attention_low = gather(grid, grad_attention.astype(BF16), grid.planes // 2, 6)

    attention_low = attention_low.reshape(length, D)
    if whole:
        first_part, qkv_grad, out_part, grad_pre_attention = attention_backward(
            seen, attention_low, *kept_heads, vectors, cosine, sine, start
        )
    else:
        if parts > 1:
            attention_low = lax.dynamic_slice_in_dim(attention_low, first_asked, asked)
        grad_attended = dot_t(attention_low, out_matrix)
        grad_sums = (grad_attended / totals).astype(BF16)
        offsets = jnp.sum(grad_attended * attended, axis=-1, keepdims=True) / totals
        grad_kernel = dot_t(grad_sums, values) - offsets
        grad_raw = (kernel * grad_kernel * (1.0 - bent * bent)).astype(BF16)
        grad_q = dot(grad_raw, keys) * scale
        grad_k = t_dot(grad_raw, queries) * scale
        grad_v = t_dot(kernel_low, grad_sums)
        q_low = rotate(grad_q, cosine_q, -sine_q).astype(BF16)
        kv_low = jnp.concatenate([rotate(grad_k, cosine, -sine), grad_v], axis=-1).astype(BF16)
        if parts == 1:
            qkv_low = jnp.concatenate([q_low, kv_low], axis=-1)
            first_part = dot_t(qkv_low, qkv_matrix)
            qkv_grad = t_dot(seen, qkv_low)
        else:
            first_part = dot_t(kv_low, qkv_matrix[:, HEAD:])
            q_back = dot_t(q_low, qkv_matrix[:, :HEAD])
            first_part = lax.dynamic_update_slice_in_dim(
                first_part, lax.dynamic_slice_in_dim(first_part, first_asked, asked) + q_back, first_asked, 0
            )
            qkv_grad = jnp.concatenate([t_dot(seen_asked, q_low), t_dot(seen, kv_low)], axis=-1)
        first_part = first_part.astype(BF16)
        grad_pre_attention = jnp.sum(first_part.astype(F32) * seen.astype(F32), axis=0) / attention_gain
        out_part = t_dot(attended_low, attention_low).astype(BF16)
    gains = jnp.stack(
        [g.reshape(D) for g in (grad_pre_attention, grad_post_attention, grad_pre_feed, grad_post_feed)]
    )
    out_part = out_part.reshape(copies, HEAD // copies, D)
    merged = (pair_got, grad_mixed, tokens, vectors) if whole else ()
    grad_in, qkv_got, out_got, down_grad, gains, *assembled = attention_back_sums(
        grid,
        first_part.reshape(2, half, block, D),
        qkv_grad.astype(BF16).reshape(n, rows_d, 3 * HEAD),
        out_part,
        down_grad,
        gains,
        merged,
        7,
    )
    if merged:
        gate_grad, up_grad = (a.astype(F32) for a in assembled)
    else:
        _, pull_in = jax.vjp(lambda value: normed(value, attention_gain), tokens.astype(F32))
        (grad_source_part,) = pull_in(grad_in.astype(F32))
        grad_in = swapped_back((grad_mixed + grad_source_part).astype(BF16))
    down_grad = down_grad.astype(F32)
    qkv_got = jnp.sum(qkv_got.astype(F32).reshape(copies, HEADS, rows_d, 3 * HEAD), axis=0)
    query_grad = jnp.transpose(qkv_got[..., :HEAD], (1, 0, 2)).reshape(rows_d, HEADS * HEAD)
    kv_grad = jnp.sum(qkv_got[..., HEAD:].reshape(KV_HEADS, pairs, rows_d, 2 * HEAD), axis=1)
    key_grad = jnp.transpose(kv_grad[..., :HEAD], (1, 0, 2)).reshape(rows_d, KV_HEADS * HEAD)
    value_grad = jnp.transpose(kv_grad[..., HEAD:], (1, 0, 2)).reshape(rows_d, KV_HEADS * HEAD)
    out_grad = jnp.sum(out_got.astype(F32), axis=0)
    return (
        output,
        grad_in,
        query_grad,
        key_grad,
        value_grad,
        out_grad,
        gate_grad,
        up_grad,
        down_grad,
    ) + tuple(gains[i] for i in range(4))


def solution(mesh):
    rows = P("seq", None)
    return jax.shard_map(
        functools.partial(on_device, Grid(mesh.shape["seq"])),
        mesh=mesh,
        in_specs=(P("batch", "seq", None), P("batch", "seq"), P("batch", "seq"), P("batch", "seq", None))
        + (rows,) * 7
        + (P(),) * 11,
        out_specs=(P("batch", "seq", None),) * 2 + (rows,) * 7 + (P(),) * 4,
        check_vma=False,
    )
```

```python
import functools

import jax
import jax.numpy as jnp
from jax import lax
from jax.experimental import pallas as pl
from jax.experimental.pallas import tpu as pltpu
from jax.sharding import PartitionSpec as P

D = 2304
HEADS = 8
KV_HEADS = 4
HEAD = 256
FF = 9216
MESH = pl.DeviceIdType.MESH
F32 = jnp.float32
BF16 = jnp.bfloat16


cap_limit = 50.0


class Grid:
    def __init__(self, n):
        self.n = n
        self.planes = 4 if n % 8 == 0 else 2
        self.plane = n // self.planes
        wide = 1
        while wide * wide < self.plane:
            wide *= 2
        self.wide = wide

    def snake(self, p):
        y, x = p // self.wide, p % self.wide
        return y * self.wide + x + (y % 2) * (self.wide - 1 - 2 * x)


def remote(src, dst, send, recv, chip, core):
    return pltpu.make_async_remote_copy(
        src_ref=src, dst_ref=dst, send_sem=send, recv_sem=recv, device_id=(chip, core), device_id_type=MESH
    )


def greet(barrier, chip, core):
    pl.semaphore_signal(barrier, inc=1, device_id=(chip, core), device_id_type=MESH)


class Place:
    def __init__(self, grid, levels):
        self.grid, self.levels = grid, levels
        self.n, self.pn = grid.n, grid.plane
        self.steps = self.pn // 2
        self.c, self.b = lax.axis_index("seq"), lax.axis_index("batch")
        self.z, p = self.c // self.pn, self.c % self.pn
        self.q = grid.snake(p)
        self.zi = self.z % levels
        self.right = self.z * self.pn + grid.snake((self.q + 1) % self.pn)
        self.left = self.z * self.pn + grid.snake((self.q + self.pn - 1) % self.pn)
        self.member = self.c // (self.n // 2)
        self.partner = (self.c + self.n // 2) % self.n

    def slot(self, zj, qj):
        return zj * self.pn + self.grid.snake((qj + 2 * self.pn) % self.pn)

    def sibling(self, src, dst, send, recv):
        return remote(src, dst, send, recv, self.c, 1 - self.b)

    def greet_near(self, halves):
        barrier = pltpu.get_barrier_semaphore()
        zi, levels = self.zi, self.levels
        greet(barrier, self.right, self.b)
        greet(barrier, self.left, self.b)
        pl.when(zi > 0)(lambda: greet(barrier, self.c - self.pn, self.b))
        pl.when(zi < levels - 1)(lambda: greet(barrier, self.c + self.pn, self.b))
        if halves:
            greet(barrier, self.partner, self.b)
        count = 2 + jnp.where(zi > 0, 1, 0) + jnp.where(zi < levels - 1, 1, 0) + (1 if halves else 0)
        pl.semaphore_wait(barrier, count)

    def greet_all(self):
        barrier = pltpu.get_barrier_semaphore()
        greet(barrier, self.c, 1 - self.b)

        def one(off, carry):
            greet(barrier, (self.c + off) % self.n, self.b)
            return carry

        lax.fori_loop(1, self.n, one, 0)
        pl.semaphore_wait(barrier, self.n)


def present(zi, sign, d, levels):
    if d == 0:
        return None
    return (zi - d >= 0) if sign < 0 else (zi + d < levels)


def guarded(condition, action):
    if condition is None:
        action()
    else:
        pl.when(condition)(action)


def dma(*shape):
    return pltpu.SemaphoreType.DMA(shape)


ANY = pl.BlockSpec(memory_space=pl.ANY)
INVMEM = pl.BlockSpec(memory_space=pltpu.VMEM)


def params(cid, mib=None):
    if mib is None:
        return pltpu.CompilerParams(collective_id=cid, has_side_effects=True)
    return pltpu.CompilerParams(collective_id=cid, has_side_effects=True, vmem_limit_bytes=mib * 2**20)


def gather_sems(grid, levels, passes=1):
    steps = grid.plane // 2
    return [
        dma(passes, 2, levels),
        dma(passes, 2, levels),
        dma(passes, 2, steps, levels),
        dma(passes, 2, steps, levels),
        dma(3),
    ]


def gather_steps(at, x_ref, out_ref, zs, zr, rs, rr, ls, passes=((0, 2),), ready=None):
    levels, steps, zi, q, pn, b = at.levels, at.steps, at.zi, at.q, at.pn, at.b
    half = x_ref.shape[1] // 2
    own = at.slot(zi, q)

    def block(us, zj, qj, part=None):
        u0, nu = us
        if part is None:
            return out_ref.at[pl.ds(u0, nu), at.slot(zj, qj)]
        return out_ref.at[pl.ds(u0, nu), at.slot(zj, qj), pl.ds(part * half, half)]

    def z_copy(k, us, zj, sign):
        way = 0 if sign > 0 else 1
        ref = block(us, zj, q)
        return remote(ref, ref, zs.at[k, way, zj], zr.at[k, way, zj], (at.c + at.n + sign * pn) % at.n, b)

    def r_copy(k, us, zj, way, step, landing=False):
        away = step if landing else step - 1
        ref = block(us, zj, q - away if way == 0 else q + away, way if step == steps else None)
        to = at.right if way == 0 else at.left
        return remote(ref, ref, rs.at[k, way, step - 1, zj], rr.at[k, way, step - 1, zj], to, b)

    def arrive(k, us, sign, d):
        zj = zi + sign * d

        def go():
            if d > 0:
                z_copy(k, us, zj, -sign).wait_recv()
            if sign <= 0:
                pl.when(zi < levels - 1)(lambda: z_copy(k, us, zj, 1).start())
            if sign >= 0:
                pl.when(zi > 0)(lambda: z_copy(k, us, zj, -1).start())
            for way in (0, 1):
                r_copy(k, us, zj, way, 1).start()

        guarded(present(zi, sign, d, levels), go)

    def onward(k, us, sign, d):
        zj = zi + sign * d

        def go():
            for step in range(1, steps + 1):
                for way in (0, 1):
                    r_copy(k, us, zj, way, step, True).wait_recv()
                    if step < steps:
                        r_copy(k, us, zj, way, step + 1).start()

        guarded(present(zi, sign, d, levels), go)

    def finish(k, us, sign, d):
        zj = zi + sign * d

        def go():
            if sign <= 0:
                pl.when(zi < levels - 1)(lambda: z_copy(k, us, zj, 1).wait_send())
            if sign >= 0:
                pl.when(zi > 0)(lambda: z_copy(k, us, zj, -1).wait_send())
            for way in (0, 1):
                for step in range(1, steps + 1):
                    r_copy(k, us, zj, way, step).wait_send()

        guarded(present(zi, sign, d, levels), go)

    waves = [
        [(k, us, sign, d) for sign in ((0,) if d == 0 else (-1, 1))] for k, us in enumerate(passes) for d in range(levels)
    ]
    for i, wave in enumerate(waves):
        k, (u0, nu), _, d = wave[0]
        if d == 0:
            if ready is not None:
                ready(k)
            local = pltpu.make_async_copy(x_ref.at[pl.ds(u0, nu)], out_ref.at[pl.ds(u0, nu), own], ls.at[k])
            local.start()
            local.wait()
        for group in wave:
            arrive(*group)
            yield
        if i > 0:
            for group in waves[i - 1]:
                onward(*group)
                yield
    for group in waves[-1]:
        onward(*group)
        yield
    for wave in waves:
        for group in wave:
            finish(*group)


def run(steps):
    for _ in steps:
        pass


def gather(grid, x, levels, cid):
    count = levels * grid.plane

    def kernel(x_ref, out_ref, *sems):
        at = Place(grid, levels)
        at.greet_near(False)
        run(gather_steps(at, x_ref, out_ref, *sems))

    return pl.pallas_call(
        kernel,
        out_shape=jax.ShapeDtypeStruct((2, count) + x.shape[1:], x.dtype),
        in_specs=[INVMEM],
        out_specs=ANY,
        scratch_shapes=gather_sems(grid, levels),
        compiler_params=params(cid, 50),
        name="gather_%d" % count,
    )(x)


def level_sems(grid, levels):
    steps = grid.plane // 2
    return gather_sems(grid, levels) + [dma(2, levels), dma(2, levels), dma(2, steps), dma(2, steps)]


class LevelGather:
    def __init__(self, split, at, x_ref, out_ref, zs, zr, rs, rr, ls, lzs, lzr, lrs, lrr):
        self.at, self.x, self.out = at, x_ref, out_ref
        self.zs, self.zr, self.rs, self.rr, self.ls = zs, zr, rs, rr, ls
        self.lzs, self.lzr, self.lrs, self.lrr = lzs, lzr, lrs, lrr
        rows = x_ref.shape[1]
        cut = rows * 3 // 4 // 16 * 16 if split else rows
        self.split, self.first, self.last = split, pl.ds(0, cut), pl.ds(cut, rows - cut)

    def block(self, zj, qj, part, rows):
        which = pl.ds(0, 2) if part is None else pl.ds(part, 1)
        return self.out.at[which, self.at.slot(zj, qj), rows]

    def z_copy(self, zj, way):
        at, ref = self.at, self.block(zj, self.at.q, None, self.first)
        to = (at.c + at.n + (at.pn if way == 0 else -at.pn)) % at.n
        return remote(ref, ref, self.zs.at[0, way, zj], self.zr.at[0, way, zj], to, at.b)

    def ring_copy(self, zj, way, step, landing, rows, send, recv):
        at = self.at
        away = step if landing else step - 1
        ref = self.block(zj, at.q - away if way == 0 else at.q + away, way if step == at.steps else None, rows)
        return remote(ref, ref, send, recv, at.right if way == 0 else at.left, at.b)

    def r_copy(self, zj, way, step, landing=False):
        sems = self.rs.at[0, way, step - 1, zj], self.rr.at[0, way, step - 1, zj]
        return self.ring_copy(zj, way, step, landing, self.first, *sems)

    def low_copy(self, way, step, landing=False):
        sems = self.lrs.at[way, step - 1], self.lrr.at[way, step - 1]
        return self.ring_copy(self.at.zi, way, step, landing, self.last, *sems)

    def low_z_copy(self, zj, way):
        at = self.at
        ref = self.out.at[:, pl.ds(zj * at.pn, at.pn), self.last]
        to = (at.c + at.n + (at.pn if way == 0 else -at.pn)) % at.n
        return remote(ref, ref, self.lzs.at[way, zj], self.lzr.at[way, zj], to, at.b)

    def begin(self):
        at = self.at
        local = pltpu.make_async_copy(self.x, self.out.at[:, at.slot(at.zi, at.q)], self.ls.at[0])
        local.start()
        local.wait()
        self.send(0)
        if self.split:
            for way in (0, 1):
                self.low_copy(way, 1).start()

    def along(self, offset, copy):
        at = self.at
        zj = at.zi + offset
        pl.when((offset <= 0) & (at.zi < at.levels - 1))(lambda: copy(zj, 0).start())
        pl.when((offset >= 0) & (at.zi > 0))(lambda: copy(zj, 1).start())

    def send(self, offset):
        self.along(offset, self.z_copy)
        for way in (0, 1):
            self.r_copy(self.at.zi + offset, way, 1).start()

    def arrive(self, sign, d):
        self.z_copy(self.at.zi + sign * d, 0 if sign < 0 else 1).wait_recv()
        self.send(sign * d)

    def low_arrive(self, sign, d):
        self.low_z_copy(self.at.zi + sign * d, 0 if sign < 0 else 1).wait_recv()
        self.along(sign * d, self.low_z_copy)

    def onward(self, sign, d):
        zj = self.at.zi + sign * d
        for step in range(1, self.at.steps):
            for way in (0, 1):
                self.r_copy(zj, way, step, True).wait_recv()
                self.r_copy(zj, way, step + 1).start()

    def low_onward(self):
        for step in range(1, self.at.steps):
            for way in (0, 1):
                self.low_copy(way, step, True).wait_recv()
                self.low_copy(way, step + 1).start()

    def low_landed(self):
        for way in (0, 1):
            self.low_copy(way, self.at.steps, True).wait_recv()
        self.along(0, self.low_z_copy)

    def landed(self, sign, d):
        zj = self.at.zi + sign * d
        for way in (0, 1):
            self.r_copy(zj, way, self.at.steps, True).wait_recv()

    def finish(self):
        at = self.at

        def one(zj, carry):
            for copy in (self.z_copy, self.low_z_copy)[: 2 if self.split else 1]:
                pl.when((zj <= at.zi) & (at.zi < at.levels - 1))(lambda: copy(zj, 0).wait_send())
                pl.when((zj >= at.zi) & (at.zi > 0))(lambda: copy(zj, 1).wait_send())
            for way in (0, 1):
                for step in range(1, at.steps + 1):
                    self.r_copy(zj, way, step).wait_send()
            return carry

        lax.fori_loop(0, at.levels, one, 0)
        for way in (0, 1) if self.split else ():
            for step in range(1, at.steps + 1):
                self.low_copy(way, step).wait_send()

    def run(self, compute, first=None):
        at = self.at
        zi, levels = at.zi, at.levels

        def wave(t):
            pl.when((t < levels) & (zi - t >= 0))(lambda: self.arrive(-1, t))
            pl.when((t < levels) & (zi + t < levels))(lambda: self.arrive(1, t))

        def both(d, action, least=0):
            pl.when((d >= least) & (d < levels) & (zi - d >= 0))(lambda: action(-1, d))
            pl.when((d > 0) & (d < levels) & (zi + d < levels))(lambda: action(1, d))

        def one(t, carry):
            wave(t)
            if self.split:
                pl.when(t == 2)(self.low_landed)
            both(t - 1, self.onward)
            if first is not None:
                pl.when(t == 2)(first)
            e = t - 2
            if self.split:
                both(e, self.low_arrive, 1)
            both(e, self.landed)

            def side(i, carry):
                zj = zi + (2 * i - 1) * e
                here = (zj >= 0) & (zj < levels) & ((e > 0) | (i == 0))
                pl.when(here)(lambda: compute(zj, e == 0))
                return carry

            lax.fori_loop(0, 2, side, 0)
            return carry

        wave(1)
        both(0, self.onward)
        if self.split:
            self.low_onward()
        lax.fori_loop(2, levels + 2, one, 0)
        self.finish()


def member_step(core, group, member):
    remainder = (core * group + member) % 3
    return jnp.where(remainder == 0, 1.0, jnp.where(remainder == 1, 16.0, 64.0)).astype(F32)


def dequantize(core, group, codes, row_scale, into, rows, first):
    def one(i, carry):
        value = codes(pl.multiple_of(i * 16, 16)).astype(F32)
        for m in range(group):
            step = member_step(core, group, m)
            offset = jnp.where(step > 1.0, 0.5 * step, 0.0)
            level = jnp.floor(value * (1.0 / step)) * step + offset
            into[m, pl.ds(pl.multiple_of(first + i * 16, 16), 16)] = (level * row_scale[...]).astype(BF16)
        return carry

    lax.fori_loop(0, rows // 16, one, 0)


GELU_A = 0.7978845608028654
GELU_B = 0.044715


EARLY = 4
PER = 4


class FeedWeights:
    def __init__(self, at, group, units, gate_ref, up_ref, down_ref, kept, refs):
        self.at, self.group, self.units = at, group, units
        self.sources, self.kept = (gate_ref, up_ref, down_ref), kept
        self.pair, self.down, self.codes, self.down_codes, self.sems = refs

    @staticmethod
    def scratch(group, units, window):
        return [
            pltpu.VMEM((group, D, 2 * window), BF16),
            pltpu.VMEM((group, window, D), BF16),
            pltpu.VMEM((D, 2 * window), BF16),
            pltpu.VMEM((units, D), jnp.int32),
            dma(5),
        ]

    def copies(self):
        window = self.codes.shape[1] // 2
        gate, up, down = self.sources
        copies = [pltpu.make_async_copy(down, self.down_codes, self.sems.at[2])]
        if gate is not None:
            copies += [
                pltpu.make_async_copy(gate, self.codes.at[:, pl.ds(0, window)], self.sems.at[0]),
                pltpu.make_async_copy(up, self.codes.at[:, pl.ds(window, window)], self.sems.at[1]),
            ]
        return copies

    def keeps(self):
        return [
            pltpu.make_async_copy(self.pair, self.kept[0], self.sems.at[3]),
            pltpu.make_async_copy(self.down, self.kept[1], self.sems.at[4]),
        ]

    def load(self):
        for copy in self.copies():
            copy.start()

    def make(self, pair_scale, down_scale):
        at, group, units = self.at, self.group, self.units
        window = self.down.shape[1]
        inset = (at.c * units) % 128
        for copy in self.copies():
            copy.wait()
        dequantize(at.b, group, lambda r: self.codes[pl.ds(r, 16)], pair_scale, self.pair, D, 0)

        def clear(i, carry):
            for m in range(group):
                self.down[m, pl.ds(pl.multiple_of(i * 16, 16), 16)] = jnp.zeros((16, D), BF16)
            return carry

        if window > units:
            lax.fori_loop(0, inset // 16, clear, 0)
            lax.fori_loop((inset + units) // 16, window // 16, clear, 0)
        dequantize(at.b, group, lambda r: self.down_codes[pl.ds(r, 16)], down_scale, self.down, units, inset)
        for copy in self.keeps():
            copy.start()

    def finish(self):
        for copy in self.keeps():
            copy.wait()


def feed_blocks(grid):
    return 4 if grid.plane % 4 == 0 else grid.plane


def each_chunk(grid, zj, fresh, loads, stores, compute):
    size = feed_blocks(grid)
    m = zj // (grid.planes // 2)

    def one(i, carry):
        first = zj * grid.plane + i * size
        reads, writes = loads(first), stores(first)
        for copy in reads:
            copy.start()

        @pl.when(jnp.logical_not(fresh & (i == 0)))
        def _():
            for copy in writes:
                copy.wait()

        compute(m, reads)
        for copy in writes:
            copy.start()
        return carry

    lax.fori_loop(0, grid.plane // size, one, 0)


def copies_of(blocks, pairs, sems, first):
    return [
        pltpu.make_async_copy(a.at[:, blocks] if far_a else a, b if far_a else b.at[:, blocks], sems.at[first + k])
        for k, (a, b, far_a) in enumerate(pairs)
    ]


def forward_chunks(weights, all_ref, pair_ref, part_ref, xs, gu, part, sems):
    _, size, rows, _ = gu.shape
    window = weights.down.shape[1]

    def loads(first):
        return copies_of(pl.ds(first, size), [(all_ref, xs, True)], sems, 0)

    def stores(first):
        return copies_of(pl.ds(first, size), [(gu, pair_ref, False), (part, part_ref, False)], sems, 1)

    def compute(m, reads):
        reads[0].wait()
        both = dot(xs[...].reshape(2 * size * rows, D), weights.pair[m])
        gu[...] = both.astype(BF16).reshape(gu.shape)
        gate, up = both[:, :window], both[:, window:]
        bend = jnp.tanh(GELU_A * (gate + GELU_B * gate * gate * gate))
        hidden = (0.5 * gate * (1.0 + bend) * up).astype(BF16)
        part[...] = dot(hidden, weights.down[m]).astype(BF16).reshape(part.shape)

    return loads, stores, compute


def backward_chunks(wp, wd, all_ref, pair_ref, part_ref, dgu_ref, hid_ref, ys, gu, part, dgu, hid, sems):
    _, size, rows, _ = ys.shape
    window = wd.shape[1]
    count = 2 * size * rows

    def loads(first):
        return copies_of(pl.ds(first, size), [(all_ref, ys, True), (pair_ref, gu, True)], sems, 0)

    def stores(first):
        pairs = [(part, part_ref, False), (dgu, dgu_ref, False), (hid, hid_ref, False)]
        return copies_of(pl.ds(first, size), pairs, sems, 2)

    def compute(m, reads):
        reads[0].wait()
        grad_hidden = dot_t(ys[...].reshape(count, D), wd[m])
        reads[1].wait()
        both = gu[...].reshape(count, 2 * window).astype(F32)
        gate, up = both[:, :window], both[:, window:]
        bend = jnp.tanh(GELU_A * (gate + GELU_B * gate * gate * gate))
        bell = 0.5 * gate * (1.0 + bend)
        slope = 0.5 * (1.0 + bend) + 0.5 * gate * (1.0 - bend * bend) * GELU_A * (1.0 + 3.0 * GELU_B * gate * gate)
        dgu[:, :, :, :window] = (grad_hidden * up * slope).astype(BF16).reshape(hid.shape)
        dgu[:, :, :, window:] = (grad_hidden * bell).astype(BF16).reshape(hid.shape)
        hid[...] = (bell * up).astype(BF16).reshape(hid.shape)
        part[...] = dot_t(dgu[...].reshape(count, 2 * window), wp[m]).astype(BF16).reshape(part.shape)

    return loads, stores, compute


def chunk_buffers(size, rows, *widths):
    return [pltpu.VMEM((2, size, rows, width), BF16) for width in widths]


def feed_forward(grid, x, gate_codes, up_codes, down_codes, pair_scale, down_scale, cid):
    group, rows, _ = x.shape
    n, levels = grid.n, grid.planes
    units, window, _ = feed_windows(grid)
    gs, ws = level_sems(grid, levels), FeedWeights.scratch(group, units, window)
    size = feed_blocks(grid)

    def kernel(
        x_ref, gate_ref, up_ref, down_ref, ps_ref, ds_ref, all_ref, pair_ref, part_ref, wp_ref, wd_ref, *scratch
    ):
        refs = Split(scratch)
        at = Place(grid, levels)
        weights = FeedWeights(at, group, units, gate_ref, up_ref, down_ref, (wp_ref, wd_ref), refs.take(len(ws)))
        weights.load()
        moving = LevelGather(True, at, x_ref, all_ref, *refs.take(len(gs)))
        loads, stores, compute = forward_chunks(weights, all_ref, pair_ref, part_ref, *refs.take(4))
        at.greet_near(False)
        moving.begin()
        weights.make(ps_ref, ds_ref)
        moving.run(lambda zj, fresh: each_chunk(grid, zj, fresh, loads, stores, compute))
        for copy in stores(0):
            copy.wait()
        weights.finish()

    def blocks(width):
        return jax.ShapeDtypeStruct((group, n, rows, width), BF16)

    return pl.pallas_call(
        kernel,
        out_shape=(
            blocks(D),
            blocks(2 * window),
            blocks(D),
            jax.ShapeDtypeStruct((group, D, 2 * window), BF16),
            jax.ShapeDtypeStruct((group, window, D), BF16),
        ),
        in_specs=[INVMEM, ANY, ANY, ANY, INVMEM, INVMEM],
        out_specs=(ANY,) * 5,
        scratch_shapes=ws + gs + chunk_buffers(size, rows, D, 2 * window, D) + [dma(3)],
        compiler_params=params(cid, 60),
        name="feed_forward",
    )(x, gate_codes, up_codes, down_codes, pair_scale, down_scale)


def feed_backward(grid, x, pair, pair_matrices, down_matrices, cid):
    group, rows, _ = x.shape
    n, levels = grid.n, grid.planes
    _, window, _ = feed_windows(grid)
    gs = level_sems(grid, levels)
    size = feed_blocks(grid)

    def kernel(x_ref, pair_ref, wp_ref, wd_ref, all_ref, part_ref, dgu_ref, hid_ref, *scratch):
        refs = Split(scratch)
        at = Place(grid, levels)
        moving = LevelGather(True, at, x_ref, all_ref, *refs.take(len(gs)))
        wp, wd, fetch_sems = refs.take(3)
        fetch = [
            pltpu.make_async_copy(wp_ref, wp, fetch_sems.at[0]),
            pltpu.make_async_copy(wd_ref, wd, fetch_sems.at[1]),
        ]
        for copy in fetch:
            copy.start()
        loads, stores, compute = backward_chunks(
            wp, wd, all_ref, pair_ref, part_ref, dgu_ref, hid_ref, *refs.take(6)
        )
        at.greet_near(False)
        moving.begin()
        for copy in fetch:
            copy.wait()
        moving.run(lambda zj, fresh: each_chunk(grid, zj, fresh, loads, stores, compute))
        for copy in stores(0):
            copy.wait()

    def blocks(width):
        return jax.ShapeDtypeStruct((group, n, rows, width), BF16)

    return pl.pallas_call(
        kernel,
        out_shape=(blocks(D), blocks(D), blocks(2 * window), blocks(window)),
        in_specs=[INVMEM] + [ANY] * 3,
        out_specs=(ANY,) * 4,
        scratch_shapes=gs
        + [pltpu.VMEM((group, D, 2 * window), BF16), pltpu.VMEM((group, window, D), BF16), dma(2)]
        + chunk_buffers(size, rows, D, 2 * window, D, 2 * window, window)
        + [dma(5)],
        compiler_params=params(cid, 62),
        name="feed_backward",
    )(x, pair, pair_matrices, down_matrices)


def scatter_scratch(grid, levels, rows, width):
    steps = grid.plane // 2
    return [
        pltpu.VMEM((2, levels * grid.plane, rows, width), BF16),
        pltpu.VMEM((2, levels, 2, rows // 2, width), BF16),
        pltpu.VMEM((2, max(steps - 1, 1), levels, 2, rows, width), BF16),
        pltpu.VMEM((2, levels, 2, rows, width), BF16),
        dma(1),
        dma(1, 2, levels),
        dma(1, 2, levels),
        dma(1, 2, steps, levels),
        dma(1, 2, steps, levels),
    ]


def scatter_steps(at, out_ref, acc, ring_half, ring_full, line, ls, zs, zr, rs, rr):
    levels, steps, zi, q, pn, b = at.levels, at.steps, at.zi, at.q, at.pn, at.b
    rows = acc.shape[2]
    half = rows // 2
    passes = [(0, 2)]

    def block(us, zj, qj, part=None):
        u0, nu = us
        if part is None:
            return acc.at[pl.ds(u0, nu), at.slot(zj, qj)]
        return acc.at[pl.ds(u0, nu), at.slot(zj, qj), pl.ds(part * half, half)]

    def add(us, s, others, lo, count):
        u0, nu = us

        def one(i, carry):
            u, r = u0 + i // (count // 16), lo + (i % (count // 16)) * 16
            total = acc[u, s, pl.ds(r, 16)].astype(F32)
            for other in others:
                total = total + other(u, r)[...].astype(F32)
            acc[u, s, pl.ds(r, 16)] = total.astype(BF16)
            return carry

        lax.fori_loop(0, nu * (count // 16), one, 0)

    def full_at(way, step, zj):
        return lambda u, r: ring_full.at[way, step - 2, zj, u, pl.ds(r, 16)]

    def half_at(way, zj):
        return lambda u, r: ring_half.at[way, zj, u, pl.ds(r - way * half, 16)]

    def line_at(way, zj):
        return lambda u, r: line.at[way, zj, u, pl.ds(r, 16)]

    def r_copy(k, us, zj, way, step):
        u0, nu = us
        sign = 1 if way == 0 else -1
        target = q + sign * (steps + 1 - step)
        if step == 1:
            src, dst = block(us, zj, target, way), ring_half.at[way, zj, pl.ds(u0, nu)]
        else:
            src, dst = block(us, zj, target), ring_full.at[way, step - 2, zj, pl.ds(u0, nu)]
        to = at.right if way == 0 else at.left
        return remote(src, dst, rs.at[k, way, step - 1, zj], rr.at[k, way, step - 1, zj], to, b)

    def z_copy(k, us, zj, way):
        u0, nu = us
        to = (at.c + at.n + (pn if way == 0 else -pn)) % at.n
        return remote(block(us, zj, q), line.at[way, zj, pl.ds(u0, nu)], zs.at[k, way, zj], zr.at[k, way, zj], to, b)

    def begin(k, us, sign, d):
        def go():
            for way in (0, 1):
                r_copy(k, us, zi + sign * d, way, 1).start()

        guarded(present(zi, sign, d, levels), go)

    def middle(k, us, sign, d):
        zj = zi + sign * d

        def go():
            for step in range(1, steps):
                for way in (0, 1):
                    r_copy(k, us, zj, way, step).wait_recv()
                    s = at.slot(zj, q + (1 if way == 0 else -1) * (steps - step))
                    if step == 1:
                        add(us, s, [half_at(way, zj)], way * half, half)
                    else:
                        add(us, s, [full_at(way, step, zj)], 0, rows)
                    r_copy(k, us, zj, way, step + 1).start()

        guarded(present(zi, sign, d, levels), go)

    def last(k, us, sign, d):
        zj = zi + sign * d

        def go():
            for way in (0, 1):
                r_copy(k, us, zj, way, steps).wait_recv()
            s = at.slot(zj, q)
            if steps > 1:
                add(us, s, [full_at(0, steps, zj), full_at(1, steps, zj)], 0, rows)
            else:
                add(us, s, [half_at(0, zj)], 0, half)
                add(us, s, [half_at(1, zj)], half, half)

            def passed(way):
                z_copy(k, us, zj, way).wait_recv()
                add(us, s, [line_at(way, zj)], 0, rows)

            if sign >= 0:
                pl.when(zi > 0)(lambda: passed(0))
            if sign <= 0:
                pl.when(zi < levels - 1)(lambda: passed(1))
            if sign > 0:
                z_copy(k, us, zj, 0).start()
            if sign < 0:
                z_copy(k, us, zj, 1).start()

        guarded(present(zi, sign, d, levels), go)

    def finish(k, us, sign, d):
        zj = zi + sign * d

        def go():
            for way in (0, 1):
                for step in range(1, steps + 1):
                    r_copy(k, us, zj, way, step).wait_send()
            if sign != 0:
                z_copy(k, us, zj, 0 if sign > 0 else 1).wait_send()

        guarded(present(zi, sign, d, levels), go)

    waves = [
        [(k, us, sign, d) for sign in ((0,) if d == 0 else (-1, 1))]
        for k, us in enumerate(passes)
        for d in range(levels - 1, -1, -1)
    ]
    own = at.slot(zi, q)
    def each(action, i):
        if i < len(waves):
            for group in waves[i]:
                action(*group)

    each(begin, 0)
    each(begin, 1)
    each(middle, 0)
    yield
    for i in range(len(waves)):
        each(begin, i + 2)
        each(middle, i + 1)
        yield
        each(last, i)
    yield

    def give(src, u):
        def one(i, carry):
            out_ref[u, pl.ds(i * 16, 16)] = src.at[pl.ds(i * 16, 16)][...]
            return carry

        lax.fori_loop(0, rows // 16, one, 0)

    give(acc.at[0, own], 0)
    give(acc.at[1, own], 1)
    for wave in waves:
        for group in wave:
            finish(*group)


def split_scratch(grid, levels, rows, width):
    steps, pn = grid.plane // 2, grid.plane
    cut = rows * 3 // 4 // 16 * 16
    more = max(steps - 1, 1)
    return [
        pltpu.VMEM((2, levels * pn, rows, width), BF16),
        pltpu.VMEM((2, levels, cut, width), BF16),
        pltpu.VMEM((2, more, levels, 2, cut, width), BF16),
        pltpu.VMEM((2, levels, 2, cut, width), BF16),
        pltpu.VMEM((2, rows - cut, width), BF16),
        pltpu.VMEM((2, more, 2, rows - cut, width), BF16),
        pltpu.VMEM((2, levels, 2, pn, rows - cut, width), BF16),
        dma(1),
        dma(2, levels),
        dma(2, levels),
        dma(2, steps, levels),
        dma(2, steps, levels),
        dma(2, levels),
        dma(2, levels),
        dma(2, steps),
        dma(2, steps),
    ]


def split_scatter_steps(
    at, out_ref, acc, half_ref, full_ref, line_ref, low_half, low_full, low_line,
    ls, zs, zr, rs, rr, lzs, lzr, lrs, lrr,
):
    levels, steps, zi, q, pn, b = at.levels, at.steps, at.zi, at.q, at.pn, at.b
    rows = acc.shape[2]
    cut = half_ref.shape[2]
    upper, lower = pl.ds(0, cut), pl.ds(cut, rows - cut)

    def add(target, others, pieces):
        def one(i, carry):
            total = target(i)[...].astype(F32)
            for other in others:
                total = total + other(i)[...].astype(F32)
            target(i)[...] = total.astype(BF16)
            return carry

        lax.fori_loop(0, pieces, one, 0)

    def spans(ref, first, count):
        per = count // 16
        return lambda i: ref.at[i // per, pl.ds(pl.multiple_of(first + (i % per) * 16, 16), 16)]

    def along(way):
        return (at.c + at.n + (pn if way == 0 else -pn)) % at.n

    def r_copy(zj, way, step):
        target = at.slot(zj, q + (1 if way == 0 else -1) * (steps + 1 - step))
        if step == 1:
            src, dst = acc.at[way, target, upper], half_ref.at[way, zj]
        else:
            src, dst = acc.at[:, target, upper], full_ref.at[way, step - 2, zj]
        to = at.right if way == 0 else at.left
        return remote(src, dst, rs.at[way, step - 1, zj], rr.at[way, step - 1, zj], to, b)

    def z_copy(zj, way):
        return remote(
            acc.at[:, at.slot(zj, q), upper], line_ref.at[way, zj], zs.at[way, zj], zr.at[way, zj], along(way), b
        )

    def begin(sign, d):
        for way in (0, 1):
            r_copy(zi + sign * d, way, 1).start()

    def middle(sign, d):
        zj = zi + sign * d
        for step in range(1, steps):
            for way in (0, 1):
                r_copy(zj, way, step).wait_recv()
                s = at.slot(zj, q + (1 if way == 0 else -1) * (steps - step))
                if step == 1:
                    add(
                        lambda i: acc.at[way, s, pl.ds(pl.multiple_of(i * 16, 16), 16)],
                        [lambda i: half_ref.at[way, zj, pl.ds(pl.multiple_of(i * 16, 16), 16)]],
                        cut // 16,
                    )
                else:
                    add(spans(acc.at[:, s], 0, cut), [spans(full_ref.at[way, step - 2, zj], 0, cut)], 2 * cut // 16)
                r_copy(zj, way, step + 1).start()

    def last(sign, d):
        zj = zi + sign * d
        for way in (0, 1):
            r_copy(zj, way, steps).wait_recv()
        s = at.slot(zj, q)
        mine = spans(acc.at[:, s], 0, cut)
        add(mine, [spans(full_ref.at[way, steps - 2, zj], 0, cut) for way in (0, 1)], 2 * cut // 16)

        def passed(way):
            z_copy(zj, way).wait_recv()
            add(mine, [spans(line_ref.at[way, zj], 0, cut)], 2 * cut // 16)

        if sign >= 0:
            pl.when(zi > 0)(lambda: passed(0))
        if sign <= 0:
            pl.when(zi < levels - 1)(lambda: passed(1))
        if sign != 0:
            z_copy(zj, 0 if sign > 0 else 1).start()

    def done(sign, d):
        zj = zi + sign * d
        for way in (0, 1):
            for step in range(1, steps + 1):
                r_copy(zj, way, step).wait_send()
        if sign != 0:
            z_copy(zj, 0 if sign > 0 else 1).wait_send()

    def low_z_copy(zj, way):
        ref = acc.at[:, pl.ds(zj * pn, pn), lower]
        return remote(ref, low_line.at[way, zj], lzs.at[way, zj], lzr.at[way, zj], along(way), b)

    def low_passed(zj, way):
        low_z_copy(zj, way).wait_recv()
        per = (rows - cut) // 16

        def piece(i):
            return i // (pn * per), (i // per) % pn, (i % per) * 16

        def into(i):
            u, j, r = piece(i)
            return acc.at[u, zj * pn + j, pl.ds(pl.multiple_of(cut + r, 16), 16)]

        def come(i):
            u, j, r = piece(i)
            return low_line.at[way, zj, u, j, pl.ds(pl.multiple_of(r, 16), 16)]

        add(into, [come], 2 * pn * per)

    def low_start():
        for zj in range(levels - 1, 0, -1):
            pl.when(zi == 0)(lambda: low_z_copy(zj, 0).start())
        for zj in range(levels - 1):
            pl.when(zi == levels - 1)(lambda: low_z_copy(zj, 1).start())

    def low_stage(a):
        up, down = zi + levels - 1 - a, a - (levels - 1 - zi)

        def from_below():
            low_passed(up, 0)
            pl.when(up > zi)(lambda: low_z_copy(up, 0).start())

        def from_above():
            low_passed(down, 1)
            pl.when(down < zi)(lambda: low_z_copy(down, 1).start())

        pl.when((zi > 0) & (up >= zi) & (up < levels))(from_below)
        pl.when((zi < levels - 1) & (down >= 0) & (down <= zi))(from_above)

    def low_r_copy(way, step):
        target = at.slot(zi, q + (1 if way == 0 else -1) * (steps + 1 - step))
        if step == 1:
            src, dst = acc.at[way, target, lower], low_half.at[way]
        else:
            src, dst = acc.at[:, target, lower], low_full.at[way, step - 2]
        to = at.right if way == 0 else at.left
        return remote(src, dst, lrs.at[way, step - 1], lrr.at[way, step - 1], to, b)

    def low_middle():
        for step in range(1, steps):
            for way in (0, 1):
                low_r_copy(way, step).wait_recv()
                s = at.slot(zi, q + (1 if way == 0 else -1) * (steps - step))
                if step == 1:
                    add(
                        lambda i: acc.at[way, s, pl.ds(pl.multiple_of(cut + i * 16, 16), 16)],
                        [lambda i: low_half.at[way, pl.ds(pl.multiple_of(i * 16, 16), 16)]],
                        (rows - cut) // 16,
                    )
                else:
                    add(
                        spans(acc.at[:, s], cut, rows - cut),
                        [spans(low_full.at[way, step - 2], 0, rows - cut)],
                        2 * (rows - cut) // 16,
                    )
                low_r_copy(way, step + 1).start()

    def low_last():
        for way in (0, 1):
            low_r_copy(way, steps).wait_recv()
        add(
            spans(acc.at[:, at.slot(zi, q)], cut, rows - cut),
            [spans(low_full.at[way, steps - 2], 0, rows - cut) for way in (0, 1)],
            2 * (rows - cut) // 16,
        )

    def each(action, d):
        if d >= 0:
            for sign in (0,) if d == 0 else (-1, 1):
                guarded(present(zi, sign, d, levels), lambda: action(sign, d))

    far = levels - 1
    each(begin, far)
    low_start()
    each(begin, far - 1)
    each(middle, far)
    yield
    for a in range(1, levels):
        low_stage(a)
        d = far - a
        each(begin, d - 1)
        each(middle, d)
        yield
        each(last, d + 1)
    for way in (0, 1):
        low_r_copy(way, 1).start()
    low_middle()
    each(last, 0)
    low_last()
    yield

    def give(i, carry):
        r = pl.ds(pl.multiple_of((i % (rows // 16)) * 16, 16), 16)
        out_ref[i // (rows // 16), r] = acc[i // (rows // 16), at.slot(zi, q), r]
        return carry

    lax.fori_loop(0, 2 * (rows // 16), give, 0)
    for d in range(levels):
        each(done, d)
    for zj in range(levels):
        pl.when(zj > zi)(lambda: low_z_copy(zj, 0).wait_send())
        pl.when(zj < zi)(lambda: low_z_copy(zj, 1).wait_send())
    for way in (0, 1):
        for step in range(1, steps + 1):
            low_r_copy(way, step).wait_send()


def scatter_parts(grid, levels, rows, width):
    blocks = 2 * (2 * levels * (grid.plane // 2 + 2) + levels * grid.plane)
    parts = 1
    while blocks * rows * (width // parts) * 2 > 40 * 2**20:
        parts += 1
        while width % (128 * parts):
            parts += 1
    return parts


def in_parts(grid, levels, call, p, extra):
    parts = scatter_parts(grid, levels, p.shape[2], p.shape[3])
    if parts == 1:
        return call(p, extra)
    piece = p.shape[3] // parts
    sums, others = [], ()
    for i in range(parts):
        got = call(p[..., i * piece : (i + 1) * piece], extra if i == 0 else None)
        sums.append(got[0])
        others = got[1:] if i == 0 else others
    return (jnp.concatenate(sums, axis=-1),) + tuple(others)


def pairwise(n, c, b):
    def to(i):
        return (c + 2 * i + b) % n

    def frm(i, core):
        return (c + n - 2 * i - core) % n

    return to, frm


def middle_out(half):
    return sorted(range(1, half), key=lambda i: abs(2 * i - half))


def share_task(at, sources, views, ss, sr, fs, fr):
    n, c, b = at.n, at.c, at.b
    half = n // 2
    to, frm = pairwise(n, c, b)
    kinds = len(sources)

    def out_copy(k, i):
        return remote(sources[k](to(i)), views[k](c), ss.at[k, i], sr.at[k, i], to(i), b)

    def landed(k, i):
        return remote(sources[k](c), views[k](frm(i, b)), ss.at[k, i], sr.at[k, i], to(i), b)

    def pass_on(k, i, core):
        ref = views[k](frm(i, core))
        return at.sibling(ref, ref, fs.at[k, i], fr.at[k, i])

    def local(k):
        return pltpu.make_async_copy(sources[k](c), views[k](c), sr.at[k, 0])

    order = middle_out(half) + [0]

    def issue():
        for i in order:
            for k in range(kinds):
                if i > 0:
                    out_copy(k, i).start()
                else:
                    pl.when(b == 1)(lambda: out_copy(k, 0).start())
                    pl.when(b == 0)(lambda: local(k).start())
            yield

    def finish():
        for i in order:
            for k in range(kinds):
                if i > 0:
                    landed(k, i).wait_recv()
                else:
                    pl.when(b == 1)(lambda: landed(k, 0).wait_recv())
                    pl.when(b == 0)(lambda: local(k).wait())
                pass_on(k, i, b).start()
        for k in range(kinds):
            for i in range(half):
                pass_on(k, i, 1 - b).wait_recv()
            for i in range(half):
                pass_on(k, i, b).wait_send()
            for i in range(1, half):
                out_copy(k, i).wait_send()
            pl.when(b == 1)(lambda: out_copy(k, 0).wait_send())

    return issue(), finish


def share_sems(grid, kinds):
    return [dma(kinds, grid.n // 2) for _ in range(4)]


def tell_task(at, small_ref, all_ref, ts, tr):
    n, c, b = at.n, at.c, at.b

    def tell(off, slot):
        return remote(small_ref, all_ref.at[slot], ts.at[off], tr.at[off], (c + off) % n, b)

    keep = pltpu.make_async_copy(small_ref, all_ref.at[c], ts.at[0])

    def issue():
        keep.start()
        for off in range(1, n):
            tell(off, c).start()
        yield

    def finish():
        keep.wait()
        for off in range(1, n):
            tell(off, (c + n - off) % n).wait_recv()
        for off in range(1, n):
            tell(off, c).wait_send()

    return issue(), finish


def head_rows_task(at, x_ref, out_ref, hs, hr, fs, fr):
    c, b = at.c, at.b
    copies = at.n // HEADS
    head, rank = c % HEADS, c // HEADS
    mine = rank % 2 == b

    def out_copy(k):
        to = c // copies + HEADS * (2 * k + b)
        return to, remote(x_ref, out_ref.at[c % copies], hs.at[k], hr.at[c % copies], to, b)

    def landed(j):
        return remote(x_ref, out_ref.at[j], hs.at[0], hr.at[j], head * copies + j, b)

    def here(j):
        return pltpu.make_async_copy(x_ref, out_ref.at[j], hr.at[j])

    def pass_on(j):
        return at.sibling(out_ref.at[j], out_ref.at[j], fs.at[j], fr.at[j])

    def issue():
        for k in range(copies // 2):
            to, copy = out_copy(k)
            pl.when(to != c)(lambda: copy.start())
            pl.when(to == c)(lambda: here(c % copies).start())
            yield

    def finish():
        @pl.when(mine)
        def _():
            for j in range(copies):
                pl.when(head * copies + j != c)(lambda: landed(j).wait_recv())
                pl.when(head * copies + j == c)(lambda: here(j).wait())
                pass_on(j).start()
            for j in range(copies):
                pass_on(j).wait_send()

        @pl.when(jnp.logical_not(mine))
        def _():
            for j in range(copies):
                pass_on(j).wait_recv()

        for k in range(copies // 2):
            to, copy = out_copy(k)
            pl.when(to != c)(lambda: copy.wait_send())

    return issue(), finish


def head_rows_sems(grid):
    copies = grid.n // HEADS
    return [dma(copies), dma(copies), dma(copies), dma(copies)]


def add_rows(into, other, rows):
    step = 16 if rows % 16 == 0 else rows

    def one(r, carry):
        at = pl.ds(pl.multiple_of(r * step, step), step)
        into[at] = (into[at].astype(F32) + other[at].astype(F32)).astype(BF16)
        return carry

    lax.fori_loop(0, rows // step, one, 0)


def return_task(at, x_ref, out_ref, mine, theirs, ls, ps, pr, ss, sr, fs, fr, given=None, fill=None, prepare=None, per=2):
    n, c, b = at.n, at.c, at.b
    half = n // 2
    to, frm = pairwise(n, c, b)
    other_to, _ = pairwise(n, c, 1 - b)

    def load(i):
        return pltpu.make_async_copy(x_ref.at[to(i)], mine.at[i], ls.at[i])

    def give(i):
        source = x_ref.at[other_to(i)] if given is None else given.at[i]
        return at.sibling(source, theirs.at[i], ps.at[i], pr.at[i])

    def out_copy(i):
        return remote(mine.at[i], out_ref.at[c], ss.at[i], sr.at[i], to(i), b)

    def landed(i):
        return remote(mine.at[i], out_ref.at[frm(i, b)], ss.at[i], sr.at[i], to(i), b)

    def pass_on(i, core):
        ref = out_ref.at[frm(i, core)]
        return at.sibling(ref, ref, fs.at[i], fr.at[i])

    local = pltpu.make_async_copy(mine.at[0], out_ref.at[c], ss.at[0])
    order = middle_out(half) + [0]

    def issue():
        if prepare is not None:
            yield from prepare()
        for i in order:
            if fill is None:
                load(i).start()
            else:
                fill(i)
            give(i).start()
        for j, i in enumerate(order):
            if fill is None:
                load(i).wait()
            give(i).wait_recv()
            add_rows(mine.at[i], theirs.at[i], mine.shape[1])
            if i > 0:
                out_copy(i).start()
            else:
                pl.when(b == 1)(lambda: out_copy(0).start())
                pl.when(b == 0)(lambda: local.start())
            if j % per == per - 1:
                yield

    def finish():
        for i in order:
            if i > 0:
                landed(i).wait_recv()
            else:
                pl.when(b == 1)(lambda: landed(0).wait_recv())
                pl.when(b == 0)(lambda: local.wait())
            pass_on(i, b).start()
        for i in range(half):
            pass_on(i, 1 - b).wait_recv()
        for i in range(half):
            give(i).wait_send()
            pass_on(i, b).wait_send()
        for i in range(1, half):
            out_copy(i).wait_send()
        pl.when(b == 1)(lambda: out_copy(0).wait_send())

    return issue(), finish


def return_scratch(grid, shape):
    blocks = (grid.n // 2,) + shape
    return [pltpu.VMEM(blocks, BF16), pltpu.VMEM(blocks, BF16)] + [dma(grid.n // 2) for _ in range(7)]


def head_return_task(at, x_ref, out_ref, mine, theirs, ls, ps, pr, hs, hr, fs, fr):
    c, b = at.c, at.b
    copies = at.n // HEADS
    head, rank = c % HEADS, c // HEADS
    taken = (c % copies) % 2 == b

    def load(k):
        return pltpu.make_async_copy(x_ref.at[2 * k + b], mine.at[k], ls.at[k])

    def give(k):
        return at.sibling(x_ref.at[2 * k + 1 - b], theirs.at[k], ps.at[k], pr.at[k])

    def out_copy(k):
        to = head * copies + 2 * k + b
        return to, remote(mine.at[k], out_ref.at[rank], hs.at[k], hr.at[rank], to, b)

    def landed(i):
        return remote(mine.at[0], out_ref.at[i], hs.at[0], hr.at[i], c // copies + HEADS * i, b)

    def here(k, i):
        return pltpu.make_async_copy(mine.at[k], out_ref.at[i], hr.at[i])

    def pass_on(i):
        return at.sibling(out_ref.at[i], out_ref.at[i], fs.at[i], fr.at[i])

    def issue():
        for k in range(copies // 2):
            load(k).start()
            give(k).start()
        for k in range(copies // 2):
            load(k).wait()
            give(k).wait_recv()
            add_rows(mine.at[k], theirs.at[k], x_ref.shape[1])
            to, copy = out_copy(k)
            pl.when(to != c)(lambda: copy.start())
            pl.when(to == c)(lambda: here(k, rank).start())
            yield

    def finish():
        @pl.when(taken)
        def _():
            for i in range(copies):
                frm = c // copies + HEADS * i
                pl.when(frm != c)(lambda: landed(i).wait_recv())
                pl.when(frm == c)(lambda: here(0, i).wait())
                pass_on(i).start()
            for i in range(copies):
                pass_on(i).wait_send()

        @pl.when(jnp.logical_not(taken))
        def _():
            for i in range(copies):
                pass_on(i).wait_recv()

        for k in range(copies // 2):
            give(k).wait_send()
            to, copy = out_copy(k)
            pl.when(to != c)(lambda: copy.wait_send())

    return issue(), finish


def head_return_scratch(grid, shape):
    copies = grid.n // HEADS
    blocks = (copies // 2,) + shape
    return [pltpu.VMEM(blocks, BF16), pltpu.VMEM(blocks, BF16)] + [dma(copies) for _ in range(7)]


def pair_task(at, x_ref, first, out_ref, other, sems):
    count = out_ref.shape[0]
    copy = at.sibling(x_ref.at[pl.ds(pl.multiple_of(first, 16), count)], other, sems.at[0], sems.at[1])

    def issue():
        copy.start()
        yield

    def finish():
        copy.wait_recv()

        def one(r, carry):
            rows = pl.ds(pl.multiple_of(r * 16, 16), 16)
            mine = x_ref[pl.ds(pl.multiple_of(first + r * 16, 16), 16)]
            out_ref[rows] = (mine.astype(F32) + other[rows].astype(F32)).astype(out_ref.dtype)
            return carry

        lax.fori_loop(0, count // 16, one, 0)
        copy.wait_send()

    return issue(), finish


class Split:
    def __init__(self, refs):
        self.refs = list(refs)

    def take(self, count):
        got, self.refs = self.refs[:count], self.refs[count:]
        return got


def together(main, *tasks):
    for _ in main:
        for issue, _finish in tasks:
            next(issue, None)
    for issue, finish in tasks:
        run(issue)
    for issue, finish in tasks:
        finish()


def narrow_task(sources, targets, wide, low, loads, stores):
    width = wide.shape[2]
    pieces = [(k, i) for k in range(len(sources)) for i in range(sources[k].shape[1] // width)]

    def load(j):
        k, i = pieces[j]
        return pltpu.make_async_copy(sources[k].at[:, pl.ds(i * width, width)], wide.at[j % 2], loads.at[j % 2])

    def store(j):
        k, i = pieces[j]
        return pltpu.make_async_copy(low.at[j % 2], targets[k].at[:, pl.ds(i * width, width)], stores.at[j % 2])

    def issue():
        load(0).start()
        load(1).start()
        yield
        for j in range(len(pieces)):
            load(j).wait()
            if j >= 2:
                store(j - 2).wait()
            low[j % 2] = wide[j % 2].astype(F32).astype(BF16)
            store(j).start()
            if j + 2 < len(pieces):
                load(j + 2).start()
            yield

    def finish():
        for j in range(len(pieces) - 2, len(pieces)):
            store(j).wait()

    return issue(), finish


def swap_copy(at, source, target, send, recv):
    return remote(source, target.at[at.member], send, recv, at.partner, at.b)


def swap_task(at, source, target, sems):
    there = swap_copy(at, source, target, sems.at[0], sems.at[1])
    here = remote(source, target.at[1 - at.member], sems.at[0], sems.at[1], at.partner, at.b)

    def issue():
        there.start()
        yield

    def finish():
        here.wait_recv()
        there.wait_send()

    return issue(), finish


def open_kernel(grid, tokens, gain, qkv_parts, out_codes, small, gate_codes, up_codes, rows_too, cid):
    x = tokens
    n, levels = grid.n, grid.planes // 2
    rows_d, width = qkv_parts.shape[1:]
    flat = rows_d % 16 == 0
    copies = n // HEADS
    gs, ss, ts, hs = gather_sems(grid, levels, 2), share_sems(grid, 1), [dma(n), dma(n)], head_rows_sems(grid)

    piece = FF // 2
    ns = [
        pltpu.VMEM((2, rows_d, piece), jnp.int32),
        pltpu.VMEM((2, rows_d, piece), BF16),
        dma(2),
        dma(2),
    ]

    def kernel(
        x_ref, gain_ref, w_ref, o_ref, small_ref, gate_ref, up_ref,
        kept_ref, seen_ref, codes_ref, rows_ref, all_ref, gl_ref, ul_ref, *scratch,
    ):
        at = Place(grid, levels)
        refs = Split(scratch)
        normed_ref, token_sems = refs.take(2)
        member = at.member
        at.greet_all()
        token_issue, token_finish = swap_task(at, x_ref.at[1 - member], kept_ref, token_sems)
        run(token_issue)

        def view(j):
            return codes_ref.at[pl.ds(j * rows_d, rows_d)] if flat else codes_ref.at[j]

        def ready(k):
            u = member if k == 0 else 1 - member
            if k == 1:
                token_finish()

            def one(_, r):
                if k == 0:
                    kept_ref[u, r] = x_ref[u, r]
                value = kept_ref[u, r].astype(F32)
                normed_ref[u, r] = (value * inverse_rms(value) * gain_ref[0:1]).astype(BF16)

            each_rows(1, x_ref.shape[1], one)

        together(
            gather_steps(
                at, normed_ref, seen_ref, *refs.take(len(gs)), passes=[(member, 1), (1 - member, 1)], ready=ready
            ),
            narrow_task([gate_ref, up_ref], [gl_ref, ul_ref], *refs.take(4)),
            tell_task(at, small_ref, all_ref, *refs.take(2)),
            share_task(at, [lambda to: w_ref.at[to % HEADS]], [view], *refs.take(len(ss))),
            *([head_rows_task(at, o_ref, rows_ref, *refs.take(4))] if rows_too else []),
        )
        if not rows_too:
            rows_ref[...] = o_ref[...]

    codes_shape = (n * rows_d, width) if flat else (n, rows_d, width)
    return pl.pallas_call(
        kernel,
        out_shape=(
            jax.ShapeDtypeStruct(x.shape, BF16),
            jax.ShapeDtypeStruct((2, levels * grid.plane) + x.shape[1:], BF16),
            jax.ShapeDtypeStruct(codes_shape, BF16),
            jax.ShapeDtypeStruct((copies,) + out_codes.shape if rows_too else out_codes.shape, BF16),
            jax.ShapeDtypeStruct((n,) + small.shape, small.dtype),
            jax.ShapeDtypeStruct(gate_codes.shape, BF16),
            jax.ShapeDtypeStruct(up_codes.shape, BF16),
        ),
        in_specs=[INVMEM] * 5 + [ANY] * 2,
        out_specs=(INVMEM, ANY, ANY, ANY if rows_too else INVMEM) + (ANY,) * 3,
        scratch_shapes=[pltpu.VMEM(x.shape, BF16), dma(2)] + gs + ns + ts + ss + hs,
        compiler_params=params(cid, 50),
        name="open",
    )(tokens, gain, qkv_parts, out_codes, small, gate_codes, up_codes)


def scatter_kernel(grid, levels, cid, name, tasks=None, end=None):
    made, in_specs, out_shapes, out_specs, extra_scratch = tasks if tasks else (None, [], (), (), [])

    def call(p, extra):
        rows, width = p.shape[2:]
        more = () if extra is None else tuple(extra)
        own = scatter_scratch(grid, levels, rows, width)

        def kernel(*refs):
            refs = Split(refs)
            (p_ref,) = refs.take(1)
            more_refs = refs.take(len(more))
            (out_ref,) = refs.take(1)
            out_refs = refs.take(len(out_shapes) if more else 0)
            mine = refs.take(len(own))
            at = Place(grid, levels)
            load = pltpu.make_async_copy(p_ref, mine[0], mine[4].at[0])
            load.start()
            if more:
                at.greet_all()
            else:
                at.greet_near(False)
            load.wait()
            sums = refs.take(1)[0] if end else out_ref
            others = made(at, more_refs, out_refs, refs) if more else []
            if end is None:
                together(scatter_steps(at, out_ref, *mine), *others)
                return
            for _ in scatter_steps(at, sums, *mine):
                for issue, _finish in others:
                    next(issue, None)
            last = end(at, more_refs, sums, out_ref, refs)
            together((), *others)
            last()

        return pl.pallas_call(
            kernel,
            out_shape=(jax.ShapeDtypeStruct((2, rows, width), BF16),) + (out_shapes if more else ()),
            in_specs=[ANY] + (in_specs if more else []),
            out_specs=(INVMEM,) + (out_specs if more else ()),
            scratch_shapes=own + (extra_scratch if more else []),
            compiler_params=params(cid + (0 if more else 20), 60),
            name=name,
        )(p, *more)

    return call


def feed_windows(grid):
    units = FF // grid.n
    window = 128 * max(-(-((c * units) % 128 + units) // 128) for c in range(grid.n))
    return units, window, lambda c: ((c * units) // 128) * 128


def attention_sums(grid, p, gate_codes, up_codes, cid):
    n, levels = grid.n, grid.planes // 2
    rows_d = gate_codes.shape[0]
    flat = rows_d % 16 == 0
    units, window, start = feed_windows(grid)
    ss = share_sems(grid, 2)

    def tasks(at, ins, outs, refs):
        def source(ref):
            return lambda to: ref.at[:, pl.ds(pl.multiple_of(start(to), 128), window)]

        def view(ref):
            return lambda j: ref.at[pl.ds(j * rows_d, rows_d)] if flat else ref.at[j]

        return [share_task(at, [source(r) for r in ins], [view(r) for r in outs], *refs.take(len(ss)))]

    shape = (n * rows_d, window) if flat else (n, rows_d, window)
    call = scatter_kernel(
        grid,
        levels,
        cid,
        "attention_sums",
        (tasks, [INVMEM, INVMEM], (jax.ShapeDtypeStruct(shape, BF16),) * 2, (ANY, ANY), ss),
    )
    return in_parts(grid, levels, call, p, (gate_codes, up_codes))


def feed_sums(grid, p, cid):
    return in_parts(grid, grid.planes, scatter_kernel(grid, grid.planes, cid, "feed_sums"), p, None)[0]


def feed_back_sums(grid, p, pair_grad, cid):
    rs = return_scratch(grid, pair_grad.shape[1:])

    def tasks(at, ins, outs, refs):
        return [return_task(at, ins[0], outs[0], *refs.take(len(rs)))]

    call = scatter_kernel(
        grid,
        grid.planes,
        cid,
        "feed_back_sums",
        (tasks, [ANY], (jax.ShapeDtypeStruct(pair_grad.shape, BF16),), (ANY,), rs),
    )
    return in_parts(grid, grid.planes, call, p, (pair_grad,))


def attention_back_sums(grid, p, qkv_grad, out_grad, down_grad, gains, merged, cid):
    n, levels = grid.n, grid.planes // 2
    rs, hs = return_scratch(grid, qkv_grad.shape[1:]), head_return_scratch(grid, out_grad.shape[1:])
    units, _, _ = feed_windows(grid)
    ps = [pltpu.VMEM((units, D), BF16), dma(2)]
    every = pltpu.VMEM((n,) + gains.shape, F32)
    gs = [pltpu.VMEM(gains.shape, F32), pltpu.VMEM(gains.shape, F32), every, dma(2)] + share_sems(grid, 1)
    us = assemble_scratch(grid) if merged else []
    rows, width = p.shape[2:]
    tail = [pltpu.VMEM((2, rows, width), BF16), dma(2)] if merged else []
    inputs = [qkv_grad, out_grad, down_grad, gains] + list(merged)
    in_specs = [ANY, ANY, INVMEM, INVMEM] + ([ANY] + [INVMEM] * 3 if merged else [])
    shapes = (
        jax.ShapeDtypeStruct(qkv_grad.shape, BF16),
        jax.ShapeDtypeStruct(out_grad.shape, BF16),
        jax.ShapeDtypeStruct((units, D), BF16),
        jax.ShapeDtypeStruct(gains.shape, F32),
    ) + (jax.ShapeDtypeStruct((D // n, FF), BF16),) * (2 if merged else 0)
    out_specs = (ANY, ANY, INVMEM, INVMEM) + ((ANY, ANY) if merged else ())
    sums = [pltpu.VMEM((2, rows, width), BF16)] if merged else []
    scratch = sums + rs + hs + ps + gs + us + tail

    def tasks(at, ins, outs, refs):
        made = [
            return_task(at, ins[0], outs[0], *refs.take(len(rs)), per=PER),
            head_return_task(at, ins[1], outs[1], *refs.take(len(hs))),
            pair_task(at, ins[2], (at.c * units) % 128, outs[2], *refs.take(2)),
            gains_task(at, ins[3], outs[3], *refs.take(len(gs))),
        ]
        if merged:
            made.insert(0, assemble_task(grid, ins[4], outs[4:6], *refs.take(len(us))))
        return made

    def end(at, ins, sums, out_ref, refs):
        kept, sems = refs.take(2)
        grad_ref, tokens_ref, gain_ref = ins[5:8]

        def one(u, r):
            dy, v = sums[u, r].astype(F32), tokens_ref[u, r].astype(F32)
            kept[u, r] = (grad_ref[u, r] + norm_back(v, inverse_rms(v), dy * gain_ref[0:1])).astype(BF16)

        each_rows(2, rows, one)
        issue, finish = swap_task(at, kept.at[1 - at.member], out_ref, sems)
        run(issue)
        out_ref[at.member] = kept[at.member]
        return finish

    call = scatter_kernel(
        grid,
        levels,
        cid,
        "attention_back_sums",
        (tasks, in_specs, shapes, out_specs, scratch),
        end if merged else None,
    )
    return in_parts(grid, levels, call, p, inputs)


SCALE = HEAD ** (-0.5)


def rotated(u, cosine, sine):
    half = u.shape[1] // 2
    first, second = u[:, :half], u[:, half:]
    return jnp.concatenate([first * cosine - second * sine, second * cosine + first * sine], axis=1)


def scores(q, k, start, first):
    bent = jnp.tanh(dot_t(q, k) * (SCALE / cap_limit))
    key = lax.broadcasted_iota(jnp.int32, bent.shape, 1)
    query = first + lax.broadcasted_iota(jnp.int32, bent.shape, 0)
    return jnp.where((key <= query) & (key >= start), jnp.exp(cap_limit * bent), 0.0), bent


def scale_rows(core, member, codes, column_scale, into, rows):
    step = member_step(core, 2, member)
    offset = jnp.where(step > 1.0, 0.5 * step, 0.0)

    def one(i, carry):
        r = pl.ds(pl.multiple_of(i * 16, 16), 16)
        level = jnp.floor(codes[r].astype(F32) * (1.0 / step)) * step + offset
        into[r] = (level * column_scale).astype(BF16)
        return carry

    lax.fori_loop(0, rows // 16, one, 0)


def attention_body(w, o, x_rows, put, ready, cos_ref, sin_ref, start_ref, q_ref, k_ref, v_ref, a_ref, t_ref, block=256):
    length = q_ref.shape[0]
    for i in range(length // block):
        r = pl.ds(i * block, block)
        lin = dot(x_rows(i), w[...])
        q_ref[r] = rotated(lin[:, :HEAD], cos_ref[r], sin_ref[r]).astype(BF16)
        k_ref[r] = rotated(lin[:, HEAD : 2 * HEAD], cos_ref[r], sin_ref[r]).astype(BF16)
        v_ref[r] = lin[:, 2 * HEAD :].astype(BF16)
    ready()
    for i in range(length // block):
        r, keys = pl.ds(i * block, block), pl.ds(0, (i + 1) * block)
        e, _ = scores(q_ref[r], k_ref[keys], start_ref[r], i * block)
        total = jnp.sum(e, axis=1, keepdims=True)
        attended = (dot(e.astype(BF16), v_ref[keys]) / total).astype(BF16)
        a_ref[r] = attended
        t_ref[r] = total
        put(i, dot(attended, o[...]).astype(BF16))


def attention_backward(seen, grad, w, o, q, k, v, attended, totals, vectors, cosine, sine, start):
    length = seen.shape[0]
    block, tile = 256, 768

    def kernel(
        x_ref, g_ref, w_ref, o_ref, q_ref, k_ref, v_ref, a_ref, t_ref, vec_ref, cos_ref, sin_ref, start_ref,
        part_ref, wg_ref, og_ref, gain_ref, xs, gs, w, part, wg, dk, dv, low, sems, out_sems,
    ):
        load_w = pltpu.make_async_copy(w_ref, w, sems.at[2])
        give_part = pltpu.make_async_copy(part, part_ref, sems.at[3])

        def give_rows(j):
            rows = pl.ds(pl.multiple_of(j * tile, tile), tile)
            return pltpu.make_async_copy(wg.at[rows], wg_ref.at[rows], out_sems.at[j])

        load_g = pltpu.make_async_copy(g_ref, gs, sems.at[0])
        load_x = pltpu.make_async_copy(x_ref, xs, sems.at[1])
        load_g.start()
        load_x.start()
        load_w.start()
        dk[...] = jnp.zeros_like(dk)
        dv[...] = jnp.zeros_like(dv)
        load_g.wait()
        for i in range(length // block):
            r, keys = pl.ds(i * block, block), pl.ds(0, (i + 1) * block)
            grad_attended = dot_t(gs[r], o_ref[...])
            total = t_ref[r]
            grad_sums = (grad_attended / total).astype(BF16)
            offset = jnp.sum(grad_attended * a_ref[r].astype(F32), axis=1, keepdims=True) / total
            e, bent = scores(q_ref[r], k_ref[keys], start_ref[r], i * block)
            grad_e = dot_t(grad_sums, v_ref[keys]) - offset
            grad_s = (e * grad_e * (1.0 - bent * bent)).astype(BF16)
            dv[keys] += t_dot(e.astype(BF16), grad_sums)
            dk[keys] += t_dot(grad_s, q_ref[r])
            low[r, :HEAD] = rotated(dot(grad_s, k_ref[keys]) * SCALE, cos_ref[r], -sin_ref[r]).astype(BF16)
        for i in range(length // block):
            r = pl.ds(i * block, block)
            low[r, HEAD : 2 * HEAD] = rotated(dk[r] * SCALE, cos_ref[r], -sin_ref[r]).astype(BF16)
            low[r, 2 * HEAD :] = dv[r].astype(BF16)
        load_x.wait()
        load_w.wait()
        gain_ref[...] = jnp.zeros_like(gain_ref)

        def parts(i, carry):
            r = pl.ds(pl.multiple_of(i * block, block), block)
            term = dot_t(low[r], w[...])
            part[r] = term.astype(BF16)
            gain_ref[...] += jnp.sum(term * xs[r].astype(F32), axis=0, keepdims=True)
            return carry

        lax.fori_loop(0, length // block, parts, 0)
        give_part.start()
        gain_ref[...] = gain_ref[...] / vec_ref[0:1]

        def grads(j, carry):
            cols = pl.ds(pl.multiple_of(j * tile, tile), tile)
            wg[cols] = t_dot(xs[:, cols], low[...]).astype(BF16)
            give_rows(j).start()
            og_ref[:, cols] = t_dot(a_ref[...], gs[:, cols]).astype(BF16)
            return carry

        lax.fori_loop(0, D // tile, grads, 0)
        give_part.wait()
        for j in range(D // tile):
            give_rows(j).wait()

    return pl.pallas_call(
        kernel,
        out_shape=(
            jax.ShapeDtypeStruct((length, D), BF16),
            jax.ShapeDtypeStruct((D, 3 * HEAD), BF16),
            jax.ShapeDtypeStruct((HEAD, D), BF16),
            jax.ShapeDtypeStruct((1, D), F32),
        ),
        in_specs=[ANY, ANY, ANY] + [INVMEM] * 10,
        out_specs=(ANY, ANY, INVMEM, INVMEM),
        scratch_shapes=[
            pltpu.VMEM(seen.shape, BF16),
            pltpu.VMEM(seen.shape, BF16),
            pltpu.VMEM((D, 3 * HEAD), BF16),
            pltpu.VMEM((length, D), BF16),
            pltpu.VMEM((D, 3 * HEAD), BF16),
            pltpu.VMEM((length, HEAD), F32),
            pltpu.VMEM((length, HEAD), F32),
            pltpu.VMEM((length, 3 * HEAD), BF16),
            dma(4),
            dma(D // tile),
        ],
        compiler_params=pltpu.CompilerParams(vmem_limit_bytes=60 * 2**20),
        name="attention_backward",
    )(seen, grad, w, o, q, k, v, attended, totals, vectors, cosine, sine, start)


def inverse_rms(v):
    return lax.rsqrt(jnp.mean(v * v, axis=-1, keepdims=True) + 1e-06)


def norm_back(v, r, weighted):
    return r * weighted - v * (r * r * r * jnp.mean(weighted * v, axis=-1, keepdims=True))


def each_rows(group, rows, step):
    def one(i, carry):
        step(i // (rows // 16), pl.ds(pl.multiple_of((i % (rows // 16)) * 16, 16), 16))
        return carry

    lax.fori_loop(0, group * (rows // 16), one, 0)


def fits(grid, rows):
    return (D // grid.n) % 16 == 0 and scatter_parts(grid, grid.planes, rows, D) == 1


def forward_kernel(
    grid, seen, qkv_codes, out_codes, qkv_scale, cosine, sine, begins, tokens, cotangent, gate_codes, up_codes, down_codes,
    pair_scale, vectors, cid,
):
    n, levels = grid.n, grid.planes
    group, rows, _ = tokens.shape
    rows_d = gate_codes.shape[0]
    units, window, start = feed_windows(grid)
    size = feed_blocks(grid)
    sc = scatter_scratch(grid, levels // 2, rows, D)
    ss = share_sems(grid, 2)
    ws, gs = FeedWeights.scratch(group, units, window), level_sems(grid, levels)

    length = seen.shape[0]
    block = 256
    here = block // rows
    hs = head_rows_sems(grid)

    def kernel(
        x_ref, codes_ref, rows_ref, scale_ref, cos_ref, sin_ref, start_ref, tokens_ref, cot_ref, gate_ref, up_ref, down_ref,
        ps_ref, vec_ref,
        w_ref, o_ref, q_ref, k_ref, v_ref, a_ref, t_ref,
        kept_cot_ref, raw_ref, mixed_ref, all_ref, pair_ref, part_ref, wp_ref, wd_ref, *scratch,
    ):
        refs = Split(scratch)
        half_at, at = Place(grid, levels // 2), Place(grid, levels)
        mine = refs.take(len(sc))
        share_refs = refs.take(len(ss))
        weights = FeedWeights(at, group, units, None, None, down_ref, (wp_ref, wd_ref), refs.take(len(ws)))
        gather_refs = refs.take(len(gs))
        x, xs, o_codes, head_sems, cot_sems = refs.take(5)
        head_refs = refs.take(len(hs))
        loads, stores, compute = forward_chunks(weights, all_ref, pair_ref, part_ref, *refs.take(4))
        w = weights.pair.at[0, :, pl.ds(0, 3 * HEAD)]
        w_codes = weights.pair.at[1, :, pl.ds(0, 3 * HEAD)]
        o = weights.down.at[0, pl.ds(0, HEAD)]
        acc = mine[0]
        load_w = pltpu.make_async_copy(codes_ref, w_codes, head_sems.at[0])
        load_x = pltpu.make_async_copy(x_ref, xs, head_sems.at[1])
        load_w.start()
        load_x.start()
        weights.sources = (None, None, down_ref)
        weights.load()
        at.greet_all()

        def source(ref):
            return lambda to: ref.at[:, pl.ds(pl.multiple_of(start(to), 128), window)]

        def view(k):
            return lambda j: weights.codes.at[
                pl.ds(pl.multiple_of(j * rows_d, 16), rows_d), pl.ds(k * window, window)
            ]

        heads, heads_finish = head_rows_task(at, rows_ref, o_codes, *head_refs)
        run(heads)
        issue, finish = share_task(at, [source(gate_ref), source(up_ref)], [view(0), view(1)], *share_refs)
        load_w.wait()
        scale_rows(at.b, at.member, w_codes, scale_ref[...], w, D)
        keep_w = pltpu.make_async_copy(w, w_ref, head_sems.at[2])
        keep_o = pltpu.make_async_copy(o, o_ref, head_sems.at[3])
        keep_w.start()
        load_x.wait()

        def ready():
            heads_finish()
            for _ in range(EARLY):
                next(issue, None)
            each = o_codes.shape[1]
            for j in range(o_codes.shape[0]):
                scale_rows(at.b, at.member, o_codes.at[j], vec_ref[4:5], o.at[pl.ds(j * each, each)], each)
            keep_o.start()

        def put(i, value):
            first = i * here
            half = grid.n // 2
            acc[first // half, pl.ds(first % half, here)] = value.reshape(here, rows, D)

        attention_body(
            w,
            o,
            lambda i: xs[pl.ds(i * block, block)],
            put,
            ready,
            cos_ref,
            sin_ref,
            start_ref,
            q_ref,
            k_ref,
            v_ref,
            a_ref,
            t_ref,
        )
        for _ in scatter_steps(half_at, raw_ref, *mine):
            next(issue, None)

        def norms(u, r):
            raw = raw_ref[u, r].astype(F32)
            mixed = tokens_ref[u, r].astype(F32) + raw * inverse_rms(raw) * vec_ref[1:2]
            mixed_ref[u, r] = mixed
            x[u, r] = (mixed * inverse_rms(mixed) * vec_ref[2:3]).astype(BF16)

        each_rows(group, rows, norms)
        moving = LevelGather(False, at, x, all_ref, *gather_refs)
        moving.begin()
        run(issue)
        give_cot, take_cot = swap_task(at, cot_ref.at[1 - at.member], kept_cot_ref, cot_sems)
        run(give_cot)
        kept_cot_ref[at.member] = cot_ref[at.member]

        def first():
            finish()
            keep_w.wait()
            keep_o.wait()
            weights.make(ps_ref, vec_ref.at[5:6])

        moving.run(lambda zj, fresh: each_chunk(grid, zj, fresh, loads, stores, compute), first)
        for copy in stores(0):
            copy.wait()
        weights.finish()
        take_cot()

    def blocks(width):
        return jax.ShapeDtypeStruct((group, n, rows, width), BF16)

    head = jax.ShapeDtypeStruct((length, HEAD), BF16)
    return pl.pallas_call(
        kernel,
        out_shape=(
            jax.ShapeDtypeStruct((D, 3 * HEAD), BF16),
            jax.ShapeDtypeStruct((HEAD, D), BF16),
            head,
            head,
            head,
            head,
            jax.ShapeDtypeStruct((length, 1), F32),
            jax.ShapeDtypeStruct(tokens.shape, BF16),
            jax.ShapeDtypeStruct(tokens.shape, BF16),
            jax.ShapeDtypeStruct(tokens.shape, F32),
            blocks(D),
            blocks(2 * window),
            blocks(D),
            jax.ShapeDtypeStruct((group, D, 2 * window), BF16),
            jax.ShapeDtypeStruct((group, window, D), BF16),
        ),
        in_specs=[ANY, ANY] + [INVMEM] * 7 + [ANY] * 3 + [INVMEM] * 2,
        out_specs=(ANY, ANY) + (INVMEM,) * 8 + (ANY,) * 5,
        scratch_shapes=sc
        + ss
        + ws
        + gs
        + [
            pltpu.VMEM(tokens.shape, BF16),
            pltpu.VMEM(seen.shape, BF16),
            pltpu.VMEM((n // HEADS,) + out_codes.shape, BF16),
            dma(4),
            dma(2),
        ]
        + hs
        + chunk_buffers(size, rows, D, 2 * window, D)
        + [dma(3)],
        compiler_params=params(cid, 62),
        name="forward",
    )(
        seen, qkv_codes, out_codes, qkv_scale, cosine, sine, begins, tokens, cotangent, gate_codes, up_codes, down_codes,
        pair_scale, vectors,
    )


def turn_kernel(grid, p, mixed, cotangent, pair, pair_matrices, down_matrices, vectors, cid):
    n, levels = grid.n, grid.planes
    group, rows, _ = mixed.shape
    units, window, _ = feed_windows(grid)
    size = feed_blocks(grid)
    sc, gs = split_scratch(grid, levels, rows, D), level_sems(grid, levels)

    def kernel(
        p_ref, mixed_ref, cot_ref, pair_ref, wp_ref, wd_ref, vec_ref,
        out_ref, gain_ref, all_ref, part_ref, dgu_ref, hid_ref, *scratch,
    ):
        refs = Split(scratch)
        at = Place(grid, levels)
        mine, gather_refs = refs.take(len(sc)), refs.take(len(gs))
        raw, x, kept_out, wp, wd, fetch_sems, swap_sems = refs.take(7)
        load = pltpu.make_async_copy(p_ref, mine[0], mine[7].at[0])
        load.start()
        fetch = [
            pltpu.make_async_copy(wp_ref, wp, fetch_sems.at[0]),
            pltpu.make_async_copy(wd_ref, wd, fetch_sems.at[1]),
        ]
        loads, stores, compute = backward_chunks(
            wp, wd, all_ref, pair_ref, part_ref, dgu_ref, hid_ref, *refs.take(6)
        )
        at.greet_near(True)
        load.wait()
        for copy in fetch:
            copy.start()
        run(split_scatter_steps(at, raw, *mine))
        gain_ref[...] = jnp.zeros_like(gain_ref)

        def norms(u, r):
            v, dy = raw[u, r].astype(F32), cot_ref[u, r].astype(F32)
            inverse, gain = inverse_rms(v), vec_ref[3:4]
            kept_out[u, r] = (mixed_ref[u, r] + v * inverse * gain).astype(BF16)
            x[u, r] = norm_back(v, inverse, dy * gain).astype(BF16)
            gain_ref[...] += jnp.sum(dy * v * inverse, axis=0, keepdims=True)

        each_rows(group, rows, norms)
        moving = LevelGather(True, at, x, all_ref, *gather_refs)
        moving.begin()
        give_out, take_out = swap_task(at, kept_out.at[1 - at.member], out_ref, swap_sems)
        run(give_out)
        out_ref[at.member] = kept_out[at.member]
        for copy in fetch:
            copy.wait()

        moving.run(lambda zj, fresh: each_chunk(grid, zj, fresh, loads, stores, compute))
        take_out()
        for copy in stores(0):
            copy.wait()

    def blocks(width):
        return jax.ShapeDtypeStruct((group, n, rows, width), BF16)

    return pl.pallas_call(
        kernel,
        out_shape=(
            jax.ShapeDtypeStruct(mixed.shape, BF16),
            jax.ShapeDtypeStruct((1, D), F32),
            blocks(D),
            blocks(D),
            blocks(2 * window),
            blocks(window),
        ),
        in_specs=[ANY, INVMEM, INVMEM, ANY, ANY, ANY, INVMEM],
        out_specs=(INVMEM, INVMEM) + (ANY,) * 4,
        scratch_shapes=sc
        + gs
        + [
            pltpu.VMEM(mixed.shape, BF16),
            pltpu.VMEM(mixed.shape, BF16),
            pltpu.VMEM(mixed.shape, BF16),
            pltpu.VMEM((group, D, 2 * window), BF16),
            pltpu.VMEM((group, window, D), BF16),
            dma(2),
            dma(2),
        ]
        + chunk_buffers(size, rows, D, 2 * window, D, 2 * window, window)
        + [dma(5)],
        compiler_params=params(cid, 62),
        name="turn",
    )(p, mixed, cotangent, pair, pair_matrices, down_matrices, vectors)


def back_kernel(grid, p, fed, down_low, pair_low, hidden, mixed, raw, cotangent, vectors, cid):
    n, levels = grid.n, grid.planes
    group, rows, _ = mixed.shape
    units, window, _ = feed_windows(grid)
    size = feed_blocks(grid)
    chunks = n // size
    count = group * size * rows
    rows_d = D // n
    half = n // 2
    tile = 256
    sc, gs = scatter_scratch(grid, levels, rows, D), gather_sems(grid, levels // 2)
    rs = return_scratch(grid, (rows_d, 2 * window))

    def kernel(
        p_ref, fed_ref, low_ref, dgu_ref, hid_ref, mixed_ref, raw_ref, cot_ref, vec_ref,
        grad_ref, feed_ref, post_ref, all_ref, got_ref, down_ref, *scratch,
    ):
        refs = Split(scratch)
        half_at, at = Place(grid, levels // 2), Place(grid, levels)
        mine, gather_refs, return_refs = refs.take(len(sc)), refs.take(len(gs)), refs.take(len(rs))
        raw2, x, xs, ys, dgu, hid, pair_sum, down_sum, given, down_out, sems = refs.take(11)
        load = pltpu.make_async_copy(p_ref, mine[0], mine[4].at[0])
        load.start()

        def loads(i):
            at_blocks = pl.ds(i * size, size)
            return [
                pltpu.make_async_copy(fed_ref.at[:, at_blocks], xs, sems.at[0]),
                pltpu.make_async_copy(low_ref.at[:, at_blocks], ys, sems.at[1]),
                pltpu.make_async_copy(dgu_ref.at[:, at_blocks], dgu, sems.at[2]),
                pltpu.make_async_copy(hid_ref.at[:, at_blocks], hid, sems.at[3]),
            ]

        for copy in loads(0):
            copy.start()
        at.greet_all()
        load.wait()

        def sums(i):
            def one(j, carry):
                cols = pl.ds(pl.multiple_of(j * tile, tile), tile)
                pair_term = t_dot(xs[:, :, :, cols].reshape(count, tile), dgu[...].reshape(count, 2 * window))
                down_term = t_dot(hid[...].reshape(count, window), ys[:, :, :, cols].reshape(count, tile))
                if i == 0:
                    pair_sum[cols] = pair_term
                    down_sum[:, cols] = down_term
                else:
                    pair_sum[cols] = pair_sum[cols] + pair_term
                    down_sum[:, cols] = down_sum[:, cols] + down_term
                return carry

            for copy in loads(i):
                copy.wait()
            lax.fori_loop(0, D // tile, one, 0)
            if i + 1 < chunks:
                for copy in loads(i + 1):
                    copy.start()

        to, _ = pairwise(n, at.c, at.b)
        other_to, _ = pairwise(n, at.c, 1 - at.b)
        give_down = pltpu.make_async_copy(down_out, down_ref, sems.at[4])

        def lowered(i):
            def one(r, carry):
                here = pl.ds(pl.multiple_of(r * 16, 16), 16)
                mine_at = pl.ds(pl.multiple_of(to(i) * rows_d + r * 16, 16), 16)
                other_at = pl.ds(pl.multiple_of(other_to(i) * rows_d + r * 16, 16), 16)
                return_refs[0][i, here] = pair_sum[mine_at].astype(BF16)
                given[i, here] = pair_sum[other_at].astype(BF16)
                return carry

            lax.fori_loop(0, rows_d // 16, one, 0)

        def lowered_down():
            def one(r, carry):
                here = pl.ds(pl.multiple_of(r * 16, 16), 16)
                down_out[here] = down_sum[here].astype(BF16)
                return carry

            lax.fori_loop(0, window // 16, one, 0)
            give_down.start()

        def prepare():
            for i in range(chunks):
                sums(i)
                if i % 2 == 1:
                    yield
            lowered_down()

        issue, finish = return_task(at, None, got_ref, *return_refs, given=given, fill=lowered, prepare=prepare)

        def main():
            yield from scatter_steps(at, raw2, *mine)
            feed_ref[...] = jnp.zeros_like(feed_ref)
            post_ref[...] = jnp.zeros_like(post_ref)

            def norms(u, r):
                dy, v = raw2[u, r].astype(F32), mixed_ref[u, r]
                inverse = inverse_rms(v)
                grad = cot_ref[u, r].astype(F32) + norm_back(v, inverse, dy * vec_ref[2:3])
                feed_ref[...] += jnp.sum(dy * v * inverse, axis=0, keepdims=True)
                grad_ref[u, r] = grad
                w = raw_ref[u, r].astype(F32)
                inverse = inverse_rms(w)
                x[u, r] = norm_back(w, inverse, grad * vec_ref[1:2]).astype(BF16)
                post_ref[...] += jnp.sum(grad * w * inverse, axis=0, keepdims=True)

            each_rows(group, rows, norms)
            yield from gather_steps(half_at, x, all_ref, *gather_refs)

        together(main(), (issue, finish))
        give_down.wait()

    return pl.pallas_call(
        kernel,
        out_shape=(
            jax.ShapeDtypeStruct(mixed.shape, F32),
            jax.ShapeDtypeStruct((1, D), F32),
            jax.ShapeDtypeStruct((1, D), F32),
            jax.ShapeDtypeStruct((2, half, rows, D), BF16),
            jax.ShapeDtypeStruct((n, rows_d, 2 * window), BF16),
            jax.ShapeDtypeStruct((window, D), BF16),
        ),
        in_specs=[ANY] * 5 + [INVMEM] * 4,
        out_specs=(INVMEM,) * 3 + (ANY,) * 3,
        scratch_shapes=sc
        + gs
        + rs
        + [
            pltpu.VMEM(mixed.shape, BF16),
            pltpu.VMEM(mixed.shape, BF16),
            pltpu.VMEM((group, size, rows, D), BF16),
            pltpu.VMEM((group, size, rows, D), BF16),
            pltpu.VMEM((group, size, rows, 2 * window), BF16),
            pltpu.VMEM((group, size, rows, window), BF16),
            pltpu.VMEM((D, 2 * window), F32),
            pltpu.VMEM((window, D), F32),
            pltpu.VMEM((half, rows_d, 2 * window), BF16),
            pltpu.VMEM((window, D), BF16),
            dma(5),
        ],
        compiler_params=params(cid, 63),
        name="back",
    )(p, fed, down_low, pair_low, hidden, mixed, raw, cotangent, vectors)


def assemble_task(grid, got_ref, targets, wide, high, load_sem, stores):
    n = grid.n
    units, window, _ = feed_windows(grid)
    inner = n // HEADS
    whole = inner * units
    starts = [i * units // 128 * 128 for i in range(inner)]
    load = pltpu.make_async_copy(got_ref, wide, load_sem.at[0])

    def store(k):
        return pltpu.make_async_copy(high.at[k], targets[k], stores.at[k])

    def put(g, k):
        for t in range(0, whole, 128):
            total = 0.0
            for i in range(inner):
                if 0 <= t - starts[i] < window:
                    total = total + wide[g * inner + i, :, pl.ds(k * window + t - starts[i], 128)].astype(F32)
            high[k, :, pl.ds(pl.multiple_of(g * whole + t, 128), 128)] = total.astype(BF16)

    def issue():
        load.start()
        yield
        yield
        load.wait()
        for k in range(2):

            def one(g, carry):
                put(g, k)
                return carry

            lax.fori_loop(0, n // inner, one, 0)
            store(k).start()
            yield

    def finish():
        for k in range(2):
            store(k).wait()

    return issue(), finish


def assemble_scratch(grid):
    _, window, _ = feed_windows(grid)
    rows_d = D // grid.n
    return [pltpu.VMEM((grid.n, rows_d, 2 * window), BF16), pltpu.VMEM((2, rows_d, FF), BF16), dma(1), dma(2)]


def gains_task(at, x_ref, out_ref, total, other, every, sems, *share_refs):
    copy = at.sibling(x_ref, other, sems.at[0], sems.at[1])
    later, end = share_task(at, [lambda to: total], [lambda j: every.at[j]], *share_refs)

    def issue():
        copy.start()
        yield
        copy.wait()
        total[...] = x_ref[...] + other[...]
        yield from later

    def finish():
        end()
        out_ref[...] = jnp.sum(every[...], axis=0)

    return issue(), finish


def normed(value, gain):
    return value * lax.rsqrt(jnp.mean(value * value, axis=-1, keepdims=True) + 1e-06) * gain


def angles(places, head):
    freqs = 10000.0 ** (-(jnp.arange(head // 2, dtype=F32) * 2.0 / head))
    return places.astype(F32)[..., None] * freqs


def rotate(values, cosine, sine):
    half = values.shape[-1] // 2
    first = values[..., :half]
    second = values[..., half:]
    return jnp.concatenate([first * cosine - second * sine, second * cosine + first * sine], axis=-1)


def width_step(number):
    remainder = number % 3
    return jnp.where(remainder == 0, 1.0, jnp.where(remainder == 1, 16.0, 64.0)).astype(F32)


def dequantized(codes, column_scale, step):
    offset = jnp.where(step > 1.0, 0.5 * step, 0.0)
    level = jnp.floor(codes.astype(F32) / step) * step + offset
    return (level * column_scale[None, :]).astype(BF16)


def dot(left, right):
    return jnp.dot(left, right, preferred_element_type=F32)


def dot_t(left, right):
    return lax.dot_general(left, right, (((1,), (1,)), ((), ())), preferred_element_type=F32)


def t_dot(left, right):
    return lax.dot_general(left, right, (((0,), (0,)), ((), ())), preferred_element_type=F32)


def unwindowed(grid, got):
    n, rows, window = got.shape
    units = FF // n
    inner = n // HEADS
    whole = inner * units
    got = got.astype(F32).reshape(n // inner, inner, rows, window)
    total = 0.0
    for i in range(inner):
        start = i * units // 128 * 128
        total = total + jnp.pad(got[:, i], ((0, 0), (0, 0), (start, whole - start - window)))
    return jnp.transpose(total, (1, 0, 2)).reshape(rows, FF)


def on_device(
    grid,
    tokens,
    segments,
    positions,
    cotangent,
    query_codes,
    key_codes,
    value_codes,
    output_codes,
    gate_codes,
    up_codes,
    down_codes,
    query_scale,
    key_scale,
    value_scale,
    output_scale,
    gate_scale,
    up_scale,
    down_scale,
    attention_gain,
    attention_post_gain,
    feed_gain,
    feed_post_gain,
):
    n = grid.n
    group, block, _ = tokens.shape
    length = n * block
    pairs = HEADS // KV_HEADS
    scale = HEAD ** (-0.5)
    chip, core = lax.axis_index("seq"), lax.axis_index("batch")
    half = n // 2
    member = chip // half
    head = chip % HEADS
    kv_head = head // pairs
    parts = half // HEADS
    copies = n // HEADS
    asked = length // parts
    first_asked = ((chip % half) // HEADS) * asked
    steps = [width_step(core * group + m) for m in range(group)]
    step = width_step(core * group + member)
    rows_d = D // n
    units, window, _ = feed_windows(grid)

    whole = fits(grid, block) and parts == 1
    vectors = jnp.stack(
        [attention_gain, attention_post_gain, feed_gain, feed_post_gain, output_scale, down_scale]
    )

    q_parts = jnp.transpose(query_codes.reshape(rows_d, HEADS, HEAD), (1, 0, 2))
    k_parts = jnp.repeat(jnp.transpose(key_codes.reshape(rows_d, KV_HEADS, HEAD), (1, 0, 2)), pairs, axis=0)
    v_parts = jnp.repeat(jnp.transpose(value_codes.reshape(rows_d, KV_HEADS, HEAD), (1, 0, 2)), pairs, axis=0)
    qkv_parts = jnp.concatenate([q_parts, k_parts, v_parts], axis=-1).astype(BF16)
    small = jnp.zeros((8, 128), jnp.int32).at[:group, :block].set(positions)
    tokens, seen, qkv_codes, out_codes, all_places, gate_low, up_low = open_kernel(
        grid,
        tokens,
        vectors,
        qkv_parts,
        output_codes.astype(BF16),
        small,
        gate_codes,
        up_codes,
        not whole,
        1,
    )
    seen = seen.reshape(length, D)

    qkv_scale = jnp.concatenate(
        [
            lax.dynamic_slice_in_dim(query_scale, head * HEAD, HEAD),
            lax.dynamic_slice_in_dim(key_scale, kv_head * HEAD, HEAD),
            lax.dynamic_slice_in_dim(value_scale, kv_head * HEAD, HEAD),
        ]
    )
    def swapped_back(kept):
        own, other = (lax.dynamic_index_in_dim(kept, u, 0, False) for u in (member, 1 - member))
        other = lax.ppermute(other, "seq", [(c, (c + half) % n) for c in range(n)])
        return jnp.where(member == 0, jnp.stack([own, other]), jnp.stack([other, own]))

    def spread(part):
        if parts > 1:
            part = lax.dynamic_update_slice_in_dim(jnp.zeros((length, D), BF16), part, first_asked, 0)
        return part.reshape(2, half, block, D)

    places_all = lax.dynamic_index_in_dim(all_places[:, :group, :block], member, 1, False).reshape(length)
    turn = angles(places_all, HEAD)
    cosine, sine = jnp.cos(turn), jnp.sin(turn)
    q_index = first_asked + jnp.arange(asked, dtype=jnp.int32)
    pair_scale = jnp.concatenate(
        [lax.dynamic_slice_in_dim(s, chip * units // 128 * 128, window) for s in (gate_scale, up_scale)]
    )[None]
    if whole:
        start = (q_index - places_all)[:, None]
        (
            *kept_heads, cotangent, attention_raw, mixed, fed, gate_up, down_part, pair_matrices, down_matrices,
        ) = forward_kernel(
            grid,
            seen,
            qkv_codes.reshape(D, 3 * HEAD),
            out_codes,
            qkv_scale[None],
            cosine,
            sine,
            start,
            tokens,
            cotangent,
            gate_low,
            up_low,
            down_codes,
            pair_scale,
            vectors,
            2,
        )
    else:
        qkv_matrix = dequantized(qkv_codes.reshape(D, 3 * HEAD), qkv_scale, step)
        out_matrix = dequantized(out_codes.reshape(HEAD, D), output_scale, step)
        if parts == 1:
            seen_asked, places_asked, cosine_q, sine_q = seen, places_all, cosine, sine
            projected = dot(seen, qkv_matrix)
            q_lin, kv_lin = projected[:, :HEAD], projected[:, HEAD:]
        else:
            seen_asked, places_asked, cosine_q, sine_q = [
                lax.dynamic_slice_in_dim(a, first_asked, asked) for a in (seen, places_all, cosine, sine)
            ]
            q_lin, kv_lin = dot(seen_asked, qkv_matrix[:, :HEAD]), dot(seen, qkv_matrix[:, HEAD:])
        queries = rotate(q_lin, cosine_q, sine_q).astype(BF16)
        keys = rotate(kv_lin[:, :HEAD], cosine, sine).astype(BF16)
        values = kv_lin[:, HEAD:].astype(BF16)
        key_index = jnp.arange(length, dtype=jnp.int32)
        allowed = (key_index[None, :] <= q_index[:, None]) & (key_index[None, :] >= (q_index - places_asked)[:, None])
        bent = jnp.tanh(dot_t(queries, keys) * scale / cap_limit)
        kernel = jnp.where(allowed, jnp.exp(cap_limit * bent), 0.0)
        totals = jnp.sum(kernel, axis=-1, keepdims=True)
        kernel_low = kernel.astype(BF16)
        attended = dot(kernel_low, values) / totals
        attended_low = attended.astype(BF16)

        out_part = spread(dot(attended_low, out_matrix).astype(BF16))
    first_column = chip * units // 128 * 128
    if whole:
        output, grad_post_feed, down_low, second_part, pair_low, hidden = turn_kernel(
            grid, down_part, mixed, cotangent, gate_up, pair_matrices, down_matrices, vectors, 3
        )
        grad_mixed, grad_pre_feed, grad_post_attention, attention_low, pair_got, down_grad = back_kernel(
            grid,
            second_part,
            fed,
            down_low,
            pair_low,
            hidden,
            mixed,
            attention_raw,
            cotangent,
            vectors,
            4,
        )
    else:
        cotangent = swapped_back(cotangent)
        attention_raw, gate_got, up_got = attention_sums(grid, out_part, gate_low, up_low, 2)
        attention_raw = attention_raw.astype(F32)
        feed_weights = (
            gate_got.reshape(D, window),
            up_got.reshape(D, window),
            down_codes,
            pair_scale,
            down_scale[None],
        )
        mixed = tokens.astype(F32) + normed(attention_raw, attention_post_gain)
        second_normed = normed(mixed, feed_gain).astype(BF16)
        fed, gate_up, down_part, pair_matrices, down_matrices = feed_forward(grid, second_normed, *feed_weights, 3)
        down_raw = feed_sums(grid, down_part, 4).astype(F32)
        branch, pull_out = jax.vjp(normed, down_raw, feed_post_gain)
        output = swapped_back((mixed + branch).astype(BF16))
        upstream = cotangent.astype(F32)
        grad_down_raw, grad_post_feed = pull_out(upstream)
        down_low, second_part, pair_low, hidden = feed_backward(
            grid, grad_down_raw.astype(BF16), gate_up, pair_matrices, down_matrices, 9
        )
        count = group * length
        pair_grad = t_dot(fed.reshape(count, D), pair_low.reshape(count, 2 * window)).astype(BF16)
        down_grad = t_dot(hidden.reshape(count, window), down_low.reshape(count, D)).astype(BF16)
        grad_second, pair_got = feed_back_sums(grid, second_part, pair_grad.reshape(n, rows_d, 2 * window), 5)
        gate_grad, up_grad = (unwindowed(grid, pair_got[..., i * window : (i + 1) * window]) for i in range(2))
        _, pull_feed = jax.vjp(normed, mixed, feed_gain)
        grad_mixed_part, grad_pre_feed = pull_feed(grad_second.astype(F32))
        grad_mixed = upstream + grad_mixed_part
        _, pull_post = jax.vjp(normed, attention_raw, attention_post_gain)
        grad_attention, grad_post_attention = pull_post(grad_mixed)
        attention_low = gather(grid, grad_attention.astype(BF16), grid.planes // 2, 6)

    attention_low = attention_low.reshape(length, D)
    if whole:
        first_part, qkv_grad, out_part, grad_pre_attention = attention_backward(
            seen, attention_low, *kept_heads, vectors, cosine, sine, start
        )
    else:
        if parts > 1:
            attention_low = lax.dynamic_slice_in_dim(attention_low, first_asked, asked)
        grad_attended = dot_t(attention_low, out_matrix)
        grad_sums = (grad_attended / totals).astype(BF16)
        offsets = jnp.sum(grad_attended * attended, axis=-1, keepdims=True) / totals
        grad_kernel = dot_t(grad_sums, values) - offsets
        grad_raw = (kernel * grad_kernel * (1.0 - bent * bent)).astype(BF16)
        grad_q = dot(grad_raw, keys) * scale
        grad_k = t_dot(grad_raw, queries) * scale
        grad_v = t_dot(kernel_low, grad_sums)
        q_low = rotate(grad_q, cosine_q, -sine_q).astype(BF16)
        kv_low = jnp.concatenate([rotate(grad_k, cosine, -sine), grad_v], axis=-1).astype(BF16)
        if parts == 1:
            qkv_low = jnp.concatenate([q_low, kv_low], axis=-1)
            first_part = dot_t(qkv_low, qkv_matrix)
            qkv_grad = t_dot(seen, qkv_low)
        else:
            first_part = dot_t(kv_low, qkv_matrix[:, HEAD:])
            q_back = dot_t(q_low, qkv_matrix[:, :HEAD])
            first_part = lax.dynamic_update_slice_in_dim(
                first_part, lax.dynamic_slice_in_dim(first_part, first_asked, asked) + q_back, first_asked, 0
            )
            qkv_grad = jnp.concatenate([t_dot(seen_asked, q_low), t_dot(seen, kv_low)], axis=-1)
        first_part = first_part.astype(BF16)
        grad_pre_attention = jnp.sum(first_part.astype(F32) * seen.astype(F32), axis=0) / attention_gain
        out_part = t_dot(attended_low, attention_low).astype(BF16)
    gains = jnp.stack(
        [g.reshape(D) for g in (grad_pre_attention, grad_post_attention, grad_pre_feed, grad_post_feed)]
    )
    out_part = out_part.reshape(copies, HEAD // copies, D)
    merged = (pair_got, grad_mixed, tokens, vectors) if whole else ()
    grad_in, qkv_got, out_got, down_grad, gains, *assembled = attention_back_sums(
        grid,
        first_part.reshape(2, half, block, D),
        qkv_grad.astype(BF16).reshape(n, rows_d, 3 * HEAD),
        out_part,
        down_grad,
        gains,
        merged,
        7,
    )
    if merged:
        gate_grad, up_grad = (a.astype(F32) for a in assembled)
    else:
        _, pull_in = jax.vjp(lambda value: normed(value, attention_gain), tokens.astype(F32))
        (grad_source_part,) = pull_in(grad_in.astype(F32))
        grad_in = swapped_back((grad_mixed + grad_source_part).astype(BF16))
    down_grad = down_grad.astype(F32)
    qkv_got = jnp.sum(qkv_got.astype(F32).reshape(copies, HEADS, rows_d, 3 * HEAD), axis=0)
    query_grad = jnp.transpose(qkv_got[..., :HEAD], (1, 0, 2)).reshape(rows_d, HEADS * HEAD)
    kv_grad = jnp.sum(qkv_got[..., HEAD:].reshape(KV_HEADS, pairs, rows_d, 2 * HEAD), axis=1)
    key_grad = jnp.transpose(kv_grad[..., :HEAD], (1, 0, 2)).reshape(rows_d, KV_HEADS * HEAD)
    value_grad = jnp.transpose(kv_grad[..., HEAD:], (1, 0, 2)).reshape(rows_d, KV_HEADS * HEAD)
    out_grad = jnp.sum(out_got.astype(F32), axis=0)
    return (
        output,
        grad_in,
        query_grad,
        key_grad,
        value_grad,
        out_grad,
        gate_grad,
        up_grad,
        down_grad,
    ) + tuple(gains[i] for i in range(4))


def solution(mesh):
    rows = P("seq", None)
    return jax.shard_map(
        functools.partial(on_device, Grid(mesh.shape["seq"])),
        mesh=mesh,
        in_specs=(P("batch", "seq", None), P("batch", "seq"), P("batch", "seq"), P("batch", "seq", None))
        + (rows,) * 7
        + (P(),) * 11,
        out_specs=(P("batch", "seq", None),) * 2 + (rows,) * 7 + (P(),) * 4,
        check_vma=False,
    )
```
